32 devices in a mesh: blk: 8 (over y, x, core), head: 4 (over z).
Axes of the slice: x: 2, y: 2, z: 4, core: 2. Of those that a mesh axis runs over, the one named last changes fastest.
Arguments:
- tokens: bfloat16 [2, 2048, 768], P(None, ('blk', 'head')), may hold values from -6 to 6
- starts: int32 [2, 16], replicated, may hold values from 0 to 2047, as said below
- w_qkv: bfloat16 [768, 2304], P(('blk', 'head')), may hold values from -0.21875 to 0.21875
- bias_q: bfloat16 [768], P(('blk', 'head')), may hold values from -3 to 3
- bias_v: bfloat16 [768], P(('blk', 'head')), may hold values from -3 to 3
- w_out: bfloat16 [768, 768], P(('blk', 'head'))
- bias_out: bfloat16 [768], P(('blk', 'head')), may hold values from -3 to 3
- gain_one: bfloat16 [768], P(('blk', 'head')), may hold values from 0.25 to 1.75
- shift_one: bfloat16 [768], P(('blk', 'head')), may hold values from -3 to 3
- w_up: bfloat16 [768, 3072], P(('blk', 'head')), may hold values from -0.21875 to 0.21875
- bias_up: bfloat16 [3072], P(('blk', 'head')), may hold values from -3 to 3
- w_down: bfloat16 [3072, 768], P(('blk', 'head')), may hold values from -0.109375 to 0.109375
- bias_down: bfloat16 [768], P(('blk', 'head')), may hold values from -3 to 3
- gain_two: bfloat16 [768], P(('blk', 'head')), may hold values from 0.25 to 1.75
- shift_two: bfloat16 [768], P(('blk', 'head')), may hold values from -3 to 3
- cotangent: bfloat16 [2, 2048, 768], P(None, ('blk', 'head')), may hold values from -6 to 6
Outputs:
- output: float32 [2, 2048, 768], P(None, ('blk', 'head'))
- grad_tokens: float32 [2, 2048, 768], P(None, ('blk', 'head'))
- grad_w_qkv: float32 [768, 2304], P(('blk', 'head'))
- grad_bias_q: float32 [768], P(('blk', 'head'))
- grad_bias_v: float32 [768], P(('blk', 'head'))
- grad_w_out: float32 [768, 768], P(('blk', 'head'))
- grad_bias_out: float32 [768], P(('blk', 'head'))
- grad_gain_one: float32 [768], P(('blk', 'head'))
- grad_shift_one: float32 [768], P(('blk', 'head'))
- grad_w_up: float32 [768, 3072], P(('blk', 'head'))
- grad_bias_up: float32 [3072], P(('blk', 'head'))
- grad_w_down: float32 [3072, 768], P(('blk', 'head'))
- grad_bias_down: float32 [768], P(('blk', 'head'))
- grad_gain_two: float32 [768], P(('blk', 'head'))
- grad_shift_two: float32 [768], P(('blk', 'head'))
The draws below stay inside these ranges and needn't reach their ends.
Inputs may be any that keep to these rules, and one draw needn't show every extreme that they name: Each row of 16 document starts is strictly increasing and begins with 0. In one row, drawn from the seed, entry 7 lies below 256, entry 8 above 1792, and the last entry is 2047. In every other row consecutive starts, and the last start and 2048, lie at most 1024 apart, and exactly 1024 apart for one document of the row.
All inputs are finite; a program needn't handle non-finite values.
Results may differ from the reference program's by a relative error of at most 0.04.
Values may be sent and summed in bfloat16 or wider, within the bound.
A program may use at most 448 MiB of HBM per device.

```python
import math
import jax
import jax.numpy as jnp
from jax import lax

D = 768
H = 12
HD = 64
FF = 3072
MB = 2
NDOC = 16
BLK_TOK = 256
TOK_MB = 2048
DOC_MAX = 1024
N_BLK = 8


def spanning_row(key):
    first_key, last_key = jax.random.split(key)
    front = jnp.sort(jax.random.permutation(first_key, BLK_TOK - 1)[:NDOC // 2 - 1] + 1)
    back = jnp.sort(jax.random.permutation(last_key, BLK_TOK - 2)[:NDOC // 2 - 1] + (TOK_MB - BLK_TOK + 1))
    final = jnp.full((1,), TOK_MB - 1, jnp.int32)
    return jnp.concatenate([jnp.zeros((1,), jnp.int32), front.astype(jnp.int32), back.astype(jnp.int32), final])


def packed_row(key):
    pick_key, cut_key = jax.random.split(key)
    remaining = TOK_MB - DOC_MAX
    stride = remaining // (NDOC - 1)
    jitter = jax.random.randint(cut_key, (NDOC - 2,), 0, max(stride // 2, 1)).astype(jnp.int32)
    inner = jnp.arange(1, NDOC - 1, dtype=jnp.int32) * stride + jitter
    cuts = jnp.concatenate([jnp.zeros((1,), jnp.int32), inner, jnp.full((1,), remaining, jnp.int32)])
    others = cuts[1:] - cuts[:-1]
    longest = jax.random.randint(pick_key, (), 0, NDOC).astype(jnp.int32)
    index = jnp.arange(NDOC, dtype=jnp.int32)
    source = jnp.clip(jnp.where(index < longest, index, index - 1), 0, NDOC - 2).astype(jnp.int32)
    lengths = jnp.where(index == longest, jnp.int32(DOC_MAX), others[source]).astype(jnp.int32)
    ends = jnp.cumsum(lengths).astype(jnp.int32)
    return jnp.concatenate([jnp.zeros((1,), jnp.int32), ends[:-1]])


def draw_starts(key, part):
    chosen = jax.random.randint(jax.random.fold_in(key, 7), (), 0, MB).astype(jnp.int32)
    rows_out = []
    for part_index in range(MB):
        long_key, short_key = jax.random.split(jax.random.fold_in(key, part_index + 11))
        rows_out.append(jnp.where(chosen == part_index, spanning_row(long_key), packed_row(short_key)))
    return jnp.stack(rows_out)


def draw_w_out(key, part):
    spread = math.sqrt(TOK_MB / (3.0 * D * math.sqrt(NDOC)))
    return (jax.random.normal(key, (D, D), jnp.float32) * spread).astype(jnp.bfloat16)


def steps_of(rng, extent, cuts, smallest, largest):
    factor_of = 1.0
    for dim, parts in cuts:
        draws = jax.random.uniform(jax.random.fold_in(jax.random.fold_in(rng, 6), dim), (parts,), jnp.float32, smallest / len(cuts), largest / len(cuts))
        factor_of = factor_of * jnp.repeat(jnp.exp(draws), extent[dim] // parts).reshape((-1,) + (1,) * (len(extent) - 1 - dim))
    return factor_of


def noise(stream_key, shape, scale, bound, pieces=(), kind=jnp.bfloat16):
    values = scale * jax.random.normal(stream_key, shape, jnp.float32)
    if pieces:
        values = values * steps_of(stream_key, shape, pieces, -0.22, 0.18)
    return jnp.clip(values, -bound, bound).astype(kind)


def setup_inputs(seed: int = 0) -> dict:
    arg_keys = jax.random.split(jax.random.key(seed), 17)
    return {
        "tokens": noise(arg_keys[0], (MB, TOK_MB, D), 1.0, 6.0, ((1, 32),)),
        "starts": draw_starts(jax.random.fold_in(arg_keys[16], 71), 0),
        "w_qkv": noise(arg_keys[2], (D, 3 * D), D ** -0.5, 0.21875, ((0, 32),)),
        "bias_q": noise(arg_keys[3], (D,), 0.5, 3.0, ((0, 32),)),
        "bias_v": noise(arg_keys[4], (D,), 0.5, 3.0, ((0, 32),)),
        "w_out": draw_w_out(jax.random.fold_in(arg_keys[16], 71), 0),
        "bias_out": noise(arg_keys[6], (D,), 0.5, 3.0, ((0, 32),)),
        "gain_one": jnp.clip(1.0 + 0.15 * jax.random.normal(arg_keys[7], (D,), jnp.float32), 0.25, 1.75).astype(jnp.bfloat16),
        "shift_one": noise(arg_keys[8], (D,), 0.5, 3.0, ((0, 32),)),
        "w_up": noise(arg_keys[9], (D, FF), D ** -0.5, 0.21875, ((0, 32),)),
        "bias_up": noise(arg_keys[10], (FF,), 0.5, 3.0, ((0, 32),)),
        "w_down": noise(arg_keys[11], (FF, D), FF ** -0.5, 0.109375, ((0, 32),)),
        "bias_down": noise(arg_keys[12], (D,), 0.5, 3.0, ((0, 32),)),
        "gain_two": jnp.clip(1.0 + 0.15 * jax.random.normal(arg_keys[13], (D,), jnp.float32), 0.25, 1.75).astype(jnp.bfloat16),
        "shift_two": noise(arg_keys[14], (D,), 0.5, 3.0, ((0, 32),)),
        "cotangent": noise(arg_keys[15], (MB, TOK_MB, D), 1.0, 6.0, ((1, 32),)),
    }


EPS = 1e-05
NEG = -1e+30
HIGH = lax.Precision.HIGHEST

@jax.custom_vjp
def low(v):
    return lax.optimization_barrier(v.astype(jnp.bfloat16)).astype(jnp.float32)

@jax.custom_vjp
def low_back(v):
    return v

def low_keep(v):
    return (low(v), None)

def low_pass(kept, grad):
    return (grad,)

def back_keep(v):
    return (v, None)

def back_low(kept, grad):
    return (low(grad),)
low.defvjp(low_keep, low_pass)
low_back.defvjp(back_keep, back_low)

def narrow_both(values):
    return low(low_back(values))

def layer_norm(values, gain_vec, shift_vec):
    center = values - lax.optimization_barrier(jnp.mean(values, axis=-1, keepdims=True))
    inverse = lax.rsqrt(lax.optimization_barrier(jnp.mean(center * center, axis=-1, keepdims=True)) + EPS)
    return center * inverse * gain_vec + shift_vec

def segment_of(starts_row, positions):
    return lax.optimization_barrier(jnp.sum((starts_row[None, :] <= positions[:, None]).astype(jnp.int32), axis=1)) - 1

def block_attention(query_block, query_doc, key_heads, value_heads, key_doc):
    scores = jnp.einsum('qhd,khd->hqk', query_block, key_heads, precision=HIGH) * HD ** (-0.5)
    scores = low_back(jnp.where((query_doc[:, None] == key_doc[None, :])[None], scores, NEG))
    row_top = lax.optimization_barrier(jnp.max(scores, axis=-1, keepdims=True))
    exp_score = jnp.exp(scores - row_top)
    row_total = lax.optimization_barrier(jnp.sum(exp_score, axis=-1, keepdims=True))
    numer = low_back(jnp.einsum('hqk,khd->qhd', low(exp_score), value_heads, precision=HIGH))
    return numer / jnp.transpose(row_total, (1, 0, 2))

def forward_part(inputs, starts_row, params):
    w_qkv, bias_q, bias_v, w_out, bias_out, gain_one, shift_one, w_up, bias_up, w_down, bias_down, gain_two, shift_two = params
    projected = jnp.dot(inputs, w_qkv, precision=HIGH)
    query_rows = narrow_both(projected[:, :D] + bias_q)
    key_rows = narrow_both(projected[:, D:2 * D])
    value_rows = narrow_both(projected[:, 2 * D:] + bias_v)
    doc_ids = segment_of(starts_row, jnp.arange(TOK_MB, dtype=jnp.int32))
    key_heads = key_rows.reshape(TOK_MB, H, HD)
    value_heads = value_rows.reshape(TOK_MB, H, HD)

    def one_block(entry_pair):
        return block_attention(entry_pair[0], entry_pair[1], key_heads, value_heads, doc_ids)
    attended = lax.map(jax.checkpoint(one_block), (query_rows.reshape(N_BLK, BLK_TOK, H, HD), doc_ids.reshape(N_BLK, BLK_TOK)))
    mixed_heads = narrow_both(attended.reshape(TOK_MB, D))
    attn_out = low_back(jnp.dot(mixed_heads, w_out, precision=HIGH) + bias_out)
    first_norm = layer_norm(inputs + attn_out, gain_one, shift_one)
    hidden = low_back(jnp.dot(low(first_norm), w_up, precision=HIGH) + bias_up)
    active = low(jax.nn.gelu(hidden, approximate=False))
    ffn_out = low_back(jnp.dot(active, w_down, precision=HIGH) + bias_down)
    return layer_norm(first_norm + ffn_out, gain_two, shift_two)

def reference(tokens, starts, w_qkv, bias_q, bias_v, w_out, bias_out, gain_one, shift_one, w_up, bias_up, w_down, bias_down, gain_two, shift_two, cotangent):
    weights = tuple((param.astype(jnp.float32) for param in (w_qkv, bias_q, bias_v, w_out, bias_out, gain_one, shift_one, w_up, bias_up, w_down, bias_down, gain_two, shift_two)))

    def whole(inputs, *params):
        return jnp.stack([forward_part(inputs[part_index], starts[part_index], params) for part_index in range(MB)])
    output, pull = jax.vjp(whole, tokens.astype(jnp.float32), *weights)
    grad_list = pull(cotangent.astype(jnp.float32))
    return (output, grad_list[0], grad_list[1], grad_list[2], grad_list[3], grad_list[4], grad_list[5], grad_list[6], grad_list[7], grad_list[8], grad_list[9], grad_list[10], grad_list[11], grad_list[12], grad_list[13])
```

```python
from functools import partial
from types import SimpleNamespace

import jax
import jax.numpy as jnp
from jax import lax
from jax.experimental import pallas as pl
from jax.experimental.pallas import tpu as pltpu
from jax.sharding import PartitionSpec as P

BLK = "blk"
HEAD = "head"
BOTH = (BLK, HEAD)
H = 12
HD = 64
MB = 2


EPS = 1e-05
NEG = -1e30


def norm_forward(values, gain_vec, shift_vec):
    center = values - jnp.mean(values, axis=-1, keepdims=True)
    inverse = lax.rsqrt(jnp.mean(center * center, axis=-1, keepdims=True) + EPS)
    normed = center * inverse
    return (normed * gain_vec + shift_vec, normed, inverse)


def norm_backward(upstream, normed, inverse, gain_vec):
    scaled = upstream * gain_vec
    inner = (
        scaled
        - jnp.mean(scaled, axis=-1, keepdims=True)
        - normed * jnp.mean(scaled * normed, axis=-1, keepdims=True)
    )
    return inner * inverse


def segment_of(starts_row, positions):
    return jnp.sum((starts_row[None, :] <= positions[:, None]).astype(jnp.int32), axis=1) - 1


def masked_scores(query_heads, key_heads, in_doc):
    scores = jnp.einsum(
        "qhd,khd->hqk", query_heads, key_heads, preferred_element_type=jnp.float32
    ) * HD ** (-0.5)
    return jnp.where(in_doc, scores, NEG)


def score_grads(query_heads, key_heads, value_heads, grad_numer, row_top, correction, in_doc):
    exp_score = jnp.where(
        in_doc, jnp.exp(masked_scores(query_heads, key_heads, in_doc) - row_top), 0.0
    )
    grad_weights = jnp.einsum(
        "qhd,khd->hqk", grad_numer, value_heads, preferred_element_type=jnp.float32
    )
    grad_scores = (exp_score * (grad_weights - correction)).astype(jnp.bfloat16)
    return (exp_score.astype(jnp.bfloat16), grad_scores)


def scatter_end(parts):
    (
        grad_proj_in,
        grad_query_bias,
        grad_value_bias,
        grad_proj_out,
        grad_out_bias,
        grad_norm_gain,
        grad_norm_shift,
        grad_up,
        grad_up_bias,
        grad_down,
        grad_down_bias,
        grad_final_gain,
        grad_final_shift,
    ) = parts
    return (
        lax.psum_scatter(grad_proj_in, BOTH, scatter_dimension=0, tiled=True),
        lax.psum_scatter(grad_query_bias, BOTH, scatter_dimension=0, tiled=True),
        lax.psum_scatter(grad_value_bias, BOTH, scatter_dimension=0, tiled=True),
        lax.psum_scatter(grad_proj_out, BOTH, scatter_dimension=0, tiled=True),
        lax.psum_scatter(grad_out_bias, BOTH, scatter_dimension=0, tiled=True),
        lax.psum_scatter(grad_norm_gain, BOTH, scatter_dimension=0, tiled=True),
        lax.psum_scatter(grad_norm_shift, BOTH, scatter_dimension=0, tiled=True),
        lax.psum_scatter(grad_up, BOTH, scatter_dimension=0, tiled=True),
        lax.psum_scatter(grad_up_bias, BOTH, scatter_dimension=0, tiled=True),
        lax.psum_scatter(grad_down, BOTH, scatter_dimension=0, tiled=True),
        lax.psum_scatter(grad_down_bias, BOTH, scatter_dimension=0, tiled=True),
        lax.psum_scatter(grad_final_gain, BOTH, scatter_dimension=0, tiled=True),
        lax.psum_scatter(grad_final_shift, BOTH, scatter_dimension=0, tiled=True),
    )


def per_device(
    tokens,
    starts,
    w_qkv,
    bias_q,
    bias_v,
    w_out,
    bias_out,
    gain_one,
    shift_one,
    w_up,
    bias_up,
    w_down,
    bias_down,
    gain_two,
    shift_two,
    cotangent,
):
    (
        proj_in,
        query_bias,
        value_bias,
        proj_out,
        out_bias,
        norm_gain,
        norm_shift,
        up_full,
        up_bias,
        down_full,
        down_bias,
        final_gain,
        final_shift,
    ) = (
        lax.all_gather(w_qkv, BOTH, axis=0, tiled=True),
        lax.all_gather(bias_q, BOTH, axis=0, tiled=True),
        lax.all_gather(bias_v, BOTH, axis=0, tiled=True),
        lax.all_gather(w_out, BOTH, axis=0, tiled=True),
        lax.all_gather(bias_out, BOTH, axis=0, tiled=True),
        lax.all_gather(gain_one, BOTH, axis=0, tiled=True),
        lax.all_gather(shift_one, BOTH, axis=0, tiled=True),
        lax.all_gather(w_up, BOTH, axis=0, tiled=True),
        lax.all_gather(bias_up, BOTH, axis=0, tiled=True),
        lax.all_gather(w_down, BOTH, axis=0, tiled=True),
        lax.all_gather(bias_down, BOTH, axis=0, tiled=True),
        lax.all_gather(gain_two, BOTH, axis=0, tiled=True),
        lax.all_gather(shift_two, BOTH, axis=0, tiled=True),
    )
    query_bias = query_bias.astype(jnp.float32)
    value_bias = value_bias.astype(jnp.float32)
    out_bias = out_bias.astype(jnp.float32)
    norm_gain = norm_gain.astype(jnp.float32)
    norm_shift = norm_shift.astype(jnp.float32)
    up_bias = up_bias.astype(jnp.float32)
    down_bias = down_bias.astype(jnp.float32)
    final_gain = final_gain.astype(jnp.float32)
    final_shift = final_shift.astype(jnp.float32)
    model_width = proj_out.shape[0]
    row_count = tokens.shape[1]
    head_count = lax.axis_size(HEAD)
    block_rows = row_count * head_count
    heads_dev = H // head_count
    local_width = heads_dev * HD
    scale = HD ** (-0.5)
    local_pos = lax.axis_index(BLK) * block_rows + jnp.arange(block_rows, dtype=jnp.int32)
    kept_list = []
    outputs = []
    for part_index in range(MB):
        inputs = tokens[part_index]
        starts_row = starts[part_index]
        projected = jnp.dot(inputs, proj_in, preferred_element_type=jnp.float32)
        query_rows = (projected[:, :model_width] + query_bias).astype(jnp.bfloat16)
        key_rows = projected[:, model_width : 2 * model_width].astype(jnp.bfloat16)
        value_rows = (projected[:, 2 * model_width :] + value_bias).astype(jnp.bfloat16)
        query_loc, key_loc, value_loc = (
            lax.all_to_all(query_rows, HEAD, split_axis=1, concat_axis=0, tiled=True),
            lax.all_to_all(key_rows, HEAD, split_axis=1, concat_axis=0, tiled=True),
            lax.all_to_all(value_rows, HEAD, split_axis=1, concat_axis=0, tiled=True),
        )
        doc_local = segment_of(starts_row, local_pos)
        query_heads = query_loc.reshape(block_rows, heads_dev, HD)

        def fold_keys(running, portion):
            row_top, row_total, weighted = running
            key_part, value_part = portion
            piece_len = key_part.shape[0]
            key_doc = segment_of(starts_row, jnp.arange(piece_len, dtype=jnp.int32))
            in_doc = (doc_local[:, None] == key_doc[None, :])[None]
            scores = masked_scores(query_heads, key_part.reshape(piece_len, heads_dev, HD), in_doc)
            new_top = jnp.maximum(row_top, jnp.max(scores, axis=-1, keepdims=True))
            exp_score = jnp.where(in_doc, jnp.exp(scores - new_top), 0.0)
            row_total = jnp.sum(exp_score, axis=-1, keepdims=True)
            weighted = jnp.einsum(
                "hqk,khd->hqd",
                exp_score.astype(jnp.bfloat16),
                value_part.reshape(piece_len, heads_dev, HD),
                preferred_element_type=jnp.float32,
            )
            return (new_top, row_total, weighted)

        start_state = (
            jnp.full((heads_dev, block_rows, 1), NEG, jnp.float32),
            jnp.zeros((heads_dev, block_rows, 1), jnp.float32),
            jnp.zeros((heads_dev, block_rows, HD), jnp.float32),
        )
        row_top, row_total, weighted = fold_keys(
            start_state,
            (
                lax.all_gather(key_loc, BLK, axis=0, tiled=True),
                lax.all_gather(value_loc, BLK, axis=0, tiled=True),
            ),
        )
        attended = jnp.transpose(weighted / row_total, (1, 0, 2))
        mixed_rows = lax.all_to_all(
            attended.reshape(block_rows, local_width).astype(jnp.bfloat16),
            HEAD,
            split_axis=0,
            concat_axis=1,
            tiled=True,
        )
        attn_out = jnp.dot(mixed_rows, proj_out, preferred_element_type=jnp.float32) + out_bias
        first_norm, normed_one, inverse_one = norm_forward(
            inputs.astype(jnp.float32) + attn_out, norm_gain, norm_shift
        )
        first_low = first_norm.astype(jnp.bfloat16)
        hidden = jnp.dot(first_low, up_full, preferred_element_type=jnp.float32) + up_bias
        active = jax.nn.gelu(hidden, approximate=False).astype(jnp.bfloat16)
        ffn_out = jnp.dot(active, down_full, preferred_element_type=jnp.float32) + down_bias
        result, normed_two, inverse_two = norm_forward(
            first_norm + ffn_out, final_gain, final_shift
        )
        outputs.append(result)
        kept_list.append(
            (
                inputs,
                starts_row,
                query_loc,
                key_loc,
                value_loc,
                doc_local,
                row_top,
                row_total,
                attended,
                mixed_rows,
                normed_one,
                inverse_one,
                first_low,
                hidden,
                active,
                normed_two,
                inverse_two,
            )
        )
    input_grads = []
    grad_sum = None
    for part_index in range(MB):
        (
            inputs,
            starts_row,
            query_loc,
            key_loc,
            value_loc,
            doc_local,
            row_top,
            row_total,
            attended,
            mixed_rows,
            normed_one,
            inverse_one,
            first_low,
            hidden,
            active,
            normed_two,
            inverse_two,
        ) = kept_list[part_index]
        grad_result = cotangent[part_index].astype(jnp.float32)
        grad_final_gain = jnp.sum(grad_result * normed_two, axis=0)
        grad_final_shift = jnp.sum(grad_result, axis=0)
        grad_two = norm_backward(grad_result, normed_two, inverse_two, final_gain)
        grad_ffn = grad_two.astype(jnp.bfloat16)
        grad_down_bias = jnp.sum(grad_ffn.astype(jnp.float32), axis=0)
        grad_down = jnp.einsum("rf,rd->fd", active, grad_ffn, preferred_element_type=jnp.float32)
        grad_active = jnp.einsum(
            "rd,fd->rf", grad_ffn, down_full, preferred_element_type=jnp.float32
        )
        gelu_pull = jax.vjp(partial(jax.nn.gelu, approximate=False), hidden)[1]
        grad_hidden = gelu_pull(grad_active)[0].astype(jnp.bfloat16)
        grad_up_bias = jnp.sum(grad_hidden.astype(jnp.float32), axis=0)
        grad_up = jnp.einsum(
            "rd,rf->df", first_low, grad_hidden, preferred_element_type=jnp.float32
        )
        grad_first = grad_two + jnp.einsum(
            "rf,df->rd", grad_hidden, up_full, preferred_element_type=jnp.float32
        )
        grad_norm_gain = jnp.sum(grad_first * normed_one, axis=0)
        grad_norm_shift = jnp.sum(grad_first, axis=0)
        grad_one = norm_backward(grad_first, normed_one, inverse_one, norm_gain)
        grad_attn = grad_one.astype(jnp.bfloat16)
        grad_out_bias = jnp.sum(grad_attn.astype(jnp.float32), axis=0)
        grad_proj_out = jnp.einsum(
            "rc,rd->cd", mixed_rows, grad_attn, preferred_element_type=jnp.float32
        )
        grad_mixed = jnp.einsum(
            "rd,cd->rc", grad_attn, proj_out, preferred_element_type=jnp.float32
        ).astype(jnp.bfloat16)
        grad_loc = lax.all_to_all(grad_mixed, HEAD, split_axis=1, concat_axis=0, tiled=True)
        grad_heads = grad_loc.astype(jnp.float32).reshape(block_rows, heads_dev, HD)
        total_rows = jnp.transpose(row_total, (1, 0, 2))
        correction = jnp.transpose(
            jnp.sum(grad_heads * attended, axis=-1, keepdims=True) / total_rows, (1, 0, 2)
        )
        grad_numer = (grad_heads / total_rows).astype(jnp.bfloat16)
        query_heads = query_loc.reshape(block_rows, heads_dev, HD)
        key_heads_loc = key_loc.reshape(block_rows, heads_dev, HD)
        value_heads_loc = value_loc.reshape(block_rows, heads_dev, HD)
        fold_key_part = lax.all_gather(key_loc, BLK, axis=0, tiled=True)
        fold_value_part = lax.all_gather(value_loc, BLK, axis=0, tiled=True)
        fold_piece_len = fold_key_part.shape[0]
        fold_key_doc = segment_of(starts_row, jnp.arange(fold_piece_len, dtype=jnp.int32))
        fold_in_doc = (doc_local[:, None] == fold_key_doc[None, :])[None]
        key_heads = fold_key_part.reshape(fold_piece_len, heads_dev, HD)
        exp_low, grad_scores = score_grads(
            query_heads,
            key_heads,
            fold_value_part.reshape(fold_piece_len, heads_dev, HD),
            grad_numer,
            row_top,
            correction,
            fold_in_doc,
        )
        grad_query = (
            jnp.einsum("hqk,khd->qhd", grad_scores, key_heads, preferred_element_type=jnp.float32)
            * scale
        )
        top_rows = jnp.transpose(row_top[:, :, 0])
        corr_rows = jnp.transpose(correction[:, :, 0])

        def fold_keygrad(portion):
            query_part, numer_part, top_part, corr_part = portion
            piece_len = query_part.shape[0]
            query_doc = segment_of(starts_row, jnp.arange(piece_len, dtype=jnp.int32))
            in_doc = (query_doc[:, None] == doc_local[None, :])[None]
            query_piece = query_part.reshape(piece_len, heads_dev, HD)
            numer_piece = numer_part.reshape(piece_len, heads_dev, HD)
            exp_low, grad_scores = score_grads(
                query_piece,
                key_heads_loc,
                value_heads_loc,
                numer_piece,
                jnp.transpose(top_part)[:, :, None],
                jnp.transpose(corr_part)[:, :, None],
                in_doc,
            )
            grad_key_run = (
                jnp.einsum(
                    "hqk,qhd->khd", grad_scores, query_piece, preferred_element_type=jnp.float32
                )
                * scale
            )
            grad_value_run = jnp.einsum(
                "hqk,qhd->khd", exp_low, numer_piece, preferred_element_type=jnp.float32
            )
            return (grad_key_run, grad_value_run)

        grad_key, grad_value = fold_keygrad(
            (
                lax.all_gather(query_loc, BLK, axis=0, tiled=True),
                lax.all_gather(
                    grad_numer.reshape(block_rows, local_width), BLK, axis=0, tiled=True
                ),
                lax.all_gather(top_rows.astype(jnp.bfloat16), BLK, axis=0, tiled=True).astype(
                    jnp.float32
                ),
                lax.all_gather(corr_rows.astype(jnp.bfloat16), BLK, axis=0, tiled=True).astype(
                    jnp.float32
                ),
            )
        )
        grad_q_rows, grad_k_rows, grad_v_rows = (
            lax.all_to_all(
                grad_query.reshape(block_rows, local_width).astype(jnp.bfloat16),
                HEAD,
                split_axis=0,
                concat_axis=1,
                tiled=True,
            ),
            lax.all_to_all(
                grad_key.reshape(block_rows, local_width).astype(jnp.bfloat16),
                HEAD,
                split_axis=0,
                concat_axis=1,
                tiled=True,
            ),
            lax.all_to_all(
                grad_value.reshape(block_rows, local_width).astype(jnp.bfloat16),
                HEAD,
                split_axis=0,
                concat_axis=1,
                tiled=True,
            ),
        )
        grad_proj = jnp.concatenate([grad_q_rows, grad_k_rows, grad_v_rows], axis=1)
        grad_query_bias = jnp.sum(grad_q_rows.astype(jnp.float32), axis=0)
        grad_value_bias = jnp.sum(grad_v_rows.astype(jnp.float32), axis=0)
        grad_proj_in = jnp.einsum(
            "rd,re->de", inputs, grad_proj, preferred_element_type=jnp.float32
        )
        input_grads.append(
            grad_one
            + jnp.einsum("re,de->rd", grad_proj, proj_in, preferred_element_type=jnp.float32)
        )
        part_grads = (
            grad_proj_in,
            grad_query_bias,
            grad_value_bias,
            grad_proj_out,
            grad_out_bias,
            grad_norm_gain,
            grad_norm_shift,
            grad_up,
            grad_up_bias,
            grad_down,
            grad_down_bias,
            grad_final_gain,
            grad_final_shift,
        )
        grad_sum = (
            part_grads
            if grad_sum is None
            else tuple((left + right for left, right in zip(grad_sum, part_grads)))
        )
    grad_sum = scatter_end(grad_sum)
    (
        grad_proj_in,
        grad_query_bias,
        grad_value_bias,
        grad_proj_out,
        grad_out_bias,
        grad_norm_gain,
        grad_norm_shift,
        grad_up,
        grad_up_bias,
        grad_down,
        grad_down_bias,
        grad_final_gain,
        grad_final_shift,
    ) = grad_sum
    return (
        jnp.stack(outputs),
        jnp.stack(input_grads),
        grad_proj_in,
        grad_query_bias,
        grad_value_bias,
        grad_proj_out,
        grad_out_bias,
        grad_norm_gain,
        grad_norm_shift,
        grad_up,
        grad_up_bias,
        grad_down,
        grad_down_bias,
        grad_final_gain,
        grad_final_shift,
    )


MESH = pl.DeviceIdType.MESH
F32 = jnp.float32
BF16 = jnp.bfloat16
DM = 768
FF = 3072
TOK = 64
SEQ = 2048
HALF = DM // 2
QKV_N = 3 * HALF
UP_N = FF // 2
CHUNK = 256

QKV, OUT, UP, DOWN = range(4)
SHAPES = (
    (4, 2, 4, 24, QKV_N),
    (4, 4, 24, DM),
    (4, 2, 4, 24, UP_N),
    (4, 4, 96, DM),
)


def by_column(kind):
    return kind in (QKV, UP)


def half_shape(kind):
    shape = SHAPES[kind]
    return shape[2:] if by_column(kind) else (2,) + shape[2:]


def piece_shape(kind):
    shape = SHAPES[kind]
    return (2,) + shape[3:] if by_column(kind) else shape[2:]


def when(cond, run):
    if cond is None:
        run()
    else:
        pl.when(cond)(run)


def both(left, right):
    if left is None:
        return right
    if right is None:
        return left
    return jnp.logical_and(left, right)


class Place:
    def __init__(self):
        b = lax.axis_index(BLK)
        z = lax.axis_index(HEAD)
        c = lax.rem(b, 2)
        x = lax.rem(lax.div(b, 2), 2)
        y = lax.div(b, 4)
        self.b, self.z, self.c, self.x, self.y = b, z, c, x, y
        self.line = 4 * b + z
        self.chip = 4 * lax.div(b, 2) + z
        self.sib = (b + 1 - 2 * c, z)
        self.dx = (4 * y + 2 * (1 - x) + c, z)
        self.dy = (4 * (1 - y) + 2 * x + c, z)
        self.up = (b, jnp.minimum(z + 1, 3))
        self.down = (b, jnp.maximum(z - 1, 0))
        self.swap = (4 * c + 2 * x + y, z)
        self.stays = y == c
        self.moves = y != c
        self.not_top = z < 3
        self.not_bottom = z > 0
        q = 2 * y + x
        self.q = q
        turn = lax.rem(q - z + 4, 4)
        self.active = turn < 3
        self.pair = jnp.where(self.active, 4 * turn + z, 0)
        self.part = lax.div(self.pair, 6)

    def cols(self, kind):
        x, y = self.x, self.y
        if by_column(kind):
            return (2 * y + x, 2 * y + 1 - x, 2 * (1 - y) + x, 2 * (1 - y) + 1 - x)
        return (2 * x + y, 2 * (1 - x) + y, 2 * x + 1 - y, 2 * (1 - x) + 1 - y)


def pair_place(pair):
    z = pair % 4
    return ((pair // 4 + z) % 4, z)


def chunk(kind, ref, col, z):
    return ref.at[col, :, z] if by_column(kind) else ref.at[col, z]


def half(kind, ref, col, h):
    return ref.at[col, h] if by_column(kind) else ref.at[col, pl.ds(2 * h, 2)]


class Links:
    def __init__(self, sems, here):
        self.sems, self.here, self.count, self.pending = sems, here, 0, []

    def alloc(self, n=1):
        at = self.count
        self.count += n
        return at

    def make(self, src, dst, s, r, dev):
        return pltpu.make_async_remote_copy(
            src_ref=src, dst_ref=dst, send_sem=self.sems.at[s], recv_sem=self.sems.at[r],
            device_id=dev, device_id_type=MESH,
        )

    def send(self, src, dst, s, r, dev, cond=None, keep=True):
        when(cond, lambda: self.make(src, dst, s, r, dev).start())
        if keep:
            self.pending.append((cond, src, dst, s, r, dev))

    def recv(self, dst, r, cond=None):
        when(cond, lambda: self.make(dst, dst, r, r, self.here.sib).wait_recv())

    def sent(self, src, dst, s, r, dev, cond=None):
        when(cond, lambda: self.make(src, dst, s, r, dev).wait_send())

    def finish(self):
        for cond, src, dst, s, r, dev in self.pending:
            self.sent(src, dst, s, r, dev, cond)
        self.pending = []


class Gather:
    def __init__(self, links, here, kind, ref):
        self.links, self.here, self.kind, self.ref = links, here, kind, ref
        self.s0, self.r0 = links.alloc(), links.alloc()
        self.su, self.sd, self.rz = links.alloc(4), links.alloc(4), links.alloc(4)
        self.s_col = links.alloc(4)
        self.r_col = links.alloc(4)
        self.col, self.col_x, self.col_y, self.col_d = here.cols(kind)

    def first_wait(self):
        here, kind = self.here, self.kind
        if by_column(kind):
            self.links.recv(self.ref.at[self.col, 1 - here.c, here.z], self.r0)
        else:
            self.links.recv(self.ref.at[self.col, here.z], self.r0, here.moves)

    def z_hop(self, z, up, cond):
        piece = chunk(self.kind, self.ref, self.col, z)
        base = self.su if up else self.sd
        self.links.send(piece, piece, base + z, self.rz + z, self.here.up if up else self.here.down, cond)

    def z_own(self):
        self.first_wait()
        here = self.here
        self.z_hop(here.z, True, here.not_top)
        self.z_hop(here.z, False, here.not_bottom)

    def z_relay(self, r):
        here = self.here
        from_below = here.z >= r
        from_above = here.z <= 3 - r
        low = jnp.maximum(here.z - r, 0)
        high = jnp.minimum(here.z + r, 3)
        self.links.recv(chunk(self.kind, self.ref, self.col, low), self.rz + low, from_below)
        if r < 3:
            self.z_hop(low, True, both(from_below, here.not_top))
        self.links.recv(chunk(self.kind, self.ref, self.col, high), self.rz + high, from_above)
        if r < 3:
            self.z_hop(high, False, both(from_above, here.not_bottom))

    def plane_send(self):
        piece = self.ref.at[self.col]
        self.links.send(piece, piece, self.s_col, self.r_col, self.here.dx)
        self.links.send(piece, piece, self.s_col + 1, self.r_col + 1, self.here.dy)

    def plane_relay(self):
        self.links.recv(self.ref.at[self.col_x], self.r_col)
        piece = half(self.kind, self.ref, self.col_x, 0)
        self.links.send(piece, piece, self.s_col + 2, self.r_col + 2, self.here.dy)
        self.links.recv(self.ref.at[self.col_y], self.r_col + 1)
        piece = half(self.kind, self.ref, self.col_y, 1)
        self.links.send(piece, piece, self.s_col + 3, self.r_col + 3, self.here.dx)

    def plane_done(self):
        self.links.recv(half(self.kind, self.ref, self.col_d, 0), self.r_col + 2)
        self.links.recv(half(self.kind, self.ref, self.col_d, 1), self.r_col + 3)


def add_into(dst, terms, steps):
    def one(i, carry):
        total = terms[0][i].astype(F32)
        for term in terms[1:]:
            total = total + term[i].astype(F32)
        dst[i] = total.astype(dst.dtype)
        return carry

    lax.fori_loop(0, steps, one, 0)


class Scatter:
    def __init__(self, links, here, kind, refs):
        self.links, self.here, self.kind = links, here, kind
        self.grad, self.rx, self.ry, self.cx, self.cy, self.zb, self.zu, self.zd, self.fin, self.last = refs
        self.s = links.alloc(6)
        self.r = links.alloc(6)
        self.su, self.ru = links.alloc(4), links.alloc(4)
        self.sd, self.rd = links.alloc(4), links.alloc(4)
        self.s_end, self.r_end = links.alloc(), links.alloc()
        self.col, self.col_x, self.col_y, self.col_d = here.cols(kind)

    def half_of(self, ref, h):
        return ref.at[h] if by_column(self.kind) else ref.at[pl.ds(2 * h, 2)]

    def plane_send(self):
        links, here, kind = self.links, self.here, self.kind
        s, r = self.s, self.r
        links.send(half(kind, self.grad, self.col_d, 0), self.rx, s, r, here.dx)
        links.send(half(kind, self.grad, self.col_d, 1), self.ry, s + 1, r + 1, here.dy)
        links.send(half(kind, self.grad, self.col_x, 0), self.half_of(self.cx, 0), s + 2, r + 2, here.dx)
        links.send(half(kind, self.grad, self.col_y, 1), self.half_of(self.cy, 1), s + 3, r + 3, here.dy)

    def plane_relay(self):
        links, here, kind = self.links, self.here, self.kind
        steps = half_shape(kind)[0]
        s, r = self.s, self.r
        links.recv(self.rx, r)
        piece = half(kind, self.grad, self.col_y, 0)
        add_into(piece, (piece, self.rx), steps)
        links.send(piece, self.half_of(self.cy, 0), s + 4, r + 4, here.dy)
        links.recv(self.ry, r + 1)
        piece = half(kind, self.grad, self.col_x, 1)
        add_into(piece, (piece, self.ry), steps)
        links.send(piece, self.half_of(self.cx, 1), s + 5, r + 5, here.dx)

    def plane_done(self):
        links, kind = self.links, self.kind
        r = self.r
        links.recv(self.half_of(self.cx, 0), r + 2)
        links.recv(self.half_of(self.cy, 1), r + 3)
        links.recv(self.half_of(self.cy, 0), r + 4)
        links.recv(self.half_of(self.cx, 1), r + 5)
        own = self.grad.at[self.col]
        if by_column(kind):
            for h in range(2):
                add_into(self.zb.at[h], (own.at[h], self.cx.at[h], self.cy.at[h]), 4)
        else:
            add_into(self.zb, (own, self.cx, self.cy), 4)

    def z_piece(self, z):
        return self.zb.at[:, z] if by_column(self.kind) else self.zb.at[z]

    def z_add(self, z, other):
        if by_column(self.kind):
            for h in range(2):
                self.zb[h, z] = (self.zb[h, z].astype(F32) + other[z, h].astype(F32)).astype(BF16)
        else:
            self.zb[z] = (self.zb[z].astype(F32) + other[z].astype(F32)).astype(BF16)

    def z_step(self, target, up):
        links, here = self.links, self.here
        if up:
            cond, more, buf, s, r, dev = here.z < target, here.not_bottom, self.zu, self.su, self.ru, here.up
        else:
            cond, more, buf, s, r, dev = here.z > target, here.not_top, self.zd, self.sd, self.rd, here.down

        def add():
            self.z_add(target, buf)

        links.recv(buf.at[target], r + target, both(cond, more))
        when(both(cond, more), add)
        links.send(self.z_piece(target), buf.at[target], s + target, r + target, dev, cond)

    def z_first(self):
        for target, up in ((3, True), (0, False), (2, True), (1, False), (1, True), (2, False)):
            self.z_step(target, up)

    def z_last(self):
        links, here = self.links, self.here
        z = here.z
        links.recv(self.zu.at[z], self.ru + z, here.not_bottom)
        links.recv(self.zd.at[z], self.rd + z, here.not_top)
        if by_column(self.kind):
            for h in range(2):
                self.fin[h] = self.zb[h, z].astype(F32)
        else:
            self.fin[...] = self.zb[z].astype(F32)

        def add_low():
            self.fin[...] += self.zu[z].astype(F32)

        def add_high():
            self.fin[...] += self.zd[z].astype(F32)

        when(here.not_bottom, add_low)
        when(here.not_top, add_high)
        if by_column(self.kind):
            links.send(self.fin.at[1 - here.c], self.last, self.s_end, self.r_end, here.sib)
        else:
            links.send(self.fin, self.last, self.s_end, self.r_end, here.swap, here.moves)

    def finish(self, out):
        links, here, kind = self.links, self.here, self.kind
        c = here.c
        if kind == QKV:
            for j in range(3):
                at = pl.multiple_of(DM * j + HALF * c, 128)
                out[:, pl.ds(at, HALF)] = self.fin[c, :, HALF * j : HALF * (j + 1)]
            links.recv(self.last, self.r_end)
            for j in range(3):
                at = pl.multiple_of(DM * j + HALF * (1 - c), 128)
                out[:, pl.ds(at, HALF)] = self.last[:, HALF * j : HALF * (j + 1)]
        elif kind == UP:
            out[:, pl.ds(pl.multiple_of(UP_N * c, 128), UP_N)] = self.fin[c]
            links.recv(self.last, self.r_end)
            out[:, pl.ds(pl.multiple_of(UP_N * (1 - c), 128), UP_N)] = self.last[...]
        else:
            links.recv(self.last, self.r_end, here.moves)

            def keep():
                out[...] = self.fin[...]

            def take():
                out[...] = self.last[...]

            when(here.stays, keep)
            when(here.moves, take)


def dot(a, b):
    return jnp.dot(a, b, preferred_element_type=F32)


def dot_nt(a, b):
    return lax.dot_general(a, b, (((1,), (1,)), ((), ())), preferred_element_type=F32)


def dot_tn(a, b):
    return lax.dot_general(a, b, (((0,), (0,)), ((), ())), preferred_element_type=F32)


def row_sum(values):
    return jnp.sum(values, axis=0, keepdims=True)


def div24(n):
    return lax.shift_right_logical(n * 2731, 16)


def iota(shape, dim):
    return lax.broadcasted_iota(jnp.int32, shape, dim)


def select_24():
    n = iota((128, DM), 1)
    return (iota((128, DM), 0) == n - 24 * div24(n)).astype(BF16)


def select_96():
    n = iota((128, UP_N), 1)
    run = lax.shift_right_logical(div24(n), 2)
    return (iota((128, UP_N), 0) == 32 + n - 96 * run).astype(BF16)


def owner_24(lead):
    shape = (lead, 8, DM)
    return div24(iota(shape, 2)) == iota(shape, 0)


def owner_96():
    shape = (16, UP_N)
    return lax.shift_right_logical(div24(iota(shape, 1)), 2) == iota(shape, 0)


def exact_nt(values, select):
    high = values.astype(BF16)
    rest = values - high.astype(F32)
    mid = rest.astype(BF16)
    low = (rest - mid.astype(F32)).astype(BF16)
    return dot_nt(high, select) + dot_nt(mid, select) + dot_nt(low, select)


SCRATCH = dict(
    wq=((24, QKV_N), BF16),
    vec_all=((32, 8, 128), F32),
    vec_rows=((8, DM), F32),
    up_row=((1, UP_N), F32),
    x_chip=((2, 2, TOK, DM), BF16),
    fl_chip=((2, 2, TOK, DM), BF16),
    gf_chip=((2, 2, TOK, DM), BF16),
    ga_chip=((2, 2, TOK, DM), BF16),
    partial=((2, 2, TOK, DM), F32),
    back0=((2, TOK, DM), F32),
    back1=((2, TOK, DM), F32),
    back2=((2, TOK, DM), F32),
    back3=((2, TOK, DM), F32),
    send_q=((12, 192, 128), BF16),
    qkv_t=((192, SEQ), BF16),
    k_rows=((SEQ, HD), BF16),
    v_rows=((SEQ, HD), BF16),
    q_rows=((SEQ, HD), BF16),
    g_rows=((SEQ, HD), BF16),
    key_doc=((SEQ, 128), jnp.int32),
    query_doc=((1, SEQ), jnp.int32),
    scores=((SEQ, CHUNK), F32),
    weights=((SEQ, SEQ), BF16),
    total=((1, SEQ), F32),
    att_t=((HD, SEQ), F32),
    att_send=((HD, SEQ), BF16),
    mix_in=((12, HD, 128), BF16),
    g_send=((12, HD, 128), BF16),
    g_t=((HD, SEQ), BF16),
    gn_t=((HD, SEQ), BF16),
    corr=((1, SEQ), F32),
    ds=((CHUNK, SEQ), BF16),
    dq_t=((HD, SEQ), F32),
    d_send=((192, SEQ), BF16),
    d_in=((12, 192, 128), BF16),
    mixed_t=((HALF, 2 * 128), BF16),
    first=((2 * TOK, DM), F32),
    normed1=((2 * TOK, DM), F32),
    inv1=((2 * TOK, 1), F32),
    active=((4 * TOK, UP_N), BF16),
    slope=((4 * TOK, UP_N), F32),
    gh=((4 * TOK, UP_N), BF16),
    gh2=((2 * TOK, DM), F32),
    gh1=((2 * TOK, DM), F32),
    gp=((4 * TOK, QKV_N), BF16),
    vec_grad=((8, DM), F32),
    up_grad=((1, UP_N), F32),
    vec_send=((32, 8, 128), F32),
    vec_recv=((32, 8, 128), F32),
)


def kind_scratch(kind):
    shape = SHAPES[kind]
    piece = piece_shape(kind)
    last = piece[1:] if by_column(kind) else piece
    low = [shape, shape, half_shape(kind), half_shape(kind), shape[1:], shape[1:], shape[1:]]
    low += [(4,) + piece, (4,) + piece]
    return [(s, BF16) for s in low] + [(piece, F32), (last, F32)]


def all_scratch():
    shapes = list(SCRATCH.values())
    for kind in range(4):
        shapes += kind_scratch(kind)
    return [pltpu.VMEM(shape, dtype) for shape, dtype in shapes] + [pltpu.SemaphoreType.DMA((N_SEM,))]


N_SEM = 512


def layer_kernel(
    tokens, starts, w_qkv, w_out, w_up, w_down, vecs, cotangent,
    o_out, o_tok, o_qkv, o_bq, o_bv, o_wout, o_bo, o_g1, o_s1, o_up, o_bup, o_down, o_bd, o_g2, o_s2,
    *scratch,
):
    named = len(SCRATCH)
    m = SimpleNamespace(**dict(zip(SCRATCH, scratch)))
    kinds = [scratch[named + 11 * kind : named + 11 * (kind + 1)] for kind in range(4)]
    sems = scratch[-1]
    here = Place()
    links = Links(sems, here)
    b, z, c = here.b, here.z, here.c
    line, chip = here.line, here.chip
    gathers = [Gather(links, here, kind, kinds[kind][0]) for kind in range(4)]
    scatters = [Scatter(links, here, kind, kinds[kind][1:]) for kind in range(4)]

    def peer(d):
        other = lax.rem(line + d, 32)
        return (lax.div(other, 4), lax.rem(other, 4))

    barrier = pltpu.get_barrier_semaphore()

    def greet(d, carry):
        pl.semaphore_signal(barrier, inc=1, device_id=peer(d), device_id_type=MESH)
        return carry

    lax.fori_loop(1, 32, greet, 0)
    pl.semaphore_wait(barrier, 31)

    def pack(which):
        return [w_qkv[:, pl.ds(pl.multiple_of(DM * j + HALF * which, 128), HALF)] for j in range(3)]

    for j, block in enumerate(pack(1 - c)):
        m.wq[:, HALF * j : HALF * (j + 1)] = block
    g_qkv, g_out, g_up, g_down = gathers
    slot = g_qkv.ref.at[g_qkv.col, c, z]
    links.send(m.wq, slot, g_qkv.s0, g_qkv.r0, here.sib)
    x_sem = links.alloc(2)
    x_chip = m.x_chip
    links.send(tokens, x_chip.at[:, c], x_sem, x_sem + 1, here.sib)
    links.send(
        w_up.at[:, pl.ds(pl.multiple_of(UP_N * (1 - c), 128), UP_N)],
        g_up.ref.at[g_up.col, c, z], g_up.s0, g_up.r0, here.sib,
    )
    for gather, shard in ((g_out, w_out), (g_down, w_down)):
        slot = gather.ref.at[2 * here.x + c, z]
        links.send(shard, slot, gather.s0, gather.r0, here.swap, here.moves)
    vec_sem = links.alloc(4)
    vec_all = m.vec_all

    def vec_copy(d):
        return links.make(vecs, vec_all.at[line], vec_sem, vec_sem + 1, peer(d))

    def vec_start(d, carry):
        vec_copy(d).start()
        return carry

    lax.fori_loop(1, 32, vec_start, 0)

    for j, block in enumerate(pack(c)):
        g_qkv.ref[g_qkv.col, c, z, :, HALF * j : HALF * (j + 1)] = block
    g_up.ref[g_up.col, c, z] = w_up[:, pl.ds(pl.multiple_of(UP_N * c, 128), UP_N)]

    def keep_rows():
        g_out.ref[g_out.col, z] = w_out[...]
        g_down.ref[g_down.col, z] = w_down[...]

    when(here.stays, keep_rows)
    for part in range(MB):
        x_chip[part, c] = tokens[part]
    vec_all[line] = vecs[...]
    m.vec_grad[...] = jnp.zeros((8, DM), F32)

    g_qkv.z_own()
    for r in (1, 2, 3):
        g_qkv.z_relay(r)
    g_qkv.plane_send()
    for gather in (g_up, g_out, g_down):
        gather.z_own()

    many = vec_all.at[pl.ds(0, 31)]
    links.make(many, many, vec_sem, vec_sem + 1, here.sib).wait_send()
    links.recv(many, vec_sem + 1)
    spread = dot(vec_all[...].reshape(256, 128).astype(BF16), select_24()).reshape(32, 8, DM)
    m.vec_rows[...] = jnp.sum(jnp.where(owner_24(32), spread, 0.0), axis=0)
    spread = dot(vec_all[pl.ds(16 * c, 16), 0, :].astype(BF16), select_96())
    m.up_row[...] = row_sum(jnp.where(owner_96(), spread, 0.0))

    def vector(j):
        return m.vec_rows[j : j + 1, :]

    def vector_half(j):
        return m.vec_rows[j : j + 1, pl.ds(pl.multiple_of(HALF * c, 128), HALF)]

    def documents():
        def position(n):
            q_part = lax.shift_left(lax.shift_right_logical(n, 9), 9)
            core_part = lax.shift_left(jnp.bitwise_and(lax.shift_right_logical(n, 6), 1), 8)
            z_part = lax.shift_left(jnp.bitwise_and(lax.shift_right_logical(n, 7), 3), 6)
            return q_part + core_part + z_part + jnp.bitwise_and(n, 63)

        def doc_of(n):
            place = position(n)
            doc = jnp.zeros(place.shape, jnp.int32)
            for j in range(starts.shape[1]):
                doc = doc + (starts[here.part, j] <= place).astype(jnp.int32)
            return doc

        m.query_doc[...] = doc_of(iota((1, SEQ), 1))

        def rows(i, carry):
            at = pl.multiple_of(i * 256, 256)
            m.key_doc[pl.ds(at, 256), :] = doc_of(iota((256, 128), 0) + i * 256)
            return carry

        lax.fori_loop(0, SEQ // 256, rows, 0)

    when(here.active, documents)

    links.recv(x_chip.at[:, 1 - c], x_sem + 1)
    g_qkv.plane_relay()
    for gather in (g_up, g_out, g_down):
        gather.z_relay(1)
    g_qkv.plane_done()

    def weight_qkv(j):
        return g_qkv.ref[:, :, :, :, HALF * j : HALF * (j + 1)].reshape(DM, HALF)

    def x_rows():
        return x_chip[...].reshape(4 * TOK, DM)

    send_q = m.send_q
    for j in range(3):
        rows = dot(x_rows(), weight_qkv(j))
        if j == 0:
            rows = (rows + vector_half(0)).astype(BF16) * jnp.asarray(HD ** (-0.5), BF16)
        elif j == 1:
            rows = rows.astype(BF16)
        else:
            rows = (rows + vector_half(1)).astype(BF16)
        turned = rows.T
        for part in range(MB):
            piece = turned[:, 128 * part : 128 * (part + 1)].reshape(6, HD, 128)
            send_q[6 * part : 6 * part + 6, HD * j : HD * (j + 1), :] = piece

    chip_lanes = pl.ds(pl.multiple_of(chip * 128, 128), 128)

    def to_pairs(src, dst_of, rows):
        s, r, local = links.alloc(12), links.alloc(), links.alloc()
        for pair in range(12):
            q_to, z_to = pair_place(pair)
            mine = jnp.logical_and(here.q == q_to, z == z_to)
            links.send(src.at[pair], dst_of(chip_lanes), s + pair, r, (2 * q_to + c, z_to), jnp.logical_not(mine))

        def own():
            copy = pltpu.make_async_copy(src.at[here.pair], dst_of(chip_lanes), sems.at[local])
            copy.start()
            copy.wait()

        when(here.active, own)
        return lambda: links.recv(dst_of(pl.ds(0, 15 * 128)), r, here.active)

    def to_chips(src_of, dst):
        s, r, local = links.alloc(16), links.alloc(), links.alloc()
        for other in range(16):
            cond = both(here.active, chip != other)
            lanes = pl.ds(128 * other, 128)
            links.send(
                src_of(lanes), dst.at[here.pair], s + other, r, (2 * (other // 4) + c, other % 4), cond
            )

        def own():
            copy = pltpu.make_async_copy(src_of(chip_lanes), dst.at[here.pair], sems.at[local])
            copy.start()
            copy.wait()

        when(here.active, own)

        def wait():
            links.recv(dst.at[pl.ds(0, 11)], r, here.active)
            links.recv(dst.at[pl.ds(0, 12)], r, jnp.logical_not(here.active))

        return wait

    qkv_t = m.qkv_t
    wait_q = to_pairs(send_q, lambda lanes: qkv_t.at[:, lanes], 192)
    for r in (2, 3):
        for gather in (g_up, g_out, g_down):
            gather.z_relay(r)
    for gather in (g_out, g_up, g_down):
        gather.plane_send()
    wait_q()

    weights = m.weights

    def turn_keys():
        m.k_rows[...] = qkv_t[HD : 2 * HD, :].T
        m.v_rows[...] = qkv_t[2 * HD : 3 * HD, :].T
        m.q_rows[...] = qkv_t[0:HD, :].T

    when(here.active, turn_keys)

    def attend(i):
        lanes = pl.ds(pl.multiple_of(i * CHUNK, CHUNK), CHUNK)
        query = qkv_t[0:HD, lanes]
        doc = m.query_doc[:, lanes]
        top = None
        for k in range(8):
            rows = slice(256 * k, 256 * (k + 1))
            key_doc = m.key_doc[rows, :]
            same = jnp.concatenate([key_doc, key_doc], axis=1) == doc
            scores = jnp.where(same, dot(m.k_rows[rows, :], query), NEG)
            m.scores[rows, :] = scores
            here_top = jnp.max(scores, axis=0, keepdims=True)
            top = here_top if top is None else jnp.maximum(top, here_top)
        total = None
        for k in range(8):
            rows = slice(256 * k, 256 * (k + 1))
            grown = jnp.exp(m.scores[rows, :] - top)
            weights[rows, lanes] = grown.astype(BF16)
            part_sum = row_sum(grown)
            total = part_sum if total is None else total + part_sum
        numer = dot(qkv_t[2 * HD : 3 * HD, :], weights[:, lanes])
        attended = numer / total
        m.total[:, lanes] = total
        m.att_t[:, lanes] = attended
        m.att_send[:, lanes] = attended.astype(BF16)

    def attend_some(first, last):
        def run():
            def one(i, carry):
                attend(i)
                return carry

            lax.fori_loop(first, last, one, 0)

        when(here.active, run)

    attend_some(0, 4)
    for gather in (g_out, g_up, g_down):
        gather.plane_relay()
    attend_some(4, 8)

    wait_mix = to_chips(lambda lanes: m.att_send.at[:, lanes], m.mix_in)
    wait_mix()
    for gather in (g_out, g_up, g_down):
        gather.plane_done()

    def share(buf, values):
        at = links.alloc(2)
        buf[:, c] = values.reshape(MB, TOK, DM)
        links.send(buf.at[:, c], buf.at[:, c], at, at + 1, here.sib)
        links.recv(buf.at[:, 1 - c], at + 1)

    def combine(values, back):
        at = links.alloc(2)
        partial = m.partial
        partial[...] = values.reshape(MB, 2, TOK, DM)
        links.send(partial.at[:, 1 - c], back, at, at + 1, here.sib, keep=False)
        links.recv(back, at + 1)
        total = partial[:, c].reshape(2 * TOK, DM) + back[...].reshape(2 * TOK, DM)
        links.sent(partial.at[:, 1 - c], back, at, at + 1, here.sib)
        return total

    def norm_rows(values, gain, shift):
        center = values - jnp.mean(values, axis=-1, keepdims=True)
        inverse = lax.rsqrt(jnp.mean(center * center, axis=-1, keepdims=True) + EPS)
        normed = center * inverse
        return normed * gain + shift, normed, inverse

    def norm_back(upstream, normed, inverse, gain):
        scaled = upstream * gain
        return inverse * (
            scaled
            - jnp.mean(scaled, axis=-1, keepdims=True)
            - normed * jnp.mean(scaled * normed, axis=-1, keepdims=True)
        )

    mixed_t = m.mixed_t
    mixed = []
    for part in range(MB):
        piece = m.mix_in[6 * part : 6 * part + 6].reshape(HALF, 128)
        mixed_t[:, 128 * part : 128 * (part + 1)] = piece
        mixed.append(piece.T)
    mixed = jnp.concatenate(mixed, axis=0)

    def weight_out():
        return g_out.ref[...].reshape(HALF, DM)

    attn = combine(dot(mixed, weight_out()), m.back0) + vector(2)
    first, normed_one, inverse_one = norm_rows(
        tokens[...].reshape(2 * TOK, DM).astype(F32) + attn, vector(3), vector(4)
    )
    m.first[...] = first
    m.normed1[...] = normed_one
    m.inv1[...] = inverse_one
    share(m.fl_chip, first.astype(BF16))

    def fl_rows():
        return m.fl_chip[...].reshape(4 * TOK, DM)

    def weight_up(j):
        return g_up.ref[:, :, :, :, HALF * j : HALF * (j + 1)].reshape(DM, HALF)

    def weight_down(j):
        return g_down.ref[j].reshape(HALF, DM)

    ffn = None
    for j in range(4):
        lanes = slice(HALF * j, HALF * (j + 1))
        hidden = dot(fl_rows(), weight_up(j)) + m.up_row[:, lanes]
        cdf = 0.5 * (1.0 + lax.erf(hidden * (0.5**0.5)))
        m.slope[:, lanes] = cdf + hidden * (jnp.exp(-0.5 * hidden * hidden) * 0.3989422804014327)
        m.active[:, lanes] = (hidden * cdf).astype(BF16)
        term = dot(m.active[:, lanes], weight_down(j))
        ffn = term if ffn is None else ffn + term
    ffn = combine(ffn, m.back1) + vector(5)
    result, normed_two, inverse_two = norm_rows(m.first[...] + ffn, vector(6), vector(7))
    o_out[...] = result.reshape(MB, TOK, DM)

    vec_grad = m.vec_grad
    grad_result = cotangent[...].reshape(2 * TOK, DM).astype(F32)
    vec_grad[6:7, :] = row_sum(grad_result * normed_two)
    vec_grad[7:8, :] = row_sum(grad_result)
    grad_two = norm_back(grad_result, normed_two, inverse_two, vector(6))
    m.gh2[...] = grad_two
    grad_ffn = grad_two.astype(BF16)
    vec_grad[5:6, :] = row_sum(grad_ffn.astype(F32))
    share(m.gf_chip, grad_ffn)

    def gf_rows():
        return m.gf_chip[...].reshape(4 * TOK, DM)

    s_qkv, s_out, s_up, s_down = scatters
    for j in range(4):
        lanes = slice(HALF * j, HALF * (j + 1))
        s_down.grad[j] = dot_tn(m.active[:, lanes], gf_rows()).astype(BF16).reshape(4, 96, DM)
    s_down.plane_send()
    for j in range(4):
        lanes = slice(HALF * j, HALF * (j + 1))
        grad_active = dot_nt(gf_rows(), weight_down(j))
        grad_hidden = (grad_active * m.slope[:, lanes]).astype(BF16)
        m.gh[:, lanes] = grad_hidden
        m.up_grad[:, lanes] = row_sum(grad_hidden.astype(F32))
    grad_first = None
    for j in range(4):
        lanes = slice(HALF * j, HALF * (j + 1))
        term = dot_nt(m.gh[:, lanes], weight_up(j))
        grad_first = term if grad_first is None else grad_first + term
    grad_first = m.gh2[...] + combine(grad_first, m.back2)
    normed_one = m.normed1[...]
    vec_grad[3:4, :] = row_sum(grad_first * normed_one)
    vec_grad[4:5, :] = row_sum(grad_first)
    grad_one = norm_back(grad_first, normed_one, m.inv1[...], vector(3))
    m.gh1[...] = grad_one
    grad_attn = grad_one.astype(BF16)
    vec_grad[2:3, :] = row_sum(grad_attn.astype(F32))
    share(m.ga_chip, grad_attn)

    def ga_rows():
        return m.ga_chip[...].reshape(4 * TOK, DM)

    turned = dot_nt(ga_rows(), weight_out()).astype(BF16).T
    for part in range(MB):
        m.g_send[6 * part : 6 * part + 6] = turned[:, 128 * part : 128 * (part + 1)].reshape(6, HD, 128)
    g_t = m.g_t
    wait_g = to_pairs(m.g_send, lambda lanes: g_t.at[:, lanes], HD)
    for j in range(4):
        lanes = slice(HALF * j, HALF * (j + 1))
        s_up.grad[:, :, :, :, lanes] = (
            dot_tn(fl_rows(), m.gh[:, lanes]).astype(BF16).reshape(4, 2, 4, 24, HALF)
        )
    s_up.plane_send()
    s_out.grad[...] = dot(mixed_t[...], ga_rows()).astype(BF16).reshape(SHAPES[OUT])
    s_out.plane_send()
    s_down.plane_relay()
    wait_g()

    d_send = m.d_send

    def turn_grads():
        grad = g_t[...].astype(F32)
        inverse = 1.0 / m.total[...]
        numer = grad * inverse
        m.gn_t[...] = numer.astype(BF16)
        m.g_rows[...] = numer.astype(BF16).T
        m.corr[...] = row_sum(grad * m.att_t[...]) * inverse
        m.dq_t[...] = jnp.zeros((HD, SEQ), F32)

    when(here.active, turn_grads)

    def back(k):
        at = pl.ds(pl.multiple_of(k * CHUNK, CHUNK), CHUNK)
        value = m.v_rows[at, :]
        for i in range(4):
            lanes = slice(512 * i, 512 * (i + 1))
            grad_weights = dot(value, m.gn_t[:, lanes])
            grown = weights[at, lanes].astype(F32)
            m.ds[:, lanes] = (grown * (grad_weights - m.corr[:, lanes])).astype(BF16)
        ds = m.ds
        d_send[HD : 2 * HD, at] = dot(ds[...], m.q_rows[...]).T.astype(BF16)
        d_send[2 * HD : 3 * HD, at] = dot(weights[at, :], m.g_rows[...]).T.astype(BF16)
        m.dq_t[...] += dot(qkv_t[HD : 2 * HD, at], ds[...])

    def back_some(first, last):
        def run():
            def one(i, carry):
                back(i)
                return carry

            lax.fori_loop(first, last, one, 0)

        when(here.active, run)

    back_some(0, 4)
    s_up.plane_relay()
    s_out.plane_relay()
    s_down.plane_done()
    s_down.z_first()
    back_some(4, 8)

    def last_query():
        d_send[0:HD, :] = (m.dq_t[...] * (HD ** (-0.5))).astype(BF16)

    when(here.active, last_query)
    d_in = m.d_in
    wait_d = to_chips(lambda lanes: d_send.at[:, lanes], d_in)
    s_up.plane_done()
    s_up.z_first()
    s_out.plane_done()
    s_out.z_first()
    wait_d()

    gp = m.gp
    for part in range(MB):
        for j in range(3):
            piece = d_in[6 * part : 6 * part + 6, HD * j : HD * (j + 1), :].reshape(HALF, 128)
            gp[128 * part : 128 * (part + 1), HALF * j : HALF * (j + 1)] = piece.T
    own_half = pl.ds(pl.multiple_of(HALF * c, 128), HALF)
    for j in range(3):
        lanes = slice(HALF * j, HALF * (j + 1))
        s_qkv.grad[:, :, :, :, lanes] = (
            dot_tn(x_rows(), gp[:, lanes]).astype(BF16).reshape(4, 2, 4, 24, HALF)
        )
    s_qkv.plane_send()
    vec_grad[0:1, own_half] = row_sum(gp[:, 0:HALF].astype(F32))
    vec_grad[1:2, own_half] = row_sum(gp[:, 2 * HALF : 3 * HALF].astype(F32))

    vec_send, vec_recv = m.vec_send, m.vec_recv
    spread = jnp.where(owner_24(32), vec_grad[...][None], 0.0).reshape(256, DM)
    vec_send[...] = exact_nt(spread, select_24()).reshape(32, 8, 128)
    spread = jnp.where(owner_96(), m.up_grad[...], 0.0)
    own_lines = pl.ds(16 * c, 16)
    vec_send[own_lines, 0, :] = vec_send[own_lines, 0, :] + exact_nt(spread, select_96())

    def grad_copy(d):
        other = lax.rem(line + d, 32)
        return links.make(vec_send.at[other], vec_recv.at[line], vec_sem + 2, vec_sem + 3, peer(d))

    def grad_start(d, carry):
        grad_copy(d).start()
        return carry

    lax.fori_loop(1, 32, grad_start, 0)
    vec_recv[line] = vec_send[line]

    grad_tokens = None
    for j in range(3):
        term = dot_nt(gp[:, HALF * j : HALF * (j + 1)], weight_qkv(j))
        grad_tokens = term if grad_tokens is None else grad_tokens + term
    o_tok[...] = (m.gh1[...] + combine(grad_tokens, m.back3)).reshape(MB, TOK, DM)

    for scatter, out in ((s_down, o_down), (s_up, o_up), (s_out, o_wout)):
        scatter.z_last()
    s_qkv.plane_relay()
    for scatter, out in ((s_down, o_down), (s_up, o_up), (s_out, o_wout)):
        scatter.finish(out)

    many_send, many_recv = vec_send.at[pl.ds(0, 31)], vec_recv.at[pl.ds(0, 31)]
    links.make(many_send, many_send, vec_sem + 2, vec_sem + 3, here.sib).wait_send()
    links.recv(many_recv, vec_sem + 3)
    rows = jnp.sum(vec_recv[...], axis=0)
    for j, out in enumerate((o_bq, o_bv, o_bo, o_g1, o_s1, o_bd, o_g2, o_s2)):
        out[...] = rows[j, 0:24]
    o_bup[...] = rows[0, 32:128]

    s_qkv.plane_done()
    s_qkv.z_first()
    s_qkv.z_last()
    s_qkv.finish(o_qkv)
    links.finish()


def fused(
    tokens, starts, w_qkv, bias_q, bias_v, w_out, bias_out, gain_one, shift_one,
    w_up, bias_up, w_down, bias_down, gain_two, shift_two, cotangent,
):
    rows = jnp.stack([bias_q, bias_v, bias_out, gain_one, shift_one, bias_down, gain_two, shift_two])
    vecs = jnp.pad(rows.astype(F32), ((0, 0), (0, 104)))
    vecs = vecs + jnp.pad(bias_up.astype(F32)[None], ((0, 7), (32, 0)))
    shapes = [tokens.shape] * 2 + [w_qkv.shape, bias_q.shape, bias_v.shape, w_out.shape, bias_out.shape]
    shapes += [gain_one.shape, shift_one.shape, w_up.shape, bias_up.shape, w_down.shape, bias_down.shape]
    shapes += [gain_two.shape, shift_two.shape]
    vmem = pl.BlockSpec(memory_space=pltpu.VMEM)
    return tuple(
        pl.pallas_call(
            layer_kernel,
            name="layer",
            out_shape=[jax.ShapeDtypeStruct(shape, F32) for shape in shapes],
            in_specs=[vmem, pl.BlockSpec(memory_space=pltpu.SMEM)] + [vmem] * 6,
            out_specs=[vmem] * len(shapes),
            scratch_shapes=all_scratch(),
            compiler_params=pltpu.CompilerParams(
                collective_id=0, has_side_effects=True, vmem_limit_bytes=63 * 2**20
            ),
        )(tokens, starts, w_qkv, w_out, w_up, w_down, vecs, cotangent)
    )


def solution(mesh):
    small = dict(mesh.shape) == {BLK: 8, HEAD: 4}
    return jax.shard_map(
        fused if small else per_device,
        mesh=mesh,
        in_specs=(
            P(None, BOTH, None),
            P(),
            P(BOTH, None),
            P(BOTH),
            P(BOTH),
            P(BOTH, None),
            P(BOTH),
            P(BOTH),
            P(BOTH),
            P(BOTH, None),
            P(BOTH),
            P(BOTH, None),
            P(BOTH),
            P(BOTH),
            P(BOTH),
            P(None, BOTH, None),
        ),
        out_specs=(
            P(None, BOTH, None),
            P(None, BOTH, None),
            P(BOTH, None),
            P(BOTH),
            P(BOTH),
            P(BOTH, None),
            P(BOTH),
            P(BOTH),
            P(BOTH),
            P(BOTH, None),
            P(BOTH),
            P(BOTH, None),
            P(BOTH),
            P(BOTH),
            P(BOTH),
        ),
        check_vma=False,
    )
```

```python
from functools import partial
from types import SimpleNamespace

import jax
import jax.numpy as jnp
from jax import lax
from jax.experimental import pallas as pl
from jax.experimental.pallas import tpu as pltpu
from jax.sharding import PartitionSpec as P

BLK = "blk"
HEAD = "head"
BOTH = (BLK, HEAD)
H = 12
HD = 64
MB = 2


EPS = 1e-05
NEG = -1e30


def norm_forward(values, gain_vec, shift_vec):
    center = values - jnp.mean(values, axis=-1, keepdims=True)
    inverse = lax.rsqrt(jnp.mean(center * center, axis=-1, keepdims=True) + EPS)
    normed = center * inverse
    return (normed * gain_vec + shift_vec, normed, inverse)


def norm_backward(upstream, normed, inverse, gain_vec):
    scaled = upstream * gain_vec
    inner = (
        scaled
        - jnp.mean(scaled, axis=-1, keepdims=True)
        - normed * jnp.mean(scaled * normed, axis=-1, keepdims=True)
    )
    return inner * inverse


def segment_of(starts_row, positions):
    return jnp.sum((starts_row[None, :] <= positions[:, None]).astype(jnp.int32), axis=1) - 1


def masked_scores(query_heads, key_heads, in_doc):
    scores = jnp.einsum(
        "qhd,khd->hqk", query_heads, key_heads, preferred_element_type=jnp.float32
    ) * HD ** (-0.5)
    return jnp.where(in_doc, scores, NEG)


def score_grads(query_heads, key_heads, value_heads, grad_numer, row_top, correction, in_doc):
    exp_score = jnp.where(
        in_doc, jnp.exp(masked_scores(query_heads, key_heads, in_doc) - row_top), 0.0
    )
    grad_weights = jnp.einsum(
        "qhd,khd->hqk", grad_numer, value_heads, preferred_element_type=jnp.float32
    )
    grad_scores = (exp_score * (grad_weights - correction)).astype(jnp.bfloat16)
    return (exp_score.astype(jnp.bfloat16), grad_scores)


def scatter_end(parts):
    (
        grad_proj_in,
        grad_query_bias,
        grad_value_bias,
        grad_proj_out,
        grad_out_bias,
        grad_norm_gain,
        grad_norm_shift,
        grad_up,
        grad_up_bias,
        grad_down,
        grad_down_bias,
        grad_final_gain,
        grad_final_shift,
    ) = parts
    return (
        lax.psum_scatter(grad_proj_in, BOTH, scatter_dimension=0, tiled=True),
        lax.psum_scatter(grad_query_bias, BOTH, scatter_dimension=0, tiled=True),
        lax.psum_scatter(grad_value_bias, BOTH, scatter_dimension=0, tiled=True),
        lax.psum_scatter(grad_proj_out, BOTH, scatter_dimension=0, tiled=True),
        lax.psum_scatter(grad_out_bias, BOTH, scatter_dimension=0, tiled=True),
        lax.psum_scatter(grad_norm_gain, BOTH, scatter_dimension=0, tiled=True),
        lax.psum_scatter(grad_norm_shift, BOTH, scatter_dimension=0, tiled=True),
        lax.psum_scatter(grad_up, BOTH, scatter_dimension=0, tiled=True),
        lax.psum_scatter(grad_up_bias, BOTH, scatter_dimension=0, tiled=True),
        lax.psum_scatter(grad_down, BOTH, scatter_dimension=0, tiled=True),
        lax.psum_scatter(grad_down_bias, BOTH, scatter_dimension=0, tiled=True),
        lax.psum_scatter(grad_final_gain, BOTH, scatter_dimension=0, tiled=True),
        lax.psum_scatter(grad_final_shift, BOTH, scatter_dimension=0, tiled=True),
    )


def per_device(
    tokens,
    starts,
    w_qkv,
    bias_q,
    bias_v,
    w_out,
    bias_out,
    gain_one,
    shift_one,
    w_up,
    bias_up,
    w_down,
    bias_down,
    gain_two,
    shift_two,
    cotangent,
):
    (
        proj_in,
        query_bias,
        value_bias,
        proj_out,
        out_bias,
        norm_gain,
        norm_shift,
        up_full,
        up_bias,
        down_full,
        down_bias,
        final_gain,
        final_shift,
    ) = (
        lax.all_gather(w_qkv, BOTH, axis=0, tiled=True),
        lax.all_gather(bias_q, BOTH, axis=0, tiled=True),
        lax.all_gather(bias_v, BOTH, axis=0, tiled=True),
        lax.all_gather(w_out, BOTH, axis=0, tiled=True),
        lax.all_gather(bias_out, BOTH, axis=0, tiled=True),
        lax.all_gather(gain_one, BOTH, axis=0, tiled=True),
        lax.all_gather(shift_one, BOTH, axis=0, tiled=True),
        lax.all_gather(w_up, BOTH, axis=0, tiled=True),
        lax.all_gather(bias_up, BOTH, axis=0, tiled=True),
        lax.all_gather(w_down, BOTH, axis=0, tiled=True),
        lax.all_gather(bias_down, BOTH, axis=0, tiled=True),
        lax.all_gather(gain_two, BOTH, axis=0, tiled=True),
        lax.all_gather(shift_two, BOTH, axis=0, tiled=True),
    )
    query_bias = query_bias.astype(jnp.float32)
    value_bias = value_bias.astype(jnp.float32)
    out_bias = out_bias.astype(jnp.float32)
    norm_gain = norm_gain.astype(jnp.float32)
    norm_shift = norm_shift.astype(jnp.float32)
    up_bias = up_bias.astype(jnp.float32)
    down_bias = down_bias.astype(jnp.float32)
    final_gain = final_gain.astype(jnp.float32)
    final_shift = final_shift.astype(jnp.float32)
    model_width = proj_out.shape[0]
    row_count = tokens.shape[1]
    head_count = lax.axis_size(HEAD)
    block_rows = row_count * head_count
    heads_dev = H // head_count
    local_width = heads_dev * HD
    scale = HD ** (-0.5)
    local_pos = lax.axis_index(BLK) * block_rows + jnp.arange(block_rows, dtype=jnp.int32)
    kept_list = []
    outputs = []
    for part_index in range(MB):
        inputs = tokens[part_index]
        starts_row = starts[part_index]
        projected = jnp.dot(inputs, proj_in, preferred_element_type=jnp.float32)
        query_rows = (projected[:, :model_width] + query_bias).astype(jnp.bfloat16)
        key_rows = projected[:, model_width : 2 * model_width].astype(jnp.bfloat16)
        value_rows = (projected[:, 2 * model_width :] + value_bias).astype(jnp.bfloat16)
        query_loc, key_loc, value_loc = (
            lax.all_to_all(query_rows, HEAD, split_axis=1, concat_axis=0, tiled=True),
            lax.all_to_all(key_rows, HEAD, split_axis=1, concat_axis=0, tiled=True),
            lax.all_to_all(value_rows, HEAD, split_axis=1, concat_axis=0, tiled=True),
        )
        doc_local = segment_of(starts_row, local_pos)
        query_heads = query_loc.reshape(block_rows, heads_dev, HD)

        def fold_keys(running, portion):
            row_top, row_total, weighted = running
            key_part, value_part = portion
            piece_len = key_part.shape[0]
            key_doc = segment_of(starts_row, jnp.arange(piece_len, dtype=jnp.int32))
            in_doc = (doc_local[:, None] == key_doc[None, :])[None]
            scores = masked_scores(query_heads, key_part.reshape(piece_len, heads_dev, HD), in_doc)
            new_top = jnp.maximum(row_top, jnp.max(scores, axis=-1, keepdims=True))
            exp_score = jnp.where(in_doc, jnp.exp(scores - new_top), 0.0)
            row_total = jnp.sum(exp_score, axis=-1, keepdims=True)
            weighted = jnp.einsum(
                "hqk,khd->hqd",
                exp_score.astype(jnp.bfloat16),
                value_part.reshape(piece_len, heads_dev, HD),
                preferred_element_type=jnp.float32,
            )
            return (new_top, row_total, weighted)

        start_state = (
            jnp.full((heads_dev, block_rows, 1), NEG, jnp.float32),
            jnp.zeros((heads_dev, block_rows, 1), jnp.float32),
            jnp.zeros((heads_dev, block_rows, HD), jnp.float32),
        )
        row_top, row_total, weighted = fold_keys(
            start_state,
            (
                lax.all_gather(key_loc, BLK, axis=0, tiled=True),
                lax.all_gather(value_loc, BLK, axis=0, tiled=True),
            ),
        )
        attended = jnp.transpose(weighted / row_total, (1, 0, 2))
        mixed_rows = lax.all_to_all(
            attended.reshape(block_rows, local_width).astype(jnp.bfloat16),
            HEAD,
            split_axis=0,
            concat_axis=1,
            tiled=True,
        )
        attn_out = jnp.dot(mixed_rows, proj_out, preferred_element_type=jnp.float32) + out_bias
        first_norm, normed_one, inverse_one = norm_forward(
            inputs.astype(jnp.float32) + attn_out, norm_gain, norm_shift
        )
        first_low = first_norm.astype(jnp.bfloat16)
        hidden = jnp.dot(first_low, up_full, preferred_element_type=jnp.float32) + up_bias
        active = jax.nn.gelu(hidden, approximate=False).astype(jnp.bfloat16)
        ffn_out = jnp.dot(active, down_full, preferred_element_type=jnp.float32) + down_bias
        result, normed_two, inverse_two = norm_forward(
            first_norm + ffn_out, final_gain, final_shift
        )
        outputs.append(result)
        kept_list.append(
            (
                inputs,
                starts_row,
                query_loc,
                key_loc,
                value_loc,
                doc_local,
                row_top,
                row_total,
                attended,
                mixed_rows,
                normed_one,
                inverse_one,
                first_low,
                hidden,
                active,
                normed_two,
                inverse_two,
            )
        )
    input_grads = []
    grad_sum = None
    for part_index in range(MB):
        (
            inputs,
            starts_row,
            query_loc,
            key_loc,
            value_loc,
            doc_local,
            row_top,
            row_total,
            attended,
            mixed_rows,
            normed_one,
            inverse_one,
            first_low,
            hidden,
            active,
            normed_two,
            inverse_two,
        ) = kept_list[part_index]
        grad_result = cotangent[part_index].astype(jnp.float32)
        grad_final_gain = jnp.sum(grad_result * normed_two, axis=0)
        grad_final_shift = jnp.sum(grad_result, axis=0)
        grad_two = norm_backward(grad_result, normed_two, inverse_two, final_gain)
        grad_ffn = grad_two.astype(jnp.bfloat16)
        grad_down_bias = jnp.sum(grad_ffn.astype(jnp.float32), axis=0)
        grad_down = jnp.einsum("rf,rd->fd", active, grad_ffn, preferred_element_type=jnp.float32)
        grad_active = jnp.einsum(
            "rd,fd->rf", grad_ffn, down_full, preferred_element_type=jnp.float32
        )
        gelu_pull = jax.vjp(partial(jax.nn.gelu, approximate=False), hidden)[1]
        grad_hidden = gelu_pull(grad_active)[0].astype(jnp.bfloat16)
        grad_up_bias = jnp.sum(grad_hidden.astype(jnp.float32), axis=0)
        grad_up = jnp.einsum(
            "rd,rf->df", first_low, grad_hidden, preferred_element_type=jnp.float32
        )
        grad_first = grad_two + jnp.einsum(
            "rf,df->rd", grad_hidden, up_full, preferred_element_type=jnp.float32
        )
        grad_norm_gain = jnp.sum(grad_first * normed_one, axis=0)
        grad_norm_shift = jnp.sum(grad_first, axis=0)
        grad_one = norm_backward(grad_first, normed_one, inverse_one, norm_gain)
        grad_attn = grad_one.astype(jnp.bfloat16)
        grad_out_bias = jnp.sum(grad_attn.astype(jnp.float32), axis=0)
        grad_proj_out = jnp.einsum(
            "rc,rd->cd", mixed_rows, grad_attn, preferred_element_type=jnp.float32
        )
        grad_mixed = jnp.einsum(
            "rd,cd->rc", grad_attn, proj_out, preferred_element_type=jnp.float32
        ).astype(jnp.bfloat16)
        grad_loc = lax.all_to_all(grad_mixed, HEAD, split_axis=1, concat_axis=0, tiled=True)
        grad_heads = grad_loc.astype(jnp.float32).reshape(block_rows, heads_dev, HD)
        total_rows = jnp.transpose(row_total, (1, 0, 2))
        correction = jnp.transpose(
            jnp.sum(grad_heads * attended, axis=-1, keepdims=True) / total_rows, (1, 0, 2)
        )
        grad_numer = (grad_heads / total_rows).astype(jnp.bfloat16)
        query_heads = query_loc.reshape(block_rows, heads_dev, HD)
        key_heads_loc = key_loc.reshape(block_rows, heads_dev, HD)
        value_heads_loc = value_loc.reshape(block_rows, heads_dev, HD)
        fold_key_part = lax.all_gather(key_loc, BLK, axis=0, tiled=True)
        fold_value_part = lax.all_gather(value_loc, BLK, axis=0, tiled=True)
        fold_piece_len = fold_key_part.shape[0]
        fold_key_doc = segment_of(starts_row, jnp.arange(fold_piece_len, dtype=jnp.int32))
        fold_in_doc = (doc_local[:, None] == fold_key_doc[None, :])[None]
        key_heads = fold_key_part.reshape(fold_piece_len, heads_dev, HD)
        exp_low, grad_scores = score_grads(
            query_heads,
            key_heads,
            fold_value_part.reshape(fold_piece_len, heads_dev, HD),
            grad_numer,
            row_top,
            correction,
            fold_in_doc,
        )
        grad_query = (
            jnp.einsum("hqk,khd->qhd", grad_scores, key_heads, preferred_element_type=jnp.float32)
            * scale
        )
        top_rows = jnp.transpose(row_top[:, :, 0])
        corr_rows = jnp.transpose(correction[:, :, 0])

        def fold_keygrad(portion):
            query_part, numer_part, top_part, corr_part = portion
            piece_len = query_part.shape[0]
            query_doc = segment_of(starts_row, jnp.arange(piece_len, dtype=jnp.int32))
            in_doc = (query_doc[:, None] == doc_local[None, :])[None]
            query_piece = query_part.reshape(piece_len, heads_dev, HD)
            numer_piece = numer_part.reshape(piece_len, heads_dev, HD)
            exp_low, grad_scores = score_grads(
                query_piece,
                key_heads_loc,
                value_heads_loc,
                numer_piece,
                jnp.transpose(top_part)[:, :, None],
                jnp.transpose(corr_part)[:, :, None],
                in_doc,
            )
            grad_key_run = (
                jnp.einsum(
                    "hqk,qhd->khd", grad_scores, query_piece, preferred_element_type=jnp.float32
                )
                * scale
            )
            grad_value_run = jnp.einsum(
                "hqk,qhd->khd", exp_low, numer_piece, preferred_element_type=jnp.float32
            )
            return (grad_key_run, grad_value_run)

        grad_key, grad_value = fold_keygrad(
            (
                lax.all_gather(query_loc, BLK, axis=0, tiled=True),
                lax.all_gather(
                    grad_numer.reshape(block_rows, local_width), BLK, axis=0, tiled=True
                ),
                lax.all_gather(top_rows.astype(jnp.bfloat16), BLK, axis=0, tiled=True).astype(
                    jnp.float32
                ),
                lax.all_gather(corr_rows.astype(jnp.bfloat16), BLK, axis=0, tiled=True).astype(
                    jnp.float32
                ),
            )
        )
        grad_q_rows, grad_k_rows, grad_v_rows = (
            lax.all_to_all(
                grad_query.reshape(block_rows, local_width).astype(jnp.bfloat16),
                HEAD,
                split_axis=0,
                concat_axis=1,
                tiled=True,
            ),
            lax.all_to_all(
                grad_key.reshape(block_rows, local_width).astype(jnp.bfloat16),
                HEAD,
                split_axis=0,
                concat_axis=1,
                tiled=True,
            ),
            lax.all_to_all(
                grad_value.reshape(block_rows, local_width).astype(jnp.bfloat16),
                HEAD,
                split_axis=0,
                concat_axis=1,
                tiled=True,
            ),
        )
        grad_proj = jnp.concatenate([grad_q_rows, grad_k_rows, grad_v_rows], axis=1)
        grad_query_bias = jnp.sum(grad_q_rows.astype(jnp.float32), axis=0)
        grad_value_bias = jnp.sum(grad_v_rows.astype(jnp.float32), axis=0)
        grad_proj_in = jnp.einsum(
            "rd,re->de", inputs, grad_proj, preferred_element_type=jnp.float32
        )
        input_grads.append(
            grad_one
            + jnp.einsum("re,de->rd", grad_proj, proj_in, preferred_element_type=jnp.float32)
        )
        part_grads = (
            grad_proj_in,
            grad_query_bias,
            grad_value_bias,
            grad_proj_out,
            grad_out_bias,
            grad_norm_gain,
            grad_norm_shift,
            grad_up,
            grad_up_bias,
            grad_down,
            grad_down_bias,
            grad_final_gain,
            grad_final_shift,
        )
        grad_sum = (
            part_grads
            if grad_sum is None
            else tuple((left + right for left, right in zip(grad_sum, part_grads)))
        )
    grad_sum = scatter_end(grad_sum)
    (
        grad_proj_in,
        grad_query_bias,
        grad_value_bias,
        grad_proj_out,
        grad_out_bias,
        grad_norm_gain,
        grad_norm_shift,
        grad_up,
        grad_up_bias,
        grad_down,
        grad_down_bias,
        grad_final_gain,
        grad_final_shift,
    ) = grad_sum
    return (
        jnp.stack(outputs),
        jnp.stack(input_grads),
        grad_proj_in,
        grad_query_bias,
        grad_value_bias,
        grad_proj_out,
        grad_out_bias,
        grad_norm_gain,
        grad_norm_shift,
        grad_up,
        grad_up_bias,
        grad_down,
        grad_down_bias,
        grad_final_gain,
        grad_final_shift,
    )


MESH = pl.DeviceIdType.MESH
F32 = jnp.float32
BF16 = jnp.bfloat16
DM = 768
FF = 3072
TOK = 64
SEQ = 2048
HALF = DM // 2
QKV_N = 3 * HALF
UP_N = FF // 2
CHUNK = 256

QKV, OUT, UP, DOWN = range(4)
SHAPES = (
    (4, 2, 4, 24, QKV_N),
    (4, 4, 24, DM),
    (4, 2, 4, 24, UP_N),
    (4, 4, 96, DM),
)


def by_column(kind):
    return kind in (QKV, UP)


def piece_shape(kind):
    shape = SHAPES[kind]
    return (2,) + shape[3:] if by_column(kind) else shape[2:]


def when(cond, run):
    if cond is None:
        run()
    else:
        pl.when(cond)(run)


def both(left, right):
    if left is None:
        return right
    if right is None:
        return left
    return jnp.logical_and(left, right)


class Place:
    def __init__(self):
        b = lax.axis_index(BLK)
        z = lax.axis_index(HEAD)
        c = lax.rem(b, 2)
        x = lax.rem(lax.div(b, 2), 2)
        y = lax.div(b, 4)
        self.b, self.z, self.c, self.x, self.y = b, z, c, x, y
        self.line = 4 * b + z
        self.chip = 4 * lax.div(b, 2) + z
        self.sib = (b + 1 - 2 * c, z)
        self.dx = (4 * y + 2 * (1 - x) + c, z)
        self.dy = (4 * (1 - y) + 2 * x + c, z)
        self.near = z + 1 - 2 * lax.rem(z, 2)
        self.far = lax.rem(z + 2, 4)
        self.cross = 3 - z
        self.swap = (4 * c + 2 * x + y, z)
        self.stays = y == c
        self.moves = y != c
        q = 2 * y + x
        self.q = q
        turn = lax.rem(q - z + 4, 4)
        self.active = turn < 3
        self.pair = jnp.where(self.active, 4 * turn + z, 0)
        self.part = lax.div(self.pair, 6)

    def cols(self, kind):
        x, y = self.x, self.y
        if by_column(kind):
            return (2 * y + x, 2 * y + 1 - x, 2 * (1 - y) + x, 2 * (1 - y) + 1 - x)
        return (2 * x + y, 2 * (1 - x) + y, 2 * x + 1 - y, 2 * (1 - x) + 1 - y)


def pair_place(pair):
    z = pair % 4
    return ((pair // 4 + z) % 4, z)


def chunk(kind, ref, col, z):
    return ref.at[col, :, z] if by_column(kind) else ref.at[col, z]


class Links:
    def __init__(self, sems, here):
        self.sems, self.here, self.count, self.pending, self.waits = sems, here, 0, [], []

    def alloc(self, n=1):
        at = self.count
        self.count += n
        return at

    def make(self, src, dst, s, r, dev):
        return pltpu.make_async_remote_copy(
            src_ref=src, dst_ref=dst, send_sem=self.sems.at[s], recv_sem=self.sems.at[r],
            device_id=dev, device_id_type=MESH,
        )

    def send(self, src, dst, s, r, dev, cond=None, keep=True):
        when(cond, lambda: self.make(src, dst, s, r, dev).start())
        if keep:
            self.pending.append((cond, src, dst, s, r, dev))

    def recv(self, dst, r, cond=None):
        when(cond, lambda: self.make(dst, dst, r, r, self.here.sib).wait_recv())

    def sent(self, src, dst, s, r, dev, cond=None):
        when(cond, lambda: self.make(src, dst, s, r, dev).wait_send())

    def local(self, src, dst, cond=None):
        sem = self.sems.at[self.alloc()]
        when(cond, lambda: pltpu.make_async_copy(src, dst, sem).start())
        return lambda: when(cond, lambda: pltpu.make_async_copy(src, dst, sem).wait())

    def put(self, src, dst):
        self.waits.append(self.local(src, dst))

    def finish(self):
        for cond, src, dst, s, r, dev in self.pending:
            self.sent(src, dst, s, r, dev, cond)
        for wait in self.waits:
            wait()


class Gather:
    def __init__(self, links, here, kind, ref):
        self.links, self.here, self.kind, self.ref = links, here, kind, ref
        self.s0, self.r0 = links.alloc(), links.alloc()
        self.su, self.sd, self.rz = links.alloc(4), links.alloc(4), links.alloc(4)
        self.sx, self.sy, self.rx, self.ry = (links.alloc(4) for _ in range(4))
        self.s_far, self.r_far = links.alloc(4), links.alloc(4)
        self.col, self.col_x, self.col_y, self.col_d = here.cols(kind)

    def first_wait(self):
        here, kind = self.here, self.kind
        if by_column(kind):
            self.links.recv(self.ref.at[self.col, 1 - here.c, here.z], self.r0)
        else:
            self.links.recv(self.ref.at[self.col, here.z], self.r0, here.moves)

    def piece(self, col, z):
        return chunk(self.kind, self.ref, col, z)

    def z_hop(self, z, to, base):
        piece = self.piece(self.col, z)
        self.links.send(piece, piece, base + z, self.rz + z, (self.here.b, to))

    def spread(self, z):
        piece = self.piece(self.col, z)
        self.links.send(piece, piece, self.sx + z, self.rx + z, self.here.dx)
        self.links.send(piece, piece, self.sy + z, self.ry + z, self.here.dy)

    def own_z(self):
        self.first_wait()
        here = self.here
        self.z_hop(here.z, here.far, self.su)
        self.z_hop(here.z, here.near, self.sd)

    def own_plane(self):
        self.spread(self.here.z)

    def land(self, z):
        self.links.recv(self.piece(self.col, z), self.rz + z)

    def hop(self):
        self.z_hop(self.here.far, self.here.near, self.sd)

    def relay(self, z):
        here = self.here
        low = z < 2
        piece = self.piece(jnp.where(low, self.col_x, self.col_y), z)
        self.links.recv(piece, jnp.where(low, self.rx + z, self.ry + z))
        dev = (jnp.where(low, here.dy[0], here.dx[0]), here.z)
        self.links.send(piece, piece, self.s_far + z, self.r_far + z, dev)

    def done(self):
        for z in range(4):
            if z < 2:
                self.links.recv(self.piece(self.col_y, z), self.ry + z)
            else:
                self.links.recv(self.piece(self.col_x, z), self.rx + z)
            self.links.recv(self.piece(self.col_d, z), self.r_far + z)


class Scatter:
    def __init__(self, links, here, kind, refs):
        self.links, self.here, self.kind = links, here, kind
        self.grad, self.far, self.cxy, self.zb, self.zr, self.fin, self.last = refs
        self.s_far, self.r_far = links.alloc(4), links.alloc(4)
        self.sxy, self.rxy = links.alloc(8), links.alloc(8)
        self.sz, self.rz = links.alloc(4), links.alloc(4)
        self.s_end, self.r_end = links.alloc(), links.alloc()
        self.col, self.col_x, self.col_y, self.col_d = here.cols(kind)

    def piece(self, col, z):
        return chunk(self.kind, self.grad, col, z)

    def add(self, dst, terms):
        blocks = [(h,) for h in range(2)] if by_column(self.kind) else [(slice(0, None),)]
        for at in blocks:
            total = terms[0][at].astype(F32)
            for term in terms[1:]:
                total = total + term[at].astype(F32)
            dst[at] = total.astype(dst.dtype)

    def side(self, z, first):
        here = self.here
        to_x = z < 2 if first else z >= 2
        col = jnp.where(to_x, self.col_x, self.col_y)
        dev = (jnp.where(to_x, here.dx[0], here.dy[0]), here.z)
        slot = jnp.where(to_x, z, 4 + z)
        self.links.send(self.piece(col, z), self.cxy.at[slot], self.sxy + slot, self.rxy + slot, dev)

    def send(self, z):
        here = self.here
        dev = (jnp.where(z < 2, here.dx[0], here.dy[0]), here.z)
        self.links.send(self.piece(self.col_d, z), self.far.at[z], self.s_far + z, self.r_far + z, dev)
        self.side(z, True)

    def relay(self, z):
        self.links.recv(self.far.at[z], self.r_far + z)
        piece = self.piece(jnp.where(z < 2, self.col_y, self.col_x), z)
        self.add(piece, (piece, self.far.at[z]))
        self.side(z, False)

    def plane(self, z):
        self.links.recv(self.cxy.at[z], self.rxy + z)
        self.links.recv(self.cxy.at[4 + z], self.rxy + 4 + z)
        self.add(self.zb.at[z], (self.piece(self.col, z), self.cxy.at[z], self.cxy.at[4 + z]))

    def z_first(self):
        here = self.here
        for i, z in enumerate((here.near, here.cross)):
            self.links.send(self.zb.at[z], self.zr.at[i], self.sz + i, self.rz + i, (here.b, here.near))

    def z_second(self):
        here = self.here
        self.links.recv(self.zr.at[1], self.rz + 1)
        piece = self.zb.at[here.far]
        self.add(piece, (piece, self.zr.at[1]))
        self.links.send(piece, self.zr.at[2], self.sz + 2, self.rz + 2, (here.b, here.far))

    def z_direct(self, z):
        here = self.here
        self.links.send(self.zb.at[z], self.zr.at[here.z], self.sz + z, self.rz + here.z, (here.b, z))

    def z_last(self, direct=False):
        links, here = self.links, self.here
        own = self.zb.at[here.z]
        if direct:
            others = (here.near, here.cross, here.far)
        else:
            others = (0, 2)
        for z in others:
            links.recv(self.zr.at[z], self.rz + z)
        self.add(self.fin, [own] + [self.zr.at[z] for z in others])
        if by_column(self.kind):
            links.send(self.fin.at[1 - here.c], self.last, self.s_end, self.r_end, here.sib)
        else:
            links.send(self.fin, self.last, self.s_end, self.r_end, here.swap, here.moves)

    def finish(self, out):
        links, here, kind = self.links, self.here, self.kind
        c = here.c
        if kind == QKV:
            for j in range(3):
                at = pl.multiple_of(DM * j + HALF * c, 128)
                out[:, pl.ds(at, HALF)] = self.fin[c, :, HALF * j : HALF * (j + 1)]
            links.recv(self.last, self.r_end)
            for j in range(3):
                at = pl.multiple_of(DM * j + HALF * (1 - c), 128)
                out[:, pl.ds(at, HALF)] = self.last[:, HALF * j : HALF * (j + 1)]
        elif kind == UP:
            out[:, pl.ds(pl.multiple_of(UP_N * c, 128), UP_N)] = self.fin[c]
            links.recv(self.last, self.r_end)
            out[:, pl.ds(pl.multiple_of(UP_N * (1 - c), 128), UP_N)] = self.last[...]
        else:
            links.recv(self.last, self.r_end, here.moves)

            def keep():
                out[...] = self.fin[...]

            def take():
                out[...] = self.last[...]

            when(here.stays, keep)
            when(here.moves, take)


def dot(a, b):
    return jnp.dot(a, b, preferred_element_type=F32)


def dot_nt(a, b):
    return lax.dot_general(a, b, (((1,), (1,)), ((), ())), preferred_element_type=F32)


def dot_tn(a, b):
    return lax.dot_general(a, b, (((0,), (0,)), ((), ())), preferred_element_type=F32)


def row_sum(values):
    return jnp.sum(values, axis=0, keepdims=True)


def div24(n):
    return lax.shift_right_logical(n * 2731, 16)


def iota(shape, dim):
    return lax.broadcasted_iota(jnp.int32, shape, dim)


def select_24():
    n = iota((128, DM), 1)
    return (iota((128, DM), 0) == n - 24 * div24(n)).astype(BF16)


def select_96():
    n = iota((128, UP_N), 1)
    run = lax.shift_right_logical(div24(n), 2)
    return (iota((128, UP_N), 0) == 32 + n - 96 * run).astype(BF16)


def owner_24(lead):
    shape = (lead, 8, DM)
    return div24(iota(shape, 2)) == iota(shape, 0)


def owner_96():
    shape = (16, UP_N)
    return lax.shift_right_logical(div24(iota(shape, 1)), 2) == iota(shape, 0)


def exact_nt(values, select):
    high = values.astype(BF16)
    rest = values - high.astype(F32)
    mid = rest.astype(BF16)
    low = (rest - mid.astype(F32)).astype(BF16)
    return dot_nt(high, select) + dot_nt(mid, select) + dot_nt(low, select)


SCRATCH = dict(
    vecs=((8, 128), F32),
    cot=((2, TOK, DM), BF16),
    b_out=((2, TOK, DM), F32),
    b_tok=((2, TOK, DM), F32),
    b_qkv=((24, 2 * QKV_N), F32),
    b_wout=((24, DM), F32),
    b_up=((24, FF), F32),
    b_down=((96, DM), F32),
    b_vec=((8, 128), F32),
    vec_all=((32, 8, 128), F32),
    vec_rows=((8, DM), F32),
    up_row=((1, UP_N), F32),
    x_chip=((2, 2, TOK, DM), BF16),
    fl_chip=((2, 2, TOK, DM), BF16),
    gf_chip=((2, 2, TOK, DM), BF16),
    ga_chip=((2, 2, TOK, DM), BF16),
    partial=((2, 2, TOK, DM), F32),
    back0=((2, TOK, DM), F32),
    back1=((2, TOK, DM), F32),
    back2=((2, TOK, DM), F32),
    back3=((2, TOK, DM), F32),
    send_q=((12, 192, 128), BF16),
    qkv_t=((192, SEQ), BF16),
    k_rows=((SEQ, HD), BF16),
    v_rows=((SEQ, HD), BF16),
    q_rows=((SEQ, HD), BF16),
    g_rows=((SEQ, HD), BF16),
    key_doc=((SEQ, 128), jnp.int32),
    query_doc=((1, SEQ), jnp.int32),
    scores=((SEQ, CHUNK), F32),
    weights=((SEQ, SEQ), BF16),
    total=((1, SEQ), F32),
    att_t=((HD, SEQ), F32),
    att_send=((HD, SEQ), BF16),
    mix_in=((12, HD, 128), BF16),
    g_send=((12, HD, 128), BF16),
    g_t=((HD, SEQ), BF16),
    gn_t=((HD, SEQ), BF16),
    corr=((1, SEQ), F32),
    ds=((CHUNK, SEQ), BF16),
    dq_t=((HD, SEQ), F32),
    d_send=((192, SEQ), BF16),
    d_in=((12, 192, 128), BF16),
    mixed_t=((HALF, 2 * 128), BF16),
    first=((2 * TOK, DM), F32),
    normed1=((2 * TOK, DM), F32),
    inv1=((2 * TOK, 1), F32),
    active=((4 * TOK, UP_N), BF16),
    slope=((4 * TOK, UP_N), F32),
    gh=((4 * TOK, UP_N), BF16),
    gh2=((2 * TOK, DM), F32),
    gh1=((2 * TOK, DM), F32),
    gp=((4 * TOK, QKV_N), BF16),
    vec_grad=((8, DM), F32),
    up_grad=((1, UP_N), F32),
    vec_send=((32, 8, 128), F32),
    vec_recv=((32, 8, 128), F32),
)


def kind_scratch(kind):
    shape = SHAPES[kind]
    piece = piece_shape(kind)
    last = piece[1:] if by_column(kind) else piece
    low = [shape, shape, (4,) + piece, (8,) + piece, (4,) + piece, (4,) + piece]
    return [(s, BF16) for s in low] + [(piece, F32), (last, F32)]


def all_scratch():
    shapes = list(SCRATCH.values())
    for kind in range(4):
        shapes += kind_scratch(kind)
    shapes += [((24,), BF16)] * 8 + [((96,), BF16)]
    return [pltpu.VMEM(shape, dtype) for shape, dtype in shapes] + [pltpu.SemaphoreType.DMA((N_SEM,))]


N_SEM = 414


def layer_kernel(
    tokens, starts, w_qkv, w_out, w_up, w_down,
    v0, v1, v2, v3, v4, v5, v6, v7, v8, cotangent,
    o_out, o_tok, o_qkv, o_wout, o_up, o_down, o_vec,
    *scratch,
):
    vec_in = (v0, v1, v2, v3, v4, v5, v6, v7, v8)
    named = len(SCRATCH)
    m = SimpleNamespace(**dict(zip(SCRATCH, scratch)))
    kinds = [scratch[named + 8 * kind : named + 8 * (kind + 1)] for kind in range(4)]
    vec_rows_in = scratch[-10:-1]
    sems = scratch[-1]
    here = Place()
    links = Links(sems, here)
    b, z, c = here.b, here.z, here.c
    line, chip = here.line, here.chip
    gathers = [Gather(links, here, kind, kinds[kind][0]) for kind in range(4)]
    scatters = [Scatter(links, here, kind, kinds[kind][1:]) for kind in range(4)]

    def peer(d):
        other = lax.rem(line + d, 32)
        return (lax.div(other, 4), lax.rem(other, 4))

    g_qkv, g_out, g_up, g_down = gathers
    x_chip = m.x_chip

    def third(j, which):
        return w_qkv.at[:, pl.ds(pl.multiple_of(DM * j + HALF * which, 128), HALF)]

    def up_part(which):
        return w_up.at[:, pl.ds(pl.multiple_of(UP_N * which, 128), UP_N)]

    def slot_part(j):
        return g_qkv.ref.at[g_qkv.col, c, z, :, pl.ds(HALF * j, HALF)]

    vec_waits = [links.local(src, dst) for src, dst in zip(vec_in, vec_rows_in)]
    qkv_waits = [links.local(third(j, c), slot_part(j)) for j in range(3)]
    x_wait = links.local(tokens, x_chip.at[:, c])
    up_wait = links.local(up_part(c), g_up.ref.at[g_up.col, c, z])
    row_waits = [
        links.local(shard, gather.ref.at[gather.col, z], here.stays)
        for gather, shard in ((g_out, w_out), (g_down, w_down))
    ]
    cot_wait = links.local(cotangent, m.cot)
    m.vec_grad[...] = jnp.zeros((8, DM), F32)
    m.vecs[...] = jnp.zeros((8, 128), F32)
    for wait in vec_waits:
        wait()
    for j in range(8):
        m.vecs[j : j + 1, 0:24] = vec_rows_in[j][...].astype(F32).reshape(1, 24)
    m.vecs[0:1, 32:128] = vec_rows_in[8][...].astype(F32).reshape(1, 96)

    barrier = pltpu.get_barrier_semaphore()

    def greet(d, carry):
        pl.semaphore_signal(barrier, inc=1, device_id=peer(d), device_id_type=MESH)
        return carry

    lax.fori_loop(1, 32, greet, 0)
    pl.semaphore_wait(barrier, 31)

    q_sem = links.alloc(3)
    for j in range(3):
        links.send(third(j, 1 - c), slot_part(j), q_sem + j, g_qkv.r0, here.sib)
    x_sem = links.alloc(2)
    links.send(tokens, x_chip.at[:, c], x_sem, x_sem + 1, here.sib)
    links.send(up_part(1 - c), g_up.ref.at[g_up.col, c, z], g_up.s0, g_up.r0, here.sib)
    for gather, shard in ((g_out, w_out), (g_down, w_down)):
        slot = gather.ref.at[2 * here.x + c, z]
        links.send(shard, slot, gather.s0, gather.r0, here.swap, here.moves)
    vec_sem = links.alloc(4)
    vec_all = m.vec_all

    def vec_copy(d):
        return links.make(m.vecs, vec_all.at[line], vec_sem, vec_sem + 1, peer(d))

    def vec_start(d, carry):
        vec_copy(d).start()
        return carry

    lax.fori_loop(1, 32, vec_start, 0)
    vec_all[line] = m.vecs[...]
    for wait in (*qkv_waits, x_wait, up_wait, *row_waits, cot_wait):
        wait()

    g_qkv.own_z()
    g_qkv.own_plane()
    rest = (g_out, g_up, g_down)

    def documents():
        def position(n):
            q_part = lax.shift_left(lax.shift_right_logical(n, 9), 9)
            core_part = lax.shift_left(jnp.bitwise_and(lax.shift_right_logical(n, 6), 1), 8)
            z_part = lax.shift_left(jnp.bitwise_and(lax.shift_right_logical(n, 7), 3), 6)
            return q_part + core_part + z_part + jnp.bitwise_and(n, 63)

        def doc_of(n):
            place = position(n)
            doc = jnp.zeros(place.shape, jnp.int32)
            for j in range(starts.shape[1]):
                doc = doc + (starts[here.part, j] <= place).astype(jnp.int32)
            return doc

        m.query_doc[...] = doc_of(iota((1, SEQ), 1))

        def rows(i, carry):
            at = pl.multiple_of(i * 256, 256)
            m.key_doc[pl.ds(at, 256), :] = doc_of(iota((256, 128), 0) + i * 256)
            return carry

        lax.fori_loop(0, SEQ // 256, rows, 0)

    when(here.active, documents)

    g_qkv.relay(z)
    g_qkv.land(here.far)
    g_qkv.hop()
    g_qkv.spread(here.far)
    for gather in rest[:2]:
        gather.own_z()
    many = vec_all.at[pl.ds(0, 31)]
    links.make(many, many, vec_sem, vec_sem + 1, here.sib).wait_send()
    links.recv(many, vec_sem + 1)
    spread = dot(vec_all[...].reshape(256, 128).astype(BF16), select_24()).reshape(32, 8, DM)
    m.vec_rows[...] = jnp.sum(jnp.where(owner_24(32), spread, 0.0), axis=0)
    spread = dot(vec_all[pl.ds(16 * c, 16), 0, :].astype(BF16), select_96())
    m.up_row[...] = row_sum(jnp.where(owner_96(), spread, 0.0))

    def vector(j):
        return m.vec_rows[j : j + 1, :]

    def vector_half(j):
        return m.vec_rows[j : j + 1, pl.ds(pl.multiple_of(HALF * c, 128), HALF)]

    g_qkv.land(here.near)
    g_qkv.spread(here.near)
    g_qkv.relay(here.far)
    for gather in rest[:2]:
        gather.own_plane()
    g_qkv.land(here.cross)
    g_qkv.spread(here.cross)
    g_qkv.relay(here.near)
    g_qkv.relay(here.cross)
    for gather in rest[:2]:
        gather.land(here.far)
        gather.hop()
    links.recv(x_chip.at[:, 1 - c], x_sem + 1)
    g_qkv.done()

    def weight_qkv(j):
        return g_qkv.ref[:, :, :, :, HALF * j : HALF * (j + 1)].reshape(DM, HALF)

    def x_rows():
        return x_chip[...].reshape(4 * TOK, DM)

    send_q = m.send_q
    for j in range(3):
        rows = dot(x_rows(), weight_qkv(j))
        if j == 0:
            rows = (rows + vector_half(0)).astype(BF16) * jnp.asarray(HD ** (-0.5), BF16)
        elif j == 1:
            rows = rows.astype(BF16)
        else:
            rows = (rows + vector_half(1)).astype(BF16)
        turned = rows.T
        for part in range(MB):
            piece = turned[:, 128 * part : 128 * (part + 1)].reshape(6, HD, 128)
            send_q[6 * part : 6 * part + 6, HD * j : HD * (j + 1), :] = piece

    chip_lanes = pl.ds(pl.multiple_of(chip * 128, 128), 128)

    def to_pairs(src, dst_of, rows):
        s, r, local = links.alloc(12), links.alloc(), links.alloc()
        for pair in range(12):
            q_to, z_to = pair_place(pair)
            mine = jnp.logical_and(here.q == q_to, z == z_to)
            links.send(src.at[pair], dst_of(chip_lanes), s + pair, r, (2 * q_to + c, z_to), jnp.logical_not(mine))

        def own():
            copy = pltpu.make_async_copy(src.at[here.pair], dst_of(chip_lanes), sems.at[local])
            copy.start()
            copy.wait()

        when(here.active, own)
        return lambda: links.recv(dst_of(pl.ds(0, 15 * 128)), r, here.active)

    class ToChips:
        def __init__(self, src_of, dst_of, own):
            self.src_of, self.dst_of, self.own = src_of, dst_of, own
            self.s, self.r = links.alloc(16), links.alloc()

        def start(self, other):
            src, dst = self.src_of(pl.ds(pl.multiple_of(128 * other, 128), 128)), self.dst_of(here.pair)
            dev = (2 * lax.div(other, 4) + c, lax.rem(other, 4))
            links.send(src, dst, self.s + other, self.r, dev, chip != other, keep=False)

        def finish(self):
            for other in range(16):
                src, dst = self.src_of(pl.ds(128 * other, 128)), self.dst_of(here.pair)
                links.pending.append((both(here.active, chip != other), src, dst, self.s + other, self.r, here.sib))
            when(here.active, self.own)

        def wait(self):
            links.recv(self.dst_of(pl.ds(0, 11)), self.r, here.active)
            links.recv(self.dst_of(pl.ds(0, 12)), self.r, jnp.logical_not(here.active))

    qkv_t = m.qkv_t
    wait_q = to_pairs(send_q, lambda lanes: qkv_t.at[:, lanes], 192)
    for gather in rest[:2]:
        gather.spread(here.far)
    for gather in rest[:2]:
        gather.relay(z)
    for gather in rest[:2]:
        gather.land(here.near)
        gather.spread(here.near)
    for gather in rest[:2]:
        gather.relay(here.far)
    wait_q()
    g_down.own_z()
    for gather in rest[:2]:
        gather.land(here.cross)
        gather.spread(here.cross)
    g_down.own_plane()

    def own_mix():
        m.mix_in[here.pair] = m.att_send[:, chip_lanes]

    mix = ToChips(lambda lanes: m.att_send.at[:, lanes], lambda pair: m.mix_in.at[pair], own_mix)

    weights = m.weights

    def turn_keys():
        m.k_rows[...] = qkv_t[HD : 2 * HD, :].T
        m.v_rows[...] = qkv_t[2 * HD : 3 * HD, :].T
        m.q_rows[...] = qkv_t[0:HD, :].T

    when(here.active, turn_keys)

    def attend(i):
        lanes = pl.ds(pl.multiple_of(i * CHUNK, CHUNK), CHUNK)
        query = qkv_t[0:HD, lanes]
        doc = m.query_doc[:, lanes]
        top = None
        for k in range(8):
            rows = slice(256 * k, 256 * (k + 1))
            key_doc = m.key_doc[rows, :]
            same = jnp.concatenate([key_doc, key_doc], axis=1) == doc
            scores = jnp.where(same, dot(m.k_rows[rows, :], query), NEG)
            m.scores[rows, :] = scores
            here_top = jnp.max(scores, axis=0, keepdims=True)
            top = here_top if top is None else jnp.maximum(top, here_top)
        total = None
        for k in range(8):
            rows = slice(256 * k, 256 * (k + 1))
            grown = jnp.exp(m.scores[rows, :] - top)
            weights[rows, lanes] = grown.astype(BF16)
            part_sum = row_sum(grown)
            total = part_sum if total is None else total + part_sum
        numer = dot(qkv_t[2 * HD : 3 * HD, :], weights[:, lanes])
        attended = numer / total
        m.total[:, lanes] = total
        m.att_t[:, lanes] = attended
        m.att_send[:, lanes] = attended.astype(BF16)
        mix.start(2 * i)
        mix.start(2 * i + 1)

    def attend_some(first, last):
        def run():
            def one(i, carry):
                attend(i)
                return carry

            lax.fori_loop(first, last, one, 0)

        when(here.active, run)

    attend_some(0, 2)
    for gather in rest[:2]:
        gather.relay(here.near)
    g_down.land(here.far)
    g_down.hop()
    g_down.spread(here.far)
    attend_some(2, 5)
    for gather in rest[:2]:
        gather.relay(here.cross)
    g_down.land(here.near)
    g_down.spread(here.near)
    g_down.relay(z)
    attend_some(5, 8)

    g_down.land(here.cross)
    g_down.spread(here.cross)
    g_down.relay(here.far)
    mix.finish()
    mix.wait()
    g_out.done()
    def share(buf, values):
        at = links.alloc(2)
        buf[:, c] = values.reshape(MB, TOK, DM)
        links.send(buf.at[:, c], buf.at[:, c], at, at + 1, here.sib)
        links.recv(buf.at[:, 1 - c], at + 1)

    def combine(values, back):
        at = links.alloc(2)
        partial = m.partial
        partial[...] = values.reshape(MB, 2, TOK, DM)
        links.send(partial.at[:, 1 - c], back, at, at + 1, here.sib, keep=False)
        links.recv(back, at + 1)
        total = partial[:, c].reshape(2 * TOK, DM) + back[...].reshape(2 * TOK, DM)
        links.sent(partial.at[:, 1 - c], back, at, at + 1, here.sib)
        return total

    def norm_rows(values, gain, shift):
        center = values - jnp.mean(values, axis=-1, keepdims=True)
        inverse = lax.rsqrt(jnp.mean(center * center, axis=-1, keepdims=True) + EPS)
        normed = center * inverse
        return normed * gain + shift, normed, inverse

    def norm_back(upstream, normed, inverse, gain):
        scaled = upstream * gain
        return inverse * (
            scaled
            - jnp.mean(scaled, axis=-1, keepdims=True)
            - normed * jnp.mean(scaled * normed, axis=-1, keepdims=True)
        )

    mixed_t = m.mixed_t
    mixed = []
    for part in range(MB):
        piece = m.mix_in[6 * part : 6 * part + 6].reshape(HALF, 128)
        mixed_t[:, 128 * part : 128 * (part + 1)] = piece
        mixed.append(piece.T)
    mixed = jnp.concatenate(mixed, axis=0)

    def weight_out():
        return g_out.ref[...].reshape(HALF, DM)

    attn = combine(dot(mixed, weight_out()), m.back0) + vector(2)
    first, normed_one, inverse_one = norm_rows(
        x_chip[:, c].reshape(2 * TOK, DM).astype(F32) + attn, vector(3), vector(4)
    )
    m.first[...] = first
    m.normed1[...] = normed_one
    m.inv1[...] = inverse_one
    share(m.fl_chip, first.astype(BF16))

    g_down.relay(here.near)
    g_up.done()
    def fl_rows():
        return m.fl_chip[...].reshape(4 * TOK, DM)

    def weight_up(j):
        return g_up.ref[:, :, :, :, HALF * j : HALF * (j + 1)].reshape(DM, HALF)

    def weight_down(j):
        return g_down.ref[j].reshape(HALF, DM)

    for j in range(4):
        lanes = slice(HALF * j, HALF * (j + 1))
        hidden = dot(fl_rows(), weight_up(j)) + m.up_row[:, lanes]
        cdf = 0.5 * (1.0 + lax.erf(hidden * (0.5**0.5)))
        m.slope[:, lanes] = cdf + hidden * (jnp.exp(-0.5 * hidden * hidden) * 0.3989422804014327)
        m.active[:, lanes] = (hidden * cdf).astype(BF16)
    g_down.relay(here.cross)
    g_down.done()
    ffn = None
    for j in range(4):
        lanes = slice(HALF * j, HALF * (j + 1))
        term = dot(m.active[:, lanes], weight_down(j))
        ffn = term if ffn is None else ffn + term
    ffn = combine(ffn, m.back1) + vector(5)
    result, normed_two, inverse_two = norm_rows(m.first[...] + ffn, vector(6), vector(7))
    m.b_out[...] = result.reshape(MB, TOK, DM)
    links.put(m.b_out, o_out)

    vec_grad = m.vec_grad
    grad_result = m.cot[...].reshape(2 * TOK, DM).astype(F32)
    vec_grad[6:7, :] = row_sum(grad_result * normed_two)
    vec_grad[7:8, :] = row_sum(grad_result)
    grad_two = norm_back(grad_result, normed_two, inverse_two, vector(6))
    m.gh2[...] = grad_two
    grad_ffn = grad_two.astype(BF16)
    vec_grad[5:6, :] = row_sum(grad_ffn.astype(F32))
    share(m.gf_chip, grad_ffn)

    def gf_rows():
        return m.gf_chip[...].reshape(4 * TOK, DM)

    s_qkv, s_out, s_up, s_down = scatters
    targets = (here.near, here.cross, here.far, z)
    for j in range(4):
        lanes = slice(HALF * j, HALF * (j + 1))
        s_down.grad[j] = dot_tn(m.active[:, lanes], gf_rows()).astype(BF16).reshape(4, 96, DM)
    for t in targets:
        s_down.send(t)
    for j in range(4):
        lanes = slice(HALF * j, HALF * (j + 1))
        grad_active = dot_nt(gf_rows(), weight_down(j))
        grad_hidden = (grad_active * m.slope[:, lanes]).astype(BF16)
        m.gh[:, lanes] = grad_hidden
        m.up_grad[:, lanes] = row_sum(grad_hidden.astype(F32))
    grad_first = None
    for j in range(4):
        lanes = slice(HALF * j, HALF * (j + 1))
        term = dot_nt(m.gh[:, lanes], weight_up(j))
        grad_first = term if grad_first is None else grad_first + term
    grad_first = m.gh2[...] + combine(grad_first, m.back2)
    normed_one = m.normed1[...]
    vec_grad[3:4, :] = row_sum(grad_first * normed_one)
    vec_grad[4:5, :] = row_sum(grad_first)
    grad_one = norm_back(grad_first, normed_one, m.inv1[...], vector(3))
    m.gh1[...] = grad_one
    grad_attn = grad_one.astype(BF16)
    vec_grad[2:3, :] = row_sum(grad_attn.astype(F32))
    share(m.ga_chip, grad_attn)

    def ga_rows():
        return m.ga_chip[...].reshape(4 * TOK, DM)

    turned = dot_nt(ga_rows(), weight_out()).astype(BF16).T
    for part in range(MB):
        m.g_send[6 * part : 6 * part + 6] = turned[:, 128 * part : 128 * (part + 1)].reshape(6, HD, 128)
    g_t = m.g_t
    wait_g = to_pairs(m.g_send, lambda lanes: g_t.at[:, lanes], HD)
    for j in range(4):
        lanes = slice(HALF * j, HALF * (j + 1))
        s_up.grad[:, :, :, :, lanes] = (
            dot_tn(fl_rows(), m.gh[:, lanes]).astype(BF16).reshape(4, 2, 4, 24, HALF)
        )
    for t in targets:
        s_up.send(t)
    s_out.grad[...] = dot(mixed_t[...], ga_rows()).astype(BF16).reshape(SHAPES[OUT])
    for t in targets:
        s_out.send(t)
    for t in targets:
        s_down.relay(t)
    wait_g()

    d_in = m.d_in

    def own_kv():
        d_in[here.pair, HD : 3 * HD, :] = d_send[HD : 3 * HD, chip_lanes]

    def own_q():
        d_in[here.pair, 0:HD, :] = d_send[0:HD, chip_lanes]

    grad_kv = ToChips(
        lambda lanes: d_send.at[pl.ds(HD, 2 * HD), lanes], lambda pair: d_in.at[pair, pl.ds(HD, 2 * HD)], own_kv
    )
    grad_q = ToChips(lambda lanes: d_send.at[pl.ds(0, HD), lanes], lambda pair: d_in.at[pair, pl.ds(0, HD)], own_q)
    d_send = m.d_send

    def turn_grads():
        grad = g_t[...].astype(F32)
        inverse = 1.0 / m.total[...]
        numer = grad * inverse
        m.gn_t[...] = numer.astype(BF16)
        m.g_rows[...] = numer.astype(BF16).T
        m.corr[...] = row_sum(grad * m.att_t[...]) * inverse
        m.dq_t[...] = jnp.zeros((HD, SEQ), F32)

    when(here.active, turn_grads)

    def back(k):
        at = pl.ds(pl.multiple_of(k * CHUNK, CHUNK), CHUNK)
        value = m.v_rows[at, :]
        for i in range(4):
            lanes = slice(512 * i, 512 * (i + 1))
            grad_weights = dot(value, m.gn_t[:, lanes])
            grown = weights[at, lanes].astype(F32)
            m.ds[:, lanes] = (grown * (grad_weights - m.corr[:, lanes])).astype(BF16)
        ds = m.ds
        d_send[HD : 2 * HD, at] = dot(ds[...], m.q_rows[...]).T.astype(BF16)
        d_send[2 * HD : 3 * HD, at] = dot(weights[at, :], m.g_rows[...]).T.astype(BF16)
        grad_kv.start(2 * k)
        grad_kv.start(2 * k + 1)
        m.dq_t[...] += dot(qkv_t[HD : 2 * HD, at], ds[...])

    def back_some(first, last):
        def run():
            def one(i, carry):
                back(i)
                return carry

            lax.fori_loop(first, last, one, 0)

        when(here.active, run)

    back_some(0, 4)
    back_some(4, 8)

    def last_query():
        d_send[0:HD, :] = (m.dq_t[...] * (HD ** (-0.5))).astype(BF16)
        for other in range(16):
            grad_q.start(other)

    when(here.active, last_query)
    grad_kv.finish()
    grad_q.finish()
    for t in targets:
        s_up.relay(t)
    for t in targets:
        s_out.relay(t)
    for t in targets:
        s_down.plane(t)
        if t is here.cross:
            s_down.z_first()
    grad_kv.wait()
    grad_q.wait()
    s_down.z_second()
    gp = m.gp
    for part in range(MB):
        for j in range(3):
            piece = d_in[6 * part : 6 * part + 6, HD * j : HD * (j + 1), :].reshape(HALF, 128)
            gp[128 * part : 128 * (part + 1), HALF * j : HALF * (j + 1)] = piece.T
    own_half = pl.ds(pl.multiple_of(HALF * c, 128), HALF)
    for j in range(3):
        lanes = slice(HALF * j, HALF * (j + 1))
        s_qkv.grad[:, :, :, :, lanes] = (
            dot_tn(x_rows(), gp[:, lanes]).astype(BF16).reshape(4, 2, 4, 24, HALF)
        )
    for t in targets:
        s_qkv.send(t)
    vec_grad[0:1, own_half] = row_sum(gp[:, 0:HALF].astype(F32))
    vec_grad[1:2, own_half] = row_sum(gp[:, 2 * HALF : 3 * HALF].astype(F32))

    vec_send, vec_recv = m.vec_send, m.vec_recv
    spread = jnp.where(owner_24(32), vec_grad[...][None], 0.0).reshape(256, DM)
    vec_send[...] = exact_nt(spread, select_24()).reshape(32, 8, 128)
    spread = jnp.where(owner_96(), m.up_grad[...], 0.0)
    own_lines = pl.ds(16 * c, 16)
    vec_send[own_lines, 0, :] = vec_send[own_lines, 0, :] + exact_nt(spread, select_96())

    def grad_copy(d):
        other = lax.rem(line + d, 32)
        return links.make(vec_send.at[other], vec_recv.at[line], vec_sem + 2, vec_sem + 3, peer(d))

    def grad_start(d, carry):
        grad_copy(d).start()
        return carry

    lax.fori_loop(1, 32, grad_start, 0)
    vec_recv[line] = vec_send[line]

    grad_tokens = None
    for j in range(3):
        term = dot_nt(gp[:, HALF * j : HALF * (j + 1)], weight_qkv(j))
        grad_tokens = term if grad_tokens is None else grad_tokens + term
    m.b_tok[...] = (m.gh1[...] + combine(grad_tokens, m.back3)).reshape(MB, TOK, DM)
    links.put(m.b_tok, o_tok)

    for scatter in (s_up, s_out):
        for t in targets:
            scatter.plane(t)
            if t is here.cross:
                scatter.z_first()
    for t in targets:
        s_qkv.relay(t)
    s_up.z_second()
    s_out.z_second()
    for t in targets:
        s_qkv.plane(t)
        if t is not z:
            s_qkv.z_direct(t)
    for scatter in (s_down, s_up, s_out):
        scatter.z_last()
    for scatter, out, to in ((s_down, m.b_down, o_down), (s_up, m.b_up, o_up), (s_out, m.b_wout, o_wout)):
        scatter.finish(out)
        links.put(out, to)

    many_send, many_recv = vec_send.at[pl.ds(0, 31)], vec_recv.at[pl.ds(0, 31)]
    links.make(many_send, many_send, vec_sem + 2, vec_sem + 3, here.sib).wait_send()
    links.recv(many_recv, vec_sem + 3)
    m.b_vec[...] = jnp.sum(vec_recv[...], axis=0)
    links.put(m.b_vec, o_vec)

    s_qkv.z_last(direct=True)
    s_qkv.finish(m.b_qkv)
    links.put(m.b_qkv, o_qkv)
    links.finish()
    assert links.count == N_SEM, links.count


def place_kernel(*refs):
    ins, big_out, vec_out = refs[0:7], refs[7:13], refs[13:22]
    held, rows, sems = refs[22:29], refs[29:38], refs[38]
    loads = [pltpu.make_async_copy(src, dst, sems.at[i]) for i, (src, dst) in enumerate(zip(ins, held))]
    for load in reversed(loads):
        load.start()
    stores = [pltpu.make_async_copy(src, dst, sems.at[7 + i]) for i, (src, dst) in enumerate(zip(held, big_out))]
    stores += [pltpu.make_async_copy(src, dst, sems.at[13 + i]) for i, (src, dst) in enumerate(zip(rows, vec_out))]
    loads[6].wait()
    for j in range(8):
        rows[j][...] = held[6][j, 0:24]
    rows[8][...] = held[6][0, 32:128]
    for store in stores[6:]:
        store.start()
    for load, store in zip(loads, stores[:6]):
        load.wait()
        store.start()
    for store in stores:
        store.wait()


def fused(
    tokens, starts, w_qkv, bias_q, bias_v, w_out, bias_out, gain_one, shift_one,
    w_up, bias_up, w_down, bias_down, gain_two, shift_two, cotangent,
):
    anywhere = pl.BlockSpec(memory_space=pl.ANY)
    vectors = (bias_q, bias_v, bias_out, gain_one, shift_one, bias_down, gain_two, shift_two, bias_up)
    big = [tokens.shape, tokens.shape, w_qkv.shape, w_out.shape, w_up.shape, w_down.shape]
    big = [jax.ShapeDtypeStruct(shape, F32) for shape in big]
    small = [jax.ShapeDtypeStruct(vector.shape, F32) for vector in vectors]
    made = pl.pallas_call(
        layer_kernel,
        name="layer",
        out_shape=big + [jax.ShapeDtypeStruct((8, 128), F32)],
        in_specs=[anywhere, pl.BlockSpec(memory_space=pltpu.SMEM)] + [anywhere] * 14,
        out_specs=[anywhere] * 7,
        scratch_shapes=all_scratch(),
        compiler_params=pltpu.CompilerParams(
            collective_id=0, has_side_effects=True, vmem_limit_bytes=63 * 2**20
        ),
    )(tokens, starts, w_qkv, w_out, w_up, w_down, *vectors, cotangent)
    placed = pl.pallas_call(
        place_kernel,
        name="place",
        out_shape=big + small,
        in_specs=[anywhere] * 7,
        out_specs=[anywhere] * 15,
        scratch_shapes=[pltpu.VMEM(array.shape, F32) for array in (*made, *vectors)]
        + [pltpu.SemaphoreType.DMA((22,))],
    )(*made)
    out, tok, g_qkv, g_wout, g_up, g_down, bq, bv, bo, g1, s1, bd, g2, s2, bup = placed
    return (out, tok, g_qkv, bq, bv, g_wout, bo, g1, s1, g_up, bup, g_down, bd, g2, s2)


def solution(mesh):
    small = dict(mesh.shape) == {BLK: 8, HEAD: 4}
    return jax.shard_map(
        fused if small else per_device,
        mesh=mesh,
        in_specs=(
            P(None, BOTH, None),
            P(),
            P(BOTH, None),
            P(BOTH),
            P(BOTH),
            P(BOTH, None),
            P(BOTH),
            P(BOTH),
            P(BOTH),
            P(BOTH, None),
            P(BOTH),
            P(BOTH, None),
            P(BOTH),
            P(BOTH),
            P(BOTH),
            P(None, BOTH, None),
        ),
        out_specs=(
            P(None, BOTH, None),
            P(None, BOTH, None),
            P(BOTH, None),
            P(BOTH),
            P(BOTH),
            P(BOTH, None),
            P(BOTH),
            P(BOTH),
            P(BOTH),
            P(BOTH, None),
            P(BOTH),
            P(BOTH, None),
            P(BOTH),
            P(BOTH),
            P(BOTH),
        ),
        check_vma=False,
    )
```

```python
from functools import partial
from types import SimpleNamespace

import jax
import jax.numpy as jnp
from jax import lax
from jax.experimental import pallas as pl
from jax.experimental.pallas import tpu as pltpu
from jax.sharding import PartitionSpec as P

BLK = "blk"
HEAD = "head"
BOTH = (BLK, HEAD)
H = 12
HD = 64
MB = 2


EPS = 1e-05
NEG = -1e30


def norm_forward(values, gain_vec, shift_vec):
    center = values - jnp.mean(values, axis=-1, keepdims=True)
    inverse = lax.rsqrt(jnp.mean(center * center, axis=-1, keepdims=True) + EPS)
    normed = center * inverse
    return (normed * gain_vec + shift_vec, normed, inverse)


def norm_backward(upstream, normed, inverse, gain_vec):
    scaled = upstream * gain_vec
    inner = (
        scaled
        - jnp.mean(scaled, axis=-1, keepdims=True)
        - normed * jnp.mean(scaled * normed, axis=-1, keepdims=True)
    )
    return inner * inverse


def segment_of(starts_row, positions):
    return jnp.sum((starts_row[None, :] <= positions[:, None]).astype(jnp.int32), axis=1) - 1


def masked_scores(query_heads, key_heads, in_doc):
    scores = jnp.einsum(
        "qhd,khd->hqk", query_heads, key_heads, preferred_element_type=jnp.float32
    ) * HD ** (-0.5)
    return jnp.where(in_doc, scores, NEG)


def score_grads(query_heads, key_heads, value_heads, grad_numer, row_top, correction, in_doc):
    exp_score = jnp.where(
        in_doc, jnp.exp(masked_scores(query_heads, key_heads, in_doc) - row_top), 0.0
    )
    grad_weights = jnp.einsum(
        "qhd,khd->hqk", grad_numer, value_heads, preferred_element_type=jnp.float32
    )
    grad_scores = (exp_score * (grad_weights - correction)).astype(jnp.bfloat16)
    return (exp_score.astype(jnp.bfloat16), grad_scores)


def scatter_end(parts):
    (
        grad_proj_in,
        grad_query_bias,
        grad_value_bias,
        grad_proj_out,
        grad_out_bias,
        grad_norm_gain,
        grad_norm_shift,
        grad_up,
        grad_up_bias,
        grad_down,
        grad_down_bias,
        grad_final_gain,
        grad_final_shift,
    ) = parts
    return (
        lax.psum_scatter(grad_proj_in, BOTH, scatter_dimension=0, tiled=True),
        lax.psum_scatter(grad_query_bias, BOTH, scatter_dimension=0, tiled=True),
        lax.psum_scatter(grad_value_bias, BOTH, scatter_dimension=0, tiled=True),
        lax.psum_scatter(grad_proj_out, BOTH, scatter_dimension=0, tiled=True),
        lax.psum_scatter(grad_out_bias, BOTH, scatter_dimension=0, tiled=True),
        lax.psum_scatter(grad_norm_gain, BOTH, scatter_dimension=0, tiled=True),
        lax.psum_scatter(grad_norm_shift, BOTH, scatter_dimension=0, tiled=True),
        lax.psum_scatter(grad_up, BOTH, scatter_dimension=0, tiled=True),
        lax.psum_scatter(grad_up_bias, BOTH, scatter_dimension=0, tiled=True),
        lax.psum_scatter(grad_down, BOTH, scatter_dimension=0, tiled=True),
        lax.psum_scatter(grad_down_bias, BOTH, scatter_dimension=0, tiled=True),
        lax.psum_scatter(grad_final_gain, BOTH, scatter_dimension=0, tiled=True),
        lax.psum_scatter(grad_final_shift, BOTH, scatter_dimension=0, tiled=True),
    )


def per_device(
    tokens,
    starts,
    w_qkv,
    bias_q,
    bias_v,
    w_out,
    bias_out,
    gain_one,
    shift_one,
    w_up,
    bias_up,
    w_down,
    bias_down,
    gain_two,
    shift_two,
    cotangent,
):
    (
        proj_in,
        query_bias,
        value_bias,
        proj_out,
        out_bias,
        norm_gain,
        norm_shift,
        up_full,
        up_bias,
        down_full,
        down_bias,
        final_gain,
        final_shift,
    ) = (
        lax.all_gather(w_qkv, BOTH, axis=0, tiled=True),
        lax.all_gather(bias_q, BOTH, axis=0, tiled=True),
        lax.all_gather(bias_v, BOTH, axis=0, tiled=True),
        lax.all_gather(w_out, BOTH, axis=0, tiled=True),
        lax.all_gather(bias_out, BOTH, axis=0, tiled=True),
        lax.all_gather(gain_one, BOTH, axis=0, tiled=True),
        lax.all_gather(shift_one, BOTH, axis=0, tiled=True),
        lax.all_gather(w_up, BOTH, axis=0, tiled=True),
        lax.all_gather(bias_up, BOTH, axis=0, tiled=True),
        lax.all_gather(w_down, BOTH, axis=0, tiled=True),
        lax.all_gather(bias_down, BOTH, axis=0, tiled=True),
        lax.all_gather(gain_two, BOTH, axis=0, tiled=True),
        lax.all_gather(shift_two, BOTH, axis=0, tiled=True),
    )
    query_bias = query_bias.astype(jnp.float32)
    value_bias = value_bias.astype(jnp.float32)
    out_bias = out_bias.astype(jnp.float32)
    norm_gain = norm_gain.astype(jnp.float32)
    norm_shift = norm_shift.astype(jnp.float32)
    up_bias = up_bias.astype(jnp.float32)
    down_bias = down_bias.astype(jnp.float32)
    final_gain = final_gain.astype(jnp.float32)
    final_shift = final_shift.astype(jnp.float32)
    model_width = proj_out.shape[0]
    row_count = tokens.shape[1]
    head_count = lax.axis_size(HEAD)
    block_rows = row_count * head_count
    heads_dev = H // head_count
    local_width = heads_dev * HD
    scale = HD ** (-0.5)
    local_pos = lax.axis_index(BLK) * block_rows + jnp.arange(block_rows, dtype=jnp.int32)
    kept_list = []
    outputs = []
    for part_index in range(MB):
        inputs = tokens[part_index]
        starts_row = starts[part_index]
        projected = jnp.dot(inputs, proj_in, preferred_element_type=jnp.float32)
        query_rows = (projected[:, :model_width] + query_bias).astype(jnp.bfloat16)
        key_rows = projected[:, model_width : 2 * model_width].astype(jnp.bfloat16)
        value_rows = (projected[:, 2 * model_width :] + value_bias).astype(jnp.bfloat16)
        query_loc, key_loc, value_loc = (
            lax.all_to_all(query_rows, HEAD, split_axis=1, concat_axis=0, tiled=True),
            lax.all_to_all(key_rows, HEAD, split_axis=1, concat_axis=0, tiled=True),
            lax.all_to_all(value_rows, HEAD, split_axis=1, concat_axis=0, tiled=True),
        )
        doc_local = segment_of(starts_row, local_pos)
        query_heads = query_loc.reshape(block_rows, heads_dev, HD)

        def fold_keys(running, portion):
            row_top, row_total, weighted = running
            key_part, value_part = portion
            piece_len = key_part.shape[0]
            key_doc = segment_of(starts_row, jnp.arange(piece_len, dtype=jnp.int32))
            in_doc = (doc_local[:, None] == key_doc[None, :])[None]
            scores = masked_scores(query_heads, key_part.reshape(piece_len, heads_dev, HD), in_doc)
            new_top = jnp.maximum(row_top, jnp.max(scores, axis=-1, keepdims=True))
            exp_score = jnp.where(in_doc, jnp.exp(scores - new_top), 0.0)
            row_total = jnp.sum(exp_score, axis=-1, keepdims=True)
            weighted = jnp.einsum(
                "hqk,khd->hqd",
                exp_score.astype(jnp.bfloat16),
                value_part.reshape(piece_len, heads_dev, HD),
                preferred_element_type=jnp.float32,
            )
            return (new_top, row_total, weighted)

        start_state = (
            jnp.full((heads_dev, block_rows, 1), NEG, jnp.float32),
            jnp.zeros((heads_dev, block_rows, 1), jnp.float32),
            jnp.zeros((heads_dev, block_rows, HD), jnp.float32),
        )
        row_top, row_total, weighted = fold_keys(
            start_state,
            (
                lax.all_gather(key_loc, BLK, axis=0, tiled=True),
                lax.all_gather(value_loc, BLK, axis=0, tiled=True),
            ),
        )
        attended = jnp.transpose(weighted / row_total, (1, 0, 2))
        mixed_rows = lax.all_to_all(
            attended.reshape(block_rows, local_width).astype(jnp.bfloat16),
            HEAD,
            split_axis=0,
            concat_axis=1,
            tiled=True,
        )
        attn_out = jnp.dot(mixed_rows, proj_out, preferred_element_type=jnp.float32) + out_bias
        first_norm, normed_one, inverse_one = norm_forward(
            inputs.astype(jnp.float32) + attn_out, norm_gain, norm_shift
        )
        first_low = first_norm.astype(jnp.bfloat16)
        hidden = jnp.dot(first_low, up_full, preferred_element_type=jnp.float32) + up_bias
        active = jax.nn.gelu(hidden, approximate=False).astype(jnp.bfloat16)
        ffn_out = jnp.dot(active, down_full, preferred_element_type=jnp.float32) + down_bias
        result, normed_two, inverse_two = norm_forward(
            first_norm + ffn_out, final_gain, final_shift
        )
        outputs.append(result)
        kept_list.append(
            (
                inputs,
                starts_row,
                query_loc,
                key_loc,
                value_loc,
                doc_local,
                row_top,
                row_total,
                attended,
                mixed_rows,
                normed_one,
                inverse_one,
                first_low,
                hidden,
                active,
                normed_two,
                inverse_two,
            )
        )
    input_grads = []
    grad_sum = None
    for part_index in range(MB):
        (
            inputs,
            starts_row,
            query_loc,
            key_loc,
            value_loc,
            doc_local,
            row_top,
            row_total,
            attended,
            mixed_rows,
            normed_one,
            inverse_one,
            first_low,
            hidden,
            active,
            normed_two,
            inverse_two,
        ) = kept_list[part_index]
        grad_result = cotangent[part_index].astype(jnp.float32)
        grad_final_gain = jnp.sum(grad_result * normed_two, axis=0)
        grad_final_shift = jnp.sum(grad_result, axis=0)
        grad_two = norm_backward(grad_result, normed_two, inverse_two, final_gain)
        grad_ffn = grad_two.astype(jnp.bfloat16)
        grad_down_bias = jnp.sum(grad_ffn.astype(jnp.float32), axis=0)
        grad_down = jnp.einsum("rf,rd->fd", active, grad_ffn, preferred_element_type=jnp.float32)
        grad_active = jnp.einsum(
            "rd,fd->rf", grad_ffn, down_full, preferred_element_type=jnp.float32
        )
        gelu_pull = jax.vjp(partial(jax.nn.gelu, approximate=False), hidden)[1]
        grad_hidden = gelu_pull(grad_active)[0].astype(jnp.bfloat16)
        grad_up_bias = jnp.sum(grad_hidden.astype(jnp.float32), axis=0)
        grad_up = jnp.einsum(
            "rd,rf->df", first_low, grad_hidden, preferred_element_type=jnp.float32
        )
        grad_first = grad_two + jnp.einsum(
            "rf,df->rd", grad_hidden, up_full, preferred_element_type=jnp.float32
        )
        grad_norm_gain = jnp.sum(grad_first * normed_one, axis=0)
        grad_norm_shift = jnp.sum(grad_first, axis=0)
        grad_one = norm_backward(grad_first, normed_one, inverse_one, norm_gain)
        grad_attn = grad_one.astype(jnp.bfloat16)
        grad_out_bias = jnp.sum(grad_attn.astype(jnp.float32), axis=0)
        grad_proj_out = jnp.einsum(
            "rc,rd->cd", mixed_rows, grad_attn, preferred_element_type=jnp.float32
        )
        grad_mixed = jnp.einsum(
            "rd,cd->rc", grad_attn, proj_out, preferred_element_type=jnp.float32
        ).astype(jnp.bfloat16)
        grad_loc = lax.all_to_all(grad_mixed, HEAD, split_axis=1, concat_axis=0, tiled=True)
        grad_heads = grad_loc.astype(jnp.float32).reshape(block_rows, heads_dev, HD)
        total_rows = jnp.transpose(row_total, (1, 0, 2))
        correction = jnp.transpose(
            jnp.sum(grad_heads * attended, axis=-1, keepdims=True) / total_rows, (1, 0, 2)
        )
        grad_numer = (grad_heads / total_rows).astype(jnp.bfloat16)
        query_heads = query_loc.reshape(block_rows, heads_dev, HD)
        key_heads_loc = key_loc.reshape(block_rows, heads_dev, HD)
        value_heads_loc = value_loc.reshape(block_rows, heads_dev, HD)
        fold_key_part = lax.all_gather(key_loc, BLK, axis=0, tiled=True)
        fold_value_part = lax.all_gather(value_loc, BLK, axis=0, tiled=True)
        fold_piece_len = fold_key_part.shape[0]
        fold_key_doc = segment_of(starts_row, jnp.arange(fold_piece_len, dtype=jnp.int32))
        fold_in_doc = (doc_local[:, None] == fold_key_doc[None, :])[None]
        key_heads = fold_key_part.reshape(fold_piece_len, heads_dev, HD)
        exp_low, grad_scores = score_grads(
            query_heads,
            key_heads,
            fold_value_part.reshape(fold_piece_len, heads_dev, HD),
            grad_numer,
            row_top,
            correction,
            fold_in_doc,
        )
        grad_query = (
            jnp.einsum("hqk,khd->qhd", grad_scores, key_heads, preferred_element_type=jnp.float32)
            * scale
        )
        top_rows = jnp.transpose(row_top[:, :, 0])
        corr_rows = jnp.transpose(correction[:, :, 0])

        def fold_keygrad(portion):
            query_part, numer_part, top_part, corr_part = portion
            piece_len = query_part.shape[0]
            query_doc = segment_of(starts_row, jnp.arange(piece_len, dtype=jnp.int32))
            in_doc = (query_doc[:, None] == doc_local[None, :])[None]
            query_piece = query_part.reshape(piece_len, heads_dev, HD)
            numer_piece = numer_part.reshape(piece_len, heads_dev, HD)
            exp_low, grad_scores = score_grads(
                query_piece,
                key_heads_loc,
                value_heads_loc,
                numer_piece,
                jnp.transpose(top_part)[:, :, None],
                jnp.transpose(corr_part)[:, :, None],
                in_doc,
            )
            grad_key_run = (
                jnp.einsum(
                    "hqk,qhd->khd", grad_scores, query_piece, preferred_element_type=jnp.float32
                )
                * scale
            )
            grad_value_run = jnp.einsum(
                "hqk,qhd->khd", exp_low, numer_piece, preferred_element_type=jnp.float32
            )
            return (grad_key_run, grad_value_run)

        grad_key, grad_value = fold_keygrad(
            (
                lax.all_gather(query_loc, BLK, axis=0, tiled=True),
                lax.all_gather(
                    grad_numer.reshape(block_rows, local_width), BLK, axis=0, tiled=True
                ),
                lax.all_gather(top_rows.astype(jnp.bfloat16), BLK, axis=0, tiled=True).astype(
                    jnp.float32
                ),
                lax.all_gather(corr_rows.astype(jnp.bfloat16), BLK, axis=0, tiled=True).astype(
                    jnp.float32
                ),
            )
        )
        grad_q_rows, grad_k_rows, grad_v_rows = (
            lax.all_to_all(
                grad_query.reshape(block_rows, local_width).astype(jnp.bfloat16),
                HEAD,
                split_axis=0,
                concat_axis=1,
                tiled=True,
            ),
            lax.all_to_all(
                grad_key.reshape(block_rows, local_width).astype(jnp.bfloat16),
                HEAD,
                split_axis=0,
                concat_axis=1,
                tiled=True,
            ),
            lax.all_to_all(
                grad_value.reshape(block_rows, local_width).astype(jnp.bfloat16),
                HEAD,
                split_axis=0,
                concat_axis=1,
                tiled=True,
            ),
        )
        grad_proj = jnp.concatenate([grad_q_rows, grad_k_rows, grad_v_rows], axis=1)
        grad_query_bias = jnp.sum(grad_q_rows.astype(jnp.float32), axis=0)
        grad_value_bias = jnp.sum(grad_v_rows.astype(jnp.float32), axis=0)
        grad_proj_in = jnp.einsum(
            "rd,re->de", inputs, grad_proj, preferred_element_type=jnp.float32
        )
        input_grads.append(
            grad_one
            + jnp.einsum("re,de->rd", grad_proj, proj_in, preferred_element_type=jnp.float32)
        )
        part_grads = (
            grad_proj_in,
            grad_query_bias,
            grad_value_bias,
            grad_proj_out,
            grad_out_bias,
            grad_norm_gain,
            grad_norm_shift,
            grad_up,
            grad_up_bias,
            grad_down,
            grad_down_bias,
            grad_final_gain,
            grad_final_shift,
        )
        grad_sum = (
            part_grads
            if grad_sum is None
            else tuple((left + right for left, right in zip(grad_sum, part_grads)))
        )
    grad_sum = scatter_end(grad_sum)
    (
        grad_proj_in,
        grad_query_bias,
        grad_value_bias,
        grad_proj_out,
        grad_out_bias,
        grad_norm_gain,
        grad_norm_shift,
        grad_up,
        grad_up_bias,
        grad_down,
        grad_down_bias,
        grad_final_gain,
        grad_final_shift,
    ) = grad_sum
    return (
        jnp.stack(outputs),
        jnp.stack(input_grads),
        grad_proj_in,
        grad_query_bias,
        grad_value_bias,
        grad_proj_out,
        grad_out_bias,
        grad_norm_gain,
        grad_norm_shift,
        grad_up,
        grad_up_bias,
        grad_down,
        grad_down_bias,
        grad_final_gain,
        grad_final_shift,
    )


MESH = pl.DeviceIdType.MESH
F32 = jnp.float32
BF16 = jnp.bfloat16
DM = 768
FF = 3072
TOK = 64
SEQ = 2048
HALF = DM // 2
GROUP = 3 * HD
UP_N = FF // 2
CHUNK = 256
PAIRS = 6

QKV, OUT, UP, DOWN, KV, Q = range(6)
SHAPES = (
    (2, 2, 2, 4, 24, 3 * GROUP),
    (4, 4, 24, DM),
    (4, 2, 4, 24, UP_N),
    (4, 4, 96, DM),
    (2, 2, 2, 4, 24, 2 * GROUP),
    (2, 2, 2, 4, 24, GROUP),
)


def by_column(kind):
    return kind == UP


def piece_shape(kind):
    shape = SHAPES[kind]
    if kind in (QKV, KV, Q):
        return shape[1:3] + shape[4:]
    return (2,) + shape[3:] if by_column(kind) else shape[2:]


def when(cond, run):
    if cond is None:
        run()
    else:
        pl.when(cond)(run)


def both(left, right):
    return jnp.logical_and(left, right)


class Place:
    def __init__(self):
        b = lax.axis_index(BLK)
        z = lax.axis_index(HEAD)
        c = lax.rem(b, 2)
        x = lax.rem(lax.div(b, 2), 2)
        y = lax.div(b, 4)
        self.b, self.z, self.c, self.x, self.y = b, z, c, x, y
        self.line = 4 * b + z
        self.sib = (b + 1 - 2 * c, z)
        self.dx = (4 * y + 2 * (1 - x) + c, z)
        self.dy = (4 * (1 - y) + 2 * x + c, z)
        self.dx_other = (4 * y + 2 * (1 - x) + 1 - c, z)
        self.near = z + 1 - 2 * lax.rem(z, 2)
        self.far = lax.rem(z + 2, 4)
        self.cross = 3 - z
        self.swap = (4 * c + 2 * x + y, z)
        self.stays = y == c
        self.moves = y != c
        self.group = 2 * c + x
        self.seat = 4 * y + z
        self.chip = 2 * self.seat + x
        idle = jnp.logical_or(both(z == 0, y == 1), both(z == 3, y == 0))
        self.active = jnp.logical_not(idle)
        inner = jnp.where(z == 1, 4 * y, 1 + 4 * y)
        outer = jnp.where(z == 0, 2, 3)
        self.pair = jnp.where(jnp.logical_or(z == 1, z == 2), inner, outer)
        self.part = lax.div(self.pair, 3)

    def cols(self, kind):
        x, y = self.x, self.y
        if by_column(kind):
            return (2 * y + x, 2 * y + 1 - x, 2 * (1 - y) + x, 2 * (1 - y) + 1 - x)
        return (2 * x + y, 2 * (1 - x) + y, 2 * x + 1 - y, 2 * (1 - x) + 1 - y)


SEATS = ((0, 1), (0, 2), (0, 0), (1, 3), (1, 1), (1, 2))


def chunk(kind, ref, col, z):
    return ref.at[col, :, z] if by_column(kind) else ref.at[col, z]


class Links:
    def __init__(self, sems, here):
        self.sems, self.here, self.count = sems, here, 0
        self.waits = []

    def alloc(self, n=1):
        at = self.count
        self.count += n
        return at

    def make(self, src, dst, s, r, dev):
        return pltpu.make_async_remote_copy(
            src_ref=src, dst_ref=dst, send_sem=self.sems.at[s], recv_sem=self.sems.at[r],
            device_id=dev, device_id_type=MESH,
        )

    def send(self, src, dst, s, r, dev, cond=None):
        when(cond, lambda: self.make(src, dst, s, r, dev).start())

    def recv(self, dst, r, cond=None):
        when(cond, lambda: self.make(dst, dst, r, r, self.here.sib).wait_recv())

    def sent(self, src, s, cond=None):
        when(cond, lambda: self.make(src, src, s, s, self.here.sib).wait_send())

    def drain(self, like, s, cond=None):
        self.waits.append(lambda: self.sent(like, s, cond))

    def local(self, src, dst, cond=None):
        sem = self.sems.at[self.alloc()]
        when(cond, lambda: pltpu.make_async_copy(src, dst, sem).start())
        return lambda: when(cond, lambda: pltpu.make_async_copy(src, dst, sem).wait())

    def put(self, src, dst):
        self.waits.append(self.local(src, dst))

    def finish(self):
        for wait in self.waits:
            wait()


class Gather:
    def __init__(self, links, here, kind, ref):
        self.links, self.here, self.kind, self.ref = links, here, kind, ref
        self.s0, self.r0 = links.alloc(), links.alloc()
        self.sz, self.rz = links.alloc(), links.alloc(4)
        self.s_plane, self.s_relay = links.alloc(), links.alloc()
        self.r_relay, self.r_rest = links.alloc(4), links.alloc()
        self.col, self.col_x, self.col_y, self.col_d = here.cols(kind)
        links.drain(ref.at[0, :, pl.ds(0, 3)] if by_column(kind) else ref.at[0, pl.ds(0, 3)], self.sz)
        links.drain(ref.at[pl.ds(0, 2)], self.s_plane)
        links.drain(ref.at[0], self.s_relay)

    def first_wait(self):
        here = self.here
        if by_column(self.kind):
            self.links.recv(self.ref.at[self.col, 1 - here.c, here.z], self.r0)
        else:
            self.links.recv(self.ref.at[self.col, here.z], self.r0, here.moves)

    def piece(self, col, z):
        return chunk(self.kind, self.ref, col, z)

    def z_hop(self, z, to):
        piece = self.piece(self.col, z)
        self.links.send(piece, piece, self.sz, self.rz + z, (self.here.b, to))

    def spread(self, z):
        piece = self.piece(self.col, z)
        on_y = z < 1
        to_x = jnp.where(on_y, self.r_relay + z, self.r_rest)
        to_y = jnp.where(on_y, self.r_rest, self.r_relay + z)
        self.links.send(piece, piece, self.s_plane, to_x, self.here.dx)
        self.links.send(piece, piece, self.s_plane, to_y, self.here.dy)

    def own_z(self):
        here = self.here
        self.z_hop(here.z, here.far)
        self.z_hop(here.z, here.near)

    def own_plane(self):
        self.spread(self.here.z)

    def land(self, z):
        self.links.recv(self.piece(self.col, z), self.rz + z)

    def hop(self):
        self.z_hop(self.here.far, self.here.near)

    def relay(self, z):
        here = self.here
        on_y = z < 1
        piece = self.piece(jnp.where(on_y, self.col_x, self.col_y), z)
        self.links.recv(piece, self.r_relay + z)
        dev = (jnp.where(on_y, here.dy[0], here.dx[0]), here.z)
        self.links.send(piece, piece, self.s_relay, self.r_rest, dev)

    def done(self):
        self.links.recv(self.ref.at[pl.ds(0, 2)], self.r_rest)


class PairGather:
    def __init__(self, links, here, ref):
        self.links, self.here, self.ref = links, here, ref
        self.s0, self.r0 = links.alloc(), links.alloc()
        self.sz, self.rz = links.alloc(), links.alloc(4)
        self.sy, self.ry = links.alloc(), links.alloc()
        links.drain(ref.at[0, 0, 0, pl.ds(0, 3)], self.s0)
        links.drain(ref.at[0, :, :, pl.ds(0, 3)], self.sz)
        links.drain(ref.at[0], self.sy)

    def first_wait(self):
        self.links.recv(self.ref.at[0, 0, 0, pl.ds(0, 3)], self.r0)

    def piece(self, z):
        return self.ref.at[self.here.y, :, :, z]

    def z_hop(self, z, to):
        self.links.send(self.piece(z), self.piece(z), self.sz, self.rz + z, (self.here.b, to))

    def own_z(self):
        here = self.here
        self.z_hop(here.z, here.far)
        self.z_hop(here.z, here.near)

    def land(self, z):
        self.links.recv(self.piece(z), self.rz + z)

    def hop(self):
        self.z_hop(self.here.far, self.here.near)

    def spread(self, z):
        self.links.send(self.piece(z), self.piece(z), self.sy, self.ry, self.here.dy)

    def done(self):
        self.links.recv(self.ref.at[0], self.ry)


def add_blocks(dst, terms, blocks):
    for at in blocks:
        total = terms[0][at].astype(F32)
        for term in terms[1:]:
            total = total + term[at].astype(F32)
        dst[at] = total.astype(dst.dtype)


class Scatter:
    def __init__(self, links, here, kind, refs):
        self.links, self.here, self.kind = links, here, kind
        self.grad, self.far, self.cxy, self.zb, self.zr, self.fin, self.last = refs
        self.s_first, self.s_relay, self.sz = links.alloc(), links.alloc(), links.alloc()
        self.r_far, self.r_plane, self.rz = links.alloc(4), links.alloc(4), links.alloc(3)
        self.s_end, self.r_end = links.alloc(), links.alloc()
        self.col, self.col_x, self.col_y, self.col_d = here.cols(kind)
        links.drain(self.cxy, self.s_first)
        links.drain(self.far, self.s_relay)
        links.drain(self.zr.at[pl.ds(0, 3)], self.sz)
        if by_column(kind):
            links.drain(self.last, self.s_end)
        else:
            links.drain(self.last, self.s_end, here.moves)

    def piece(self, col, z):
        return chunk(self.kind, self.grad, col, z)

    def add(self, dst, terms):
        add_blocks(dst, terms, [(h,) for h in range(2)] if by_column(self.kind) else [(slice(0, None),)])

    def side(self, z, to_x, sem):
        here = self.here
        col = jnp.where(to_x, self.col_x, self.col_y)
        dev = (jnp.where(to_x, here.dx[0], here.dy[0]), here.z)
        slot = jnp.where(to_x, z, 4 + z)
        self.links.send(self.piece(col, z), self.cxy.at[slot], sem, self.r_plane + z, dev)

    def send(self, z):
        here = self.here
        to_x = z >= 2
        dev = (jnp.where(to_x, here.dx[0], here.dy[0]), here.z)
        self.links.send(self.piece(self.col_d, z), self.far.at[z], self.s_first, self.r_far + z, dev)
        self.side(z, to_x, self.s_first)

    def relay(self, z):
        to_y = z >= 2
        self.links.recv(self.far.at[z], self.r_far + z)
        piece = self.piece(jnp.where(to_y, self.col_y, self.col_x), z)
        self.add(piece, (piece, self.far.at[z]))
        self.side(z, jnp.logical_not(to_y), self.s_relay)

    def plane(self, z):
        self.links.recv(self.cxy.at[pl.ds(0, 2)], self.r_plane + z)
        self.add(self.zb.at[z], (self.piece(self.col, z), self.cxy.at[z], self.cxy.at[4 + z]))

    def z_first(self):
        here = self.here
        for i, z in enumerate((here.near, here.cross)):
            self.links.send(self.zb.at[z], self.zr.at[i], self.sz, self.rz + i, (here.b, here.near))

    def z_second(self):
        here = self.here
        self.links.recv(self.zr.at[1], self.rz + 1)
        piece = self.zb.at[here.far]
        self.add(piece, (piece, self.zr.at[1]))
        self.links.send(piece, self.zr.at[2], self.sz, self.rz + 2, (here.b, here.far))

    def z_last(self):
        links, here = self.links, self.here
        links.recv(self.zr.at[0], self.rz)
        links.recv(self.zr.at[2], self.rz + 2)
        self.add(self.fin, [self.zb.at[here.z], self.zr.at[0], self.zr.at[2]])
        if by_column(self.kind):
            links.send(self.fin.at[1 - here.c], self.last, self.s_end, self.r_end, here.sib)
        else:
            links.send(self.fin, self.last, self.s_end, self.r_end, here.swap, here.moves)

    def finish(self, out):
        links, here, kind = self.links, self.here, self.kind
        c = here.c
        if by_column(kind):
            out[:, pl.ds(pl.multiple_of(UP_N * c, 128), UP_N)] = self.fin[c]
            links.recv(self.last, self.r_end)
            out[:, pl.ds(pl.multiple_of(UP_N * (1 - c), 128), UP_N)] = self.last[...]
        else:
            links.recv(self.last, self.r_end, here.moves)

            def keep():
                out[...] = self.fin[...]

            def take():
                out[...] = self.last[...]

            when(here.stays, keep)
            when(here.moves, take)


class PairScatter:
    def __init__(self, links, here, kind, refs):
        self.links, self.here, self.kind = links, here, kind
        self.grad, self.cy, self.zb, self.zr, self.fin, self.last = refs
        self.sy, self.ry = links.alloc(), links.alloc(4)
        self.sz, self.rz = links.alloc(), links.alloc(3)
        self.s_end, self.r_end = links.alloc(), links.alloc()
        links.drain(self.cy, self.sy)
        links.drain(self.zr.at[pl.ds(0, 3)], self.sz)
        links.drain(self.last.at[pl.ds(0, 3)], self.s_end)

    def add(self, dst, terms):
        add_blocks(dst, terms, [(i, j) for i in range(2) for j in range(2)])

    def send(self, z):
        here = self.here
        self.links.send(self.grad.at[1 - here.y, :, :, z], self.cy.at[z], self.sy, self.ry + z, here.dy)

    def plane(self, z):
        self.links.recv(self.cy.at[z], self.ry + z)
        self.add(self.zb.at[z], (self.grad.at[self.here.y, :, :, z], self.cy.at[z]))

    def z_first(self):
        here = self.here
        for i, z in enumerate((here.near, here.cross)):
            self.links.send(self.zb.at[z], self.zr.at[i], self.sz, self.rz + i, (here.b, here.near))

    def z_second(self):
        here = self.here
        self.links.recv(self.zr.at[1], self.rz + 1)
        piece = self.zb.at[here.far]
        self.add(piece, (piece, self.zr.at[1]))
        self.links.send(piece, self.zr.at[2], self.sz, self.rz + 2, (here.b, here.far))

    def z_last(self):
        links, here = self.links, self.here
        links.recv(self.zr.at[0], self.rz)
        links.recv(self.zr.at[2], self.rz + 2)
        self.add(self.fin, [self.zb.at[here.z], self.zr.at[0], self.zr.at[2]])
        x, c = here.x, here.c
        slot = self.last.at[here.group]
        links.send(self.fin.at[1 - x, c], slot, self.s_end, self.r_end, here.dx)
        links.send(self.fin.at[1 - x, 1 - c], slot, self.s_end, self.r_end, here.dx_other)
        links.send(self.fin.at[x, 1 - c], slot, self.s_end, self.r_end, here.sib)

    def finish(self, out):
        self.last[self.here.group] = self.fin[self.here.x, self.here.c]
        self.links.recv(self.last.at[pl.ds(0, 3)], self.r_end)
        for group in range(4):
            if self.kind == Q:
                out[:, GROUP * group : GROUP * (group + 1)] = self.last[group]
            else:
                for i in range(2):
                    at = DM * (i + 1) + GROUP * group
                    out[:, at : at + GROUP] = self.last[group, :, GROUP * i : GROUP * (i + 1)]


def dot(a, b):
    return jnp.dot(a, b, preferred_element_type=F32)


def dot_nt(a, b):
    return lax.dot_general(a, b, (((1,), (1,)), ((), ())), preferred_element_type=F32)


def dot_tn(a, b):
    return lax.dot_general(a, b, (((0,), (0,)), ((), ())), preferred_element_type=F32)


def row_sum(values):
    return jnp.sum(values, axis=0, keepdims=True)


def div24(n):
    return lax.shift_right_logical(n * 2731, 16)


def iota(shape, dim):
    return lax.broadcasted_iota(jnp.int32, shape, dim)


def select_24():
    n = iota((128, DM), 1)
    return (iota((128, DM), 0) == n - 24 * div24(n)).astype(BF16)


def select_96():
    n = iota((128, UP_N), 1)
    run = lax.shift_right_logical(div24(n), 2)
    return (iota((128, UP_N), 0) == 32 + n - 96 * run).astype(BF16)


def owner_24(lead):
    shape = (lead, 8, DM)
    return div24(iota(shape, 2)) == iota(shape, 0)


def owner_96():
    shape = (16, UP_N)
    return lax.shift_right_logical(div24(iota(shape, 1)), 2) == iota(shape, 0)


def exact_nt(values, select):
    high = values.astype(BF16)
    rest = values - high.astype(F32)
    mid = rest.astype(BF16)
    low = (rest - mid.astype(F32)).astype(BF16)
    return dot_nt(high, select) + dot_nt(mid, select) + dot_nt(low, select)


SCRATCH = dict(
    w_rows=((24, 3 * DM), BF16),
    w_parts=((4, 24, 3 * GROUP), BF16),
    vecs=((8, 128), F32),
    cot=((2, TOK, DM), BF16),
    b_out=((2, TOK, DM), F32),
    b_tok=((2, TOK, DM), F32),
    b_qkv=((24, 3 * DM), F32),
    b_wout=((24, DM), F32),
    b_up=((24, FF), F32),
    b_down=((96, DM), F32),
    b_vec=((8, 128), F32),
    vec_all=((32, 8, 128), F32),
    vec_rows=((8, DM), F32),
    up_row=((1, UP_N), F32),
    x_pair=((2, 2, 2, TOK, DM), BF16),
    fl_chip=((2, 2, TOK, DM), BF16),
    gf_chip=((2, 2, TOK, DM), BF16),
    ga_chip=((2, 2, TOK, DM), BF16),
    partial=((2, 2, TOK, DM), F32),
    back0=((2, TOK, DM), F32),
    back1=((2, TOK, DM), F32),
    back2=((2, TOK, DM), F32),
    tok_part=((2, 2, 2, TOK, DM), F32),
    tok_back=((2, 2, TOK, DM), F32),
    tok_send=((2, TOK, DM), BF16),
    tok_last=((2, TOK, DM), BF16),
    send_q=((PAIRS, GROUP, 256), BF16),
    qkv_t=((GROUP, SEQ), BF16),
    k_rows=((SEQ, HD), BF16),
    v_rows=((SEQ, HD), BF16),
    q_rows=((SEQ, HD), BF16),
    g_rows=((SEQ, HD), BF16),
    key_doc=((SEQ, 128), jnp.int32),
    query_doc=((1, SEQ), jnp.int32),
    scores=((SEQ, CHUNK), F32),
    weights=((SEQ, SEQ), BF16),
    total=((1, SEQ), F32),
    att_t=((HD, SEQ), F32),
    att_send=((HD, SEQ), BF16),
    mix_in=((12, HD, 128), BF16),
    g_send=((12, HD, 128), BF16),
    g_t=((HD, SEQ), BF16),
    gn_t=((HD, SEQ), BF16),
    corr=((1, SEQ), F32),
    ds=((CHUNK, SEQ), BF16),
    dq_t=((HD, SEQ), F32),
    d_send=((GROUP, SEQ), BF16),
    d_in=((PAIRS, GROUP, 256), BF16),
    mixed_t=((HALF, 2 * 128), BF16),
    first=((2 * TOK, DM), F32),
    normed1=((2 * TOK, DM), F32),
    inv1=((2 * TOK, 1), F32),
    active=((4 * TOK, UP_N), BF16),
    slope=((4 * TOK, UP_N), F32),
    gh=((4 * TOK, UP_N), BF16),
    gh2=((2 * TOK, DM), F32),
    gh1=((2 * TOK, DM), F32),
    gp_kv=((8 * TOK, 2 * GROUP), BF16),
    gp_q=((8 * TOK, GROUP), BF16),
    vec_grad=((8, DM), F32),
    up_grad=((1, UP_N), F32),
    vec_send=((32, 8, 128), F32),
    vec_recv=((32, 8, 128), F32),
)


def sum_scratch(kind):
    piece = piece_shape(kind)
    if kind in (KV, Q):
        low = [SHAPES[kind]] + [(4,) + piece] * 3
        last = (4,) + piece[2:]
    else:
        low = [SHAPES[kind], (4,) + piece, (8,) + piece, (4,) + piece, (4,) + piece]
        last = piece[1:] if by_column(kind) else piece
    return [(shape, BF16) for shape in low] + [(piece, F32), (last, F32)]


GATHERED = (QKV, OUT, UP, DOWN)
SUMMED = (OUT, UP, DOWN, KV, Q)
N_SEM = 180


def all_scratch():
    shapes = list(SCRATCH.values())
    shapes += [(SHAPES[kind], BF16) for kind in GATHERED]
    for kind in SUMMED:
        shapes += sum_scratch(kind)
    shapes += [((24,), BF16)] * 8 + [((96,), BF16)]
    return [pltpu.VMEM(shape, dtype) for shape, dtype in shapes] + [pltpu.SemaphoreType.DMA((N_SEM,))]


def layer_kernel(
    tokens, starts, w_qkv, w_out, w_up, w_down,
    v0, v1, v2, v3, v4, v5, v6, v7, v8, cotangent,
    o_out, o_tok, o_qkv, o_wout, o_up, o_down, o_vec,
    *scratch,
):
    vec_in = (v0, v1, v2, v3, v4, v5, v6, v7, v8)
    m = SimpleNamespace(**dict(zip(SCRATCH, scratch)))
    at = len(SCRATCH)
    gathered = scratch[at : at + 4]
    at += 4
    summed = []
    for kind in SUMMED:
        n = len(sum_scratch(kind))
        summed.append(scratch[at : at + n])
        at += n
    vec_rows_in = scratch[at : at + 9]
    sems = scratch[-1]
    here = Place()
    links = Links(sems, here)
    b, z, c, x = here.b, here.z, here.c, here.x
    line, chip, group = here.line, here.chip, here.group
    g_qkv = PairGather(links, here, gathered[0])
    g_out, g_up, g_down = [Gather(links, here, kind, ref) for kind, ref in zip(GATHERED[1:], gathered[1:])]
    s_out, s_up, s_down = [Scatter(links, here, kind, refs) for kind, refs in zip(SUMMED[:3], summed[:3])]
    s_kv, s_q = [PairScatter(links, here, kind, refs) for kind, refs in zip(SUMMED[3:], summed[3:])]
    ahead = (g_out, g_up)

    def peer(d):
        other = lax.rem(line + d, 32)
        return (lax.div(other, 4), lax.rem(other, 4))

    x_pair = m.x_pair

    def up_part(which):
        return w_up.at[:, pl.ds(pl.multiple_of(UP_N * which, 128), UP_N)]

    qkv_wait = links.local(w_qkv, m.w_rows)
    vec_waits = [links.local(src, dst) for src, dst in zip(vec_in, vec_rows_in)]
    x_wait = links.local(tokens, x_pair.at[:, x, c])
    up_wait = links.local(up_part(c), g_up.ref.at[g_up.col, c, z])
    row_waits = [
        links.local(shard, gather.ref.at[gather.col, z], here.stays)
        for gather, shard in ((g_out, w_out), (g_down, w_down))
    ]
    cot_wait = links.local(cotangent, m.cot)
    m.vec_grad[...] = jnp.zeros((8, DM), F32)
    m.vecs[...] = jnp.zeros((8, 128), F32)
    for wait in vec_waits:
        wait()
    for j in range(8):
        m.vecs[j : j + 1, 0:24] = vec_rows_in[j][...].astype(F32).reshape(1, 24)
    m.vecs[0:1, 32:128] = vec_rows_in[8][...].astype(F32).reshape(1, 96)
    qkv_wait()
    for k in range(4):
        for j in range(3):
            block = m.w_rows[:, DM * j + GROUP * k : DM * j + GROUP * (k + 1)]
            m.w_parts[k, :, GROUP * j : GROUP * (j + 1)] = block

    barrier = pltpu.get_barrier_semaphore()

    def greet(d, carry):
        pl.semaphore_signal(barrier, inc=1, device_id=peer(d), device_id_type=MESH)
        return carry

    lax.fori_loop(1, 32, greet, 0)
    pl.semaphore_wait(barrier, 31)

    slot = g_qkv.ref.at[here.y, x, c, z]
    links.send(m.w_parts.at[2 * c + 1 - x], slot, g_qkv.s0, g_qkv.r0, here.dx)
    links.send(m.w_parts.at[2 * (1 - c) + 1 - x], slot, g_qkv.s0, g_qkv.r0, here.dx_other)
    links.send(m.w_parts.at[2 * (1 - c) + x], slot, g_qkv.s0, g_qkv.r0, here.sib)
    x_sem = links.alloc(6)
    own_x = x_pair.at[:, x, c]
    links.send(tokens, own_x, x_sem, x_sem + 1, here.dx)
    links.send(tokens, own_x, x_sem + 2, x_sem + 3, here.sib)
    links.drain(own_x, x_sem)
    links.drain(own_x, x_sem + 2)
    up_slot = g_up.ref.at[g_up.col, c, z]
    links.send(up_part(1 - c), up_slot, g_up.s0, g_up.r0, here.sib)
    links.drain(up_slot, g_up.s0)
    for gather, shard in ((g_out, w_out), (g_down, w_down)):
        slot = gather.ref.at[2 * x + c, z]
        links.send(shard, slot, gather.s0, gather.r0, here.swap, here.moves)
        links.drain(slot, gather.s0, here.moves)
    vec_sem = links.alloc(4)
    vec_all = m.vec_all

    def vec_copy(d):
        return links.make(m.vecs, vec_all.at[line], vec_sem, vec_sem + 1, peer(d))

    def vec_start(d, carry):
        vec_copy(d).start()
        return carry

    lax.fori_loop(1, 32, vec_start, 0)
    vec_all[line] = m.vecs[...]
    g_qkv.ref[here.y, x, c, z] = m.w_parts[group]
    for wait in (x_wait, up_wait, *row_waits, cot_wait):
        wait()

    g_qkv.first_wait()
    g_qkv.own_z()
    g_qkv.spread(z)
    for gather in ahead:
        gather.first_wait()
        gather.own_plane()

    def documents():
        def position(n):
            z_part = lax.shift_left(jnp.bitwise_and(lax.shift_right_logical(n, 8), 3), 6)
            xc_part = lax.shift_left(jnp.bitwise_and(lax.shift_right_logical(n, 6), 3), 8)
            y_part = lax.shift_left(lax.shift_right_logical(n, 10), 10)
            return y_part + xc_part + z_part + jnp.bitwise_and(n, 63)

        def doc_of(n):
            place = position(n)
            doc = jnp.zeros(place.shape, jnp.int32)
            for j in range(starts.shape[1]):
                doc = doc + (starts[here.part, j] <= place).astype(jnp.int32)
            return doc

        m.query_doc[...] = doc_of(iota((1, SEQ), 1))

        def rows(i, carry):
            start = pl.multiple_of(i * 256, 256)
            m.key_doc[pl.ds(start, 256), :] = doc_of(iota((256, 128), 0) + i * 256)
            return carry

        lax.fori_loop(0, SEQ // 256, rows, 0)

    when(here.active, documents)

    other_x = x_pair.at[:, 1 - x, c]
    links.recv(other_x, x_sem + 1)
    links.send(other_x, other_x, x_sem + 4, x_sem + 5, here.sib)
    links.drain(other_x, x_sem + 4)
    g_qkv.land(here.far)
    g_qkv.hop()
    g_qkv.spread(here.far)
    for gather in ahead:
        gather.own_z()
    many = vec_all.at[pl.ds(0, 31)]
    links.sent(many, vec_sem)
    links.recv(many, vec_sem + 1)
    spread = dot(vec_all[...].reshape(256, 128).astype(BF16), select_24()).reshape(32, 8, DM)
    m.vec_rows[...] = jnp.sum(jnp.where(owner_24(32), spread, 0.0), axis=0)
    spread = dot(vec_all[pl.ds(16 * c, 16), 0, :].astype(BF16), select_96())
    m.up_row[...] = row_sum(jnp.where(owner_96(), spread, 0.0))

    def vector(j):
        return m.vec_rows[j : j + 1, :]

    def vector_group(j):
        total = jnp.zeros((1, GROUP), F32)
        for k in range(4):
            total = total + jnp.where(group == k, m.vec_rows[j : j + 1, GROUP * k : GROUP * (k + 1)], 0.0)
        return total

    g_qkv.land(here.near)
    g_qkv.spread(here.near)
    for gather in ahead:
        gather.relay(z)
    g_qkv.land(here.cross)
    g_qkv.spread(here.cross)
    for gather in ahead:
        gather.land(here.far)
        gather.hop()
        gather.spread(here.far)
    links.recv(x_pair.at[:, x, 1 - c], x_sem + 3)
    links.recv(x_pair.at[:, 1 - x, 1 - c], x_sem + 5)
    g_qkv.done()

    def weight_qkv():
        return g_qkv.ref[...].reshape(DM, 3 * GROUP)

    def x_rows():
        return x_pair[...].reshape(8 * TOK, DM)

    send_q = m.send_q
    bias = jnp.concatenate([vector_group(0), jnp.zeros((1, GROUP), F32), vector_group(1)], axis=1)
    for part in range(MB):
        rows = (dot(x_pair[part].reshape(4 * TOK, DM), weight_qkv()) + bias).astype(BF16)
        turned = rows.T
        for i in range(3):
            for j in range(3):
                block = turned[GROUP * j + HD * i : GROUP * j + HD * (i + 1), :]
                if j == 0:
                    block = block * jnp.asarray(HD ** (-0.5), BF16)
                send_q[3 * part + i, HD * j : HD * (j + 1), :] = block

    chip_lanes = pl.ds(pl.multiple_of(chip * 128, 128), 128)
    seat_lanes = pl.ds(pl.multiple_of(here.seat * 256, 256), 256)
    idle = jnp.logical_not(here.active)

    def seat_dev(y_to, z_to, x_to):
        return (4 * y_to + 2 * x_to + c, z_to)

    qkv_t = m.qkv_t
    q_sem = links.alloc(3)
    for pair in range(PAIRS):
        mine = both(here.active, here.pair == pair)
        dev = seat_dev(*SEATS[pair], x)
        links.send(send_q.at[pair], qkv_t.at[:, seat_lanes], q_sem, q_sem + 1, dev, jnp.logical_not(mine))
    links.drain(send_q.at[pl.ds(0, PAIRS - 1)], q_sem, here.active)
    links.drain(send_q, q_sem, idle)

    def own_q():
        qkv_t[:, seat_lanes] = send_q[here.pair]

    when(here.active, own_q)

    class ToSeats:
        def __init__(self, src_of, dst_of, slot, slots, seats, own):
            self.src_of, self.dst_of, self.slot, self.slots = src_of, dst_of, slot, slots
            self.seats, self.own = seats, own
            self.s, self.r = links.alloc(), links.alloc()
            self.width = SEQ // seats

        def start(self, other):
            start = pl.multiple_of(self.width * other, self.width)
            src, dst = self.src_of(pl.ds(start, self.width)), self.dst_of(self.slot)
            if self.seats == 16:
                place, x_to, mine = lax.div(other, 2), lax.rem(other, 2), chip
            else:
                place, x_to, mine = other, x, here.seat
            dev = seat_dev(lax.div(place, 4), lax.rem(place, 4), x_to)
            links.send(src, dst, self.s, self.r, dev, mine != other)

        def finish(self):
            links.drain(self.src_of(pl.ds(0, SEQ - self.width)), self.s, here.active)
            when(here.active, self.own)

        def wait(self):
            links.recv(self.dst_of(pl.ds(0, self.slots - 1)), self.r, here.active)
            links.recv(self.dst_of(pl.ds(0, self.slots)), self.r, idle)

    g_down.first_wait()
    g_down.own_plane()
    g_down.own_z()
    for gather in ahead:
        gather.land(here.near)
        gather.spread(here.near)
    for gather in ahead:
        gather.relay(here.far)
    for gather in ahead:
        gather.land(here.cross)
        gather.spread(here.cross)
    links.recv(qkv_t.at[:, pl.ds(0, SEQ - 256)], q_sem + 1, here.active)
    for gather in ahead:
        gather.relay(here.near)
    g_down.relay(z)

    weights = m.weights
    mix_slot = 6 * here.part + 3 * x + here.pair - 3 * here.part

    def own_mix():
        m.mix_in[mix_slot] = m.att_send[:, chip_lanes]

    mix = ToSeats(
        lambda lanes: m.att_send.at[:, lanes], lambda slot: m.mix_in.at[slot], mix_slot, 12, 16, own_mix
    )

    def turn_keys():
        m.k_rows[...] = qkv_t[HD : 2 * HD, :].T
        m.v_rows[...] = qkv_t[2 * HD : 3 * HD, :].T
        m.q_rows[...] = qkv_t[0:HD, :].T

    when(here.active, turn_keys)

    def attend(i):
        lanes = pl.ds(pl.multiple_of(i * CHUNK, CHUNK), CHUNK)
        query = qkv_t[0:HD, lanes]
        doc = m.query_doc[:, lanes]
        top = None
        for k in range(8):
            rows = slice(256 * k, 256 * (k + 1))
            key_doc = m.key_doc[rows, :]
            same = jnp.concatenate([key_doc, key_doc], axis=1) == doc
            scores = jnp.where(same, dot(m.k_rows[rows, :], query), NEG)
            m.scores[rows, :] = scores
            here_top = jnp.max(scores, axis=0, keepdims=True)
            top = here_top if top is None else jnp.maximum(top, here_top)
        total = None
        for k in range(8):
            rows = slice(256 * k, 256 * (k + 1))
            grown = jnp.exp(m.scores[rows, :] - top)
            weights[rows, lanes] = grown.astype(BF16)
            part_sum = row_sum(grown)
            total = part_sum if total is None else total + part_sum
        numer = dot(qkv_t[2 * HD : 3 * HD, :], weights[:, lanes])
        attended = numer / total
        m.total[:, lanes] = total
        m.att_t[:, lanes] = attended
        m.att_send[:, lanes] = attended.astype(BF16)
        mix.start(2 * i)
        mix.start(2 * i + 1)

    def some(body, first, last):
        def run():
            def one(i, carry):
                body(i)
                return carry

            lax.fori_loop(first, last, one, 0)

        when(here.active, run)

    some(attend, 0, 2)
    for gather in ahead:
        gather.relay(here.cross)
    g_down.land(here.far)
    g_down.hop()
    g_down.spread(here.far)
    some(attend, 2, 5)
    g_down.land(here.near)
    g_down.spread(here.near)
    some(attend, 5, 7)
    g_down.relay(here.far)
    some(attend, 7, 8)
    g_down.land(here.cross)
    g_down.spread(here.cross)
    mix.finish()
    mix.wait()
    g_out.done()
    g_down.relay(here.near)

    def share(buf, values):
        sem = links.alloc(2)
        buf[:, c] = values.reshape(MB, TOK, DM)
        links.send(buf.at[:, c], buf.at[:, c], sem, sem + 1, here.sib)
        links.drain(buf.at[:, c], sem)
        links.recv(buf.at[:, 1 - c], sem + 1)

    def combine(values, back):
        sem = links.alloc(2)
        partial = m.partial
        partial[...] = values.reshape(MB, 2, TOK, DM)
        links.send(partial.at[:, 1 - c], back, sem, sem + 1, here.sib)
        links.recv(back, sem + 1)
        total = partial[:, c].reshape(2 * TOK, DM) + back[...].reshape(2 * TOK, DM)
        links.sent(partial.at[:, 1 - c], sem)
        return total

    def norm_rows(values, gain, shift):
        center = values - jnp.mean(values, axis=-1, keepdims=True)
        inverse = lax.rsqrt(jnp.mean(center * center, axis=-1, keepdims=True) + EPS)
        normed = center * inverse
        return normed * gain + shift, normed, inverse

    def norm_back(upstream, normed, inverse, gain):
        scaled = upstream * gain
        return inverse * (
            scaled
            - jnp.mean(scaled, axis=-1, keepdims=True)
            - normed * jnp.mean(scaled * normed, axis=-1, keepdims=True)
        )

    mixed_t = m.mixed_t
    mixed = []
    for part in range(MB):
        piece = m.mix_in[6 * part : 6 * part + 6].reshape(HALF, 128)
        mixed_t[:, 128 * part : 128 * (part + 1)] = piece
        mixed.append(piece.T)
    mixed = jnp.concatenate(mixed, axis=0)

    def weight_out():
        return g_out.ref[...].reshape(HALF, DM)

    attn = combine(dot(mixed, weight_out()), m.back0) + vector(2)
    own_tokens = x_pair[:, x, c].reshape(2 * TOK, DM).astype(F32)
    first, normed_one, inverse_one = norm_rows(own_tokens + attn, vector(3), vector(4))
    m.first[...] = first
    m.normed1[...] = normed_one
    m.inv1[...] = inverse_one
    share(m.fl_chip, first.astype(BF16))

    g_up.done()
    def fl_rows():
        return m.fl_chip[...].reshape(4 * TOK, DM)

    def weight_up(j):
        return g_up.ref[:, :, :, :, HALF * j : HALF * (j + 1)].reshape(DM, HALF)

    def weight_down(j):
        return g_down.ref[j].reshape(HALF, DM)

    for j in range(4):
        lanes = slice(HALF * j, HALF * (j + 1))
        hidden = dot(fl_rows(), weight_up(j)) + m.up_row[:, lanes]
        cdf = 0.5 * (1.0 + lax.erf(hidden * (0.5**0.5)))
        m.slope[:, lanes] = cdf + hidden * (jnp.exp(-0.5 * hidden * hidden) * 0.3989422804014327)
        m.active[:, lanes] = (hidden * cdf).astype(BF16)
    g_down.relay(here.cross)
    g_down.done()
    ffn = None
    for j in range(4):
        lanes = slice(HALF * j, HALF * (j + 1))
        term = dot(m.active[:, lanes], weight_down(j))
        ffn = term if ffn is None else ffn + term
    ffn = combine(ffn, m.back1) + vector(5)
    result, normed_two, inverse_two = norm_rows(m.first[...] + ffn, vector(6), vector(7))
    m.b_out[...] = result.reshape(MB, TOK, DM)
    links.put(m.b_out, o_out)

    targets = (here.near, here.cross, here.far, z)
    vec_grad = m.vec_grad
    grad_result = m.cot[...].reshape(2 * TOK, DM).astype(F32)
    vec_grad[6:7, :] = row_sum(grad_result * normed_two)
    vec_grad[7:8, :] = row_sum(grad_result)
    grad_two = norm_back(grad_result, normed_two, inverse_two, vector(6))
    m.gh2[...] = grad_two
    grad_ffn = grad_two.astype(BF16)
    vec_grad[5:6, :] = row_sum(grad_ffn.astype(F32))
    share(m.gf_chip, grad_ffn)

    def gf_rows():
        return m.gf_chip[...].reshape(4 * TOK, DM)

    for j in range(4):
        lanes = slice(HALF * j, HALF * (j + 1))
        s_down.grad[j] = dot_tn(m.active[:, lanes], gf_rows()).astype(BF16).reshape(4, 96, DM)
    for t in targets:
        s_down.send(t)
    grad_first = None
    for j in range(4):
        lanes = slice(HALF * j, HALF * (j + 1))
        grad_active = dot_nt(gf_rows(), weight_down(j))
        grad_hidden = (grad_active * m.slope[:, lanes]).astype(BF16)
        m.gh[:, lanes] = grad_hidden
        m.up_grad[:, lanes] = row_sum(grad_hidden.astype(F32))
    for j in range(4):
        lanes = slice(HALF * j, HALF * (j + 1))
        term = dot_nt(m.gh[:, lanes], weight_up(j))
        grad_first = term if grad_first is None else grad_first + term
    grad_first = m.gh2[...] + combine(grad_first, m.back2)
    normed_one = m.normed1[...]
    vec_grad[3:4, :] = row_sum(grad_first * normed_one)
    vec_grad[4:5, :] = row_sum(grad_first)
    grad_one = norm_back(grad_first, normed_one, m.inv1[...], vector(3))
    m.gh1[...] = grad_one
    grad_attn = grad_one.astype(BF16)
    vec_grad[2:3, :] = row_sum(grad_attn.astype(F32))
    share(m.ga_chip, grad_attn)

    def ga_rows():
        return m.ga_chip[...].reshape(4 * TOK, DM)

    turned = dot_nt(ga_rows(), weight_out()).astype(BF16).T
    for part in range(MB):
        m.g_send[6 * part : 6 * part + 6] = turned[:, 128 * part : 128 * (part + 1)].reshape(6, HD, 128)
    g_t = m.g_t
    g_sem = links.alloc(2)
    for slot in range(12):
        part, head = slot // 6, slot % 6
        pair, x_to = 3 * part + head % 3, head // 3
        mine = both(here.active, both(here.pair == pair, x == x_to))
        dev = seat_dev(*SEATS[pair], x_to)
        links.send(m.g_send.at[slot], g_t.at[:, chip_lanes], g_sem, g_sem + 1, dev, jnp.logical_not(mine))
    links.drain(m.g_send.at[pl.ds(0, 11)], g_sem, here.active)
    links.drain(m.g_send, g_sem, idle)

    def own_g():
        g_t[:, chip_lanes] = m.g_send[mix_slot]

    when(here.active, own_g)
    for j in range(4):
        lanes = slice(HALF * j, HALF * (j + 1))
        s_up.grad[:, :, :, :, lanes] = (
            dot_tn(fl_rows(), m.gh[:, lanes]).astype(BF16).reshape(4, 2, 4, 24, HALF)
        )
    s_out.grad[...] = dot(mixed_t[...], ga_rows()).astype(BF16).reshape(SHAPES[OUT])
    for t in targets:
        s_down.relay(t)
    for t in targets:
        s_up.send(t)
    for t in targets:
        s_out.send(t)
    links.recv(g_t.at[:, pl.ds(0, SEQ - 128)], g_sem + 1, here.active)

    d_send, d_in = m.d_send, m.d_in

    def own_kv():
        d_in[here.pair, HD : 3 * HD, :] = d_send[HD : 3 * HD, seat_lanes]

    def own_dq():
        d_in[here.pair, 0:HD, :] = d_send[0:HD, seat_lanes]

    grad_kv = ToSeats(
        lambda lanes: d_send.at[pl.ds(HD, 2 * HD), lanes], lambda slot: d_in.at[slot, pl.ds(HD, 2 * HD)],
        here.pair, PAIRS, 8, own_kv,
    )
    grad_q = ToSeats(
        lambda lanes: d_send.at[pl.ds(0, HD), lanes], lambda slot: d_in.at[slot, pl.ds(0, HD)],
        here.pair, PAIRS, 8, own_dq,
    )

    def turn_grads():
        grad = g_t[...].astype(F32)
        inverse = 1.0 / m.total[...]
        numer = grad * inverse
        m.gn_t[...] = numer.astype(BF16)
        m.g_rows[...] = numer.astype(BF16).T
        m.corr[...] = row_sum(grad * m.att_t[...]) * inverse
        m.dq_t[...] = jnp.zeros((HD, SEQ), F32)

    when(here.active, turn_grads)

    def back(k):
        keys = pl.ds(pl.multiple_of(k * CHUNK, CHUNK), CHUNK)
        value = m.v_rows[keys, :]
        for i in range(4):
            lanes = slice(512 * i, 512 * (i + 1))
            grad_weights = dot(value, m.gn_t[:, lanes])
            grown = weights[keys, lanes].astype(F32)
            m.ds[:, lanes] = (grown * (grad_weights - m.corr[:, lanes])).astype(BF16)
        ds = m.ds
        d_send[HD : 2 * HD, keys] = dot(ds[...], m.q_rows[...]).T.astype(BF16)
        d_send[2 * HD : 3 * HD, keys] = dot(weights[keys, :], m.g_rows[...]).T.astype(BF16)
        grad_kv.start(k)
        m.dq_t[...] += dot(qkv_t[HD : 2 * HD, keys], ds[...])

    some(back, 0, 8)

    def last_query():
        d_send[0:HD, :] = (m.dq_t[...] * (HD ** (-0.5))).astype(BF16)
        for other in range(8):
            grad_q.start(other)

    when(here.active, last_query)
    grad_kv.finish()
    grad_q.finish()
    for t in targets:
        s_down.plane(t)
        if t is here.cross:
            s_down.z_first()
    for t in targets:
        s_up.relay(t)
    for t in targets:
        s_out.relay(t)
    grad_kv.wait()
    s_down.z_second()
    gp_kv, gp_q = m.gp_kv, m.gp_q
    for part in range(MB):
        heads = slice(3 * part, 3 * part + 3)
        rows = [d_in[heads, HD * j : HD * (j + 1), :].reshape(GROUP, 256) for j in (1, 2)]
        gp_kv[256 * part : 256 * (part + 1), :] = jnp.concatenate(rows, axis=0).T
    s_kv.grad[...] = dot_tn(x_rows(), gp_kv[...]).astype(BF16).reshape(SHAPES[KV])
    for t in targets:
        s_kv.send(t)
    for t in targets:
        s_up.plane(t)
        if t is here.cross:
            s_up.z_first()
    grad_q.wait()
    for part in range(MB):
        gp_q[256 * part : 256 * (part + 1), :] = d_in[3 * part : 3 * part + 3, 0:HD, :].reshape(GROUP, 256).T
    s_q.grad[...] = dot_tn(x_rows(), gp_q[...]).astype(BF16).reshape(SHAPES[Q])
    for t in targets:
        s_q.send(t)
    all_weights = weight_qkv()
    t_sem = links.alloc(4)
    for part in range(MB):
        rows = slice(256 * part, 256 * (part + 1))
        terms = dot_nt(gp_q[rows, :], all_weights[:, 0:GROUP]) + dot_nt(gp_kv[rows, :], all_weights[:, GROUP:])
        m.tok_part[part] = terms.reshape(2, 2, TOK, DM)
    links.send(m.tok_part.at[:, :, 1 - c], m.tok_back, t_sem, t_sem + 1, here.sib)
    links.drain(m.tok_back, t_sem)
    sum_q = row_sum(gp_q[...].astype(F32))
    sum_v = row_sum(gp_kv[:, GROUP:].astype(F32))
    for k in range(4):
        lanes = slice(GROUP * k, GROUP * (k + 1))
        vec_grad[0:1, lanes] = jnp.where(group == k, sum_q, 0.0)
        vec_grad[1:2, lanes] = jnp.where(group == k, sum_v, 0.0)
    links.recv(m.tok_back, t_sem + 1)
    for part in range(MB):
        m.tok_send[part] = (m.tok_part[part, 1 - x, c] + m.tok_back[part, 1 - x]).astype(BF16)
    links.send(m.tok_send, m.tok_last, t_sem + 2, t_sem + 3, here.dx)
    links.drain(m.tok_send, t_sem + 2)

    vec_send, vec_recv = m.vec_send, m.vec_recv
    spread = jnp.where(owner_24(32), vec_grad[...][None], 0.0).reshape(256, DM)
    vec_send[...] = exact_nt(spread, select_24()).reshape(32, 8, 128)
    spread = jnp.where(owner_96(), m.up_grad[...], 0.0)
    own_lines = pl.ds(16 * c, 16)
    vec_send[own_lines, 0, :] = vec_send[own_lines, 0, :] + exact_nt(spread, select_96())

    def grad_start(d, carry):
        other = lax.rem(line + d, 32)
        links.make(vec_send.at[other], vec_recv.at[line], vec_sem + 2, vec_sem + 3, peer(d)).start()
        return carry

    lax.fori_loop(1, 32, grad_start, 0)
    vec_recv[line] = vec_send[line]

    for t in targets:
        s_out.plane(t)
        if t is here.cross:
            s_out.z_first()
    for t in targets:
        s_kv.plane(t)
        if t is here.cross:
            s_kv.z_first()
    s_up.z_second()
    for t in targets:
        s_q.plane(t)
        if t is here.cross:
            s_q.z_first()
    s_kv.z_second()
    s_q.z_second()
    s_out.z_second()
    links.recv(m.tok_last, t_sem + 3)
    for part in range(MB):
        rows = slice(TOK * part, TOK * (part + 1))
        own = m.tok_part[part, x, c] + m.tok_back[part, x]
        m.b_tok[part] = m.gh1[rows, :] + (own + m.tok_last[part].astype(F32))
    links.put(m.b_tok, o_tok)
    many_send, many_recv = vec_send.at[pl.ds(0, 31)], vec_recv.at[pl.ds(0, 31)]
    links.sent(many_send, vec_sem + 2)
    links.recv(many_recv, vec_sem + 3)
    m.b_vec[...] = jnp.sum(vec_recv[...], axis=0)
    links.put(m.b_vec, o_vec)
    s_down.z_last()
    s_down.finish(m.b_down)
    links.put(m.b_down, o_down)
    s_kv.z_last()
    s_q.z_last()
    for scatter, out, to in ((s_up, m.b_up, o_up), (s_out, m.b_wout, o_wout)):
        scatter.z_last()
    s_kv.finish(m.b_qkv)
    s_q.finish(m.b_qkv)
    links.put(m.b_qkv, o_qkv)
    for scatter, out, to in ((s_up, m.b_up, o_up), (s_out, m.b_wout, o_wout)):
        scatter.finish(out)
        links.put(out, to)
    links.finish()


def place_kernel(*refs):
    ins, big_out, vec_out = refs[0:7], refs[7:13], refs[13:22]
    held, rows, sems = refs[22:29], refs[29:38], refs[38]
    loads = [pltpu.make_async_copy(src, dst, sems.at[i]) for i, (src, dst) in enumerate(zip(ins, held))]
    for load in reversed(loads):
        load.start()
    stores = [pltpu.make_async_copy(src, dst, sems.at[7 + i]) for i, (src, dst) in enumerate(zip(held, big_out))]
    stores += [pltpu.make_async_copy(src, dst, sems.at[13 + i]) for i, (src, dst) in enumerate(zip(rows, vec_out))]
    loads[6].wait()
    for j in range(8):
        rows[j][...] = held[6][j, 0:24]
    rows[8][...] = held[6][0, 32:128]
    for store in stores[6:]:
        store.start()
    for load, store in zip(loads, stores[:6]):
        load.wait()
        store.start()
    for store in stores:
        store.wait()


def fused(
    tokens, starts, w_qkv, bias_q, bias_v, w_out, bias_out, gain_one, shift_one,
    w_up, bias_up, w_down, bias_down, gain_two, shift_two, cotangent,
):
    anywhere = pl.BlockSpec(memory_space=pl.ANY)
    vectors = (bias_q, bias_v, bias_out, gain_one, shift_one, bias_down, gain_two, shift_two, bias_up)
    big = [tokens.shape, tokens.shape, w_qkv.shape, w_out.shape, w_up.shape, w_down.shape]
    big = [jax.ShapeDtypeStruct(shape, F32) for shape in big]
    small = [jax.ShapeDtypeStruct(vector.shape, F32) for vector in vectors]
    made = pl.pallas_call(
        layer_kernel,
        name="layer",
        out_shape=big + [jax.ShapeDtypeStruct((8, 128), F32)],
        in_specs=[anywhere, pl.BlockSpec(memory_space=pltpu.SMEM)] + [anywhere] * 14,
        out_specs=[anywhere] * 7,
        scratch_shapes=all_scratch(),
        compiler_params=pltpu.CompilerParams(
            collective_id=0, has_side_effects=True, vmem_limit_bytes=63 * 2**20
        ),
    )(tokens, starts, w_qkv, w_out, w_up, w_down, *vectors, cotangent)
    placed = pl.pallas_call(
        place_kernel,
        name="place",
        out_shape=big + small,
        in_specs=[anywhere] * 7,
        out_specs=[anywhere] * 15,
        scratch_shapes=[pltpu.VMEM(array.shape, F32) for array in (*made, *vectors)]
        + [pltpu.SemaphoreType.DMA((22,))],
    )(*made)
    out, tok, g_qkv, g_wout, g_up, g_down, bq, bv, bo, g1, s1, bd, g2, s2, bup = placed
    return (out, tok, g_qkv, bq, bv, g_wout, bo, g1, s1, g_up, bup, g_down, bd, g2, s2)


def solution(mesh):
    small = dict(mesh.shape) == {BLK: 8, HEAD: 4}
    return jax.shard_map(
        fused if small else per_device,
        mesh=mesh,
        in_specs=(
            P(None, BOTH, None),
            P(),
            P(BOTH, None),
            P(BOTH),
            P(BOTH),
            P(BOTH, None),
            P(BOTH),
            P(BOTH),
            P(BOTH),
            P(BOTH, None),
            P(BOTH),
            P(BOTH, None),
            P(BOTH),
            P(BOTH),
            P(BOTH),
            P(None, BOTH, None),
        ),
        out_specs=(
            P(None, BOTH, None),
            P(None, BOTH, None),
            P(BOTH, None),
            P(BOTH),
            P(BOTH),
            P(BOTH, None),
            P(BOTH),
            P(BOTH),
            P(BOTH),
            P(BOTH, None),
            P(BOTH),
            P(BOTH, None),
            P(BOTH),
            P(BOTH),
            P(BOTH),
        ),
        check_vma=False,
    )
```

```python
from functools import partial
from types import SimpleNamespace

import jax
import jax.numpy as jnp
from jax import lax
from jax.experimental import pallas as pl
from jax.experimental.pallas import tpu as pltpu
from jax.sharding import PartitionSpec as P

BLK = "blk"
HEAD = "head"
BOTH = (BLK, HEAD)
H = 12
HD = 64
MB = 2


EPS = 1e-05
NEG = -1e30


def norm_forward(values, gain_vec, shift_vec):
    center = values - jnp.mean(values, axis=-1, keepdims=True)
    inverse = lax.rsqrt(jnp.mean(center * center, axis=-1, keepdims=True) + EPS)
    normed = center * inverse
    return (normed * gain_vec + shift_vec, normed, inverse)


def norm_backward(upstream, normed, inverse, gain_vec):
    scaled = upstream * gain_vec
    inner = (
        scaled
        - jnp.mean(scaled, axis=-1, keepdims=True)
        - normed * jnp.mean(scaled * normed, axis=-1, keepdims=True)
    )
    return inner * inverse


def segment_of(starts_row, positions):
    return jnp.sum((starts_row[None, :] <= positions[:, None]).astype(jnp.int32), axis=1) - 1


def masked_scores(query_heads, key_heads, in_doc):
    scores = jnp.einsum(
        "qhd,khd->hqk", query_heads, key_heads, preferred_element_type=jnp.float32
    ) * HD ** (-0.5)
    return jnp.where(in_doc, scores, NEG)


def score_grads(query_heads, key_heads, value_heads, grad_numer, row_top, correction, in_doc):
    exp_score = jnp.where(
        in_doc, jnp.exp(masked_scores(query_heads, key_heads, in_doc) - row_top), 0.0
    )
    grad_weights = jnp.einsum(
        "qhd,khd->hqk", grad_numer, value_heads, preferred_element_type=jnp.float32
    )
    grad_scores = (exp_score * (grad_weights - correction)).astype(jnp.bfloat16)
    return (exp_score.astype(jnp.bfloat16), grad_scores)


def scatter_end(parts):
    (
        grad_proj_in,
        grad_query_bias,
        grad_value_bias,
        grad_proj_out,
        grad_out_bias,
        grad_norm_gain,
        grad_norm_shift,
        grad_up,
        grad_up_bias,
        grad_down,
        grad_down_bias,
        grad_final_gain,
        grad_final_shift,
    ) = parts
    return (
        lax.psum_scatter(grad_proj_in, BOTH, scatter_dimension=0, tiled=True),
        lax.psum_scatter(grad_query_bias, BOTH, scatter_dimension=0, tiled=True),
        lax.psum_scatter(grad_value_bias, BOTH, scatter_dimension=0, tiled=True),
        lax.psum_scatter(grad_proj_out, BOTH, scatter_dimension=0, tiled=True),
        lax.psum_scatter(grad_out_bias, BOTH, scatter_dimension=0, tiled=True),
        lax.psum_scatter(grad_norm_gain, BOTH, scatter_dimension=0, tiled=True),
        lax.psum_scatter(grad_norm_shift, BOTH, scatter_dimension=0, tiled=True),
        lax.psum_scatter(grad_up, BOTH, scatter_dimension=0, tiled=True),
        lax.psum_scatter(grad_up_bias, BOTH, scatter_dimension=0, tiled=True),
        lax.psum_scatter(grad_down, BOTH, scatter_dimension=0, tiled=True),
        lax.psum_scatter(grad_down_bias, BOTH, scatter_dimension=0, tiled=True),
        lax.psum_scatter(grad_final_gain, BOTH, scatter_dimension=0, tiled=True),
        lax.psum_scatter(grad_final_shift, BOTH, scatter_dimension=0, tiled=True),
    )


def per_device(
    tokens,
    starts,
    w_qkv,
    bias_q,
    bias_v,
    w_out,
    bias_out,
    gain_one,
    shift_one,
    w_up,
    bias_up,
    w_down,
    bias_down,
    gain_two,
    shift_two,
    cotangent,
):
    (
        proj_in,
        query_bias,
        value_bias,
        proj_out,
        out_bias,
        norm_gain,
        norm_shift,
        up_full,
        up_bias,
        down_full,
        down_bias,
        final_gain,
        final_shift,
    ) = (
        lax.all_gather(w_qkv, BOTH, axis=0, tiled=True),
        lax.all_gather(bias_q, BOTH, axis=0, tiled=True),
        lax.all_gather(bias_v, BOTH, axis=0, tiled=True),
        lax.all_gather(w_out, BOTH, axis=0, tiled=True),
        lax.all_gather(bias_out, BOTH, axis=0, tiled=True),
        lax.all_gather(gain_one, BOTH, axis=0, tiled=True),
        lax.all_gather(shift_one, BOTH, axis=0, tiled=True),
        lax.all_gather(w_up, BOTH, axis=0, tiled=True),
        lax.all_gather(bias_up, BOTH, axis=0, tiled=True),
        lax.all_gather(w_down, BOTH, axis=0, tiled=True),
        lax.all_gather(bias_down, BOTH, axis=0, tiled=True),
        lax.all_gather(gain_two, BOTH, axis=0, tiled=True),
        lax.all_gather(shift_two, BOTH, axis=0, tiled=True),
    )
    query_bias = query_bias.astype(jnp.float32)
    value_bias = value_bias.astype(jnp.float32)
    out_bias = out_bias.astype(jnp.float32)
    norm_gain = norm_gain.astype(jnp.float32)
    norm_shift = norm_shift.astype(jnp.float32)
    up_bias = up_bias.astype(jnp.float32)
    down_bias = down_bias.astype(jnp.float32)
    final_gain = final_gain.astype(jnp.float32)
    final_shift = final_shift.astype(jnp.float32)
    model_width = proj_out.shape[0]
    row_count = tokens.shape[1]
    head_count = lax.axis_size(HEAD)
    block_rows = row_count * head_count
    heads_dev = H // head_count
    local_width = heads_dev * HD
    scale = HD ** (-0.5)
    local_pos = lax.axis_index(BLK) * block_rows + jnp.arange(block_rows, dtype=jnp.int32)
    kept_list = []
    outputs = []
    for part_index in range(MB):
        inputs = tokens[part_index]
        starts_row = starts[part_index]
        projected = jnp.dot(inputs, proj_in, preferred_element_type=jnp.float32)
        query_rows = (projected[:, :model_width] + query_bias).astype(jnp.bfloat16)
        key_rows = projected[:, model_width : 2 * model_width].astype(jnp.bfloat16)
        value_rows = (projected[:, 2 * model_width :] + value_bias).astype(jnp.bfloat16)
        query_loc, key_loc, value_loc = (
            lax.all_to_all(query_rows, HEAD, split_axis=1, concat_axis=0, tiled=True),
            lax.all_to_all(key_rows, HEAD, split_axis=1, concat_axis=0, tiled=True),
            lax.all_to_all(value_rows, HEAD, split_axis=1, concat_axis=0, tiled=True),
        )
        doc_local = segment_of(starts_row, local_pos)
        query_heads = query_loc.reshape(block_rows, heads_dev, HD)

        def fold_keys(running, portion):
            row_top, row_total, weighted = running
            key_part, value_part = portion
            piece_len = key_part.shape[0]
            key_doc = segment_of(starts_row, jnp.arange(piece_len, dtype=jnp.int32))
            in_doc = (doc_local[:, None] == key_doc[None, :])[None]
            scores = masked_scores(query_heads, key_part.reshape(piece_len, heads_dev, HD), in_doc)
            new_top = jnp.maximum(row_top, jnp.max(scores, axis=-1, keepdims=True))
            exp_score = jnp.where(in_doc, jnp.exp(scores - new_top), 0.0)
            row_total = jnp.sum(exp_score, axis=-1, keepdims=True)
            weighted = jnp.einsum(
                "hqk,khd->hqd",
                exp_score.astype(jnp.bfloat16),
                value_part.reshape(piece_len, heads_dev, HD),
                preferred_element_type=jnp.float32,
            )
            return (new_top, row_total, weighted)

        start_state = (
            jnp.full((heads_dev, block_rows, 1), NEG, jnp.float32),
            jnp.zeros((heads_dev, block_rows, 1), jnp.float32),
            jnp.zeros((heads_dev, block_rows, HD), jnp.float32),
        )
        row_top, row_total, weighted = fold_keys(
            start_state,
            (
                lax.all_gather(key_loc, BLK, axis=0, tiled=True),
                lax.all_gather(value_loc, BLK, axis=0, tiled=True),
            ),
        )
        attended = jnp.transpose(weighted / row_total, (1, 0, 2))
        mixed_rows = lax.all_to_all(
            attended.reshape(block_rows, local_width).astype(jnp.bfloat16),
            HEAD,
            split_axis=0,
            concat_axis=1,
            tiled=True,
        )
        attn_out = jnp.dot(mixed_rows, proj_out, preferred_element_type=jnp.float32) + out_bias
        first_norm, normed_one, inverse_one = norm_forward(
            inputs.astype(jnp.float32) + attn_out, norm_gain, norm_shift
        )
        first_low = first_norm.astype(jnp.bfloat16)
        hidden = jnp.dot(first_low, up_full, preferred_element_type=jnp.float32) + up_bias
        active = jax.nn.gelu(hidden, approximate=False).astype(jnp.bfloat16)
        ffn_out = jnp.dot(active, down_full, preferred_element_type=jnp.float32) + down_bias
        result, normed_two, inverse_two = norm_forward(
            first_norm + ffn_out, final_gain, final_shift
        )
        outputs.append(result)
        kept_list.append(
            (
                inputs,
                starts_row,
                query_loc,
                key_loc,
                value_loc,
                doc_local,
                row_top,
                row_total,
                attended,
                mixed_rows,
                normed_one,
                inverse_one,
                first_low,
                hidden,
                active,
                normed_two,
                inverse_two,
            )
        )
    input_grads = []
    grad_sum = None
    for part_index in range(MB):
        (
            inputs,
            starts_row,
            query_loc,
            key_loc,
            value_loc,
            doc_local,
            row_top,
            row_total,
            attended,
            mixed_rows,
            normed_one,
            inverse_one,
            first_low,
            hidden,
            active,
            normed_two,
            inverse_two,
        ) = kept_list[part_index]
        grad_result = cotangent[part_index].astype(jnp.float32)
        grad_final_gain = jnp.sum(grad_result * normed_two, axis=0)
        grad_final_shift = jnp.sum(grad_result, axis=0)
        grad_two = norm_backward(grad_result, normed_two, inverse_two, final_gain)
        grad_ffn = grad_two.astype(jnp.bfloat16)
        grad_down_bias = jnp.sum(grad_ffn.astype(jnp.float32), axis=0)
        grad_down = jnp.einsum("rf,rd->fd", active, grad_ffn, preferred_element_type=jnp.float32)
        grad_active = jnp.einsum(
            "rd,fd->rf", grad_ffn, down_full, preferred_element_type=jnp.float32
        )
        gelu_pull = jax.vjp(partial(jax.nn.gelu, approximate=False), hidden)[1]
        grad_hidden = gelu_pull(grad_active)[0].astype(jnp.bfloat16)
        grad_up_bias = jnp.sum(grad_hidden.astype(jnp.float32), axis=0)
        grad_up = jnp.einsum(
            "rd,rf->df", first_low, grad_hidden, preferred_element_type=jnp.float32
        )
        grad_first = grad_two + jnp.einsum(
            "rf,df->rd", grad_hidden, up_full, preferred_element_type=jnp.float32
        )
        grad_norm_gain = jnp.sum(grad_first * normed_one, axis=0)
        grad_norm_shift = jnp.sum(grad_first, axis=0)
        grad_one = norm_backward(grad_first, normed_one, inverse_one, norm_gain)
        grad_attn = grad_one.astype(jnp.bfloat16)
        grad_out_bias = jnp.sum(grad_attn.astype(jnp.float32), axis=0)
        grad_proj_out = jnp.einsum(
            "rc,rd->cd", mixed_rows, grad_attn, preferred_element_type=jnp.float32
        )
        grad_mixed = jnp.einsum(
            "rd,cd->rc", grad_attn, proj_out, preferred_element_type=jnp.float32
        ).astype(jnp.bfloat16)
        grad_loc = lax.all_to_all(grad_mixed, HEAD, split_axis=1, concat_axis=0, tiled=True)
        grad_heads = grad_loc.astype(jnp.float32).reshape(block_rows, heads_dev, HD)
        total_rows = jnp.transpose(row_total, (1, 0, 2))
        correction = jnp.transpose(
            jnp.sum(grad_heads * attended, axis=-1, keepdims=True) / total_rows, (1, 0, 2)
        )
        grad_numer = (grad_heads / total_rows).astype(jnp.bfloat16)
        query_heads = query_loc.reshape(block_rows, heads_dev, HD)
        key_heads_loc = key_loc.reshape(block_rows, heads_dev, HD)
        value_heads_loc = value_loc.reshape(block_rows, heads_dev, HD)
        fold_key_part = lax.all_gather(key_loc, BLK, axis=0, tiled=True)
        fold_value_part = lax.all_gather(value_loc, BLK, axis=0, tiled=True)
        fold_piece_len = fold_key_part.shape[0]
        fold_key_doc = segment_of(starts_row, jnp.arange(fold_piece_len, dtype=jnp.int32))
        fold_in_doc = (doc_local[:, None] == fold_key_doc[None, :])[None]
        key_heads = fold_key_part.reshape(fold_piece_len, heads_dev, HD)
        exp_low, grad_scores = score_grads(
            query_heads,
            key_heads,
            fold_value_part.reshape(fold_piece_len, heads_dev, HD),
            grad_numer,
            row_top,
            correction,
            fold_in_doc,
        )
        grad_query = (
            jnp.einsum("hqk,khd->qhd", grad_scores, key_heads, preferred_element_type=jnp.float32)
            * scale
        )
        top_rows = jnp.transpose(row_top[:, :, 0])
        corr_rows = jnp.transpose(correction[:, :, 0])

        def fold_keygrad(portion):
            query_part, numer_part, top_part, corr_part = portion
            piece_len = query_part.shape[0]
            query_doc = segment_of(starts_row, jnp.arange(piece_len, dtype=jnp.int32))
            in_doc = (query_doc[:, None] == doc_local[None, :])[None]
            query_piece = query_part.reshape(piece_len, heads_dev, HD)
            numer_piece = numer_part.reshape(piece_len, heads_dev, HD)
            exp_low, grad_scores = score_grads(
                query_piece,
                key_heads_loc,
                value_heads_loc,
                numer_piece,
                jnp.transpose(top_part)[:, :, None],
                jnp.transpose(corr_part)[:, :, None],
                in_doc,
            )
            grad_key_run = (
                jnp.einsum(
                    "hqk,qhd->khd", grad_scores, query_piece, preferred_element_type=jnp.float32
                )
                * scale
            )
            grad_value_run = jnp.einsum(
                "hqk,qhd->khd", exp_low, numer_piece, preferred_element_type=jnp.float32
            )
            return (grad_key_run, grad_value_run)

        grad_key, grad_value = fold_keygrad(
            (
                lax.all_gather(query_loc, BLK, axis=0, tiled=True),
                lax.all_gather(
                    grad_numer.reshape(block_rows, local_width), BLK, axis=0, tiled=True
                ),
                lax.all_gather(top_rows.astype(jnp.bfloat16), BLK, axis=0, tiled=True).astype(
                    jnp.float32
                ),
                lax.all_gather(corr_rows.astype(jnp.bfloat16), BLK, axis=0, tiled=True).astype(
                    jnp.float32
                ),
            )
        )
        grad_q_rows, grad_k_rows, grad_v_rows = (
            lax.all_to_all(
                grad_query.reshape(block_rows, local_width).astype(jnp.bfloat16),
                HEAD,
                split_axis=0,
                concat_axis=1,
                tiled=True,
            ),
            lax.all_to_all(
                grad_key.reshape(block_rows, local_width).astype(jnp.bfloat16),
                HEAD,
                split_axis=0,
                concat_axis=1,
                tiled=True,
            ),
            lax.all_to_all(
                grad_value.reshape(block_rows, local_width).astype(jnp.bfloat16),
                HEAD,
                split_axis=0,
                concat_axis=1,
                tiled=True,
            ),
        )
        grad_proj = jnp.concatenate([grad_q_rows, grad_k_rows, grad_v_rows], axis=1)
        grad_query_bias = jnp.sum(grad_q_rows.astype(jnp.float32), axis=0)
        grad_value_bias = jnp.sum(grad_v_rows.astype(jnp.float32), axis=0)
        grad_proj_in = jnp.einsum(
            "rd,re->de", inputs, grad_proj, preferred_element_type=jnp.float32
        )
        input_grads.append(
            grad_one
            + jnp.einsum("re,de->rd", grad_proj, proj_in, preferred_element_type=jnp.float32)
        )
        part_grads = (
            grad_proj_in,
            grad_query_bias,
            grad_value_bias,
            grad_proj_out,
            grad_out_bias,
            grad_norm_gain,
            grad_norm_shift,
            grad_up,
            grad_up_bias,
            grad_down,
            grad_down_bias,
            grad_final_gain,
            grad_final_shift,
        )
        grad_sum = (
            part_grads
            if grad_sum is None
            else tuple((left + right for left, right in zip(grad_sum, part_grads)))
        )
    grad_sum = scatter_end(grad_sum)
    (
        grad_proj_in,
        grad_query_bias,
        grad_value_bias,
        grad_proj_out,
        grad_out_bias,
        grad_norm_gain,
        grad_norm_shift,
        grad_up,
        grad_up_bias,
        grad_down,
        grad_down_bias,
        grad_final_gain,
        grad_final_shift,
    ) = grad_sum
    return (
        jnp.stack(outputs),
        jnp.stack(input_grads),
        grad_proj_in,
        grad_query_bias,
        grad_value_bias,
        grad_proj_out,
        grad_out_bias,
        grad_norm_gain,
        grad_norm_shift,
        grad_up,
        grad_up_bias,
        grad_down,
        grad_down_bias,
        grad_final_gain,
        grad_final_shift,
    )


MESH = pl.DeviceIdType.MESH
F32 = jnp.float32
BF16 = jnp.bfloat16
DM = 768
FF = 3072
TOK = 64
SEQ = 2048
HALF = DM // 2
GROUP = 3 * HD
UP_N = FF // 2
CHUNK = 256
PAIRS = 6

QKV, OUT, UP, DOWN, KV, Q = range(6)
SHAPES = (
    (2, 2, 2, 4, 24, 3 * GROUP),
    (4, 4, 24, DM),
    (4, 2, 4, 24, UP_N),
    (4, 4, 96, DM),
    (2, 2, 2, 4, 24, 2 * GROUP),
    (2, 2, 2, 4, 24, GROUP),
)


def by_column(kind):
    return kind == UP


def piece_shape(kind):
    shape = SHAPES[kind]
    if kind in (QKV, KV, Q):
        return shape[1:3] + shape[4:]
    return (2,) + shape[3:] if by_column(kind) else shape[2:]


def when(cond, run):
    if cond is None:
        run()
    else:
        pl.when(cond)(run)


def both(left, right):
    return jnp.logical_and(left, right)


class Place:
    def __init__(self):
        b = lax.axis_index(BLK)
        z = lax.axis_index(HEAD)
        c = lax.rem(b, 2)
        x = lax.rem(lax.div(b, 2), 2)
        y = lax.div(b, 4)
        self.b, self.z, self.c, self.x, self.y = b, z, c, x, y
        self.line = 4 * b + z
        self.sib = (b + 1 - 2 * c, z)
        self.dx = (4 * y + 2 * (1 - x) + c, z)
        self.dy = (4 * (1 - y) + 2 * x + c, z)
        self.dx_other = (4 * y + 2 * (1 - x) + 1 - c, z)
        self.near = z + 1 - 2 * lax.rem(z, 2)
        self.far = lax.rem(z + 2, 4)
        self.cross = 3 - z
        self.swap = (4 * c + 2 * x + y, z)
        self.stays = y == c
        self.moves = y != c
        self.group = 2 * c + x
        self.seat = 4 * y + z
        self.chip = 2 * self.seat + x
        idle = jnp.logical_or(both(z == 0, y == 1), both(z == 3, y == 0))
        self.active = jnp.logical_not(idle)
        inner = jnp.where(z == 1, 4 * y, 1 + 4 * y)
        outer = jnp.where(z == 0, 2, 3)
        self.pair = jnp.where(jnp.logical_or(z == 1, z == 2), inner, outer)
        self.part = lax.div(self.pair, 3)

    def cols(self, kind):
        x, y = self.x, self.y
        if by_column(kind):
            return (2 * y + x, 2 * y + 1 - x, 2 * (1 - y) + x, 2 * (1 - y) + 1 - x)
        return (2 * x + y, 2 * (1 - x) + y, 2 * x + 1 - y, 2 * (1 - x) + 1 - y)


SEATS = ((0, 1), (0, 2), (0, 0), (1, 3), (1, 1), (1, 2))


def chunk(kind, ref, col, z):
    return ref.at[col, :, z] if by_column(kind) else ref.at[col, z]


class Links:
    def __init__(self, sems, here):
        self.sems, self.here, self.count = sems, here, 0
        self.waits = []

    def alloc(self, n=1):
        at = self.count
        self.count += n
        return at

    def make(self, src, dst, s, r, dev):
        return pltpu.make_async_remote_copy(
            src_ref=src, dst_ref=dst, send_sem=self.sems.at[s], recv_sem=self.sems.at[r],
            device_id=dev, device_id_type=MESH,
        )

    def send(self, src, dst, s, r, dev, cond=None):
        when(cond, lambda: self.make(src, dst, s, r, dev).start())

    def recv(self, dst, r, cond=None):
        when(cond, lambda: self.make(dst, dst, r, r, self.here.sib).wait_recv())

    def sent(self, src, s, cond=None):
        when(cond, lambda: self.make(src, src, s, s, self.here.sib).wait_send())

    def drain(self, like, s, cond=None):
        self.waits.append(lambda: self.sent(like, s, cond))

    def local(self, src, dst, cond=None):
        sem = self.sems.at[self.alloc()]
        when(cond, lambda: pltpu.make_async_copy(src, dst, sem).start())
        return lambda: when(cond, lambda: pltpu.make_async_copy(src, dst, sem).wait())

    def put(self, src, dst):
        self.waits.append(self.local(src, dst))

    def finish(self):
        for wait in self.waits:
            wait()


class Gather:
    def __init__(self, links, here, kind, ref):
        self.links, self.here, self.kind, self.ref = links, here, kind, ref
        self.s0, self.r0 = links.alloc(), links.alloc()
        self.sz, self.rz = links.alloc(), links.alloc(4)
        self.s_plane, self.s_relay = links.alloc(), links.alloc()
        self.r_relay, self.r_rest = links.alloc(4), links.alloc()
        self.col, self.col_x, self.col_y, self.col_d = here.cols(kind)
        links.drain(ref.at[0, :, pl.ds(0, 3)] if by_column(kind) else ref.at[0, pl.ds(0, 3)], self.sz)
        links.drain(ref.at[pl.ds(0, 2)], self.s_plane)
        links.drain(ref.at[0], self.s_relay)

    def first_wait(self):
        here = self.here
        if by_column(self.kind):
            self.links.recv(self.ref.at[self.col, 1 - here.c, here.z], self.r0)
        else:
            self.links.recv(self.ref.at[self.col, here.z], self.r0, here.moves)

    def piece(self, col, z):
        return chunk(self.kind, self.ref, col, z)

    def z_hop(self, z, to):
        piece = self.piece(self.col, z)
        self.links.send(piece, piece, self.sz, self.rz + z, (self.here.b, to))

    def spread(self, z):
        piece = self.piece(self.col, z)
        on_y = z < 1
        to_x = jnp.where(on_y, self.r_relay + z, self.r_rest)
        to_y = jnp.where(on_y, self.r_rest, self.r_relay + z)
        self.links.send(piece, piece, self.s_plane, to_x, self.here.dx)
        self.links.send(piece, piece, self.s_plane, to_y, self.here.dy)

    def own_z(self):
        here = self.here
        self.z_hop(here.z, here.far)
        self.z_hop(here.z, here.near)

    def own_plane(self):
        self.spread(self.here.z)

    def land(self, z):
        self.links.recv(self.piece(self.col, z), self.rz + z)

    def hop(self):
        self.z_hop(self.here.far, self.here.near)

    def relay(self, z):
        here = self.here
        on_y = z < 1
        piece = self.piece(jnp.where(on_y, self.col_x, self.col_y), z)
        self.links.recv(piece, self.r_relay + z)
        dev = (jnp.where(on_y, here.dy[0], here.dx[0]), here.z)
        self.links.send(piece, piece, self.s_relay, self.r_rest, dev)

    def done(self):
        self.links.recv(self.ref.at[pl.ds(0, 2)], self.r_rest)


class PairGather:
    def __init__(self, links, here, ref):
        self.links, self.here, self.ref = links, here, ref
        self.s0, self.r0 = links.alloc(), links.alloc()
        self.sz, self.rz = links.alloc(), links.alloc(4)
        self.sy, self.ry = links.alloc(), links.alloc()
        links.drain(ref.at[0, 0, 0, pl.ds(0, 3)], self.s0)
        links.drain(ref.at[0, :, :, pl.ds(0, 3)], self.sz)
        links.drain(ref.at[0], self.sy)

    def first_wait(self):
        self.links.recv(self.ref.at[0, 0, 0, pl.ds(0, 3)], self.r0)

    def piece(self, z):
        return self.ref.at[self.here.y, :, :, z]

    def z_hop(self, z, to):
        self.links.send(self.piece(z), self.piece(z), self.sz, self.rz + z, (self.here.b, to))

    def own_z(self):
        here = self.here
        self.z_hop(here.z, here.far)
        self.z_hop(here.z, here.near)

    def land(self, z):
        self.links.recv(self.piece(z), self.rz + z)

    def hop(self):
        self.z_hop(self.here.far, self.here.near)

    def spread(self, z):
        self.links.send(self.piece(z), self.piece(z), self.sy, self.ry, self.here.dy)

    def done(self):
        self.links.recv(self.ref.at[0], self.ry)


def add_blocks(dst, terms, blocks):
    for at in blocks:
        total = terms[0][at].astype(F32)
        for term in terms[1:]:
            total = total + term[at].astype(F32)
        dst[at] = total.astype(dst.dtype)


class Scatter:
    def __init__(self, links, here, kind, refs):
        self.links, self.here, self.kind = links, here, kind
        self.tilt = 2
        self.grad, self.far, self.cxy, self.zb, self.zr, self.fin, self.last = refs
        self.s_first, self.s_relay, self.sz = links.alloc(), links.alloc(), links.alloc()
        self.r_far, self.r_plane, self.rz = links.alloc(4), links.alloc(4), links.alloc(3)
        self.s_end, self.r_end = links.alloc(), links.alloc()
        self.col, self.col_x, self.col_y, self.col_d = here.cols(kind)
        links.drain(self.cxy, self.s_first)
        links.drain(self.far, self.s_relay)
        links.drain(self.zr.at[pl.ds(0, 3)], self.sz)
        if by_column(kind):
            links.drain(self.last, self.s_end)
        else:
            links.drain(self.last, self.s_end, here.moves)

    def piece(self, col, z):
        return chunk(self.kind, self.grad, col, z)

    def add(self, dst, terms):
        add_blocks(dst, terms, [(h,) for h in range(2)] if by_column(self.kind) else [(slice(0, None),)])

    def side(self, z, to_x, sem):
        here = self.here
        col = jnp.where(to_x, self.col_x, self.col_y)
        dev = (jnp.where(to_x, here.dx[0], here.dy[0]), here.z)
        slot = jnp.where(to_x, z, 4 + z)
        self.links.send(self.piece(col, z), self.cxy.at[slot], sem, self.r_plane + z, dev)

    def send_far(self, order):
        here = self.here
        for z in order:
            to_x = z >= self.tilt
            dev = (jnp.where(to_x, here.dx[0], here.dy[0]), here.z)
            self.links.send(self.piece(self.col_d, z), self.far.at[z], self.s_first, self.r_far + z, dev)

    def send_sides(self, order):
        for z in order:
            self.side(z, z >= self.tilt, self.s_first)

    def relay(self, z):
        to_y = z >= self.tilt
        self.links.recv(self.far.at[z], self.r_far + z)
        piece = self.piece(jnp.where(to_y, self.col_y, self.col_x), z)
        self.add(piece, (piece, self.far.at[z]))
        self.side(z, jnp.logical_not(to_y), self.s_relay)

    def plane(self, z):
        self.links.recv(self.cxy.at[pl.ds(0, 2)], self.r_plane + z)
        self.add(self.zb.at[z], (self.piece(self.col, z), self.cxy.at[z], self.cxy.at[4 + z]))

    def z_first(self, i):
        here = self.here
        z = here.cross if i else here.near
        self.links.send(self.zb.at[z], self.zr.at[i], self.sz, self.rz + i, (here.b, here.near))

    def z_second(self):
        here = self.here
        self.links.recv(self.zr.at[1], self.rz + 1)
        piece = self.zb.at[here.far]
        self.add(piece, (piece, self.zr.at[1]))
        self.links.send(piece, self.zr.at[2], self.sz, self.rz + 2, (here.b, here.far))

    def z_last(self):
        links, here = self.links, self.here
        links.recv(self.zr.at[0], self.rz)
        links.recv(self.zr.at[2], self.rz + 2)
        self.add(self.fin, [self.zb.at[here.z], self.zr.at[0], self.zr.at[2]])
        if by_column(self.kind):
            links.send(self.fin.at[1 - here.c], self.last, self.s_end, self.r_end, here.sib)
        else:
            links.send(self.fin, self.last, self.s_end, self.r_end, here.swap, here.moves)

    def finish(self, out):
        links, here, kind = self.links, self.here, self.kind
        c = here.c
        if by_column(kind):
            out[:, pl.ds(pl.multiple_of(UP_N * c, 128), UP_N)] = self.fin[c]
            links.recv(self.last, self.r_end)
            out[:, pl.ds(pl.multiple_of(UP_N * (1 - c), 128), UP_N)] = self.last[...]
        else:
            links.recv(self.last, self.r_end, here.moves)

            def keep():
                out[...] = self.fin[...]

            def take():
                out[...] = self.last[...]

            when(here.stays, keep)
            when(here.moves, take)


class ColumnScatter(Scatter):
    def __init__(self, links, here, kind, refs):
        self.links, self.here, self.kind = links, here, kind
        self.grad, self.far, self.cxy, self.zb, self.zr, self.fin, self.last = refs
        self.s_first, self.s_relay, self.sz = links.alloc(), links.alloc(), links.alloc()
        self.r_far, self.r_plane, self.rz = links.alloc(4), links.alloc(4), links.alloc(3)
        self.s_far, self.s_column = links.alloc(), links.alloc()
        self.s_end, self.r_end = links.alloc(), links.alloc()
        self.col, self.col_x, self.col_y, self.col_d = here.cols(kind)
        links.drain(self.cxy.at[pl.ds(0, 7)], self.s_first)
        links.drain(self.far.at[0], self.s_relay)
        links.drain(self.far.at[0], self.s_far)
        links.drain(self.far.at[pl.ds(0, 3)], self.s_column)
        links.drain(self.zr.at[pl.ds(0, 3)], self.sz)
        links.drain(self.last, self.s_end, None if by_column(kind) else here.moves)

    def to_side(self, z, to_x, sem):
        here = self.here
        col, slot, dev = (self.col_x, z, here.dx) if to_x else (self.col_y, 4 + z, here.dy)
        self.links.send(self.piece(col, z), self.cxy.at[slot], sem, self.r_plane + z, dev)

    def send_sides(self, order):
        for z in order:
            self.to_side(z, True, self.s_first)
            if z is not self.here.z:
                self.to_side(z, False, self.s_first)

    def column_first(self):
        here = self.here
        for i, z in enumerate((here.near, here.cross)):
            self.links.send(self.piece(self.col_d, z), self.far.at[i], self.s_column, self.r_far + i, (here.b, here.near))

    def column_second(self):
        here = self.here
        self.links.recv(self.far.at[1], self.r_far + 1)
        piece = self.piece(self.col_d, here.far)
        self.add(piece, (piece, self.far.at[1]))
        self.links.send(piece, self.far.at[2], self.s_column, self.r_far + 2, (here.b, here.far))

    def column_last(self):
        here = self.here
        self.links.recv(self.far.at[0], self.r_far)
        self.links.recv(self.far.at[2], self.r_far + 2)
        piece = self.piece(self.col_d, here.z)
        self.add(piece, (piece, self.far.at[0], self.far.at[2]))
        self.links.send(piece, self.far.at[3], self.s_far, self.r_far + 3, here.dx)

    def relay_own(self):
        here = self.here
        self.links.recv(self.far.at[3], self.r_far + 3)
        piece = self.piece(self.col_y, here.z)
        self.add(piece, (piece, self.far.at[3]))
        self.to_side(here.z, False, self.s_relay)


class PairScatter:
    def __init__(self, links, here, kind, refs):
        self.links, self.here, self.kind = links, here, kind
        self.grad, self.cy, self.zb, self.zr, self.fin, self.last = refs
        self.sy, self.ry = links.alloc(), links.alloc(4)
        self.sz, self.rz = links.alloc(), links.alloc(3)
        self.s_end, self.r_end = links.alloc(), links.alloc()
        links.drain(self.cy, self.sy)
        links.drain(self.zr.at[pl.ds(0, 3)], self.sz)
        links.drain(self.last.at[pl.ds(0, 3)], self.s_end)

    def add(self, dst, terms):
        add_blocks(dst, terms, [(i, j) for i in range(2) for j in range(2)])

    def send(self, z):
        here = self.here
        self.links.send(self.grad.at[1 - here.y, :, :, z], self.cy.at[z], self.sy, self.ry + z, here.dy)

    def plane(self, z):
        self.links.recv(self.cy.at[z], self.ry + z)
        self.add(self.zb.at[z], (self.grad.at[self.here.y, :, :, z], self.cy.at[z]))

    def z_first(self, i):
        here = self.here
        z = here.cross if i else here.near
        self.links.send(self.zb.at[z], self.zr.at[i], self.sz, self.rz + i, (here.b, here.near))

    def z_second(self):
        here = self.here
        self.links.recv(self.zr.at[1], self.rz + 1)
        piece = self.zb.at[here.far]
        self.add(piece, (piece, self.zr.at[1]))
        self.links.send(piece, self.zr.at[2], self.sz, self.rz + 2, (here.b, here.far))

    def z_last(self):
        links, here = self.links, self.here
        links.recv(self.zr.at[0], self.rz)
        links.recv(self.zr.at[2], self.rz + 2)
        self.add(self.fin, [self.zb.at[here.z], self.zr.at[0], self.zr.at[2]])
        x, c = here.x, here.c
        slot = self.last.at[here.group]
        links.send(self.fin.at[1 - x, c], slot, self.s_end, self.r_end, here.dx)
        links.send(self.fin.at[1 - x, 1 - c], slot, self.s_end, self.r_end, here.dx_other)
        links.send(self.fin.at[x, 1 - c], slot, self.s_end, self.r_end, here.sib)

    def finish(self, out):
        self.last[self.here.group] = self.fin[self.here.x, self.here.c]
        self.links.recv(self.last.at[pl.ds(0, 3)], self.r_end)
        for group in range(4):
            if self.kind == Q:
                out[:, GROUP * group : GROUP * (group + 1)] = self.last[group]
            else:
                for i in range(2):
                    at = DM * (i + 1) + GROUP * group
                    out[:, at : at + GROUP] = self.last[group, :, GROUP * i : GROUP * (i + 1)]


def dot(a, b):
    return jnp.dot(a, b, preferred_element_type=F32)


def dot_nt(a, b):
    return lax.dot_general(a, b, (((1,), (1,)), ((), ())), preferred_element_type=F32)


def dot_tn(a, b):
    return lax.dot_general(a, b, (((0,), (0,)), ((), ())), preferred_element_type=F32)


def row_sum(values):
    return jnp.sum(values, axis=0, keepdims=True)


def div24(n):
    return lax.shift_right_logical(n * 2731, 16)


def iota(shape, dim):
    return lax.broadcasted_iota(jnp.int32, shape, dim)


def select_24():
    n = iota((128, DM), 1)
    return (iota((128, DM), 0) == n - 24 * div24(n)).astype(BF16)


def select_96():
    n = iota((128, UP_N), 1)
    run = lax.shift_right_logical(div24(n), 2)
    return (iota((128, UP_N), 0) == 32 + n - 96 * run).astype(BF16)


def owner_24(lead):
    shape = (lead, 8, DM)
    return div24(iota(shape, 2)) == iota(shape, 0)


def owner_96():
    shape = (16, UP_N)
    return lax.shift_right_logical(div24(iota(shape, 1)), 2) == iota(shape, 0)


def exact_nt(values, select):
    high = values.astype(BF16)
    rest = values - high.astype(F32)
    mid = rest.astype(BF16)
    low = (rest - mid.astype(F32)).astype(BF16)
    return dot_nt(high, select) + dot_nt(mid, select) + dot_nt(low, select)


SCRATCH = dict(
    w_rows=((24, 3 * DM), BF16),
    w_parts=((4, 24, 3 * GROUP), BF16),
    vecs=((8, 128), F32),
    cot=((2, TOK, DM), BF16),
    b_out=((2, TOK, DM), F32),
    b_tok=((2, TOK, DM), F32),
    b_qkv=((24, 3 * DM), F32),
    b_wout=((24, DM), F32),
    b_up=((24, FF), F32),
    b_down=((96, DM), F32),
    b_vec=((8, 128), F32),
    vec_all=((32, 8, 128), F32),
    vec_rows=((8, DM), F32),
    up_row=((1, UP_N), F32),
    x_pair=((2, 2, 2, TOK, DM), BF16),
    fl_chip=((2, 2, TOK, DM), BF16),
    gf_chip=((2, 2, TOK, DM), BF16),
    ga_chip=((2, 2, TOK, DM), BF16),
    partial=((2, 2, TOK, DM), F32),
    back0=((2, TOK, DM), F32),
    back1=((2, TOK, DM), F32),
    back2=((2, TOK, DM), F32),
    tok_part=((2, 2, 2, TOK, DM), F32),
    tok_back=((2, 2, TOK, DM), F32),
    tok_send=((2, TOK, DM), BF16),
    tok_last=((2, TOK, DM), BF16),
    send_q=((PAIRS, GROUP, 256), BF16),
    qkv_t=((GROUP, SEQ), BF16),
    k_rows=((SEQ, HD), BF16),
    v_rows=((SEQ, HD), BF16),
    q_rows=((SEQ, HD), BF16),
    g_rows=((SEQ, HD), BF16),
    key_doc=((SEQ, 128), jnp.int32),
    query_doc=((1, SEQ), jnp.int32),
    scores=((SEQ, CHUNK), F32),
    weights=((SEQ, SEQ), BF16),
    total=((1, SEQ), F32),
    att_t=((HD, SEQ), F32),
    att_send=((HD, SEQ), BF16),
    mix_in=((12, HD, 128), BF16),
    g_send=((12, HD, 128), BF16),
    g_t=((HD, SEQ), BF16),
    gn_t=((HD, SEQ), BF16),
    corr=((1, SEQ), F32),
    ds=((CHUNK, SEQ), BF16),
    dq_t=((HD, SEQ), F32),
    d_send=((GROUP, SEQ), BF16),
    d_in=((PAIRS, GROUP, 256), BF16),
    mixed_t=((HALF, 2 * 128), BF16),
    first=((2 * TOK, DM), F32),
    normed1=((2 * TOK, DM), F32),
    inv1=((2 * TOK, 1), F32),
    active=((4 * TOK, UP_N), BF16),
    slope=((4 * TOK, UP_N), F32),
    gh=((4 * TOK, UP_N), BF16),
    gh2=((2 * TOK, DM), F32),
    gh1=((2 * TOK, DM), F32),
    gp_kv=((8 * TOK, 2 * GROUP), BF16),
    gp_q=((8 * TOK, GROUP), BF16),
    vec_grad=((8, DM), F32),
    up_grad=((1, UP_N), F32),
    vec_send=((32, 8, 128), F32),
    vec_recv=((32, 8, 128), F32),
)


def sum_scratch(kind):
    piece = piece_shape(kind)
    if kind in (KV, Q):
        low = [SHAPES[kind]] + [(4,) + piece] * 3
        last = (4,) + piece[2:]
    else:
        low = [SHAPES[kind], (4,) + piece, (8,) + piece, (4,) + piece, (4,) + piece]
        last = piece[1:] if by_column(kind) else piece
    return [(shape, BF16) for shape in low] + [(piece, F32), (last, F32)]


GATHERED = (QKV, OUT, UP, DOWN)
SUMMED = (OUT, UP, DOWN, KV, Q)
N_SEM = 181


def all_scratch():
    shapes = list(SCRATCH.values())
    shapes += [(SHAPES[kind], BF16) for kind in GATHERED]
    for kind in SUMMED:
        shapes += sum_scratch(kind)
    shapes += [((24,), BF16)] * 8 + [((96,), BF16)]
    return [pltpu.VMEM(shape, dtype) for shape, dtype in shapes] + [pltpu.SemaphoreType.DMA((N_SEM,))]


def layer_kernel(
    tokens, starts, w_qkv, w_out, w_up, w_down,
    v0, v1, v2, v3, v4, v5, v6, v7, v8, cotangent,
    o_out, o_tok, o_qkv, o_wout, o_up, o_down, o_vec,
    *scratch,
):
    vec_in = (v0, v1, v2, v3, v4, v5, v6, v7, v8)
    m = SimpleNamespace(**dict(zip(SCRATCH, scratch)))
    at = len(SCRATCH)
    gathered = scratch[at : at + 4]
    at += 4
    summed = []
    for kind in SUMMED:
        n = len(sum_scratch(kind))
        summed.append(scratch[at : at + n])
        at += n
    vec_rows_in = scratch[at : at + 9]
    sems = scratch[-1]
    here = Place()
    links = Links(sems, here)
    b, z, c, x = here.b, here.z, here.c, here.x
    line, chip, group = here.line, here.chip, here.group
    g_qkv = PairGather(links, here, gathered[0])
    g_out, g_up, g_down = [Gather(links, here, kind, ref) for kind, ref in zip(GATHERED[1:], gathered[1:])]
    s_out, s_up, s_down = [
        make(links, here, kind, refs)
        for make, kind, refs in zip((Scatter, Scatter, ColumnScatter), SUMMED[:3], summed[:3])
    ]
    s_kv, s_q = [PairScatter(links, here, kind, refs) for kind, refs in zip(SUMMED[3:], summed[3:])]
    ahead = (g_out, g_up)

    def peer(d):
        other = lax.rem(line + d, 32)
        return (lax.div(other, 4), lax.rem(other, 4))

    x_pair = m.x_pair

    def up_part(which):
        return w_up.at[:, pl.ds(pl.multiple_of(UP_N * which, 128), UP_N)]

    qkv_wait = links.local(w_qkv, m.w_rows)
    vec_waits = [links.local(src, dst) for src, dst in zip(vec_in, vec_rows_in)]
    x_wait = links.local(tokens, x_pair.at[:, x, c])
    up_wait = links.local(up_part(c), g_up.ref.at[g_up.col, c, z])
    row_waits = [
        links.local(shard, gather.ref.at[gather.col, z], here.stays)
        for gather, shard in ((g_out, w_out), (g_down, w_down))
    ]
    cot_wait = links.local(cotangent, m.cot)
    m.vec_grad[...] = jnp.zeros((8, DM), F32)
    m.vecs[...] = jnp.zeros((8, 128), F32)
    for wait in vec_waits:
        wait()
    for j in range(8):
        m.vecs[j : j + 1, 0:24] = vec_rows_in[j][...].astype(F32).reshape(1, 24)
    m.vecs[0:1, 32:128] = vec_rows_in[8][...].astype(F32).reshape(1, 96)
    qkv_wait()
    for k in range(4):
        for j in range(3):
            block = m.w_rows[:, DM * j + GROUP * k : DM * j + GROUP * (k + 1)]
            m.w_parts[k, :, GROUP * j : GROUP * (j + 1)] = block

    barrier = pltpu.get_barrier_semaphore()

    def greet(d, carry):
        pl.semaphore_signal(barrier, inc=1, device_id=peer(d), device_id_type=MESH)
        return carry

    lax.fori_loop(1, 32, greet, 0)
    pl.semaphore_wait(barrier, 31)

    slot = g_qkv.ref.at[here.y, x, c, z]
    links.send(m.w_parts.at[2 * c + 1 - x], slot, g_qkv.s0, g_qkv.r0, here.dx)
    links.send(m.w_parts.at[2 * (1 - c) + 1 - x], slot, g_qkv.s0, g_qkv.r0, here.dx_other)
    links.send(m.w_parts.at[2 * (1 - c) + x], slot, g_qkv.s0, g_qkv.r0, here.sib)
    x_sem = links.alloc(6)
    own_x = x_pair.at[:, x, c]
    links.send(tokens, own_x, x_sem, x_sem + 1, here.dx)
    links.send(tokens, own_x, x_sem + 2, x_sem + 3, here.sib)
    links.drain(own_x, x_sem)
    links.drain(own_x, x_sem + 2)
    up_slot = g_up.ref.at[g_up.col, c, z]
    links.send(up_part(1 - c), up_slot, g_up.s0, g_up.r0, here.sib)
    links.drain(up_slot, g_up.s0)
    for gather, shard in ((g_out, w_out), (g_down, w_down)):
        slot = gather.ref.at[2 * x + c, z]
        links.send(shard, slot, gather.s0, gather.r0, here.swap, here.moves)
        links.drain(slot, gather.s0, here.moves)
    vec_sem = links.alloc(4)
    vec_all = m.vec_all

    def vec_copy(d):
        return links.make(m.vecs, vec_all.at[line], vec_sem, vec_sem + 1, peer(d))

    def vec_start(d, carry):
        vec_copy(d).start()
        return carry

    lax.fori_loop(1, 32, vec_start, 0)
    vec_all[line] = m.vecs[...]
    g_qkv.ref[here.y, x, c, z] = m.w_parts[group]
    for wait in (x_wait, up_wait, *row_waits, cot_wait):
        wait()

    g_qkv.first_wait()
    g_qkv.own_z()
    g_qkv.spread(z)
    for gather in ahead:
        gather.first_wait()
        gather.own_plane()

    def documents():
        def position(n):
            z_part = lax.shift_left(jnp.bitwise_and(lax.shift_right_logical(n, 8), 3), 6)
            xc_part = lax.shift_left(jnp.bitwise_and(lax.shift_right_logical(n, 6), 3), 8)
            y_part = lax.shift_left(lax.shift_right_logical(n, 10), 10)
            return y_part + xc_part + z_part + jnp.bitwise_and(n, 63)

        def doc_of(n):
            place = position(n)
            doc = jnp.zeros(place.shape, jnp.int32)
            for j in range(starts.shape[1]):
                doc = doc + (starts[here.part, j] <= place).astype(jnp.int32)
            return doc

        m.query_doc[...] = doc_of(iota((1, SEQ), 1))

        def rows(i, carry):
            start = pl.multiple_of(i * 256, 256)
            m.key_doc[pl.ds(start, 256), :] = doc_of(iota((256, 128), 0) + i * 256)
            return carry

        lax.fori_loop(0, SEQ // 256, rows, 0)

    when(here.active, documents)

    other_x = x_pair.at[:, 1 - x, c]
    links.recv(other_x, x_sem + 1)
    links.send(other_x, other_x, x_sem + 4, x_sem + 5, here.sib)
    links.drain(other_x, x_sem + 4)
    g_qkv.land(here.far)
    g_qkv.hop()
    g_qkv.spread(here.far)
    for gather in ahead:
        gather.own_z()
    many = vec_all.at[pl.ds(0, 31)]
    links.sent(many, vec_sem)
    links.recv(many, vec_sem + 1)
    spread = dot(vec_all[...].reshape(256, 128).astype(BF16), select_24()).reshape(32, 8, DM)
    m.vec_rows[...] = jnp.sum(jnp.where(owner_24(32), spread, 0.0), axis=0)
    spread = dot(vec_all[pl.ds(16 * c, 16), 0, :].astype(BF16), select_96())
    m.up_row[...] = row_sum(jnp.where(owner_96(), spread, 0.0))

    def vector(j):
        return m.vec_rows[j : j + 1, :]

    def vector_group(j):
        total = jnp.zeros((1, GROUP), F32)
        for k in range(4):
            total = total + jnp.where(group == k, m.vec_rows[j : j + 1, GROUP * k : GROUP * (k + 1)], 0.0)
        return total

    g_qkv.land(here.near)
    g_qkv.spread(here.near)
    for gather in ahead:
        gather.relay(z)
    g_qkv.land(here.cross)
    g_qkv.spread(here.cross)
    for gather in ahead:
        gather.land(here.far)
        gather.hop()
        gather.spread(here.far)
    links.recv(x_pair.at[:, x, 1 - c], x_sem + 3)
    links.recv(x_pair.at[:, 1 - x, 1 - c], x_sem + 5)
    g_qkv.done()

    def weight_qkv():
        return g_qkv.ref[...].reshape(DM, 3 * GROUP)

    def x_rows():
        return x_pair[...].reshape(8 * TOK, DM)

    chip_lanes = pl.ds(pl.multiple_of(chip * 128, 128), 128)
    seat_lanes = pl.ds(pl.multiple_of(here.seat * 256, 256), 256)
    idle = jnp.logical_not(here.active)

    def seat_dev(y_to, z_to, x_to):
        return (4 * y_to + 2 * x_to + c, z_to)

    send_q, qkv_t = m.send_q, m.qkv_t
    q_sem = links.alloc(2)
    bias = jnp.concatenate([vector_group(0), jnp.zeros((1, GROUP), F32), vector_group(1)], axis=1)
    for part in range(MB):
        rows = (dot(x_pair[part].reshape(4 * TOK, DM), weight_qkv()) + bias).astype(BF16)
        turned = rows.T
        for i in range(3):
            for j in range(3):
                block = turned[GROUP * j + HD * i : GROUP * j + HD * (i + 1), :]
                if j == 0:
                    block = block * jnp.asarray(HD ** (-0.5), BF16)
                send_q[3 * part + i, HD * j : HD * (j + 1), :] = block
            pair = 3 * part + i
            other = jnp.logical_not(both(here.active, here.pair == pair))
            dev = seat_dev(*SEATS[pair], x)
            links.send(send_q.at[pair], qkv_t.at[:, seat_lanes], q_sem, q_sem + 1, dev, other)

    links.drain(send_q.at[pl.ds(0, PAIRS - 1)], q_sem, here.active)
    links.drain(send_q, q_sem, idle)

    def own_q():
        qkv_t[:, seat_lanes] = send_q[here.pair]

    when(here.active, own_q)

    class ToSeats:
        def __init__(self, src_of, dst_of, slot, slots, seats, own):
            self.src_of, self.dst_of, self.slot, self.slots = src_of, dst_of, slot, slots
            self.seats, self.own = seats, own
            self.s, self.r = links.alloc(), links.alloc()
            self.width = SEQ // seats

        def start(self, other):
            start = pl.multiple_of(self.width * other, self.width)
            src, dst = self.src_of(pl.ds(start, self.width)), self.dst_of(self.slot)
            if self.seats == 16:
                place, x_to, mine = lax.div(other, 2), lax.rem(other, 2), chip
            else:
                place, x_to, mine = other, x, here.seat
            dev = seat_dev(lax.div(place, 4), lax.rem(place, 4), x_to)
            links.send(src, dst, self.s, self.r, dev, mine != other)

        def finish(self):
            links.drain(self.src_of(pl.ds(0, SEQ - self.width)), self.s, here.active)
            when(here.active, self.own)

        def wait(self):
            links.recv(self.dst_of(pl.ds(0, self.slots - 1)), self.r, here.active)
            links.recv(self.dst_of(pl.ds(0, self.slots)), self.r, idle)

    g_down.first_wait()
    g_down.own_plane()
    g_down.own_z()
    for gather in ahead:
        gather.land(here.near)
        gather.spread(here.near)
    for gather in ahead:
        gather.relay(here.far)
    for gather in ahead:
        gather.land(here.cross)
        gather.spread(here.cross)
    links.recv(qkv_t.at[:, pl.ds(0, SEQ - 256)], q_sem + 1, here.active)
    for gather in ahead:
        gather.relay(here.near)
    g_down.relay(z)

    weights = m.weights
    mix_slot = 6 * here.part + 3 * x + here.pair - 3 * here.part

    def own_mix():
        m.mix_in[mix_slot] = m.att_send[:, chip_lanes]

    mix = ToSeats(
        lambda lanes: m.att_send.at[:, lanes], lambda slot: m.mix_in.at[slot], mix_slot, 12, 16, own_mix
    )

    def turn_keys():
        m.k_rows[...] = qkv_t[HD : 2 * HD, :].T
        m.v_rows[...] = qkv_t[2 * HD : 3 * HD, :].T
        m.q_rows[...] = qkv_t[0:HD, :].T

    when(here.active, turn_keys)

    def attend(i):
        lanes = pl.ds(pl.multiple_of(i * CHUNK, CHUNK), CHUNK)
        query = qkv_t[0:HD, lanes]
        doc = m.query_doc[:, lanes]
        top = None
        for k in range(8):
            rows = slice(256 * k, 256 * (k + 1))
            key_doc = m.key_doc[rows, :]
            same = jnp.concatenate([key_doc, key_doc], axis=1) == doc
            scores = jnp.where(same, dot(m.k_rows[rows, :], query), NEG)
            m.scores[rows, :] = scores
            here_top = jnp.max(scores, axis=0, keepdims=True)
            top = here_top if top is None else jnp.maximum(top, here_top)
        total = None
        for k in range(8):
            rows = slice(256 * k, 256 * (k + 1))
            grown = jnp.exp(m.scores[rows, :] - top)
            weights[rows, lanes] = grown.astype(BF16)
            part_sum = row_sum(grown)
            total = part_sum if total is None else total + part_sum
        numer = dot(qkv_t[2 * HD : 3 * HD, :], weights[:, lanes])
        attended = numer / total
        m.total[:, lanes] = total
        m.att_t[:, lanes] = attended
        m.att_send[:, lanes] = attended.astype(BF16)
        mix.start(2 * i)
        mix.start(2 * i + 1)

    def some(body, first, last):
        def run():
            def one(i, carry):
                body(i)
                return carry

            lax.fori_loop(first, last, one, 0)

        when(here.active, run)

    some(attend, 0, 4)
    for gather in ahead:
        gather.relay(here.cross)
    g_down.land(here.far)
    g_down.hop()
    g_down.spread(here.far)
    g_down.land(here.near)
    g_down.spread(here.near)
    some(attend, 4, 7)
    g_down.land(here.cross)
    g_down.spread(here.cross)
    some(attend, 7, 8)
    g_down.relay(here.far)
    g_down.relay(here.near)
    mix.finish()
    mix.wait()
    g_out.done()
    g_down.relay(here.cross)

    def share(buf, values):
        sem = links.alloc(2)
        buf[:, c] = values.reshape(MB, TOK, DM)
        links.send(buf.at[:, c], buf.at[:, c], sem, sem + 1, here.sib)
        links.drain(buf.at[:, c], sem)
        links.recv(buf.at[:, 1 - c], sem + 1)

    def combine(values, back):
        sem = links.alloc(2)
        partial = m.partial
        partial[...] = values.reshape(MB, 2, TOK, DM)
        links.send(partial.at[:, 1 - c], back, sem, sem + 1, here.sib)
        links.recv(back, sem + 1)
        total = partial[:, c].reshape(2 * TOK, DM) + back[...].reshape(2 * TOK, DM)
        links.sent(partial.at[:, 1 - c], sem)
        return total

    def norm_rows(values, gain, shift):
        center = values - jnp.mean(values, axis=-1, keepdims=True)
        inverse = lax.rsqrt(jnp.mean(center * center, axis=-1, keepdims=True) + EPS)
        normed = center * inverse
        return normed * gain + shift, normed, inverse

    def norm_back(upstream, normed, inverse, gain):
        scaled = upstream * gain
        return inverse * (
            scaled
            - jnp.mean(scaled, axis=-1, keepdims=True)
            - normed * jnp.mean(scaled * normed, axis=-1, keepdims=True)
        )

    mixed_t = m.mixed_t
    mixed = []
    for part in range(MB):
        piece = m.mix_in[6 * part : 6 * part + 6].reshape(HALF, 128)
        mixed_t[:, 128 * part : 128 * (part + 1)] = piece
        mixed.append(piece.T)
    mixed = jnp.concatenate(mixed, axis=0)

    def weight_out():
        return g_out.ref[...].reshape(HALF, DM)

    attn = combine(dot(mixed, weight_out()), m.back0) + vector(2)
    own_tokens = x_pair[:, x, c].reshape(2 * TOK, DM).astype(F32)
    first, normed_one, inverse_one = norm_rows(own_tokens + attn, vector(3), vector(4))
    m.first[...] = first
    m.normed1[...] = normed_one
    m.inv1[...] = inverse_one
    share(m.fl_chip, first.astype(BF16))

    g_up.done()
    def fl_rows():
        return m.fl_chip[...].reshape(4 * TOK, DM)

    def weight_up(j):
        return g_up.ref[:, :, :, :, HALF * j : HALF * (j + 1)].reshape(DM, HALF)

    def weight_down(j):
        return g_down.ref[j].reshape(HALF, DM)

    for j in range(4):
        lanes = slice(HALF * j, HALF * (j + 1))
        hidden = dot(fl_rows(), weight_up(j)) + m.up_row[:, lanes]
        cdf = 0.5 * (1.0 + lax.erf(hidden * (0.5**0.5)))
        m.slope[:, lanes] = cdf + hidden * (jnp.exp(-0.5 * hidden * hidden) * 0.3989422804014327)
        m.active[:, lanes] = (hidden * cdf).astype(BF16)
    g_down.done()
    ffn = None
    for j in range(4):
        lanes = slice(HALF * j, HALF * (j + 1))
        term = dot(m.active[:, lanes], weight_down(j))
        ffn = term if ffn is None else ffn + term
    ffn = combine(ffn, m.back1) + vector(5)
    result, normed_two, inverse_two = norm_rows(m.first[...] + ffn, vector(6), vector(7))
    m.b_out[...] = result.reshape(MB, TOK, DM)
    links.put(m.b_out, o_out)

    targets = (here.near, here.cross, here.far, z)
    vec_grad = m.vec_grad
    grad_result = m.cot[...].reshape(2 * TOK, DM).astype(F32)
    vec_grad[6:7, :] = row_sum(grad_result * normed_two)
    vec_grad[7:8, :] = row_sum(grad_result)
    grad_two = norm_back(grad_result, normed_two, inverse_two, vector(6))
    m.gh2[...] = grad_two
    grad_ffn = grad_two.astype(BF16)
    vec_grad[5:6, :] = row_sum(grad_ffn.astype(F32))
    share(m.gf_chip, grad_ffn)

    def gf_rows():
        return m.gf_chip[...].reshape(4 * TOK, DM)

    for j in range(4):
        lanes = slice(HALF * j, HALF * (j + 1))
        s_down.grad[j] = dot_tn(m.active[:, lanes], gf_rows()).astype(BF16).reshape(4, 96, DM)
    s_down.send_sides(targets)
    s_down.column_first()
    grad_first = None
    for j in range(4):
        lanes = slice(HALF * j, HALF * (j + 1))
        grad_active = dot_nt(gf_rows(), weight_down(j))
        grad_hidden = (grad_active * m.slope[:, lanes]).astype(BF16)
        m.gh[:, lanes] = grad_hidden
        m.up_grad[:, lanes] = row_sum(grad_hidden.astype(F32))
    for j in range(4):
        lanes = slice(HALF * j, HALF * (j + 1))
        term = dot_nt(m.gh[:, lanes], weight_up(j))
        grad_first = term if grad_first is None else grad_first + term
    grad_first = m.gh2[...] + combine(grad_first, m.back2)
    normed_one = m.normed1[...]
    vec_grad[3:4, :] = row_sum(grad_first * normed_one)
    vec_grad[4:5, :] = row_sum(grad_first)
    grad_one = norm_back(grad_first, normed_one, m.inv1[...], vector(3))
    m.gh1[...] = grad_one
    grad_attn = grad_one.astype(BF16)
    vec_grad[2:3, :] = row_sum(grad_attn.astype(F32))
    share(m.ga_chip, grad_attn)

    def ga_rows():
        return m.ga_chip[...].reshape(4 * TOK, DM)

    turned = dot_nt(ga_rows(), weight_out()).astype(BF16).T
    for part in range(MB):
        m.g_send[6 * part : 6 * part + 6] = turned[:, 128 * part : 128 * (part + 1)].reshape(6, HD, 128)
    g_t = m.g_t
    g_sem = links.alloc(2)
    for slot in range(12):
        part, head = slot // 6, slot % 6
        pair, x_to = 3 * part + head % 3, head // 3
        mine = both(here.active, both(here.pair == pair, x == x_to))
        dev = seat_dev(*SEATS[pair], x_to)
        links.send(m.g_send.at[slot], g_t.at[:, chip_lanes], g_sem, g_sem + 1, dev, jnp.logical_not(mine))
    links.drain(m.g_send.at[pl.ds(0, 11)], g_sem, here.active)
    links.drain(m.g_send, g_sem, idle)

    def own_g():
        g_t[:, chip_lanes] = m.g_send[mix_slot]

    when(here.active, own_g)
    for j in range(4):
        lanes = slice(HALF * j, HALF * (j + 1))
        s_up.grad[:, :, :, :, lanes] = (
            dot_tn(fl_rows(), m.gh[:, lanes]).astype(BF16).reshape(4, 2, 4, 24, HALF)
        )
    s_out.grad[...] = dot(mixed_t[...], ga_rows()).astype(BF16).reshape(SHAPES[OUT])
    s_up.send_far(targets)
    s_out.send_far(targets)
    s_up.send_sides(targets)
    s_out.send_sides(targets)

    def planes(scatter, order=targets):
        for i, t in enumerate(order):
            scatter.plane(t)
            if i < 2:
                scatter.z_first(i)

    s_down.column_second()
    planes(s_down, targets[:3])
    links.recv(g_t.at[:, pl.ds(0, SEQ - 128)], g_sem + 1, here.active)

    d_send, d_in = m.d_send, m.d_in

    def own_kv():
        d_in[here.pair, HD : 3 * HD, :] = d_send[HD : 3 * HD, seat_lanes]

    def own_dq():
        d_in[here.pair, 0:HD, :] = d_send[0:HD, seat_lanes]

    grad_kv = ToSeats(
        lambda lanes: d_send.at[pl.ds(HD, 2 * HD), lanes], lambda slot: d_in.at[slot, pl.ds(HD, 2 * HD)],
        here.pair, PAIRS, 8, own_kv,
    )
    grad_q = ToSeats(
        lambda lanes: d_send.at[pl.ds(0, HD), lanes], lambda slot: d_in.at[slot, pl.ds(0, HD)],
        here.pair, PAIRS, 8, own_dq,
    )

    def turn_grads():
        grad = g_t[...].astype(F32)
        inverse = 1.0 / m.total[...]
        numer = grad * inverse
        m.gn_t[...] = numer.astype(BF16)
        m.g_rows[...] = numer.astype(BF16).T
        m.corr[...] = row_sum(grad * m.att_t[...]) * inverse
        m.dq_t[...] = jnp.zeros((HD, SEQ), F32)

    when(here.active, turn_grads)

    def back(k):
        keys = pl.ds(pl.multiple_of(k * CHUNK, CHUNK), CHUNK)
        value = m.v_rows[keys, :]
        for i in range(4):
            lanes = slice(512 * i, 512 * (i + 1))
            grad_weights = dot(value, m.gn_t[:, lanes])
            grown = weights[keys, lanes].astype(F32)
            m.ds[:, lanes] = (grown * (grad_weights - m.corr[:, lanes])).astype(BF16)
        ds = m.ds
        d_send[HD : 2 * HD, keys] = dot(ds[...], m.q_rows[...]).T.astype(BF16)
        d_send[2 * HD : 3 * HD, keys] = dot(weights[keys, :], m.g_rows[...]).T.astype(BF16)
        grad_kv.start(k)
        m.dq_t[...] += dot(qkv_t[HD : 2 * HD, keys], ds[...])

    some(back, 0, 4)
    s_down.column_last()
    for t in targets:
        s_up.relay(t)
    for t in targets:
        s_out.relay(t)
    some(back, 4, 8)

    def last_query():
        d_send[0:HD, :] = (m.dq_t[...] * (HD ** (-0.5))).astype(BF16)
        for other in range(8):
            grad_q.start(other)

    when(here.active, last_query)
    grad_kv.finish()
    grad_q.finish()
    s_down.relay_own()
    s_down.z_second()
    planes(s_up, targets[:2])
    grad_kv.wait()
    gp_kv, gp_q = m.gp_kv, m.gp_q
    for part in range(MB):
        heads = slice(3 * part, 3 * part + 3)
        rows = [d_in[heads, HD * j : HD * (j + 1), :].reshape(GROUP, 256) for j in (1, 2)]
        gp_kv[256 * part : 256 * (part + 1), :] = jnp.concatenate(rows, axis=0).T
    s_kv.grad[...] = dot_tn(x_rows(), gp_kv[...]).astype(BF16).reshape(SHAPES[KV])
    for t in targets:
        s_kv.send(t)
    for t in targets[2:]:
        s_up.plane(t)
    planes(s_out)
    s_down.plane(z)
    grad_q.wait()
    for part in range(MB):
        gp_q[256 * part : 256 * (part + 1), :] = d_in[3 * part : 3 * part + 3, 0:HD, :].reshape(GROUP, 256).T
    s_q.grad[...] = dot_tn(x_rows(), gp_q[...]).astype(BF16).reshape(SHAPES[Q])
    for t in targets:
        s_q.send(t)
    planes(s_kv)
    s_out.z_second()
    all_weights = weight_qkv()
    t_sem = links.alloc(4)
    for part in range(MB):
        rows = slice(256 * part, 256 * (part + 1))
        terms = dot_nt(gp_q[rows, :], all_weights[:, 0:GROUP]) + dot_nt(gp_kv[rows, :], all_weights[:, GROUP:])
        m.tok_part[part] = terms.reshape(2, 2, TOK, DM)
    links.send(m.tok_part.at[:, :, 1 - c], m.tok_back, t_sem, t_sem + 1, here.sib)
    links.drain(m.tok_back, t_sem)
    s_up.z_second()
    sum_q = row_sum(gp_q[...].astype(F32))
    sum_v = row_sum(gp_kv[:, GROUP:].astype(F32))
    for k in range(4):
        lanes = slice(GROUP * k, GROUP * (k + 1))
        vec_grad[0:1, lanes] = jnp.where(group == k, sum_q, 0.0)
        vec_grad[1:2, lanes] = jnp.where(group == k, sum_v, 0.0)
    links.recv(m.tok_back, t_sem + 1)
    for part in range(MB):
        m.tok_send[part] = (m.tok_part[part, 1 - x, c] + m.tok_back[part, 1 - x]).astype(BF16)
    links.send(m.tok_send, m.tok_last, t_sem + 2, t_sem + 3, here.dx)
    links.drain(m.tok_send, t_sem + 2)

    planes(s_q)
    s_kv.z_second()
    vec_send, vec_recv = m.vec_send, m.vec_recv
    spread = jnp.where(owner_24(32), vec_grad[...][None], 0.0).reshape(256, DM)
    vec_send[...] = exact_nt(spread, select_24()).reshape(32, 8, 128)
    spread = jnp.where(owner_96(), m.up_grad[...], 0.0)
    own_lines = pl.ds(16 * c, 16)
    vec_send[own_lines, 0, :] = vec_send[own_lines, 0, :] + exact_nt(spread, select_96())

    def grad_start(d, carry):
        other = lax.rem(line + d, 32)
        links.make(vec_send.at[other], vec_recv.at[line], vec_sem + 2, vec_sem + 3, peer(d)).start()
        return carry

    lax.fori_loop(1, 32, grad_start, 0)
    vec_recv[line] = vec_send[line]

    s_q.z_second()
    s_kv.z_last()
    s_down.z_last()
    s_out.z_last()
    s_up.z_last()
    s_q.z_last()
    links.recv(m.tok_last, t_sem + 3)
    for part in range(MB):
        rows = slice(TOK * part, TOK * (part + 1))
        own = m.tok_part[part, x, c] + m.tok_back[part, x]
        m.b_tok[part] = m.gh1[rows, :] + (own + m.tok_last[part].astype(F32))
    links.put(m.b_tok, o_tok)
    many_send, many_recv = vec_send.at[pl.ds(0, 31)], vec_recv.at[pl.ds(0, 31)]
    links.sent(many_send, vec_sem + 2)
    links.recv(many_recv, vec_sem + 3)
    m.b_vec[...] = jnp.sum(vec_recv[...], axis=0)
    links.put(m.b_vec, o_vec)
    s_down.finish(m.b_down)
    links.put(m.b_down, o_down)
    s_out.finish(m.b_wout)
    links.put(m.b_wout, o_wout)
    s_up.finish(m.b_up)
    links.put(m.b_up, o_up)
    s_kv.finish(m.b_qkv)
    s_q.finish(m.b_qkv)
    links.put(m.b_qkv, o_qkv)
    links.finish()


def place_kernel(*refs):
    ins, big_out, vec_out = refs[0:7], refs[7:13], refs[13:22]
    held, rows, sems = refs[22:29], refs[29:38], refs[38]
    loads = [pltpu.make_async_copy(src, dst, sems.at[i]) for i, (src, dst) in enumerate(zip(ins, held))]
    for load in reversed(loads):
        load.start()
    stores = [pltpu.make_async_copy(src, dst, sems.at[7 + i]) for i, (src, dst) in enumerate(zip(held, big_out))]
    stores += [pltpu.make_async_copy(src, dst, sems.at[13 + i]) for i, (src, dst) in enumerate(zip(rows, vec_out))]
    loads[6].wait()
    for j in range(8):
        rows[j][...] = held[6][j, 0:24]
    rows[8][...] = held[6][0, 32:128]
    for store in stores[6:]:
        store.start()
    for load, store in zip(loads, stores[:6]):
        load.wait()
        store.start()
    for store in stores:
        store.wait()


def fused(
    tokens, starts, w_qkv, bias_q, bias_v, w_out, bias_out, gain_one, shift_one,
    w_up, bias_up, w_down, bias_down, gain_two, shift_two, cotangent,
):
    anywhere = pl.BlockSpec(memory_space=pl.ANY)
    vectors = (bias_q, bias_v, bias_out, gain_one, shift_one, bias_down, gain_two, shift_two, bias_up)
    big = [tokens.shape, tokens.shape, w_qkv.shape, w_out.shape, w_up.shape, w_down.shape]
    big = [jax.ShapeDtypeStruct(shape, F32) for shape in big]
    small = [jax.ShapeDtypeStruct(vector.shape, F32) for vector in vectors]
    made = pl.pallas_call(
        layer_kernel,
        name="layer",
        out_shape=big + [jax.ShapeDtypeStruct((8, 128), F32)],
        in_specs=[anywhere, pl.BlockSpec(memory_space=pltpu.SMEM)] + [anywhere] * 14,
        out_specs=[anywhere] * 7,
        scratch_shapes=all_scratch(),
        compiler_params=pltpu.CompilerParams(
            collective_id=0, has_side_effects=True, vmem_limit_bytes=63 * 2**20
        ),
    )(tokens, starts, w_qkv, w_out, w_up, w_down, *vectors, cotangent)
    placed = pl.pallas_call(
        place_kernel,
        name="place",
        out_shape=big + small,
        in_specs=[anywhere] * 7,
        out_specs=[anywhere] * 15,
        scratch_shapes=[pltpu.VMEM(array.shape, F32) for array in (*made, *vectors)]
        + [pltpu.SemaphoreType.DMA((22,))],
    )(*made)
    out, tok, g_qkv, g_wout, g_up, g_down, bq, bv, bo, g1, s1, bd, g2, s2, bup = placed
    return (out, tok, g_qkv, bq, bv, g_wout, bo, g1, s1, g_up, bup, g_down, bd, g2, s2)


def solution(mesh):
    small = dict(mesh.shape) == {BLK: 8, HEAD: 4}
    return jax.shard_map(
        fused if small else per_device,
        mesh=mesh,
        in_specs=(
            P(None, BOTH, None),
            P(),
            P(BOTH, None),
            P(BOTH),
            P(BOTH),
            P(BOTH, None),
            P(BOTH),
            P(BOTH),
            P(BOTH),
            P(BOTH, None),
            P(BOTH),
            P(BOTH, None),
            P(BOTH),
            P(BOTH),
            P(BOTH),
            P(None, BOTH, None),
        ),
        out_specs=(
            P(None, BOTH, None),
            P(None, BOTH, None),
            P(BOTH, None),
            P(BOTH),
            P(BOTH),
            P(BOTH, None),
            P(BOTH),
            P(BOTH),
            P(BOTH),
            P(BOTH, None),
            P(BOTH),
            P(BOTH, None),
            P(BOTH),
            P(BOTH),
            P(BOTH),
        ),
        check_vma=False,
    )
```

```python
from functools import partial
from types import SimpleNamespace

import jax
import jax.numpy as jnp
from jax import lax
from jax.experimental import pallas as pl
from jax.experimental.pallas import tpu as pltpu
from jax.sharding import PartitionSpec as P

BLK = "blk"
HEAD = "head"
BOTH = (BLK, HEAD)
H = 12
HD = 64
MB = 2


EPS = 1e-05
NEG = -1e30


def norm_forward(values, gain_vec, shift_vec):
    center = values - jnp.mean(values, axis=-1, keepdims=True)
    inverse = lax.rsqrt(jnp.mean(center * center, axis=-1, keepdims=True) + EPS)
    normed = center * inverse
    return (normed * gain_vec + shift_vec, normed, inverse)


def norm_backward(upstream, normed, inverse, gain_vec):
    scaled = upstream * gain_vec
    inner = (
        scaled
        - jnp.mean(scaled, axis=-1, keepdims=True)
        - normed * jnp.mean(scaled * normed, axis=-1, keepdims=True)
    )
    return inner * inverse


def segment_of(starts_row, positions):
    return jnp.sum((starts_row[None, :] <= positions[:, None]).astype(jnp.int32), axis=1) - 1


def masked_scores(query_heads, key_heads, in_doc):
    scores = jnp.einsum(
        "qhd,khd->hqk", query_heads, key_heads, preferred_element_type=jnp.float32
    ) * HD ** (-0.5)
    return jnp.where(in_doc, scores, NEG)


def score_grads(query_heads, key_heads, value_heads, grad_numer, row_top, correction, in_doc):
    exp_score = jnp.where(
        in_doc, jnp.exp(masked_scores(query_heads, key_heads, in_doc) - row_top), 0.0
    )
    grad_weights = jnp.einsum(
        "qhd,khd->hqk", grad_numer, value_heads, preferred_element_type=jnp.float32
    )
    grad_scores = (exp_score * (grad_weights - correction)).astype(jnp.bfloat16)
    return (exp_score.astype(jnp.bfloat16), grad_scores)


def scatter_end(parts):
    (
        grad_proj_in,
        grad_query_bias,
        grad_value_bias,
        grad_proj_out,
        grad_out_bias,
        grad_norm_gain,
        grad_norm_shift,
        grad_up,
        grad_up_bias,
        grad_down,
        grad_down_bias,
        grad_final_gain,
        grad_final_shift,
    ) = parts
    return (
        lax.psum_scatter(grad_proj_in, BOTH, scatter_dimension=0, tiled=True),
        lax.psum_scatter(grad_query_bias, BOTH, scatter_dimension=0, tiled=True),
        lax.psum_scatter(grad_value_bias, BOTH, scatter_dimension=0, tiled=True),
        lax.psum_scatter(grad_proj_out, BOTH, scatter_dimension=0, tiled=True),
        lax.psum_scatter(grad_out_bias, BOTH, scatter_dimension=0, tiled=True),
        lax.psum_scatter(grad_norm_gain, BOTH, scatter_dimension=0, tiled=True),
        lax.psum_scatter(grad_norm_shift, BOTH, scatter_dimension=0, tiled=True),
        lax.psum_scatter(grad_up, BOTH, scatter_dimension=0, tiled=True),
        lax.psum_scatter(grad_up_bias, BOTH, scatter_dimension=0, tiled=True),
        lax.psum_scatter(grad_down, BOTH, scatter_dimension=0, tiled=True),
        lax.psum_scatter(grad_down_bias, BOTH, scatter_dimension=0, tiled=True),
        lax.psum_scatter(grad_final_gain, BOTH, scatter_dimension=0, tiled=True),
        lax.psum_scatter(grad_final_shift, BOTH, scatter_dimension=0, tiled=True),
    )


def per_device(
    tokens,
    starts,
    w_qkv,
    bias_q,
    bias_v,
    w_out,
    bias_out,
    gain_one,
    shift_one,
    w_up,
    bias_up,
    w_down,
    bias_down,
    gain_two,
    shift_two,
    cotangent,
):
    (
        proj_in,
        query_bias,
        value_bias,
        proj_out,
        out_bias,
        norm_gain,
        norm_shift,
        up_full,
        up_bias,
        down_full,
        down_bias,
        final_gain,
        final_shift,
    ) = (
        lax.all_gather(w_qkv, BOTH, axis=0, tiled=True),
        lax.all_gather(bias_q, BOTH, axis=0, tiled=True),
        lax.all_gather(bias_v, BOTH, axis=0, tiled=True),
        lax.all_gather(w_out, BOTH, axis=0, tiled=True),
        lax.all_gather(bias_out, BOTH, axis=0, tiled=True),
        lax.all_gather(gain_one, BOTH, axis=0, tiled=True),
        lax.all_gather(shift_one, BOTH, axis=0, tiled=True),
        lax.all_gather(w_up, BOTH, axis=0, tiled=True),
        lax.all_gather(bias_up, BOTH, axis=0, tiled=True),
        lax.all_gather(w_down, BOTH, axis=0, tiled=True),
        lax.all_gather(bias_down, BOTH, axis=0, tiled=True),
        lax.all_gather(gain_two, BOTH, axis=0, tiled=True),
        lax.all_gather(shift_two, BOTH, axis=0, tiled=True),
    )
    query_bias = query_bias.astype(jnp.float32)
    value_bias = value_bias.astype(jnp.float32)
    out_bias = out_bias.astype(jnp.float32)
    norm_gain = norm_gain.astype(jnp.float32)
    norm_shift = norm_shift.astype(jnp.float32)
    up_bias = up_bias.astype(jnp.float32)
    down_bias = down_bias.astype(jnp.float32)
    final_gain = final_gain.astype(jnp.float32)
    final_shift = final_shift.astype(jnp.float32)
    model_width = proj_out.shape[0]
    row_count = tokens.shape[1]
    head_count = lax.axis_size(HEAD)
    block_rows = row_count * head_count
    heads_dev = H // head_count
    local_width = heads_dev * HD
    scale = HD ** (-0.5)
    local_pos = lax.axis_index(BLK) * block_rows + jnp.arange(block_rows, dtype=jnp.int32)
    kept_list = []
    outputs = []
    for part_index in range(MB):
        inputs = tokens[part_index]
        starts_row = starts[part_index]
        projected = jnp.dot(inputs, proj_in, preferred_element_type=jnp.float32)
        query_rows = (projected[:, :model_width] + query_bias).astype(jnp.bfloat16)
        key_rows = projected[:, model_width : 2 * model_width].astype(jnp.bfloat16)
        value_rows = (projected[:, 2 * model_width :] + value_bias).astype(jnp.bfloat16)
        query_loc, key_loc, value_loc = (
            lax.all_to_all(query_rows, HEAD, split_axis=1, concat_axis=0, tiled=True),
            lax.all_to_all(key_rows, HEAD, split_axis=1, concat_axis=0, tiled=True),
            lax.all_to_all(value_rows, HEAD, split_axis=1, concat_axis=0, tiled=True),
        )
        doc_local = segment_of(starts_row, local_pos)
        query_heads = query_loc.reshape(block_rows, heads_dev, HD)

        def fold_keys(running, portion):
            row_top, row_total, weighted = running
            key_part, value_part = portion
            piece_len = key_part.shape[0]
            key_doc = segment_of(starts_row, jnp.arange(piece_len, dtype=jnp.int32))
            in_doc = (doc_local[:, None] == key_doc[None, :])[None]
            scores = masked_scores(query_heads, key_part.reshape(piece_len, heads_dev, HD), in_doc)
            new_top = jnp.maximum(row_top, jnp.max(scores, axis=-1, keepdims=True))
            exp_score = jnp.where(in_doc, jnp.exp(scores - new_top), 0.0)
            row_total = jnp.sum(exp_score, axis=-1, keepdims=True)
            weighted = jnp.einsum(
                "hqk,khd->hqd",
                exp_score.astype(jnp.bfloat16),
                value_part.reshape(piece_len, heads_dev, HD),
                preferred_element_type=jnp.float32,
            )
            return (new_top, row_total, weighted)

        start_state = (
            jnp.full((heads_dev, block_rows, 1), NEG, jnp.float32),
            jnp.zeros((heads_dev, block_rows, 1), jnp.float32),
            jnp.zeros((heads_dev, block_rows, HD), jnp.float32),
        )
        row_top, row_total, weighted = fold_keys(
            start_state,
            (
                lax.all_gather(key_loc, BLK, axis=0, tiled=True),
                lax.all_gather(value_loc, BLK, axis=0, tiled=True),
            ),
        )
        attended = jnp.transpose(weighted / row_total, (1, 0, 2))
        mixed_rows = lax.all_to_all(
            attended.reshape(block_rows, local_width).astype(jnp.bfloat16),
            HEAD,
            split_axis=0,
            concat_axis=1,
            tiled=True,
        )
        attn_out = jnp.dot(mixed_rows, proj_out, preferred_element_type=jnp.float32) + out_bias
        first_norm, normed_one, inverse_one = norm_forward(
            inputs.astype(jnp.float32) + attn_out, norm_gain, norm_shift
        )
        first_low = first_norm.astype(jnp.bfloat16)
        hidden = jnp.dot(first_low, up_full, preferred_element_type=jnp.float32) + up_bias
        active = jax.nn.gelu(hidden, approximate=False).astype(jnp.bfloat16)
        ffn_out = jnp.dot(active, down_full, preferred_element_type=jnp.float32) + down_bias
        result, normed_two, inverse_two = norm_forward(
            first_norm + ffn_out, final_gain, final_shift
        )
        outputs.append(result)
        kept_list.append(
            (
                inputs,
                starts_row,
                query_loc,
                key_loc,
                value_loc,
                doc_local,
                row_top,
                row_total,
                attended,
                mixed_rows,
                normed_one,
                inverse_one,
                first_low,
                hidden,
                active,
                normed_two,
                inverse_two,
            )
        )
    input_grads = []
    grad_sum = None
    for part_index in range(MB):
        (
            inputs,
            starts_row,
            query_loc,
            key_loc,
            value_loc,
            doc_local,
            row_top,
            row_total,
            attended,
            mixed_rows,
            normed_one,
            inverse_one,
            first_low,
            hidden,
            active,
            normed_two,
            inverse_two,
        ) = kept_list[part_index]
        grad_result = cotangent[part_index].astype(jnp.float32)
        grad_final_gain = jnp.sum(grad_result * normed_two, axis=0)
        grad_final_shift = jnp.sum(grad_result, axis=0)
        grad_two = norm_backward(grad_result, normed_two, inverse_two, final_gain)
        grad_ffn = grad_two.astype(jnp.bfloat16)
        grad_down_bias = jnp.sum(grad_ffn.astype(jnp.float32), axis=0)
        grad_down = jnp.einsum("rf,rd->fd", active, grad_ffn, preferred_element_type=jnp.float32)
        grad_active = jnp.einsum(
            "rd,fd->rf", grad_ffn, down_full, preferred_element_type=jnp.float32
        )
        gelu_pull = jax.vjp(partial(jax.nn.gelu, approximate=False), hidden)[1]
        grad_hidden = gelu_pull(grad_active)[0].astype(jnp.bfloat16)
        grad_up_bias = jnp.sum(grad_hidden.astype(jnp.float32), axis=0)
        grad_up = jnp.einsum(
            "rd,rf->df", first_low, grad_hidden, preferred_element_type=jnp.float32
        )
        grad_first = grad_two + jnp.einsum(
            "rf,df->rd", grad_hidden, up_full, preferred_element_type=jnp.float32
        )
        grad_norm_gain = jnp.sum(grad_first * normed_one, axis=0)
        grad_norm_shift = jnp.sum(grad_first, axis=0)
        grad_one = norm_backward(grad_first, normed_one, inverse_one, norm_gain)
        grad_attn = grad_one.astype(jnp.bfloat16)
        grad_out_bias = jnp.sum(grad_attn.astype(jnp.float32), axis=0)
        grad_proj_out = jnp.einsum(
            "rc,rd->cd", mixed_rows, grad_attn, preferred_element_type=jnp.float32
        )
        grad_mixed = jnp.einsum(
            "rd,cd->rc", grad_attn, proj_out, preferred_element_type=jnp.float32
        ).astype(jnp.bfloat16)
        grad_loc = lax.all_to_all(grad_mixed, HEAD, split_axis=1, concat_axis=0, tiled=True)
        grad_heads = grad_loc.astype(jnp.float32).reshape(block_rows, heads_dev, HD)
        total_rows = jnp.transpose(row_total, (1, 0, 2))
        correction = jnp.transpose(
            jnp.sum(grad_heads * attended, axis=-1, keepdims=True) / total_rows, (1, 0, 2)
        )
        grad_numer = (grad_heads / total_rows).astype(jnp.bfloat16)
        query_heads = query_loc.reshape(block_rows, heads_dev, HD)
        key_heads_loc = key_loc.reshape(block_rows, heads_dev, HD)
        value_heads_loc = value_loc.reshape(block_rows, heads_dev, HD)
        fold_key_part = lax.all_gather(key_loc, BLK, axis=0, tiled=True)
        fold_value_part = lax.all_gather(value_loc, BLK, axis=0, tiled=True)
        fold_piece_len = fold_key_part.shape[0]
        fold_key_doc = segment_of(starts_row, jnp.arange(fold_piece_len, dtype=jnp.int32))
        fold_in_doc = (doc_local[:, None] == fold_key_doc[None, :])[None]
        key_heads = fold_key_part.reshape(fold_piece_len, heads_dev, HD)
        exp_low, grad_scores = score_grads(
            query_heads,
            key_heads,
            fold_value_part.reshape(fold_piece_len, heads_dev, HD),
            grad_numer,
            row_top,
            correction,
            fold_in_doc,
        )
        grad_query = (
            jnp.einsum("hqk,khd->qhd", grad_scores, key_heads, preferred_element_type=jnp.float32)
            * scale
        )
        top_rows = jnp.transpose(row_top[:, :, 0])
        corr_rows = jnp.transpose(correction[:, :, 0])

        def fold_keygrad(portion):
            query_part, numer_part, top_part, corr_part = portion
            piece_len = query_part.shape[0]
            query_doc = segment_of(starts_row, jnp.arange(piece_len, dtype=jnp.int32))
            in_doc = (query_doc[:, None] == doc_local[None, :])[None]
            query_piece = query_part.reshape(piece_len, heads_dev, HD)
            numer_piece = numer_part.reshape(piece_len, heads_dev, HD)
            exp_low, grad_scores = score_grads(
                query_piece,
                key_heads_loc,
                value_heads_loc,
                numer_piece,
                jnp.transpose(top_part)[:, :, None],
                jnp.transpose(corr_part)[:, :, None],
                in_doc,
            )
            grad_key_run = (
                jnp.einsum(
                    "hqk,qhd->khd", grad_scores, query_piece, preferred_element_type=jnp.float32
                )
                * scale
            )
            grad_value_run = jnp.einsum(
                "hqk,qhd->khd", exp_low, numer_piece, preferred_element_type=jnp.float32
            )
            return (grad_key_run, grad_value_run)

        grad_key, grad_value = fold_keygrad(
            (
                lax.all_gather(query_loc, BLK, axis=0, tiled=True),
                lax.all_gather(
                    grad_numer.reshape(block_rows, local_width), BLK, axis=0, tiled=True
                ),
                lax.all_gather(top_rows.astype(jnp.bfloat16), BLK, axis=0, tiled=True).astype(
                    jnp.float32
                ),
                lax.all_gather(corr_rows.astype(jnp.bfloat16), BLK, axis=0, tiled=True).astype(
                    jnp.float32
                ),
            )
        )
        grad_q_rows, grad_k_rows, grad_v_rows = (
            lax.all_to_all(
                grad_query.reshape(block_rows, local_width).astype(jnp.bfloat16),
                HEAD,
                split_axis=0,
                concat_axis=1,
                tiled=True,
            ),
            lax.all_to_all(
                grad_key.reshape(block_rows, local_width).astype(jnp.bfloat16),
                HEAD,
                split_axis=0,
                concat_axis=1,
                tiled=True,
            ),
            lax.all_to_all(
                grad_value.reshape(block_rows, local_width).astype(jnp.bfloat16),
                HEAD,
                split_axis=0,
                concat_axis=1,
                tiled=True,
            ),
        )
        grad_proj = jnp.concatenate([grad_q_rows, grad_k_rows, grad_v_rows], axis=1)
        grad_query_bias = jnp.sum(grad_q_rows.astype(jnp.float32), axis=0)
        grad_value_bias = jnp.sum(grad_v_rows.astype(jnp.float32), axis=0)
        grad_proj_in = jnp.einsum(
            "rd,re->de", inputs, grad_proj, preferred_element_type=jnp.float32
        )
        input_grads.append(
            grad_one
            + jnp.einsum("re,de->rd", grad_proj, proj_in, preferred_element_type=jnp.float32)
        )
        part_grads = (
            grad_proj_in,
            grad_query_bias,
            grad_value_bias,
            grad_proj_out,
            grad_out_bias,
            grad_norm_gain,
            grad_norm_shift,
            grad_up,
            grad_up_bias,
            grad_down,
            grad_down_bias,
            grad_final_gain,
            grad_final_shift,
        )
        grad_sum = (
            part_grads
            if grad_sum is None
            else tuple((left + right for left, right in zip(grad_sum, part_grads)))
        )
    grad_sum = scatter_end(grad_sum)
    (
        grad_proj_in,
        grad_query_bias,
        grad_value_bias,
        grad_proj_out,
        grad_out_bias,
        grad_norm_gain,
        grad_norm_shift,
        grad_up,
        grad_up_bias,
        grad_down,
        grad_down_bias,
        grad_final_gain,
        grad_final_shift,
    ) = grad_sum
    return (
        jnp.stack(outputs),
        jnp.stack(input_grads),
        grad_proj_in,
        grad_query_bias,
        grad_value_bias,
        grad_proj_out,
        grad_out_bias,
        grad_norm_gain,
        grad_norm_shift,
        grad_up,
        grad_up_bias,
        grad_down,
        grad_down_bias,
        grad_final_gain,
        grad_final_shift,
    )


MESH = pl.DeviceIdType.MESH
F32 = jnp.float32
BF16 = jnp.bfloat16
DM = 768
FF = 3072
TOK = 64
SEQ = 2048
HALF = DM // 2
GROUP = 3 * HD
UP_N = FF // 2
CHUNK = 256
PAIRS = 6

QKV, OUT, UP, DOWN, KV, Q = range(6)
SHAPES = (
    (2, 2, 2, 4, 24, 3 * GROUP),
    (4, 4, 24, DM),
    (4, 2, 4, 24, UP_N),
    (4, 4, 96, DM),
    (2, 2, 2, 4, 24, 2 * GROUP),
    (2, 2, 2, 4, 24, GROUP),
)


def by_column(kind):
    return kind == UP


def piece_shape(kind):
    shape = SHAPES[kind]
    if kind in (QKV, KV, Q):
        return shape[1:3] + shape[4:]
    return (2,) + shape[3:] if by_column(kind) else shape[2:]


def when(cond, run):
    if cond is None:
        run()
    else:
        pl.when(cond)(run)


def both(left, right):
    return jnp.logical_and(left, right)


class Place:
    def __init__(self):
        b = lax.axis_index(BLK)
        z = lax.axis_index(HEAD)
        c = lax.rem(b, 2)
        x = lax.rem(lax.div(b, 2), 2)
        y = lax.div(b, 4)
        self.b, self.z, self.c, self.x, self.y = b, z, c, x, y
        self.line = 4 * b + z
        self.sib = (b + 1 - 2 * c, z)
        self.dx = (4 * y + 2 * (1 - x) + c, z)
        self.dy = (4 * (1 - y) + 2 * x + c, z)
        self.dx_other = (4 * y + 2 * (1 - x) + 1 - c, z)
        self.near = z + 1 - 2 * lax.rem(z, 2)
        self.far = lax.rem(z + 2, 4)
        self.cross = 3 - z
        self.swap = (4 * c + 2 * x + y, z)
        self.stays = y == c
        self.moves = y != c
        self.group = 2 * c + x
        self.seat = 4 * y + z
        self.chip = 2 * self.seat + x
        idle = jnp.logical_or(both(z == 0, y == 1), both(z == 3, y == 0))
        self.active = jnp.logical_not(idle)
        inner = jnp.where(z == 1, 4 * y, 1 + 4 * y)
        outer = jnp.where(z == 0, 2, 3)
        self.pair = jnp.where(jnp.logical_or(z == 1, z == 2), inner, outer)
        self.part = lax.div(self.pair, 3)

    def cols(self, kind):
        x, y = self.x, self.y
        if by_column(kind):
            return (2 * y + x, 2 * y + 1 - x, 2 * (1 - y) + x, 2 * (1 - y) + 1 - x)
        return (2 * x + y, 2 * (1 - x) + y, 2 * x + 1 - y, 2 * (1 - x) + 1 - y)


SEATS = ((0, 1), (0, 2), (0, 0), (1, 3), (1, 1), (1, 2))


def chunk(kind, ref, col, z):
    return ref.at[col, :, z] if by_column(kind) else ref.at[col, z]


class Links:
    def __init__(self, sems, here):
        self.sems, self.here, self.count = sems, here, 0
        self.waits = []

    def alloc(self, n=1):
        at = self.count
        self.count += n
        return at

    def make(self, src, dst, s, r, dev):
        return pltpu.make_async_remote_copy(
            src_ref=src, dst_ref=dst, send_sem=self.sems.at[s], recv_sem=self.sems.at[r],
            device_id=dev, device_id_type=MESH,
        )

    def send(self, src, dst, s, r, dev, cond=None):
        when(cond, lambda: self.make(src, dst, s, r, dev).start())

    def recv(self, dst, r, cond=None):
        when(cond, lambda: self.make(dst, dst, r, r, self.here.sib).wait_recv())

    def sent(self, src, s, cond=None):
        when(cond, lambda: self.make(src, src, s, s, self.here.sib).wait_send())

    def drain(self, like, s, cond=None):
        self.waits.append(lambda: self.sent(like, s, cond))

    def local(self, src, dst, cond=None):
        sem = self.sems.at[self.alloc()]
        when(cond, lambda: pltpu.make_async_copy(src, dst, sem).start())
        return lambda: when(cond, lambda: pltpu.make_async_copy(src, dst, sem).wait())

    def put(self, src, dst):
        self.waits.append(self.local(src, dst))

    def finish(self):
        for wait in self.waits:
            wait()


class Gather:
    def __init__(self, links, here, kind, ref):
        self.links, self.here, self.kind, self.ref = links, here, kind, ref
        self.s0, self.r0 = links.alloc(), links.alloc()
        self.sz, self.rz = links.alloc(), links.alloc(4)
        self.s_plane, self.s_relay = links.alloc(), links.alloc()
        self.r_relay, self.r_rest = links.alloc(4), links.alloc()
        self.col, self.col_x, self.col_y, self.col_d = here.cols(kind)
        links.drain(ref.at[0, :, pl.ds(0, 3)] if by_column(kind) else ref.at[0, pl.ds(0, 3)], self.sz)
        links.drain(ref.at[pl.ds(0, 2)], self.s_plane)
        links.drain(ref.at[0], self.s_relay)

    def first_wait(self):
        here = self.here
        if by_column(self.kind):
            self.links.recv(self.ref.at[self.col, 1 - here.c, here.z], self.r0)
        else:
            self.links.recv(self.ref.at[self.col, here.z], self.r0, here.moves)

    def piece(self, col, z):
        return chunk(self.kind, self.ref, col, z)

    def z_hop(self, z, to):
        piece = self.piece(self.col, z)
        self.links.send(piece, piece, self.sz, self.rz + z, (self.here.b, to))

    def spread(self, z):
        piece = self.piece(self.col, z)
        on_y = z < 1
        to_x = jnp.where(on_y, self.r_relay + z, self.r_rest)
        to_y = jnp.where(on_y, self.r_rest, self.r_relay + z)
        self.links.send(piece, piece, self.s_plane, to_x, self.here.dx)
        self.links.send(piece, piece, self.s_plane, to_y, self.here.dy)

    def own_z(self):
        here = self.here
        self.z_hop(here.z, here.far)
        self.z_hop(here.z, here.near)

    def own_plane(self):
        self.spread(self.here.z)

    def land(self, z):
        self.links.recv(self.piece(self.col, z), self.rz + z)

    def hop(self):
        self.z_hop(self.here.far, self.here.near)

    def relay(self, z):
        here = self.here
        on_y = z < 1
        piece = self.piece(jnp.where(on_y, self.col_x, self.col_y), z)
        self.links.recv(piece, self.r_relay + z)
        dev = (jnp.where(on_y, here.dy[0], here.dx[0]), here.z)
        self.links.send(piece, piece, self.s_relay, self.r_rest, dev)

    def done(self):
        self.links.recv(self.ref.at[pl.ds(0, 2)], self.r_rest)


class PairGather:
    def __init__(self, links, here, ref):
        self.links, self.here, self.ref = links, here, ref
        self.s0, self.r0 = links.alloc(), links.alloc()
        self.sz, self.rz = links.alloc(), links.alloc(4)
        self.sy, self.ry = links.alloc(), links.alloc()
        links.drain(ref.at[0, 0, 0, pl.ds(0, 3)], self.s0)
        links.drain(ref.at[0, :, :, pl.ds(0, 3)], self.sz)
        links.drain(ref.at[0], self.sy)

    def first_wait(self):
        self.links.recv(self.ref.at[0, 0, 0, pl.ds(0, 3)], self.r0)

    def piece(self, z):
        return self.ref.at[self.here.y, :, :, z]

    def z_hop(self, z, to):
        self.links.send(self.piece(z), self.piece(z), self.sz, self.rz + z, (self.here.b, to))

    def own_z(self):
        here = self.here
        self.z_hop(here.z, here.far)
        self.z_hop(here.z, here.near)

    def land(self, z):
        self.links.recv(self.piece(z), self.rz + z)

    def hop(self):
        self.z_hop(self.here.far, self.here.near)

    def spread(self, z):
        self.links.send(self.piece(z), self.piece(z), self.sy, self.ry, self.here.dy)

    def done(self):
        self.links.recv(self.ref.at[0], self.ry)


def add_blocks(dst, terms, blocks):
    for at in blocks:
        total = terms[0][at].astype(F32)
        for term in terms[1:]:
            total = total + term[at].astype(F32)
        dst[at] = total.astype(dst.dtype)


class Scatter:
    def __init__(self, links, here, kind, refs):
        self.links, self.here, self.kind = links, here, kind
        self.tilt = 2
        self.grad, self.far, self.cxy, self.zb, self.zr, self.fin, self.last = refs
        self.s_first, self.s_relay, self.sz = links.alloc(), links.alloc(), links.alloc()
        self.r_far, self.r_plane, self.rz = links.alloc(4), links.alloc(4), links.alloc(3)
        self.s_end, self.r_end = links.alloc(), links.alloc()
        self.col, self.col_x, self.col_y, self.col_d = here.cols(kind)
        links.drain(self.cxy, self.s_first)
        links.drain(self.far, self.s_relay)
        links.drain(self.zr.at[pl.ds(0, 3)], self.sz)
        if by_column(kind):
            links.drain(self.last, self.s_end)
        else:
            links.drain(self.last, self.s_end, here.moves)

    def piece(self, col, z):
        return chunk(self.kind, self.grad, col, z)

    def add(self, dst, terms):
        add_blocks(dst, terms, [(h,) for h in range(2)] if by_column(self.kind) else [(slice(0, None),)])

    def side(self, z, to_x, sem):
        here = self.here
        col = jnp.where(to_x, self.col_x, self.col_y)
        dev = (jnp.where(to_x, here.dx[0], here.dy[0]), here.z)
        slot = jnp.where(to_x, z, 4 + z)
        self.links.send(self.piece(col, z), self.cxy.at[slot], sem, self.r_plane + z, dev)

    def send_far(self, order):
        here = self.here
        for z in order:
            to_x = z >= self.tilt
            dev = (jnp.where(to_x, here.dx[0], here.dy[0]), here.z)
            self.links.send(self.piece(self.col_d, z), self.far.at[z], self.s_first, self.r_far + z, dev)

    def send_sides(self, order):
        for z in order:
            self.side(z, z >= self.tilt, self.s_first)

    def relay(self, z):
        to_y = z >= self.tilt
        self.links.recv(self.far.at[z], self.r_far + z)
        piece = self.piece(jnp.where(to_y, self.col_y, self.col_x), z)
        self.add(piece, (piece, self.far.at[z]))
        self.side(z, jnp.logical_not(to_y), self.s_relay)

    def plane(self, z):
        self.links.recv(self.cxy.at[pl.ds(0, 2)], self.r_plane + z)
        self.add(self.zb.at[z], (self.piece(self.col, z), self.cxy.at[z], self.cxy.at[4 + z]))

    def z_first(self, i):
        here = self.here
        z = here.cross if i else here.near
        self.links.send(self.zb.at[z], self.zr.at[i], self.sz, self.rz + i, (here.b, here.near))

    def z_second(self):
        here = self.here
        self.links.recv(self.zr.at[1], self.rz + 1)
        piece = self.zb.at[here.far]
        self.add(piece, (piece, self.zr.at[1]))
        self.links.send(piece, self.zr.at[2], self.sz, self.rz + 2, (here.b, here.far))

    def z_last(self):
        links, here = self.links, self.here
        links.recv(self.zr.at[0], self.rz)
        links.recv(self.zr.at[2], self.rz + 2)
        self.add(self.fin, [self.zb.at[here.z], self.zr.at[0], self.zr.at[2]])
        if by_column(self.kind):
            links.send(self.fin.at[1 - here.c], self.last, self.s_end, self.r_end, here.sib)
        else:
            links.send(self.fin, self.last, self.s_end, self.r_end, here.swap, here.moves)

    def finish(self, out):
        links, here, kind = self.links, self.here, self.kind
        c = here.c
        if by_column(kind):
            out[:, pl.ds(pl.multiple_of(UP_N * c, 128), UP_N)] = self.fin[c]
            links.recv(self.last, self.r_end)
            out[:, pl.ds(pl.multiple_of(UP_N * (1 - c), 128), UP_N)] = self.last[...]
        else:
            links.recv(self.last, self.r_end, here.moves)

            def keep():
                out[...] = self.fin[...]

            def take():
                out[...] = self.last[...]

            when(here.stays, keep)
            when(here.moves, take)


class ColumnScatter(Scatter):
    def __init__(self, links, here, kind, refs):
        self.links, self.here, self.kind = links, here, kind
        self.grad, self.far, self.cxy, self.zb, self.zr, self.fin, self.last = refs
        self.s_first, self.s_relay, self.sz = links.alloc(), links.alloc(), links.alloc()
        self.r_far, self.r_plane, self.rz = links.alloc(4), links.alloc(4), links.alloc(3)
        self.s_far, self.s_column = links.alloc(), links.alloc()
        self.s_end, self.r_end = links.alloc(), links.alloc()
        self.col, self.col_x, self.col_y, self.col_d = here.cols(kind)
        links.drain(self.cxy.at[pl.ds(0, 7)], self.s_first)
        links.drain(self.far.at[0], self.s_relay)
        links.drain(self.far.at[0], self.s_far)
        links.drain(self.far.at[pl.ds(0, 3)], self.s_column)
        links.drain(self.zr.at[pl.ds(0, 3)], self.sz)
        links.drain(self.last, self.s_end, None if by_column(kind) else here.moves)

    def to_side(self, z, to_x, sem):
        here = self.here
        col, slot, dev = (self.col_x, z, here.dx) if to_x else (self.col_y, 4 + z, here.dy)
        self.links.send(self.piece(col, z), self.cxy.at[slot], sem, self.r_plane + z, dev)

    def send_sides(self, order):
        for z in order:
            self.to_side(z, True, self.s_first)
            if z is not self.here.z:
                self.to_side(z, False, self.s_first)

    def column_first(self):
        here = self.here
        for i, z in enumerate((here.near, here.cross)):
            self.links.send(self.piece(self.col_d, z), self.far.at[i], self.s_column, self.r_far + i, (here.b, here.near))

    def column_second(self):
        here = self.here
        self.links.recv(self.far.at[1], self.r_far + 1)
        piece = self.piece(self.col_d, here.far)
        self.add(piece, (piece, self.far.at[1]))
        self.links.send(piece, self.far.at[2], self.s_column, self.r_far + 2, (here.b, here.far))

    def column_last(self):
        here = self.here
        self.links.recv(self.far.at[0], self.r_far)
        self.links.recv(self.far.at[2], self.r_far + 2)
        piece = self.piece(self.col_d, here.z)
        self.add(piece, (piece, self.far.at[0], self.far.at[2]))
        self.links.send(piece, self.far.at[3], self.s_far, self.r_far + 3, here.dx)

    def relay_own(self):
        here = self.here
        self.links.recv(self.far.at[3], self.r_far + 3)
        piece = self.piece(self.col_y, here.z)
        self.add(piece, (piece, self.far.at[3]))
        self.to_side(here.z, False, self.s_relay)


class PairScatter:
    def __init__(self, links, here, kind, refs):
        self.links, self.here, self.kind = links, here, kind
        self.grad, self.cy, self.zb, self.zr, self.fin, self.last = refs
        self.sy, self.ry = links.alloc(), links.alloc(4)
        self.sz, self.rz = links.alloc(), links.alloc(3)
        self.s_end, self.r_end = links.alloc(), links.alloc()
        links.drain(self.cy, self.sy)
        links.drain(self.zr.at[pl.ds(0, 3)], self.sz)
        links.drain(self.last.at[pl.ds(0, 3)], self.s_end)

    def add(self, dst, terms):
        add_blocks(dst, terms, [(i, j) for i in range(2) for j in range(2)])

    def send(self, z):
        here = self.here
        self.links.send(self.grad.at[1 - here.y, :, :, z], self.cy.at[z], self.sy, self.ry + z, here.dy)

    def plane(self, z):
        self.links.recv(self.cy.at[z], self.ry + z)
        self.add(self.zb.at[z], (self.grad.at[self.here.y, :, :, z], self.cy.at[z]))

    def z_first(self, i):
        here = self.here
        z = here.cross if i else here.near
        self.links.send(self.zb.at[z], self.zr.at[i], self.sz, self.rz + i, (here.b, here.near))

    def z_second(self):
        here = self.here
        self.links.recv(self.zr.at[1], self.rz + 1)
        piece = self.zb.at[here.far]
        self.add(piece, (piece, self.zr.at[1]))
        self.links.send(piece, self.zr.at[2], self.sz, self.rz + 2, (here.b, here.far))

    def z_last(self):
        links, here = self.links, self.here
        links.recv(self.zr.at[0], self.rz)
        links.recv(self.zr.at[2], self.rz + 2)
        self.add(self.fin, [self.zb.at[here.z], self.zr.at[0], self.zr.at[2]])
        x, c = here.x, here.c
        slot = self.last.at[here.group]
        links.send(self.fin.at[1 - x, c], slot, self.s_end, self.r_end, here.dx)
        links.send(self.fin.at[1 - x, 1 - c], slot, self.s_end, self.r_end, here.dx_other)
        links.send(self.fin.at[x, 1 - c], slot, self.s_end, self.r_end, here.sib)

    def finish(self, out):
        self.last[self.here.group] = self.fin[self.here.x, self.here.c]
        self.links.recv(self.last.at[pl.ds(0, 3)], self.r_end)
        for group in range(4):
            if self.kind == Q:
                out[:, GROUP * group : GROUP * (group + 1)] = self.last[group]
            else:
                for i in range(2):
                    at = DM * (i + 1) + GROUP * group
                    out[:, at : at + GROUP] = self.last[group, :, GROUP * i : GROUP * (i + 1)]


def dot(a, b):
    return jnp.dot(a, b, preferred_element_type=F32)


def dot_nt(a, b):
    return lax.dot_general(a, b, (((1,), (1,)), ((), ())), preferred_element_type=F32)


def dot_tn(a, b):
    return lax.dot_general(a, b, (((0,), (0,)), ((), ())), preferred_element_type=F32)


def row_sum(values):
    return jnp.sum(values, axis=0, keepdims=True)


def div24(n):
    return lax.shift_right_logical(n * 2731, 16)


def iota(shape, dim):
    return lax.broadcasted_iota(jnp.int32, shape, dim)


def select_24():
    n = iota((128, DM), 1)
    return (iota((128, DM), 0) == n - 24 * div24(n)).astype(BF16)


def select_96():
    n = iota((128, UP_N), 1)
    run = lax.shift_right_logical(div24(n), 2)
    return (iota((128, UP_N), 0) == 32 + n - 96 * run).astype(BF16)


def owner_24(lead):
    shape = (lead, 8, DM)
    return div24(iota(shape, 2)) == iota(shape, 0)


def owner_96():
    shape = (16, UP_N)
    return lax.shift_right_logical(div24(iota(shape, 1)), 2) == iota(shape, 0)


def exact_nt(values, select):
    high = values.astype(BF16)
    rest = values - high.astype(F32)
    mid = rest.astype(BF16)
    low = (rest - mid.astype(F32)).astype(BF16)
    return dot_nt(high, select) + dot_nt(mid, select) + dot_nt(low, select)


SCRATCH = dict(
    w_rows=((24, 3 * DM), BF16),
    w_parts=((4, 24, 3 * GROUP), BF16),
    vecs=((8, 128), F32),
    cot=((2, TOK, DM), BF16),
    b_out=((2, TOK, DM), F32),
    b_tok=((2, TOK, DM), F32),
    b_qkv=((24, 3 * DM), F32),
    b_wout=((24, DM), F32),
    b_up=((24, FF), F32),
    b_down=((96, DM), F32),
    b_vec=((8, 128), F32),
    vec_all=((32, 8, 128), F32),
    vec_rows=((8, DM), F32),
    up_row=((1, UP_N), F32),
    x_pair=((2, 2, 2, TOK, DM), BF16),
    fl_chip=((2, 2, TOK, DM), BF16),
    gf_chip=((2, 2, TOK, DM), BF16),
    ga_chip=((2, 2, TOK, DM), BF16),
    partial=((2, 2, TOK, DM), F32),
    partial_low=((2, TOK, DM), BF16),
    back0=((2, TOK, DM), BF16),
    back1=((2, TOK, DM), BF16),
    back2=((2, TOK, DM), BF16),
    tok_part=((2, 2, 2, TOK, DM), F32),
    tok_back=((2, 2, TOK, DM), F32),
    tok_send=((2, TOK, DM), BF16),
    tok_last=((2, TOK, DM), BF16),
    send_q=((PAIRS, GROUP, 256), BF16),
    qkv_t=((GROUP, SEQ), BF16),
    k_rows=((SEQ, HD), BF16),
    v_rows=((SEQ, HD), BF16),
    q_rows=((SEQ, HD), BF16),
    g_rows=((SEQ, HD), BF16),
    key_doc=((SEQ, 128), jnp.int32),
    query_doc=((1, SEQ), jnp.int32),
    scores=((SEQ, CHUNK), F32),
    weights=((SEQ, SEQ), BF16),
    total=((1, SEQ), F32),
    att_t=((HD, SEQ), F32),
    att_send=((HD, SEQ), BF16),
    mix_in=((12, HD, 128), BF16),
    g_send=((12, HD, 128), BF16),
    g_t=((HD, SEQ), BF16),
    gn_t=((HD, SEQ), BF16),
    corr=((1, SEQ), F32),
    ds=((CHUNK, SEQ), BF16),
    dq_t=((HD, SEQ), F32),
    d_send=((GROUP, SEQ), BF16),
    d_in=((PAIRS, GROUP, 256), BF16),
    mixed_t=((HALF, 2 * 128), BF16),
    first=((2 * TOK, DM), F32),
    normed1=((2 * TOK, DM), F32),
    inv1=((2 * TOK, 1), F32),
    active=((4 * TOK, UP_N), BF16),
    slope=((4 * TOK, UP_N), F32),
    gh=((4 * TOK, UP_N), BF16),
    gh2=((2 * TOK, DM), F32),
    gh1=((2 * TOK, DM), F32),
    gp_kv=((8 * TOK, 2 * GROUP), BF16),
    gp_q=((8 * TOK, GROUP), BF16),
    vec_grad=((8, DM), F32),
    up_grad=((1, UP_N), F32),
    vec_send=((32, 8, 128), F32),
    vec_recv=((32, 8, 128), F32),
)


def sum_scratch(kind):
    piece = piece_shape(kind)
    if kind in (KV, Q):
        low = [SHAPES[kind]] + [(4,) + piece] * 3
        last = (4,) + piece[2:]
    else:
        low = [SHAPES[kind], (4,) + piece, (8,) + piece, (4,) + piece, (4,) + piece]
        last = piece[1:] if by_column(kind) else piece
    return [(shape, BF16) for shape in low] + [(piece, F32), (last, F32)]


GATHERED = (QKV, OUT, UP, DOWN)
SUMMED = (OUT, UP, DOWN, KV, Q)
N_SEM = 181


def all_scratch():
    shapes = list(SCRATCH.values())
    shapes += [(SHAPES[kind], BF16) for kind in GATHERED]
    for kind in SUMMED:
        shapes += sum_scratch(kind)
    shapes += [((24,), BF16)] * 8 + [((96,), BF16)]
    return [pltpu.VMEM(shape, dtype) for shape, dtype in shapes] + [pltpu.SemaphoreType.DMA((N_SEM,))]


def layer_kernel(
    tokens, starts, w_qkv, w_out, w_up, w_down,
    v0, v1, v2, v3, v4, v5, v6, v7, v8, cotangent,
    o_out, o_tok, o_qkv, o_wout, o_up, o_down, o_vec,
    *scratch,
):
    vec_in = (v0, v1, v2, v3, v4, v5, v6, v7, v8)
    m = SimpleNamespace(**dict(zip(SCRATCH, scratch)))
    at = len(SCRATCH)
    gathered = scratch[at : at + 4]
    at += 4
    summed = []
    for kind in SUMMED:
        n = len(sum_scratch(kind))
        summed.append(scratch[at : at + n])
        at += n
    vec_rows_in = scratch[at : at + 9]
    sems = scratch[-1]
    here = Place()
    links = Links(sems, here)
    b, z, c, x = here.b, here.z, here.c, here.x
    line, chip, group = here.line, here.chip, here.group
    g_qkv = PairGather(links, here, gathered[0])
    g_out, g_up, g_down = [Gather(links, here, kind, ref) for kind, ref in zip(GATHERED[1:], gathered[1:])]
    s_out, s_up, s_down = [
        make(links, here, kind, refs)
        for make, kind, refs in zip((Scatter, Scatter, ColumnScatter), SUMMED[:3], summed[:3])
    ]
    s_kv, s_q = [PairScatter(links, here, kind, refs) for kind, refs in zip(SUMMED[3:], summed[3:])]
    ahead = (g_out, g_up)

    def peer(d):
        other = lax.rem(line + d, 32)
        return (lax.div(other, 4), lax.rem(other, 4))

    x_pair = m.x_pair

    def up_part(which):
        return w_up.at[:, pl.ds(pl.multiple_of(UP_N * which, 128), UP_N)]

    qkv_wait = links.local(w_qkv, m.w_rows)
    vec_waits = [links.local(src, dst) for src, dst in zip(vec_in, vec_rows_in)]
    x_wait = links.local(tokens, x_pair.at[:, x, c])
    up_wait = links.local(up_part(c), g_up.ref.at[g_up.col, c, z])
    row_waits = [
        links.local(shard, gather.ref.at[gather.col, z], here.stays)
        for gather, shard in ((g_out, w_out), (g_down, w_down))
    ]
    cot_wait = links.local(cotangent, m.cot)
    m.vec_grad[...] = jnp.zeros((8, DM), F32)
    m.vecs[...] = jnp.zeros((8, 128), F32)
    for wait in vec_waits:
        wait()
    for j in range(8):
        m.vecs[j : j + 1, 0:24] = vec_rows_in[j][...].astype(F32).reshape(1, 24)
    m.vecs[0:1, 32:128] = vec_rows_in[8][...].astype(F32).reshape(1, 96)
    qkv_wait()
    for k in range(4):
        for j in range(3):
            block = m.w_rows[:, DM * j + GROUP * k : DM * j + GROUP * (k + 1)]
            m.w_parts[k, :, GROUP * j : GROUP * (j + 1)] = block

    barrier = pltpu.get_barrier_semaphore()

    def greet(d, carry):
        pl.semaphore_signal(barrier, inc=1, device_id=peer(d), device_id_type=MESH)
        return carry

    lax.fori_loop(1, 32, greet, 0)
    pl.semaphore_wait(barrier, 31)

    slot = g_qkv.ref.at[here.y, x, c, z]
    links.send(m.w_parts.at[2 * c + 1 - x], slot, g_qkv.s0, g_qkv.r0, here.dx)
    links.send(m.w_parts.at[2 * (1 - c) + 1 - x], slot, g_qkv.s0, g_qkv.r0, here.dx_other)
    links.send(m.w_parts.at[2 * (1 - c) + x], slot, g_qkv.s0, g_qkv.r0, here.sib)
    x_sem = links.alloc(6)
    own_x = x_pair.at[:, x, c]
    links.send(tokens, own_x, x_sem, x_sem + 1, here.dx)
    links.send(tokens, own_x, x_sem + 2, x_sem + 3, here.sib)
    links.drain(own_x, x_sem)
    links.drain(own_x, x_sem + 2)
    up_slot = g_up.ref.at[g_up.col, c, z]
    links.send(up_part(1 - c), up_slot, g_up.s0, g_up.r0, here.sib)
    links.drain(up_slot, g_up.s0)
    for gather, shard in ((g_out, w_out), (g_down, w_down)):
        slot = gather.ref.at[2 * x + c, z]
        links.send(shard, slot, gather.s0, gather.r0, here.swap, here.moves)
        links.drain(slot, gather.s0, here.moves)
    vec_sem = links.alloc(4)
    vec_all = m.vec_all

    def vec_copy(d):
        return links.make(m.vecs, vec_all.at[line], vec_sem, vec_sem + 1, peer(d))

    def vec_start(d, carry):
        vec_copy(d).start()
        return carry

    lax.fori_loop(1, 32, vec_start, 0)
    vec_all[line] = m.vecs[...]
    g_qkv.ref[here.y, x, c, z] = m.w_parts[group]
    for wait in (x_wait, up_wait, *row_waits, cot_wait):
        wait()

    g_qkv.first_wait()
    g_qkv.own_z()
    g_qkv.spread(z)
    for gather in ahead:
        gather.first_wait()
        gather.own_plane()

    def documents():
        def position(n):
            z_part = lax.shift_left(jnp.bitwise_and(lax.shift_right_logical(n, 8), 3), 6)
            xc_part = lax.shift_left(jnp.bitwise_and(lax.shift_right_logical(n, 6), 3), 8)
            y_part = lax.shift_left(lax.shift_right_logical(n, 10), 10)
            return y_part + xc_part + z_part + jnp.bitwise_and(n, 63)

        def doc_of(n):
            place = position(n)
            doc = jnp.zeros(place.shape, jnp.int32)
            for j in range(starts.shape[1]):
                doc = doc + (starts[here.part, j] <= place).astype(jnp.int32)
            return doc

        m.query_doc[...] = doc_of(iota((1, SEQ), 1))

        def rows(i, carry):
            start = pl.multiple_of(i * 256, 256)
            m.key_doc[pl.ds(start, 256), :] = doc_of(iota((256, 128), 0) + i * 256)
            return carry

        lax.fori_loop(0, SEQ // 256, rows, 0)

    when(here.active, documents)

    other_x = x_pair.at[:, 1 - x, c]
    links.recv(other_x, x_sem + 1)
    links.send(other_x, other_x, x_sem + 4, x_sem + 5, here.sib)
    links.drain(other_x, x_sem + 4)
    g_qkv.land(here.far)
    g_qkv.hop()
    g_qkv.spread(here.far)
    for gather in ahead:
        gather.own_z()
    many = vec_all.at[pl.ds(0, 31)]
    links.sent(many, vec_sem)
    links.recv(many, vec_sem + 1)
    spread = dot(vec_all[...].reshape(256, 128).astype(BF16), select_24()).reshape(32, 8, DM)
    m.vec_rows[...] = jnp.sum(jnp.where(owner_24(32), spread, 0.0), axis=0)
    spread = dot(vec_all[pl.ds(16 * c, 16), 0, :].astype(BF16), select_96())
    m.up_row[...] = row_sum(jnp.where(owner_96(), spread, 0.0))

    def vector(j):
        return m.vec_rows[j : j + 1, :]

    def vector_group(j):
        total = jnp.zeros((1, GROUP), F32)
        for k in range(4):
            total = total + jnp.where(group == k, m.vec_rows[j : j + 1, GROUP * k : GROUP * (k + 1)], 0.0)
        return total

    g_qkv.land(here.near)
    g_qkv.spread(here.near)
    for gather in ahead:
        gather.relay(z)
    g_qkv.land(here.cross)
    g_qkv.spread(here.cross)
    for gather in ahead:
        gather.land(here.far)
        gather.hop()
        gather.spread(here.far)
    links.recv(x_pair.at[:, x, 1 - c], x_sem + 3)
    links.recv(x_pair.at[:, 1 - x, 1 - c], x_sem + 5)
    g_qkv.done()

    def weight_qkv():
        return g_qkv.ref[...].reshape(DM, 3 * GROUP)

    def x_rows():
        return x_pair[...].reshape(8 * TOK, DM)

    chip_lanes = pl.ds(pl.multiple_of(chip * 128, 128), 128)
    seat_lanes = pl.ds(pl.multiple_of(here.seat * 256, 256), 256)
    idle = jnp.logical_not(here.active)

    def seat_dev(y_to, z_to, x_to):
        return (4 * y_to + 2 * x_to + c, z_to)

    send_q, qkv_t = m.send_q, m.qkv_t
    q_sem = links.alloc(2)
    bias = jnp.concatenate([vector_group(0), jnp.zeros((1, GROUP), F32), vector_group(1)], axis=1)
    for part in range(MB):
        rows = (dot(x_pair[part].reshape(4 * TOK, DM), weight_qkv()) + bias).astype(BF16)
        turned = rows.T
        for i in range(3):
            for j in range(3):
                block = turned[GROUP * j + HD * i : GROUP * j + HD * (i + 1), :]
                if j == 0:
                    block = block * jnp.asarray(HD ** (-0.5), BF16)
                send_q[3 * part + i, HD * j : HD * (j + 1), :] = block
            pair = 3 * part + i
            other = jnp.logical_not(both(here.active, here.pair == pair))
            dev = seat_dev(*SEATS[pair], x)
            links.send(send_q.at[pair], qkv_t.at[:, seat_lanes], q_sem, q_sem + 1, dev, other)

    links.drain(send_q.at[pl.ds(0, PAIRS - 1)], q_sem, here.active)
    links.drain(send_q, q_sem, idle)

    def own_q():
        qkv_t[:, seat_lanes] = send_q[here.pair]

    when(here.active, own_q)

    class ToSeats:
        def __init__(self, src_of, dst_of, slot, slots, seats, own):
            self.src_of, self.dst_of, self.slot, self.slots = src_of, dst_of, slot, slots
            self.seats, self.own = seats, own
            self.s, self.r = links.alloc(), links.alloc()
            self.width = SEQ // seats

        def start(self, other):
            start = pl.multiple_of(self.width * other, self.width)
            src, dst = self.src_of(pl.ds(start, self.width)), self.dst_of(self.slot)
            if self.seats == 16:
                place, x_to, mine = lax.div(other, 2), lax.rem(other, 2), chip
            else:
                place, x_to, mine = other, x, here.seat
            dev = seat_dev(lax.div(place, 4), lax.rem(place, 4), x_to)
            links.send(src, dst, self.s, self.r, dev, mine != other)

        def finish(self):
            links.drain(self.src_of(pl.ds(0, SEQ - self.width)), self.s, here.active)
            when(here.active, self.own)

        def wait(self):
            links.recv(self.dst_of(pl.ds(0, self.slots - 1)), self.r, here.active)
            links.recv(self.dst_of(pl.ds(0, self.slots)), self.r, idle)

    g_down.first_wait()
    g_down.own_plane()
    g_down.own_z()
    for gather in ahead:
        gather.land(here.near)
        gather.spread(here.near)
    for gather in ahead:
        gather.relay(here.far)
    for gather in ahead:
        gather.land(here.cross)
        gather.spread(here.cross)
    links.recv(qkv_t.at[:, pl.ds(0, SEQ - 256)], q_sem + 1, here.active)
    for gather in ahead:
        gather.relay(here.near)
    g_down.relay(z)

    weights = m.weights
    mix_slot = 6 * here.part + 3 * x + here.pair - 3 * here.part

    def own_mix():
        m.mix_in[mix_slot] = m.att_send[:, chip_lanes]

    mix = ToSeats(
        lambda lanes: m.att_send.at[:, lanes], lambda slot: m.mix_in.at[slot], mix_slot, 12, 16, own_mix
    )

    def turn_keys():
        m.k_rows[...] = qkv_t[HD : 2 * HD, :].T
        m.v_rows[...] = qkv_t[2 * HD : 3 * HD, :].T
        m.q_rows[...] = qkv_t[0:HD, :].T

    when(here.active, turn_keys)

    def attend(i):
        lanes = pl.ds(pl.multiple_of(i * CHUNK, CHUNK), CHUNK)
        query = qkv_t[0:HD, lanes]
        doc = m.query_doc[:, lanes]
        top = None
        for k in range(8):
            rows = slice(256 * k, 256 * (k + 1))
            key_doc = m.key_doc[rows, :]
            same = jnp.concatenate([key_doc, key_doc], axis=1) == doc
            scores = jnp.where(same, dot(m.k_rows[rows, :], query), NEG)
            m.scores[rows, :] = scores
            here_top = jnp.max(scores, axis=0, keepdims=True)
            top = here_top if top is None else jnp.maximum(top, here_top)
        total = None
        for k in range(8):
            rows = slice(256 * k, 256 * (k + 1))
            grown = jnp.exp(m.scores[rows, :] - top)
            weights[rows, lanes] = grown.astype(BF16)
            part_sum = row_sum(grown)
            total = part_sum if total is None else total + part_sum
        numer = dot(qkv_t[2 * HD : 3 * HD, :], weights[:, lanes])
        attended = numer / total
        m.total[:, lanes] = total
        m.att_t[:, lanes] = attended
        m.att_send[:, lanes] = attended.astype(BF16)
        mix.start(2 * i)
        mix.start(2 * i + 1)

    def some(body, first, last):
        def run():
            def one(i, carry):
                body(i)
                return carry

            lax.fori_loop(first, last, one, 0)

        when(here.active, run)

    some(attend, 0, 4)
    for gather in ahead:
        gather.relay(here.cross)
    g_down.land(here.far)
    g_down.hop()
    g_down.spread(here.far)
    g_down.land(here.near)
    g_down.spread(here.near)
    some(attend, 4, 7)
    g_down.land(here.cross)
    g_down.spread(here.cross)
    some(attend, 7, 8)
    g_down.relay(here.far)
    g_down.relay(here.near)
    mix.finish()
    mix.wait()
    g_out.done()
    g_down.relay(here.cross)

    def share(buf, values):
        sem = links.alloc(2)
        buf[:, c] = values.reshape(MB, TOK, DM)
        links.send(buf.at[:, c], buf.at[:, c], sem, sem + 1, here.sib)
        links.drain(buf.at[:, c], sem)
        links.recv(buf.at[:, 1 - c], sem + 1)

    def combine(values, back):
        sem = links.alloc(2)
        partial, other = m.partial, m.partial_low
        partial[...] = values.reshape(MB, 2, TOK, DM)
        other[...] = partial[:, 1 - c].astype(BF16)
        links.send(other, back, sem, sem + 1, here.sib)
        links.recv(back, sem + 1)
        total = partial[:, c].reshape(2 * TOK, DM) + back[...].reshape(2 * TOK, DM).astype(F32)
        links.sent(other, sem)
        return total

    def norm_rows(values, gain, shift):
        center = values - jnp.mean(values, axis=-1, keepdims=True)
        inverse = lax.rsqrt(jnp.mean(center * center, axis=-1, keepdims=True) + EPS)
        normed = center * inverse
        return normed * gain + shift, normed, inverse

    def norm_back(upstream, normed, inverse, gain):
        scaled = upstream * gain
        return inverse * (
            scaled
            - jnp.mean(scaled, axis=-1, keepdims=True)
            - normed * jnp.mean(scaled * normed, axis=-1, keepdims=True)
        )

    mixed_t = m.mixed_t
    mixed = []
    for part in range(MB):
        piece = m.mix_in[6 * part : 6 * part + 6].reshape(HALF, 128)
        mixed_t[:, 128 * part : 128 * (part + 1)] = piece
        mixed.append(piece.T)
    mixed = jnp.concatenate(mixed, axis=0)

    def weight_out():
        return g_out.ref[...].reshape(HALF, DM)

    attn = combine(dot(mixed, weight_out()), m.back0) + vector(2)
    own_tokens = x_pair[:, x, c].reshape(2 * TOK, DM).astype(F32)
    first, normed_one, inverse_one = norm_rows(own_tokens + attn, vector(3), vector(4))
    m.first[...] = first
    m.normed1[...] = normed_one
    m.inv1[...] = inverse_one
    share(m.fl_chip, first.astype(BF16))

    g_up.done()
    def fl_rows():
        return m.fl_chip[...].reshape(4 * TOK, DM)

    def weight_up(j):
        return g_up.ref[:, :, :, :, HALF * j : HALF * (j + 1)].reshape(DM, HALF)

    def weight_down(j):
        return g_down.ref[j].reshape(HALF, DM)

    for j in range(4):
        lanes = slice(HALF * j, HALF * (j + 1))
        hidden = dot(fl_rows(), weight_up(j)) + m.up_row[:, lanes]
        cdf = 0.5 * (1.0 + lax.erf(hidden * (0.5**0.5)))
        m.slope[:, lanes] = cdf + hidden * (jnp.exp(-0.5 * hidden * hidden) * 0.3989422804014327)
        m.active[:, lanes] = (hidden * cdf).astype(BF16)
    g_down.done()
    ffn = None
    for j in range(4):
        lanes = slice(HALF * j, HALF * (j + 1))
        term = dot(m.active[:, lanes], weight_down(j))
        ffn = term if ffn is None else ffn + term
    ffn = combine(ffn, m.back1) + vector(5)
    result, normed_two, inverse_two = norm_rows(m.first[...] + ffn, vector(6), vector(7))
    m.b_out[...] = result.reshape(MB, TOK, DM)
    links.put(m.b_out, o_out)

    targets = (here.near, here.cross, here.far, z)
    vec_grad = m.vec_grad
    grad_result = m.cot[...].reshape(2 * TOK, DM).astype(F32)
    vec_grad[6:7, :] = row_sum(grad_result * normed_two)
    vec_grad[7:8, :] = row_sum(grad_result)
    grad_two = norm_back(grad_result, normed_two, inverse_two, vector(6))
    m.gh2[...] = grad_two
    grad_ffn = grad_two.astype(BF16)
    vec_grad[5:6, :] = row_sum(grad_ffn.astype(F32))
    share(m.gf_chip, grad_ffn)

    def gf_rows():
        return m.gf_chip[...].reshape(4 * TOK, DM)

    for j in range(4):
        lanes = slice(HALF * j, HALF * (j + 1))
        s_down.grad[j] = dot_tn(m.active[:, lanes], gf_rows()).astype(BF16).reshape(4, 96, DM)
    s_down.send_sides(targets)
    s_down.column_first()
    grad_first = None
    for j in range(4):
        lanes = slice(HALF * j, HALF * (j + 1))
        grad_active = dot_nt(gf_rows(), weight_down(j))
        grad_hidden = (grad_active * m.slope[:, lanes]).astype(BF16)
        m.gh[:, lanes] = grad_hidden
        m.up_grad[:, lanes] = row_sum(grad_hidden.astype(F32))
    for j in range(4):
        lanes = slice(HALF * j, HALF * (j + 1))
        term = dot_nt(m.gh[:, lanes], weight_up(j))
        grad_first = term if grad_first is None else grad_first + term
    grad_first = m.gh2[...] + combine(grad_first, m.back2)
    normed_one = m.normed1[...]
    vec_grad[3:4, :] = row_sum(grad_first * normed_one)
    vec_grad[4:5, :] = row_sum(grad_first)
    grad_one = norm_back(grad_first, normed_one, m.inv1[...], vector(3))
    m.gh1[...] = grad_one
    grad_attn = grad_one.astype(BF16)
    vec_grad[2:3, :] = row_sum(grad_attn.astype(F32))
    share(m.ga_chip, grad_attn)

    def ga_rows():
        return m.ga_chip[...].reshape(4 * TOK, DM)

    turned = dot_nt(ga_rows(), weight_out()).astype(BF16).T
    for part in range(MB):
        m.g_send[6 * part : 6 * part + 6] = turned[:, 128 * part : 128 * (part + 1)].reshape(6, HD, 128)
    g_t = m.g_t
    g_sem = links.alloc(2)
    for slot in range(12):
        part, head = slot // 6, slot % 6
        pair, x_to = 3 * part + head % 3, head // 3
        mine = both(here.active, both(here.pair == pair, x == x_to))
        dev = seat_dev(*SEATS[pair], x_to)
        links.send(m.g_send.at[slot], g_t.at[:, chip_lanes], g_sem, g_sem + 1, dev, jnp.logical_not(mine))
    links.drain(m.g_send.at[pl.ds(0, 11)], g_sem, here.active)
    links.drain(m.g_send, g_sem, idle)

    def own_g():
        g_t[:, chip_lanes] = m.g_send[mix_slot]

    when(here.active, own_g)
    for j in range(4):
        lanes = slice(HALF * j, HALF * (j + 1))
        s_up.grad[:, :, :, :, lanes] = (
            dot_tn(fl_rows(), m.gh[:, lanes]).astype(BF16).reshape(4, 2, 4, 24, HALF)
        )
    s_out.grad[...] = dot(mixed_t[...], ga_rows()).astype(BF16).reshape(SHAPES[OUT])
    s_up.send_far(targets)
    s_out.send_far(targets)
    s_up.send_sides(targets)
    s_out.send_sides(targets)

    def planes(scatter, order=targets):
        for i, t in enumerate(order):
            scatter.plane(t)
            if i < 2:
                scatter.z_first(i)

    s_down.column_second()
    planes(s_down, targets[:3])
    links.recv(g_t.at[:, pl.ds(0, SEQ - 128)], g_sem + 1, here.active)

    d_send, d_in = m.d_send, m.d_in

    def own_kv():
        d_in[here.pair, HD : 3 * HD, :] = d_send[HD : 3 * HD, seat_lanes]

    def own_dq():
        d_in[here.pair, 0:HD, :] = d_send[0:HD, seat_lanes]

    grad_kv = ToSeats(
        lambda lanes: d_send.at[pl.ds(HD, 2 * HD), lanes], lambda slot: d_in.at[slot, pl.ds(HD, 2 * HD)],
        here.pair, PAIRS, 8, own_kv,
    )
    grad_q = ToSeats(
        lambda lanes: d_send.at[pl.ds(0, HD), lanes], lambda slot: d_in.at[slot, pl.ds(0, HD)],
        here.pair, PAIRS, 8, own_dq,
    )

    def turn_grads():
        grad = g_t[...].astype(F32)
        inverse = 1.0 / m.total[...]
        numer = grad * inverse
        m.gn_t[...] = numer.astype(BF16)
        m.g_rows[...] = numer.astype(BF16).T
        m.corr[...] = row_sum(grad * m.att_t[...]) * inverse
        m.dq_t[...] = jnp.zeros((HD, SEQ), F32)

    when(here.active, turn_grads)

    def back(k):
        keys = pl.ds(pl.multiple_of(k * CHUNK, CHUNK), CHUNK)
        value = m.v_rows[keys, :]
        for i in range(4):
            lanes = slice(512 * i, 512 * (i + 1))
            grad_weights = dot(value, m.gn_t[:, lanes])
            grown = weights[keys, lanes].astype(F32)
            m.ds[:, lanes] = (grown * (grad_weights - m.corr[:, lanes])).astype(BF16)
        ds = m.ds
        d_send[HD : 2 * HD, keys] = dot(ds[...], m.q_rows[...]).T.astype(BF16)
        d_send[2 * HD : 3 * HD, keys] = dot(weights[keys, :], m.g_rows[...]).T.astype(BF16)
        grad_kv.start(k)
        m.dq_t[...] += dot(qkv_t[HD : 2 * HD, keys], ds[...])

    some(back, 0, 4)
    s_down.column_last()
    for t in targets:
        s_up.relay(t)
    for t in targets:
        s_out.relay(t)
    some(back, 4, 8)

    def last_query():
        d_send[0:HD, :] = (m.dq_t[...] * (HD ** (-0.5))).astype(BF16)
        for other in range(8):
            grad_q.start(other)

    when(here.active, last_query)
    grad_kv.finish()
    grad_q.finish()
    s_down.relay_own()
    s_down.z_second()
    planes(s_up, targets[:2])
    grad_kv.wait()
    gp_kv, gp_q = m.gp_kv, m.gp_q
    for part in range(MB):
        heads = slice(3 * part, 3 * part + 3)
        rows = [d_in[heads, HD * j : HD * (j + 1), :].reshape(GROUP, 256) for j in (1, 2)]
        gp_kv[256 * part : 256 * (part + 1), :] = jnp.concatenate(rows, axis=0).T
    s_kv.grad[...] = dot_tn(x_rows(), gp_kv[...]).astype(BF16).reshape(SHAPES[KV])
    for t in targets:
        s_kv.send(t)
    for t in targets[2:]:
        s_up.plane(t)
    planes(s_out)
    s_down.plane(z)
    s_up.z_second()
    grad_q.wait()
    for part in range(MB):
        gp_q[256 * part : 256 * (part + 1), :] = d_in[3 * part : 3 * part + 3, 0:HD, :].reshape(GROUP, 256).T
    s_q.grad[...] = dot_tn(x_rows(), gp_q[...]).astype(BF16).reshape(SHAPES[Q])
    for t in targets:
        s_q.send(t)
    planes(s_kv)
    s_out.z_second()
    all_weights = weight_qkv()
    t_sem = links.alloc(4)
    for part in range(MB):
        rows = slice(256 * part, 256 * (part + 1))
        terms = dot_nt(gp_q[rows, :], all_weights[:, 0:GROUP]) + dot_nt(gp_kv[rows, :], all_weights[:, GROUP:])
        m.tok_part[part] = terms.reshape(2, 2, TOK, DM)
    links.send(m.tok_part.at[:, :, 1 - c], m.tok_back, t_sem, t_sem + 1, here.sib)
    links.drain(m.tok_back, t_sem)
    sum_q = row_sum(gp_q[...].astype(F32))
    sum_v = row_sum(gp_kv[:, GROUP:].astype(F32))
    for k in range(4):
        lanes = slice(GROUP * k, GROUP * (k + 1))
        vec_grad[0:1, lanes] = jnp.where(group == k, sum_q, 0.0)
        vec_grad[1:2, lanes] = jnp.where(group == k, sum_v, 0.0)
    links.recv(m.tok_back, t_sem + 1)
    for part in range(MB):
        m.tok_send[part] = (m.tok_part[part, 1 - x, c] + m.tok_back[part, 1 - x]).astype(BF16)
    links.send(m.tok_send, m.tok_last, t_sem + 2, t_sem + 3, here.dx)
    links.drain(m.tok_send, t_sem + 2)

    planes(s_q)
    s_kv.z_second()
    s_q.z_second()
    vec_send, vec_recv = m.vec_send, m.vec_recv
    spread = jnp.where(owner_24(32), vec_grad[...][None], 0.0).reshape(256, DM)
    vec_send[...] = exact_nt(spread, select_24()).reshape(32, 8, 128)
    spread = jnp.where(owner_96(), m.up_grad[...], 0.0)
    own_lines = pl.ds(16 * c, 16)
    vec_send[own_lines, 0, :] = vec_send[own_lines, 0, :] + exact_nt(spread, select_96())

    def grad_start(d, carry):
        other = lax.rem(line + d, 32)
        links.make(vec_send.at[other], vec_recv.at[line], vec_sem + 2, vec_sem + 3, peer(d)).start()
        return carry

    lax.fori_loop(1, 32, grad_start, 0)
    vec_recv[line] = vec_send[line]

    s_kv.z_last()
    s_down.z_last()
    s_out.z_last()
    s_up.z_last()
    s_q.z_last()
    links.recv(m.tok_last, t_sem + 3)
    for part in range(MB):
        rows = slice(TOK * part, TOK * (part + 1))
        own = m.tok_part[part, x, c] + m.tok_back[part, x]
        m.b_tok[part] = m.gh1[rows, :] + (own + m.tok_last[part].astype(F32))
    links.put(m.b_tok, o_tok)
    many_send, many_recv = vec_send.at[pl.ds(0, 31)], vec_recv.at[pl.ds(0, 31)]
    links.sent(many_send, vec_sem + 2)
    links.recv(many_recv, vec_sem + 3)
    m.b_vec[...] = jnp.sum(vec_recv[...], axis=0)
    links.put(m.b_vec, o_vec)
    s_down.finish(m.b_down)
    links.put(m.b_down, o_down)
    s_out.finish(m.b_wout)
    links.put(m.b_wout, o_wout)
    s_up.finish(m.b_up)
    links.put(m.b_up, o_up)
    s_kv.finish(m.b_qkv)
    s_q.finish(m.b_qkv)
    links.put(m.b_qkv, o_qkv)
    links.finish()


def place_kernel(*refs):
    ins, big_out, vec_out = refs[0:7], refs[7:13], refs[13:22]
    held, rows, sems = refs[22:29], refs[29:38], refs[38]
    loads = [pltpu.make_async_copy(src, dst, sems.at[i]) for i, (src, dst) in enumerate(zip(ins, held))]
    for load in reversed(loads):
        load.start()
    stores = [pltpu.make_async_copy(src, dst, sems.at[7 + i]) for i, (src, dst) in enumerate(zip(held, big_out))]
    stores += [pltpu.make_async_copy(src, dst, sems.at[13 + i]) for i, (src, dst) in enumerate(zip(rows, vec_out))]
    loads[6].wait()
    for j in range(8):
        rows[j][...] = held[6][j, 0:24]
    rows[8][...] = held[6][0, 32:128]
    for store in stores[6:]:
        store.start()
    for load, store in zip(loads, stores[:6]):
        load.wait()
        store.start()
    for store in stores:
        store.wait()


def fused(
    tokens, starts, w_qkv, bias_q, bias_v, w_out, bias_out, gain_one, shift_one,
    w_up, bias_up, w_down, bias_down, gain_two, shift_two, cotangent,
):
    anywhere = pl.BlockSpec(memory_space=pl.ANY)
    vectors = (bias_q, bias_v, bias_out, gain_one, shift_one, bias_down, gain_two, shift_two, bias_up)
    big = [tokens.shape, tokens.shape, w_qkv.shape, w_out.shape, w_up.shape, w_down.shape]
    big = [jax.ShapeDtypeStruct(shape, F32) for shape in big]
    small = [jax.ShapeDtypeStruct(vector.shape, F32) for vector in vectors]
    made = pl.pallas_call(
        layer_kernel,
        name="layer",
        out_shape=big + [jax.ShapeDtypeStruct((8, 128), F32)],
        in_specs=[anywhere, pl.BlockSpec(memory_space=pltpu.SMEM)] + [anywhere] * 14,
        out_specs=[anywhere] * 7,
        scratch_shapes=all_scratch(),
        compiler_params=pltpu.CompilerParams(
            collective_id=0, has_side_effects=True, vmem_limit_bytes=63 * 2**20
        ),
    )(tokens, starts, w_qkv, w_out, w_up, w_down, *vectors, cotangent)
    placed = pl.pallas_call(
        place_kernel,
        name="place",
        out_shape=big + small,
        in_specs=[anywhere] * 7,
        out_specs=[anywhere] * 15,
        scratch_shapes=[pltpu.VMEM(array.shape, F32) for array in (*made, *vectors)]
        + [pltpu.SemaphoreType.DMA((22,))],
    )(*made)
    out, tok, g_qkv, g_wout, g_up, g_down, bq, bv, bo, g1, s1, bd, g2, s2, bup = placed
    return (out, tok, g_qkv, bq, bv, g_wout, bo, g1, s1, g_up, bup, g_down, bd, g2, s2)


def solution(mesh):
    small = dict(mesh.shape) == {BLK: 8, HEAD: 4}
    return jax.shard_map(
        fused if small else per_device,
        mesh=mesh,
        in_specs=(
            P(None, BOTH, None),
            P(),
            P(BOTH, None),
            P(BOTH),
            P(BOTH),
            P(BOTH, None),
            P(BOTH),
            P(BOTH),
            P(BOTH),
            P(BOTH, None),
            P(BOTH),
            P(BOTH, None),
            P(BOTH),
            P(BOTH),
            P(BOTH),
            P(None, BOTH, None),
        ),
        out_specs=(
            P(None, BOTH, None),
            P(None, BOTH, None),
            P(BOTH, None),
            P(BOTH),
            P(BOTH),
            P(BOTH, None),
            P(BOTH),
            P(BOTH),
            P(BOTH),
            P(BOTH, None),
            P(BOTH),
            P(BOTH, None),
            P(BOTH),
            P(BOTH),
            P(BOTH),
        ),
        check_vma=False,
    )
```

```python
from functools import partial
from types import SimpleNamespace

import jax
import jax.numpy as jnp
from jax import lax
from jax.experimental import pallas as pl
from jax.experimental.pallas import tpu as pltpu
from jax.sharding import PartitionSpec as P

BLK = "blk"
HEAD = "head"
BOTH = (BLK, HEAD)
H = 12
HD = 64
MB = 2


EPS = 1e-05
NEG = -1e30


def norm_forward(values, gain_vec, shift_vec):
    center = values - jnp.mean(values, axis=-1, keepdims=True)
    inverse = lax.rsqrt(jnp.mean(center * center, axis=-1, keepdims=True) + EPS)
    normed = center * inverse
    return (normed * gain_vec + shift_vec, normed, inverse)


def norm_backward(upstream, normed, inverse, gain_vec):
    scaled = upstream * gain_vec
    inner = (
        scaled
        - jnp.mean(scaled, axis=-1, keepdims=True)
        - normed * jnp.mean(scaled * normed, axis=-1, keepdims=True)
    )
    return inner * inverse


def segment_of(starts_row, positions):
    return jnp.sum((starts_row[None, :] <= positions[:, None]).astype(jnp.int32), axis=1) - 1


def masked_scores(query_heads, key_heads, in_doc):
    scores = jnp.einsum(
        "qhd,khd->hqk", query_heads, key_heads, preferred_element_type=jnp.float32
    ) * HD ** (-0.5)
    return jnp.where(in_doc, scores, NEG)


def score_grads(query_heads, key_heads, value_heads, grad_numer, row_top, correction, in_doc):
    exp_score = jnp.where(
        in_doc, jnp.exp(masked_scores(query_heads, key_heads, in_doc) - row_top), 0.0
    )
    grad_weights = jnp.einsum(
        "qhd,khd->hqk", grad_numer, value_heads, preferred_element_type=jnp.float32
    )
    grad_scores = (exp_score * (grad_weights - correction)).astype(jnp.bfloat16)
    return (exp_score.astype(jnp.bfloat16), grad_scores)


def scatter_end(parts):
    (
        grad_proj_in,
        grad_query_bias,
        grad_value_bias,
        grad_proj_out,
        grad_out_bias,
        grad_norm_gain,
        grad_norm_shift,
        grad_up,
        grad_up_bias,
        grad_down,
        grad_down_bias,
        grad_final_gain,
        grad_final_shift,
    ) = parts
    return (
        lax.psum_scatter(grad_proj_in, BOTH, scatter_dimension=0, tiled=True),
        lax.psum_scatter(grad_query_bias, BOTH, scatter_dimension=0, tiled=True),
        lax.psum_scatter(grad_value_bias, BOTH, scatter_dimension=0, tiled=True),
        lax.psum_scatter(grad_proj_out, BOTH, scatter_dimension=0, tiled=True),
        lax.psum_scatter(grad_out_bias, BOTH, scatter_dimension=0, tiled=True),
        lax.psum_scatter(grad_norm_gain, BOTH, scatter_dimension=0, tiled=True),
        lax.psum_scatter(grad_norm_shift, BOTH, scatter_dimension=0, tiled=True),
        lax.psum_scatter(grad_up, BOTH, scatter_dimension=0, tiled=True),
        lax.psum_scatter(grad_up_bias, BOTH, scatter_dimension=0, tiled=True),
        lax.psum_scatter(grad_down, BOTH, scatter_dimension=0, tiled=True),
        lax.psum_scatter(grad_down_bias, BOTH, scatter_dimension=0, tiled=True),
        lax.psum_scatter(grad_final_gain, BOTH, scatter_dimension=0, tiled=True),
        lax.psum_scatter(grad_final_shift, BOTH, scatter_dimension=0, tiled=True),
    )


def per_device(
    tokens,
    starts,
    w_qkv,
    bias_q,
    bias_v,
    w_out,
    bias_out,
    gain_one,
    shift_one,
    w_up,
    bias_up,
    w_down,
    bias_down,
    gain_two,
    shift_two,
    cotangent,
):
    (
        proj_in,
        query_bias,
        value_bias,
        proj_out,
        out_bias,
        norm_gain,
        norm_shift,
        up_full,
        up_bias,
        down_full,
        down_bias,
        final_gain,
        final_shift,
    ) = (
        lax.all_gather(w_qkv, BOTH, axis=0, tiled=True),
        lax.all_gather(bias_q, BOTH, axis=0, tiled=True),
        lax.all_gather(bias_v, BOTH, axis=0, tiled=True),
        lax.all_gather(w_out, BOTH, axis=0, tiled=True),
        lax.all_gather(bias_out, BOTH, axis=0, tiled=True),
        lax.all_gather(gain_one, BOTH, axis=0, tiled=True),
        lax.all_gather(shift_one, BOTH, axis=0, tiled=True),
        lax.all_gather(w_up, BOTH, axis=0, tiled=True),
        lax.all_gather(bias_up, BOTH, axis=0, tiled=True),
        lax.all_gather(w_down, BOTH, axis=0, tiled=True),
        lax.all_gather(bias_down, BOTH, axis=0, tiled=True),
        lax.all_gather(gain_two, BOTH, axis=0, tiled=True),
        lax.all_gather(shift_two, BOTH, axis=0, tiled=True),
    )
    query_bias = query_bias.astype(jnp.float32)
    value_bias = value_bias.astype(jnp.float32)
    out_bias = out_bias.astype(jnp.float32)
    norm_gain = norm_gain.astype(jnp.float32)
    norm_shift = norm_shift.astype(jnp.float32)
    up_bias = up_bias.astype(jnp.float32)
    down_bias = down_bias.astype(jnp.float32)
    final_gain = final_gain.astype(jnp.float32)
    final_shift = final_shift.astype(jnp.float32)
    model_width = proj_out.shape[0]
    row_count = tokens.shape[1]
    head_count = lax.axis_size(HEAD)
    block_rows = row_count * head_count
    heads_dev = H // head_count
    local_width = heads_dev * HD
    scale = HD ** (-0.5)
    local_pos = lax.axis_index(BLK) * block_rows + jnp.arange(block_rows, dtype=jnp.int32)
    kept_list = []
    outputs = []
    for part_index in range(MB):
        inputs = tokens[part_index]
        starts_row = starts[part_index]
        projected = jnp.dot(inputs, proj_in, preferred_element_type=jnp.float32)
        query_rows = (projected[:, :model_width] + query_bias).astype(jnp.bfloat16)
        key_rows = projected[:, model_width : 2 * model_width].astype(jnp.bfloat16)
        value_rows = (projected[:, 2 * model_width :] + value_bias).astype(jnp.bfloat16)
        query_loc, key_loc, value_loc = (
            lax.all_to_all(query_rows, HEAD, split_axis=1, concat_axis=0, tiled=True),
            lax.all_to_all(key_rows, HEAD, split_axis=1, concat_axis=0, tiled=True),
            lax.all_to_all(value_rows, HEAD, split_axis=1, concat_axis=0, tiled=True),
        )
        doc_local = segment_of(starts_row, local_pos)
        query_heads = query_loc.reshape(block_rows, heads_dev, HD)

        def fold_keys(running, portion):
            row_top, row_total, weighted = running
            key_part, value_part = portion
            piece_len = key_part.shape[0]
            key_doc = segment_of(starts_row, jnp.arange(piece_len, dtype=jnp.int32))
            in_doc = (doc_local[:, None] == key_doc[None, :])[None]
            scores = masked_scores(query_heads, key_part.reshape(piece_len, heads_dev, HD), in_doc)
            new_top = jnp.maximum(row_top, jnp.max(scores, axis=-1, keepdims=True))
            exp_score = jnp.where(in_doc, jnp.exp(scores - new_top), 0.0)
            row_total = jnp.sum(exp_score, axis=-1, keepdims=True)
            weighted = jnp.einsum(
                "hqk,khd->hqd",
                exp_score.astype(jnp.bfloat16),
                value_part.reshape(piece_len, heads_dev, HD),
                preferred_element_type=jnp.float32,
            )
            return (new_top, row_total, weighted)

        start_state = (
            jnp.full((heads_dev, block_rows, 1), NEG, jnp.float32),
            jnp.zeros((heads_dev, block_rows, 1), jnp.float32),
            jnp.zeros((heads_dev, block_rows, HD), jnp.float32),
        )
        row_top, row_total, weighted = fold_keys(
            start_state,
            (
                lax.all_gather(key_loc, BLK, axis=0, tiled=True),
                lax.all_gather(value_loc, BLK, axis=0, tiled=True),
            ),
        )
        attended = jnp.transpose(weighted / row_total, (1, 0, 2))
        mixed_rows = lax.all_to_all(
            attended.reshape(block_rows, local_width).astype(jnp.bfloat16),
            HEAD,
            split_axis=0,
            concat_axis=1,
            tiled=True,
        )
        attn_out = jnp.dot(mixed_rows, proj_out, preferred_element_type=jnp.float32) + out_bias
        first_norm, normed_one, inverse_one = norm_forward(
            inputs.astype(jnp.float32) + attn_out, norm_gain, norm_shift
        )
        first_low = first_norm.astype(jnp.bfloat16)
        hidden = jnp.dot(first_low, up_full, preferred_element_type=jnp.float32) + up_bias
        active = jax.nn.gelu(hidden, approximate=False).astype(jnp.bfloat16)
        ffn_out = jnp.dot(active, down_full, preferred_element_type=jnp.float32) + down_bias
        result, normed_two, inverse_two = norm_forward(
            first_norm + ffn_out, final_gain, final_shift
        )
        outputs.append(result)
        kept_list.append(
            (
                inputs,
                starts_row,
                query_loc,
                key_loc,
                value_loc,
                doc_local,
                row_top,
                row_total,
                attended,
                mixed_rows,
                normed_one,
                inverse_one,
                first_low,
                hidden,
                active,
                normed_two,
                inverse_two,
            )
        )
    input_grads = []
    grad_sum = None
    for part_index in range(MB):
        (
            inputs,
            starts_row,
            query_loc,
            key_loc,
            value_loc,
            doc_local,
            row_top,
            row_total,
            attended,
            mixed_rows,
            normed_one,
            inverse_one,
            first_low,
            hidden,
            active,
            normed_two,
            inverse_two,
        ) = kept_list[part_index]
        grad_result = cotangent[part_index].astype(jnp.float32)
        grad_final_gain = jnp.sum(grad_result * normed_two, axis=0)
        grad_final_shift = jnp.sum(grad_result, axis=0)
        grad_two = norm_backward(grad_result, normed_two, inverse_two, final_gain)
        grad_ffn = grad_two.astype(jnp.bfloat16)
        grad_down_bias = jnp.sum(grad_ffn.astype(jnp.float32), axis=0)
        grad_down = jnp.einsum("rf,rd->fd", active, grad_ffn, preferred_element_type=jnp.float32)
        grad_active = jnp.einsum(
            "rd,fd->rf", grad_ffn, down_full, preferred_element_type=jnp.float32
        )
        gelu_pull = jax.vjp(partial(jax.nn.gelu, approximate=False), hidden)[1]
        grad_hidden = gelu_pull(grad_active)[0].astype(jnp.bfloat16)
        grad_up_bias = jnp.sum(grad_hidden.astype(jnp.float32), axis=0)
        grad_up = jnp.einsum(
            "rd,rf->df", first_low, grad_hidden, preferred_element_type=jnp.float32
        )
        grad_first = grad_two + jnp.einsum(
            "rf,df->rd", grad_hidden, up_full, preferred_element_type=jnp.float32
        )
        grad_norm_gain = jnp.sum(grad_first * normed_one, axis=0)
        grad_norm_shift = jnp.sum(grad_first, axis=0)
        grad_one = norm_backward(grad_first, normed_one, inverse_one, norm_gain)
        grad_attn = grad_one.astype(jnp.bfloat16)
        grad_out_bias = jnp.sum(grad_attn.astype(jnp.float32), axis=0)
        grad_proj_out = jnp.einsum(
            "rc,rd->cd", mixed_rows, grad_attn, preferred_element_type=jnp.float32
        )
        grad_mixed = jnp.einsum(
            "rd,cd->rc", grad_attn, proj_out, preferred_element_type=jnp.float32
        ).astype(jnp.bfloat16)
        grad_loc = lax.all_to_all(grad_mixed, HEAD, split_axis=1, concat_axis=0, tiled=True)
        grad_heads = grad_loc.astype(jnp.float32).reshape(block_rows, heads_dev, HD)
        total_rows = jnp.transpose(row_total, (1, 0, 2))
        correction = jnp.transpose(
            jnp.sum(grad_heads * attended, axis=-1, keepdims=True) / total_rows, (1, 0, 2)
        )
        grad_numer = (grad_heads / total_rows).astype(jnp.bfloat16)
        query_heads = query_loc.reshape(block_rows, heads_dev, HD)
        key_heads_loc = key_loc.reshape(block_rows, heads_dev, HD)
        value_heads_loc = value_loc.reshape(block_rows, heads_dev, HD)
        fold_key_part = lax.all_gather(key_loc, BLK, axis=0, tiled=True)
        fold_value_part = lax.all_gather(value_loc, BLK, axis=0, tiled=True)
        fold_piece_len = fold_key_part.shape[0]
        fold_key_doc = segment_of(starts_row, jnp.arange(fold_piece_len, dtype=jnp.int32))
        fold_in_doc = (doc_local[:, None] == fold_key_doc[None, :])[None]
        key_heads = fold_key_part.reshape(fold_piece_len, heads_dev, HD)
        exp_low, grad_scores = score_grads(
            query_heads,
            key_heads,
            fold_value_part.reshape(fold_piece_len, heads_dev, HD),
            grad_numer,
            row_top,
            correction,
            fold_in_doc,
        )
        grad_query = (
            jnp.einsum("hqk,khd->qhd", grad_scores, key_heads, preferred_element_type=jnp.float32)
            * scale
        )
        top_rows = jnp.transpose(row_top[:, :, 0])
        corr_rows = jnp.transpose(correction[:, :, 0])

        def fold_keygrad(portion):
            query_part, numer_part, top_part, corr_part = portion
            piece_len = query_part.shape[0]
            query_doc = segment_of(starts_row, jnp.arange(piece_len, dtype=jnp.int32))
            in_doc = (query_doc[:, None] == doc_local[None, :])[None]
            query_piece = query_part.reshape(piece_len, heads_dev, HD)
            numer_piece = numer_part.reshape(piece_len, heads_dev, HD)
            exp_low, grad_scores = score_grads(
                query_piece,
                key_heads_loc,
                value_heads_loc,
                numer_piece,
                jnp.transpose(top_part)[:, :, None],
                jnp.transpose(corr_part)[:, :, None],
                in_doc,
            )
            grad_key_run = (
                jnp.einsum(
                    "hqk,qhd->khd", grad_scores, query_piece, preferred_element_type=jnp.float32
                )
                * scale
            )
            grad_value_run = jnp.einsum(
                "hqk,qhd->khd", exp_low, numer_piece, preferred_element_type=jnp.float32
            )
            return (grad_key_run, grad_value_run)

        grad_key, grad_value = fold_keygrad(
            (
                lax.all_gather(query_loc, BLK, axis=0, tiled=True),
                lax.all_gather(
                    grad_numer.reshape(block_rows, local_width), BLK, axis=0, tiled=True
                ),
                lax.all_gather(top_rows.astype(jnp.bfloat16), BLK, axis=0, tiled=True).astype(
                    jnp.float32
                ),
                lax.all_gather(corr_rows.astype(jnp.bfloat16), BLK, axis=0, tiled=True).astype(
                    jnp.float32
                ),
            )
        )
        grad_q_rows, grad_k_rows, grad_v_rows = (
            lax.all_to_all(
                grad_query.reshape(block_rows, local_width).astype(jnp.bfloat16),
                HEAD,
                split_axis=0,
                concat_axis=1,
                tiled=True,
            ),
            lax.all_to_all(
                grad_key.reshape(block_rows, local_width).astype(jnp.bfloat16),
                HEAD,
                split_axis=0,
                concat_axis=1,
                tiled=True,
            ),
            lax.all_to_all(
                grad_value.reshape(block_rows, local_width).astype(jnp.bfloat16),
                HEAD,
                split_axis=0,
                concat_axis=1,
                tiled=True,
            ),
        )
        grad_proj = jnp.concatenate([grad_q_rows, grad_k_rows, grad_v_rows], axis=1)
        grad_query_bias = jnp.sum(grad_q_rows.astype(jnp.float32), axis=0)
        grad_value_bias = jnp.sum(grad_v_rows.astype(jnp.float32), axis=0)
        grad_proj_in = jnp.einsum(
            "rd,re->de", inputs, grad_proj, preferred_element_type=jnp.float32
        )
        input_grads.append(
            grad_one
            + jnp.einsum("re,de->rd", grad_proj, proj_in, preferred_element_type=jnp.float32)
        )
        part_grads = (
            grad_proj_in,
            grad_query_bias,
            grad_value_bias,
            grad_proj_out,
            grad_out_bias,
            grad_norm_gain,
            grad_norm_shift,
            grad_up,
            grad_up_bias,
            grad_down,
            grad_down_bias,
            grad_final_gain,
            grad_final_shift,
        )
        grad_sum = (
            part_grads
            if grad_sum is None
            else tuple((left + right for left, right in zip(grad_sum, part_grads)))
        )
    grad_sum = scatter_end(grad_sum)
    (
        grad_proj_in,
        grad_query_bias,
        grad_value_bias,
        grad_proj_out,
        grad_out_bias,
        grad_norm_gain,
        grad_norm_shift,
        grad_up,
        grad_up_bias,
        grad_down,
        grad_down_bias,
        grad_final_gain,
        grad_final_shift,
    ) = grad_sum
    return (
        jnp.stack(outputs),
        jnp.stack(input_grads),
        grad_proj_in,
        grad_query_bias,
        grad_value_bias,
        grad_proj_out,
        grad_out_bias,
        grad_norm_gain,
        grad_norm_shift,
        grad_up,
        grad_up_bias,
        grad_down,
        grad_down_bias,
        grad_final_gain,
        grad_final_shift,
    )


MESH = pl.DeviceIdType.MESH
F32 = jnp.float32
BF16 = jnp.bfloat16
DM = 768
FF = 3072
TOK = 64
SEQ = 2048
HALF = DM // 2
GROUP = 3 * HD
UP_N = FF // 2
CHUNK = 256
PAIRS = 6

QKV, OUT, UP, DOWN, KV, Q = range(6)
SHAPES = (
    (2, 2, 2, 4, 24, 3 * GROUP),
    (4, 4, 24, DM),
    (4, 2, 4, 24, UP_N),
    (4, 4, 96, DM),
    (2, 2, 2, 4, 24, 2 * GROUP),
    (2, 2, 2, 4, 24, GROUP),
)


def by_column(kind):
    return kind == UP


def piece_shape(kind):
    shape = SHAPES[kind]
    if kind in (QKV, KV, Q):
        return shape[1:3] + shape[4:]
    return (2,) + shape[3:] if by_column(kind) else shape[2:]


def when(cond, run):
    if cond is None:
        run()
    else:
        pl.when(cond)(run)


def both(left, right):
    return jnp.logical_and(left, right)


class Place:
    def __init__(self):
        b = lax.axis_index(BLK)
        z = lax.axis_index(HEAD)
        c = lax.rem(b, 2)
        x = lax.rem(lax.div(b, 2), 2)
        y = lax.div(b, 4)
        self.b, self.z, self.c, self.x, self.y = b, z, c, x, y
        self.line = 4 * b + z
        self.sib = (b + 1 - 2 * c, z)
        self.dx = (4 * y + 2 * (1 - x) + c, z)
        self.dy = (4 * (1 - y) + 2 * x + c, z)
        self.dx_other = (4 * y + 2 * (1 - x) + 1 - c, z)
        self.near = z + 1 - 2 * lax.rem(z, 2)
        self.far = lax.rem(z + 2, 4)
        self.cross = 3 - z
        self.swap = (4 * c + 2 * x + y, z)
        self.stays = y == c
        self.moves = y != c
        self.group = 2 * c + x
        self.seat = 4 * y + z
        self.chip = 2 * self.seat + x
        idle = jnp.logical_or(both(z == 0, y == 1), both(z == 3, y == 0))
        self.active = jnp.logical_not(idle)
        inner = jnp.where(z == 1, 4 * y, 1 + 4 * y)
        outer = jnp.where(z == 0, 2, 3)
        self.pair = jnp.where(jnp.logical_or(z == 1, z == 2), inner, outer)
        self.part = lax.div(self.pair, 3)

    def cols(self, kind):
        x, y = self.x, self.y
        if by_column(kind):
            return (2 * y + x, 2 * y + 1 - x, 2 * (1 - y) + x, 2 * (1 - y) + 1 - x)
        return (2 * x + y, 2 * (1 - x) + y, 2 * x + 1 - y, 2 * (1 - x) + 1 - y)


SEATS = ((0, 1), (0, 2), (0, 0), (1, 3), (1, 1), (1, 2))


def chunk(kind, ref, col, z):
    return ref.at[col, :, z] if by_column(kind) else ref.at[col, z]


class Links:
    def __init__(self, sems, here):
        self.sems, self.here, self.count = sems, here, 0
        self.waits = []

    def alloc(self, n=1):
        at = self.count
        self.count += n
        return at

    def make(self, src, dst, s, r, dev):
        return pltpu.make_async_remote_copy(
            src_ref=src, dst_ref=dst, send_sem=self.sems.at[s], recv_sem=self.sems.at[r],
            device_id=dev, device_id_type=MESH,
        )

    def send(self, src, dst, s, r, dev, cond=None):
        when(cond, lambda: self.make(src, dst, s, r, dev).start())

    def recv(self, dst, r, cond=None):
        when(cond, lambda: self.make(dst, dst, r, r, self.here.sib).wait_recv())

    def sent(self, src, s, cond=None):
        when(cond, lambda: self.make(src, src, s, s, self.here.sib).wait_send())

    def drain(self, like, s, cond=None):
        self.waits.append(lambda: self.sent(like, s, cond))

    def local(self, src, dst, cond=None):
        sem = self.sems.at[self.alloc()]
        when(cond, lambda: pltpu.make_async_copy(src, dst, sem).start())
        return lambda: when(cond, lambda: pltpu.make_async_copy(src, dst, sem).wait())

    def put(self, src, dst):
        self.waits.append(self.local(src, dst))

    def finish(self):
        for wait in self.waits:
            wait()


class Gather:
    def __init__(self, links, here, kind, ref):
        self.links, self.here, self.kind, self.ref = links, here, kind, ref
        self.s0, self.r0 = links.alloc(), links.alloc()
        self.sz, self.rz = links.alloc(), links.alloc(4)
        self.s_plane, self.s_relay = links.alloc(), links.alloc()
        self.r_relay, self.r_rest = links.alloc(4), links.alloc()
        self.col, self.col_x, self.col_y, self.col_d = here.cols(kind)
        links.drain(ref.at[0, :, pl.ds(0, 3)] if by_column(kind) else ref.at[0, pl.ds(0, 3)], self.sz)
        links.drain(ref.at[pl.ds(0, 2)], self.s_plane)
        links.drain(ref.at[0], self.s_relay)

    def first_wait(self):
        here = self.here
        if by_column(self.kind):
            self.links.recv(self.ref.at[self.col, 1 - here.c, here.z], self.r0)
        else:
            self.links.recv(self.ref.at[self.col, here.z], self.r0, here.moves)

    def piece(self, col, z):
        return chunk(self.kind, self.ref, col, z)

    def z_hop(self, z, to):
        piece = self.piece(self.col, z)
        self.links.send(piece, piece, self.sz, self.rz + z, (self.here.b, to))

    def spread(self, z):
        piece = self.piece(self.col, z)
        on_y = z < 1
        to_x = jnp.where(on_y, self.r_relay + z, self.r_rest)
        to_y = jnp.where(on_y, self.r_rest, self.r_relay + z)
        self.links.send(piece, piece, self.s_plane, to_x, self.here.dx)
        self.links.send(piece, piece, self.s_plane, to_y, self.here.dy)

    def own_z(self):
        here = self.here
        self.z_hop(here.z, here.far)
        self.z_hop(here.z, here.near)

    def own_plane(self):
        self.spread(self.here.z)

    def land(self, z):
        self.links.recv(self.piece(self.col, z), self.rz + z)

    def hop(self):
        self.z_hop(self.here.far, self.here.near)

    def relay(self, z):
        here = self.here
        on_y = z < 1
        piece = self.piece(jnp.where(on_y, self.col_x, self.col_y), z)
        self.links.recv(piece, self.r_relay + z)
        dev = (jnp.where(on_y, here.dy[0], here.dx[0]), here.z)
        self.links.send(piece, piece, self.s_relay, self.r_rest, dev)

    def done(self):
        self.links.recv(self.ref.at[pl.ds(0, 2)], self.r_rest)


class PairGather:
    def __init__(self, links, here, ref):
        self.links, self.here, self.ref = links, here, ref
        self.s0, self.r0 = links.alloc(), links.alloc()
        self.sz, self.rz = links.alloc(), links.alloc(4)
        self.sy, self.ry = links.alloc(), links.alloc()
        links.drain(ref.at[0, 0, 0, pl.ds(0, 3)], self.s0)
        links.drain(ref.at[0, :, :, pl.ds(0, 3)], self.sz)
        links.drain(ref.at[0], self.sy)

    def first_wait(self):
        self.links.recv(self.ref.at[0, 0, 0, pl.ds(0, 3)], self.r0)

    def piece(self, z):
        return self.ref.at[self.here.y, :, :, z]

    def z_hop(self, z, to):
        self.links.send(self.piece(z), self.piece(z), self.sz, self.rz + z, (self.here.b, to))

    def own_z(self):
        here = self.here
        self.z_hop(here.z, here.far)
        self.z_hop(here.z, here.near)

    def land(self, z):
        self.links.recv(self.piece(z), self.rz + z)

    def hop(self):
        self.z_hop(self.here.far, self.here.near)

    def spread(self, z):
        self.links.send(self.piece(z), self.piece(z), self.sy, self.ry, self.here.dy)

    def done(self):
        self.links.recv(self.ref.at[0], self.ry)


def add_blocks(dst, terms, blocks):
    for at in blocks:
        total = terms[0][at].astype(F32)
        for term in terms[1:]:
            total = total + term[at].astype(F32)
        dst[at] = total.astype(dst.dtype)


class Scatter:
    def __init__(self, links, here, kind, refs):
        self.links, self.here, self.kind = links, here, kind
        self.tilt = 2
        self.grad, self.far, self.cxy, self.zb, self.zr, self.fin, self.last = refs
        self.s_first, self.s_relay, self.sz = links.alloc(), links.alloc(), links.alloc()
        self.r_far, self.r_plane, self.rz = links.alloc(4), links.alloc(4), links.alloc(3)
        self.s_end, self.r_end = links.alloc(), links.alloc()
        self.col, self.col_x, self.col_y, self.col_d = here.cols(kind)
        links.drain(self.cxy, self.s_first)
        links.drain(self.far, self.s_relay)
        links.drain(self.zr.at[pl.ds(0, 3)], self.sz)
        if by_column(kind):
            links.drain(self.last, self.s_end)
        else:
            links.drain(self.last, self.s_end, here.moves)

    def piece(self, col, z):
        return chunk(self.kind, self.grad, col, z)

    def add(self, dst, terms):
        add_blocks(dst, terms, [(h,) for h in range(2)] if by_column(self.kind) else [(slice(0, None),)])

    def side(self, z, to_x, sem):
        here = self.here
        col = jnp.where(to_x, self.col_x, self.col_y)
        dev = (jnp.where(to_x, here.dx[0], here.dy[0]), here.z)
        slot = jnp.where(to_x, z, 4 + z)
        self.links.send(self.piece(col, z), self.cxy.at[slot], sem, self.r_plane + z, dev)

    def send_far(self, order):
        here = self.here
        for z in order:
            to_x = z >= self.tilt
            dev = (jnp.where(to_x, here.dx[0], here.dy[0]), here.z)
            self.links.send(self.piece(self.col_d, z), self.far.at[z], self.s_first, self.r_far + z, dev)

    def send_sides(self, order):
        for z in order:
            self.side(z, z >= self.tilt, self.s_first)

    def relay(self, z):
        to_y = z >= self.tilt
        self.links.recv(self.far.at[z], self.r_far + z)
        piece = self.piece(jnp.where(to_y, self.col_y, self.col_x), z)
        self.add(piece, (piece, self.far.at[z]))
        self.side(z, jnp.logical_not(to_y), self.s_relay)

    def plane(self, z):
        self.links.recv(self.cxy.at[pl.ds(0, 2)], self.r_plane + z)
        self.add(self.zb.at[z], (self.piece(self.col, z), self.cxy.at[z], self.cxy.at[4 + z]))

    def z_first(self, i):
        here = self.here
        z = here.cross if i else here.near
        self.links.send(self.zb.at[z], self.zr.at[i], self.sz, self.rz + i, (here.b, here.near))

    def z_second(self):
        here = self.here
        self.links.recv(self.zr.at[1], self.rz + 1)
        piece = self.zb.at[here.far]
        self.add(piece, (piece, self.zr.at[1]))
        self.links.send(piece, self.zr.at[2], self.sz, self.rz + 2, (here.b, here.far))

    def z_last(self):
        links, here = self.links, self.here
        links.recv(self.zr.at[0], self.rz)
        links.recv(self.zr.at[2], self.rz + 2)
        self.add(self.fin, [self.zb.at[here.z], self.zr.at[0], self.zr.at[2]])
        if by_column(self.kind):
            links.send(self.fin.at[1 - here.c], self.last, self.s_end, self.r_end, here.sib)
        else:
            links.send(self.fin, self.last, self.s_end, self.r_end, here.swap, here.moves)

    def finish(self, out):
        links, here, kind = self.links, self.here, self.kind
        c = here.c
        if by_column(kind):
            out[:, pl.ds(pl.multiple_of(UP_N * c, 128), UP_N)] = self.fin[c]
            links.recv(self.last, self.r_end)
            out[:, pl.ds(pl.multiple_of(UP_N * (1 - c), 128), UP_N)] = self.last[...]
        else:
            links.recv(self.last, self.r_end, here.moves)

            def keep():
                out[...] = self.fin[...]

            def take():
                out[...] = self.last[...]

            when(here.stays, keep)
            when(here.moves, take)


class ColumnScatter(Scatter):
    def __init__(self, links, here, kind, refs):
        self.links, self.here, self.kind = links, here, kind
        self.grad, self.far, self.cxy, self.zb, self.zr, self.fin, self.last = refs
        self.s_first, self.s_relay, self.sz = links.alloc(), links.alloc(), links.alloc()
        self.r_far, self.r_plane, self.rz = links.alloc(4), links.alloc(4), links.alloc(3)
        self.s_far, self.s_column = links.alloc(), links.alloc()
        self.s_end, self.r_end = links.alloc(), links.alloc()
        self.col, self.col_x, self.col_y, self.col_d = here.cols(kind)
        links.drain(self.cxy.at[pl.ds(0, 7)], self.s_first)
        links.drain(self.far.at[0], self.s_relay)
        links.drain(self.far.at[0], self.s_far)
        links.drain(self.far.at[pl.ds(0, 3)], self.s_column)
        links.drain(self.zr.at[pl.ds(0, 3)], self.sz)
        links.drain(self.last, self.s_end, None if by_column(kind) else here.moves)

    def to_side(self, z, to_x, sem):
        here = self.here
        col, slot, dev = (self.col_x, z, here.dx) if to_x else (self.col_y, 4 + z, here.dy)
        self.links.send(self.piece(col, z), self.cxy.at[slot], sem, self.r_plane + z, dev)

    def send_sides(self, order):
        for z in order:
            self.to_side(z, True, self.s_first)
            if z is not self.here.z:
                self.to_side(z, False, self.s_first)

    def column_first(self):
        here = self.here
        for i, z in enumerate((here.near, here.cross)):
            self.links.send(self.piece(self.col_d, z), self.far.at[i], self.s_column, self.r_far + i, (here.b, here.near))

    def column_second(self):
        here = self.here
        self.links.recv(self.far.at[1], self.r_far + 1)
        piece = self.piece(self.col_d, here.far)
        self.add(piece, (piece, self.far.at[1]))
        self.links.send(piece, self.far.at[2], self.s_column, self.r_far + 2, (here.b, here.far))

    def column_last(self):
        here = self.here
        self.links.recv(self.far.at[0], self.r_far)
        self.links.recv(self.far.at[2], self.r_far + 2)
        piece = self.piece(self.col_d, here.z)
        self.add(piece, (piece, self.far.at[0], self.far.at[2]))
        self.links.send(piece, self.far.at[3], self.s_far, self.r_far + 3, here.dx)

    def relay_own(self):
        here = self.here
        self.links.recv(self.far.at[3], self.r_far + 3)
        piece = self.piece(self.col_y, here.z)
        self.add(piece, (piece, self.far.at[3]))
        self.to_side(here.z, False, self.s_relay)


class PairScatter:
    def __init__(self, links, here, kind, refs):
        self.links, self.here, self.kind = links, here, kind
        self.grad, self.cy, self.zb, self.zr, self.fin, self.last = refs
        self.sy, self.ry = links.alloc(), links.alloc(4)
        self.sz, self.rz = links.alloc(), links.alloc(3)
        self.s_end, self.r_end = links.alloc(), links.alloc()
        links.drain(self.cy, self.sy)
        links.drain(self.zr.at[pl.ds(0, 3)], self.sz)
        links.drain(self.last.at[pl.ds(0, 3)], self.s_end)

    def add(self, dst, terms):
        add_blocks(dst, terms, [(i, j) for i in range(2) for j in range(2)])

    def send(self, z):
        here = self.here
        self.links.send(self.grad.at[1 - here.y, :, :, z], self.cy.at[z], self.sy, self.ry + z, here.dy)

    def plane(self, z):
        self.links.recv(self.cy.at[z], self.ry + z)
        self.add(self.zb.at[z], (self.grad.at[self.here.y, :, :, z], self.cy.at[z]))

    def z_first(self, i):
        here = self.here
        z = here.cross if i else here.near
        self.links.send(self.zb.at[z], self.zr.at[i], self.sz, self.rz + i, (here.b, here.near))

    def z_second(self):
        here = self.here
        self.links.recv(self.zr.at[1], self.rz + 1)
        piece = self.zb.at[here.far]
        self.add(piece, (piece, self.zr.at[1]))
        self.links.send(piece, self.zr.at[2], self.sz, self.rz + 2, (here.b, here.far))

    def z_last(self):
        links, here = self.links, self.here
        links.recv(self.zr.at[0], self.rz)
        links.recv(self.zr.at[2], self.rz + 2)
        self.add(self.fin, [self.zb.at[here.z], self.zr.at[0], self.zr.at[2]])
        x, c = here.x, here.c
        slot = self.last.at[here.group]
        links.send(self.fin.at[1 - x, c], slot, self.s_end, self.r_end, here.dx)
        links.send(self.fin.at[1 - x, 1 - c], slot, self.s_end, self.r_end, here.dx_other)
        links.send(self.fin.at[x, 1 - c], slot, self.s_end, self.r_end, here.sib)

    def finish(self, out):
        self.last[self.here.group] = self.fin[self.here.x, self.here.c]
        self.links.recv(self.last.at[pl.ds(0, 3)], self.r_end)
        for group in range(4):
            if self.kind == Q:
                out[:, GROUP * group : GROUP * (group + 1)] = self.last[group]
            else:
                for i in range(2):
                    at = DM * (i + 1) + GROUP * group
                    out[:, at : at + GROUP] = self.last[group, :, GROUP * i : GROUP * (i + 1)]


def dot(a, b):
    return jnp.dot(a, b, preferred_element_type=F32)


def dot_nt(a, b):
    return lax.dot_general(a, b, (((1,), (1,)), ((), ())), preferred_element_type=F32)


def dot_tn(a, b):
    return lax.dot_general(a, b, (((0,), (0,)), ((), ())), preferred_element_type=F32)


def row_sum(values):
    return jnp.sum(values, axis=0, keepdims=True)


def div24(n):
    return lax.shift_right_logical(n * 2731, 16)


def iota(shape, dim):
    return lax.broadcasted_iota(jnp.int32, shape, dim)


def select_24():
    n = iota((128, DM), 1)
    return (iota((128, DM), 0) == n - 24 * div24(n)).astype(BF16)


def select_96():
    n = iota((128, UP_N), 1)
    run = lax.shift_right_logical(div24(n), 2)
    return (iota((128, UP_N), 0) == 32 + n - 96 * run).astype(BF16)


def owner_24(lead):
    shape = (lead, 8, DM)
    return div24(iota(shape, 2)) == iota(shape, 0)


def owner_96():
    shape = (16, UP_N)
    return lax.shift_right_logical(div24(iota(shape, 1)), 2) == iota(shape, 0)


def exact_nt(values, select):
    high = values.astype(BF16)
    rest = values - high.astype(F32)
    mid = rest.astype(BF16)
    low = (rest - mid.astype(F32)).astype(BF16)
    return dot_nt(high, select) + dot_nt(mid, select) + dot_nt(low, select)


SCRATCH = dict(
    w_rows=((24, 3 * DM), BF16),
    w_parts=((4, 24, 3 * GROUP), BF16),
    vecs=((8, 128), F32),
    cot=((2, TOK, DM), BF16),
    b_out=((2, TOK, DM), F32),
    b_tok=((2, TOK, DM), F32),
    b_qkv=((24, 3 * DM), F32),
    b_wout=((24, DM), F32),
    b_up=((24, FF), F32),
    b_down=((96, DM), F32),
    b_vec=((8, 128), F32),
    vec_all=((32, 8, 128), F32),
    vec_rows=((8, DM), F32),
    up_row=((1, UP_N), F32),
    x_pair=((2, 2, 2, TOK, DM), BF16),
    fl_chip=((2, 2, TOK, DM), BF16),
    gf_chip=((2, 2, TOK, DM), BF16),
    ga_chip=((2, 2, TOK, DM), BF16),
    partial=((2, 2, TOK, DM), F32),
    partial_low=((2, TOK, DM), BF16),
    back0=((2, TOK, DM), BF16),
    back1=((2, TOK, DM), BF16),
    back2=((2, TOK, DM), BF16),
    tok_part=((2, 2, 2, TOK, DM), F32),
    tok_back=((2, 2, TOK, DM), F32),
    tok_send=((2, TOK, DM), BF16),
    tok_last=((2, TOK, DM), BF16),
    send_q=((PAIRS, GROUP, 256), BF16),
    qkv_t=((GROUP, SEQ), BF16),
    k_rows=((SEQ, HD), BF16),
    v_rows=((SEQ, HD), BF16),
    q_rows=((SEQ, HD), BF16),
    g_rows=((SEQ, HD), BF16),
    key_doc=((SEQ, 128), jnp.int32),
    query_doc=((1, SEQ), jnp.int32),
    scores=((SEQ, CHUNK), F32),
    weights=((SEQ, SEQ), BF16),
    total=((1, SEQ), F32),
    att_t=((HD, SEQ), F32),
    att_send=((HD, SEQ), BF16),
    mix_in=((12, HD, 128), BF16),
    g_send=((12, HD, 128), BF16),
    g_t=((HD, SEQ), BF16),
    gn_t=((HD, SEQ), BF16),
    corr=((1, SEQ), F32),
    ds=((CHUNK, SEQ), BF16),
    dq_t=((HD, SEQ), F32),
    d_send=((GROUP, SEQ), BF16),
    d_in=((PAIRS, GROUP, 256), BF16),
    mixed_t=((HALF, 2 * 128), BF16),
    first=((2 * TOK, DM), F32),
    normed1=((2 * TOK, DM), F32),
    inv1=((2 * TOK, 1), F32),
    active=((4 * TOK, UP_N), BF16),
    slope=((4 * TOK, UP_N), F32),
    gh=((4 * TOK, UP_N), BF16),
    gh2=((2 * TOK, DM), F32),
    gh1=((2 * TOK, DM), F32),
    gp_kv=((8 * TOK, 2 * GROUP), BF16),
    gp_q=((8 * TOK, GROUP), BF16),
    vec_grad=((8, DM), F32),
    up_grad=((1, UP_N), F32),
    vec_send=((32, 8, 128), F32),
    vec_recv=((32, 8, 128), F32),
)


def sum_scratch(kind):
    piece = piece_shape(kind)
    if kind in (KV, Q):
        low = [SHAPES[kind]] + [(4,) + piece] * 3
        last = (4,) + piece[2:]
    else:
        low = [SHAPES[kind], (4,) + piece, (8,) + piece, (4,) + piece, (4,) + piece]
        last = piece[1:] if by_column(kind) else piece
    return [(shape, BF16) for shape in low] + [(piece, F32), (last, F32)]


GATHERED = (QKV, OUT, UP, DOWN)
SUMMED = (OUT, UP, DOWN, KV, Q)
N_SEM = 181


def all_scratch():
    shapes = list(SCRATCH.values())
    shapes += [(SHAPES[kind], BF16) for kind in GATHERED]
    for kind in SUMMED:
        shapes += sum_scratch(kind)
    shapes += [((24,), BF16)] * 8 + [((96,), BF16)]
    return [pltpu.VMEM(shape, dtype) for shape, dtype in shapes] + [pltpu.SemaphoreType.DMA((N_SEM,))]


def layer_kernel(
    tokens, starts, w_qkv, w_out, w_up, w_down,
    v0, v1, v2, v3, v4, v5, v6, v7, v8, cotangent,
    o_out, o_tok, o_qkv, o_wout, o_up, o_down, o_vec,
    *scratch,
):
    vec_in = (v0, v1, v2, v3, v4, v5, v6, v7, v8)
    m = SimpleNamespace(**dict(zip(SCRATCH, scratch)))
    at = len(SCRATCH)
    gathered = scratch[at : at + 4]
    at += 4
    summed = []
    for kind in SUMMED:
        n = len(sum_scratch(kind))
        summed.append(scratch[at : at + n])
        at += n
    vec_rows_in = scratch[at : at + 9]
    sems = scratch[-1]
    here = Place()
    links = Links(sems, here)
    b, z, c, x = here.b, here.z, here.c, here.x
    line, chip, group = here.line, here.chip, here.group
    g_qkv = PairGather(links, here, gathered[0])
    g_out, g_up, g_down = [Gather(links, here, kind, ref) for kind, ref in zip(GATHERED[1:], gathered[1:])]
    s_out, s_up, s_down = [
        make(links, here, kind, refs)
        for make, kind, refs in zip((Scatter, Scatter, ColumnScatter), SUMMED[:3], summed[:3])
    ]
    s_kv, s_q = [PairScatter(links, here, kind, refs) for kind, refs in zip(SUMMED[3:], summed[3:])]
    ahead = (g_out, g_up)

    def peer(d):
        other = lax.rem(line + d, 32)
        return (lax.div(other, 4), lax.rem(other, 4))

    x_pair = m.x_pair

    def up_part(which):
        return w_up.at[:, pl.ds(pl.multiple_of(UP_N * which, 128), UP_N)]

    qkv_wait = links.local(w_qkv, m.w_rows)
    vec_waits = [links.local(src, dst) for src, dst in zip(vec_in, vec_rows_in)]
    x_wait = links.local(tokens, x_pair.at[:, x, c])
    up_wait = links.local(up_part(c), g_up.ref.at[g_up.col, c, z])
    row_waits = [
        links.local(shard, gather.ref.at[gather.col, z], here.stays)
        for gather, shard in ((g_out, w_out), (g_down, w_down))
    ]
    cot_wait = links.local(cotangent, m.cot)
    m.vec_grad[...] = jnp.zeros((8, DM), F32)
    m.vecs[...] = jnp.zeros((8, 128), F32)
    for wait in vec_waits:
        wait()
    for j in range(8):
        m.vecs[j : j + 1, 0:24] = vec_rows_in[j][...].astype(F32).reshape(1, 24)
    m.vecs[0:1, 32:128] = vec_rows_in[8][...].astype(F32).reshape(1, 96)
    qkv_wait()
    for k in range(4):
        for j in range(3):
            block = m.w_rows[:, DM * j + GROUP * k : DM * j + GROUP * (k + 1)]
            m.w_parts[k, :, GROUP * j : GROUP * (j + 1)] = block

    barrier = pltpu.get_barrier_semaphore()

    def greet(d, carry):
        pl.semaphore_signal(barrier, inc=1, device_id=peer(d), device_id_type=MESH)
        return carry

    lax.fori_loop(1, 32, greet, 0)
    pl.semaphore_wait(barrier, 31)

    slot = g_qkv.ref.at[here.y, x, c, z]
    links.send(m.w_parts.at[2 * c + 1 - x], slot, g_qkv.s0, g_qkv.r0, here.dx)
    links.send(m.w_parts.at[2 * (1 - c) + 1 - x], slot, g_qkv.s0, g_qkv.r0, here.dx_other)
    links.send(m.w_parts.at[2 * (1 - c) + x], slot, g_qkv.s0, g_qkv.r0, here.sib)
    x_sem = links.alloc(6)
    own_x = x_pair.at[:, x, c]
    links.send(tokens, own_x, x_sem, x_sem + 1, here.dx)
    links.send(tokens, own_x, x_sem + 2, x_sem + 3, here.sib)
    links.drain(own_x, x_sem)
    links.drain(own_x, x_sem + 2)
    up_slot = g_up.ref.at[g_up.col, c, z]
    links.send(up_part(1 - c), up_slot, g_up.s0, g_up.r0, here.sib)
    links.drain(up_slot, g_up.s0)
    for gather, shard in ((g_out, w_out), (g_down, w_down)):
        slot = gather.ref.at[2 * x + c, z]
        links.send(shard, slot, gather.s0, gather.r0, here.swap, here.moves)
        links.drain(slot, gather.s0, here.moves)
    vec_sem = links.alloc(4)
    vec_all = m.vec_all

    def vec_copy(d):
        return links.make(m.vecs, vec_all.at[line], vec_sem, vec_sem + 1, peer(d))

    def vec_start(d, carry):
        vec_copy(d).start()
        return carry

    lax.fori_loop(1, 32, vec_start, 0)
    vec_all[line] = m.vecs[...]
    g_qkv.ref[here.y, x, c, z] = m.w_parts[group]
    for wait in (x_wait, up_wait, *row_waits, cot_wait):
        wait()

    g_qkv.first_wait()
    g_qkv.own_z()
    g_qkv.spread(z)
    for gather in ahead:
        gather.first_wait()
        gather.own_plane()

    def documents():
        def position(n):
            z_part = lax.shift_left(jnp.bitwise_and(lax.shift_right_logical(n, 8), 3), 6)
            xc_part = lax.shift_left(jnp.bitwise_and(lax.shift_right_logical(n, 6), 3), 8)
            y_part = lax.shift_left(lax.shift_right_logical(n, 10), 10)
            return y_part + xc_part + z_part + jnp.bitwise_and(n, 63)

        def doc_of(n):
            place = position(n)
            doc = jnp.zeros(place.shape, jnp.int32)
            for j in range(starts.shape[1]):
                doc = doc + (starts[here.part, j] <= place).astype(jnp.int32)
            return doc

        m.query_doc[...] = doc_of(iota((1, SEQ), 1))

        def rows(i, carry):
            start = pl.multiple_of(i * 256, 256)
            m.key_doc[pl.ds(start, 256), :] = doc_of(iota((256, 128), 0) + i * 256)
            return carry

        lax.fori_loop(0, SEQ // 256, rows, 0)

    when(here.active, documents)

    other_x = x_pair.at[:, 1 - x, c]
    links.recv(other_x, x_sem + 1)
    links.send(other_x, other_x, x_sem + 4, x_sem + 5, here.sib)
    links.drain(other_x, x_sem + 4)
    g_qkv.land(here.far)
    g_qkv.hop()
    g_qkv.spread(here.far)
    for gather in ahead:
        gather.own_z()
    many = vec_all.at[pl.ds(0, 31)]
    links.sent(many, vec_sem)
    links.recv(many, vec_sem + 1)
    spread = dot(vec_all[...].reshape(256, 128).astype(BF16), select_24()).reshape(32, 8, DM)
    m.vec_rows[...] = jnp.sum(jnp.where(owner_24(32), spread, 0.0), axis=0)
    spread = dot(vec_all[pl.ds(16 * c, 16), 0, :].astype(BF16), select_96())
    m.up_row[...] = row_sum(jnp.where(owner_96(), spread, 0.0))

    def vector(j):
        return m.vec_rows[j : j + 1, :]

    def vector_group(j):
        total = jnp.zeros((1, GROUP), F32)
        for k in range(4):
            total = total + jnp.where(group == k, m.vec_rows[j : j + 1, GROUP * k : GROUP * (k + 1)], 0.0)
        return total

    g_qkv.land(here.near)
    g_qkv.spread(here.near)
    for gather in ahead:
        gather.relay(z)
    g_qkv.land(here.cross)
    g_qkv.spread(here.cross)
    for gather in ahead:
        gather.land(here.far)
        gather.hop()
        gather.spread(here.far)
    links.recv(x_pair.at[:, x, 1 - c], x_sem + 3)
    links.recv(x_pair.at[:, 1 - x, 1 - c], x_sem + 5)
    g_qkv.done()

    def weight_qkv():
        return g_qkv.ref[...].reshape(DM, 3 * GROUP)

    def x_rows():
        return x_pair[...].reshape(8 * TOK, DM)

    chip_lanes = pl.ds(pl.multiple_of(chip * 128, 128), 128)
    seat_lanes = pl.ds(pl.multiple_of(here.seat * 256, 256), 256)
    idle = jnp.logical_not(here.active)

    def seat_dev(y_to, z_to, x_to):
        return (4 * y_to + 2 * x_to + c, z_to)

    send_q, qkv_t = m.send_q, m.qkv_t
    q_sem = links.alloc(2)
    bias = jnp.concatenate([vector_group(0), jnp.zeros((1, GROUP), F32), vector_group(1)], axis=1)
    for part in range(MB):
        rows = (dot(x_pair[part].reshape(4 * TOK, DM), weight_qkv()) + bias).astype(BF16)
        turned = rows.T
        for i in range(3):
            for j in range(3):
                block = turned[GROUP * j + HD * i : GROUP * j + HD * (i + 1), :]
                if j == 0:
                    block = block * jnp.asarray(HD ** (-0.5), BF16)
                send_q[3 * part + i, HD * j : HD * (j + 1), :] = block
            pair = 3 * part + i
            other = jnp.logical_not(both(here.active, here.pair == pair))
            dev = seat_dev(*SEATS[pair], x)
            links.send(send_q.at[pair], qkv_t.at[:, seat_lanes], q_sem, q_sem + 1, dev, other)

    links.drain(send_q.at[pl.ds(0, PAIRS - 1)], q_sem, here.active)
    links.drain(send_q, q_sem, idle)

    def own_q():
        qkv_t[:, seat_lanes] = send_q[here.pair]

    when(here.active, own_q)

    class ToSeats:
        def __init__(self, src_of, dst_of, slot, slots, seats, own):
            self.src_of, self.dst_of, self.slot, self.slots = src_of, dst_of, slot, slots
            self.seats, self.own = seats, own
            self.s, self.r = links.alloc(), links.alloc()
            self.width = SEQ // seats

        def start(self, other):
            start = pl.multiple_of(self.width * other, self.width)
            src, dst = self.src_of(pl.ds(start, self.width)), self.dst_of(self.slot)
            if self.seats == 16:
                place, x_to, mine = lax.div(other, 2), lax.rem(other, 2), chip
            else:
                place, x_to, mine = other, x, here.seat
            dev = seat_dev(lax.div(place, 4), lax.rem(place, 4), x_to)
            links.send(src, dst, self.s, self.r, dev, mine != other)

        def finish(self):
            links.drain(self.src_of(pl.ds(0, SEQ - self.width)), self.s, here.active)
            when(here.active, self.own)

        def wait(self):
            links.recv(self.dst_of(pl.ds(0, self.slots - 1)), self.r, here.active)
            links.recv(self.dst_of(pl.ds(0, self.slots)), self.r, idle)

    g_down.first_wait()
    g_down.own_plane()
    for gather in ahead:
        gather.land(here.near)
        gather.spread(here.near)
    for gather in ahead:
        gather.relay(here.far)
    for gather in ahead:
        gather.land(here.cross)
        gather.spread(here.cross)
    links.recv(qkv_t.at[:, pl.ds(0, SEQ - 256)], q_sem + 1, here.active)
    g_down.own_z()
    for gather in ahead:
        gather.relay(here.near)
    g_down.relay(z)

    weights = m.weights
    mix_slot = 6 * here.part + 3 * x + here.pair - 3 * here.part

    def own_mix():
        m.mix_in[mix_slot] = m.att_send[:, chip_lanes]

    mix = ToSeats(
        lambda lanes: m.att_send.at[:, lanes], lambda slot: m.mix_in.at[slot], mix_slot, 12, 16, own_mix
    )

    def turn_keys():
        m.k_rows[...] = qkv_t[HD : 2 * HD, :].T
        m.v_rows[...] = qkv_t[2 * HD : 3 * HD, :].T
        m.q_rows[...] = qkv_t[0:HD, :].T

    when(here.active, turn_keys)

    def attend(step):
        i = 4 * lax.rem(step, 2) + lax.div(step, 2)
        lanes = pl.ds(pl.multiple_of(i * CHUNK, CHUNK), CHUNK)
        query = qkv_t[0:HD, lanes]
        doc = m.query_doc[:, lanes]
        top = None
        for k in range(8):
            rows = slice(256 * k, 256 * (k + 1))
            key_doc = m.key_doc[rows, :]
            same = jnp.concatenate([key_doc, key_doc], axis=1) == doc
            scores = jnp.where(same, dot(m.k_rows[rows, :], query), NEG)
            m.scores[rows, :] = scores
            here_top = jnp.max(scores, axis=0, keepdims=True)
            top = here_top if top is None else jnp.maximum(top, here_top)
        total = None
        for k in range(8):
            rows = slice(256 * k, 256 * (k + 1))
            grown = jnp.exp(m.scores[rows, :] - top)
            weights[rows, lanes] = grown.astype(BF16)
            part_sum = row_sum(grown)
            total = part_sum if total is None else total + part_sum
        numer = dot(qkv_t[2 * HD : 3 * HD, :], weights[:, lanes])
        attended = numer / total
        m.total[:, lanes] = total
        m.att_t[:, lanes] = attended
        m.att_send[:, lanes] = attended.astype(BF16)
        mix.start(2 * i)
        mix.start(2 * i + 1)

    def some(body, first, last):
        def run():
            def one(i, carry):
                body(i)
                return carry

            lax.fori_loop(first, last, one, 0)

        when(here.active, run)

    some(attend, 0, 4)
    for gather in ahead:
        gather.relay(here.cross)
    g_down.land(here.far)
    g_down.hop()
    g_down.spread(here.far)
    g_down.land(here.near)
    g_down.spread(here.near)
    some(attend, 4, 7)
    g_down.land(here.cross)
    g_down.spread(here.cross)
    some(attend, 7, 8)
    g_down.relay(here.far)
    g_down.relay(here.near)
    mix.finish()
    mix.wait()
    g_out.done()
    g_down.relay(here.cross)

    def share(buf, values):
        sem = links.alloc(2)
        buf[:, c] = values.reshape(MB, TOK, DM)
        links.send(buf.at[:, c], buf.at[:, c], sem, sem + 1, here.sib)
        links.drain(buf.at[:, c], sem)
        links.recv(buf.at[:, 1 - c], sem + 1)

    def combine(values, back):
        sem = links.alloc(2)
        partial, other = m.partial, m.partial_low
        partial[...] = values.reshape(MB, 2, TOK, DM)
        other[...] = partial[:, 1 - c].astype(BF16)
        links.send(other, back, sem, sem + 1, here.sib)
        links.recv(back, sem + 1)
        total = partial[:, c].reshape(2 * TOK, DM) + back[...].reshape(2 * TOK, DM).astype(F32)
        links.sent(other, sem)
        return total

    def norm_rows(values, gain, shift):
        center = values - jnp.mean(values, axis=-1, keepdims=True)
        inverse = lax.rsqrt(jnp.mean(center * center, axis=-1, keepdims=True) + EPS)
        normed = center * inverse
        return normed * gain + shift, normed, inverse

    def norm_back(upstream, normed, inverse, gain):
        scaled = upstream * gain
        return inverse * (
            scaled
            - jnp.mean(scaled, axis=-1, keepdims=True)
            - normed * jnp.mean(scaled * normed, axis=-1, keepdims=True)
        )

    mixed_t = m.mixed_t
    mixed = []
    for part in range(MB):
        piece = m.mix_in[6 * part : 6 * part + 6].reshape(HALF, 128)
        mixed_t[:, 128 * part : 128 * (part + 1)] = piece
        mixed.append(piece.T)
    mixed = jnp.concatenate(mixed, axis=0)

    def weight_out():
        return g_out.ref[...].reshape(HALF, DM)

    attn = combine(dot(mixed, weight_out()), m.back0) + vector(2)
    own_tokens = x_pair[:, x, c].reshape(2 * TOK, DM).astype(F32)
    first, normed_one, inverse_one = norm_rows(own_tokens + attn, vector(3), vector(4))
    m.first[...] = first
    m.normed1[...] = normed_one
    m.inv1[...] = inverse_one
    share(m.fl_chip, first.astype(BF16))

    g_up.done()
    def fl_rows():
        return m.fl_chip[...].reshape(4 * TOK, DM)

    def weight_up(j):
        return g_up.ref[:, :, :, :, HALF * j : HALF * (j + 1)].reshape(DM, HALF)

    def weight_down(j):
        return g_down.ref[j].reshape(HALF, DM)

    for j in range(4):
        lanes = slice(HALF * j, HALF * (j + 1))
        hidden = dot(fl_rows(), weight_up(j)) + m.up_row[:, lanes]
        cdf = 0.5 * (1.0 + lax.erf(hidden * (0.5**0.5)))
        m.slope[:, lanes] = cdf + hidden * (jnp.exp(-0.5 * hidden * hidden) * 0.3989422804014327)
        m.active[:, lanes] = (hidden * cdf).astype(BF16)
    g_down.done()
    ffn = None
    for j in range(4):
        lanes = slice(HALF * j, HALF * (j + 1))
        term = dot(m.active[:, lanes], weight_down(j))
        ffn = term if ffn is None else ffn + term
    ffn = combine(ffn, m.back1) + vector(5)
    result, normed_two, inverse_two = norm_rows(m.first[...] + ffn, vector(6), vector(7))
    m.b_out[...] = result.reshape(MB, TOK, DM)
    links.put(m.b_out, o_out)

    targets = (here.near, here.cross, here.far, z)
    vec_grad = m.vec_grad
    grad_result = m.cot[...].reshape(2 * TOK, DM).astype(F32)
    vec_grad[6:7, :] = row_sum(grad_result * normed_two)
    vec_grad[7:8, :] = row_sum(grad_result)
    grad_two = norm_back(grad_result, normed_two, inverse_two, vector(6))
    m.gh2[...] = grad_two
    grad_ffn = grad_two.astype(BF16)
    vec_grad[5:6, :] = row_sum(grad_ffn.astype(F32))
    share(m.gf_chip, grad_ffn)

    def gf_rows():
        return m.gf_chip[...].reshape(4 * TOK, DM)

    for j in range(4):
        lanes = slice(HALF * j, HALF * (j + 1))
        s_down.grad[j] = dot_tn(m.active[:, lanes], gf_rows()).astype(BF16).reshape(4, 96, DM)
    s_down.send_sides(targets)
    s_down.column_first()
    grad_first = None
    for j in range(4):
        lanes = slice(HALF * j, HALF * (j + 1))
        grad_active = dot_nt(gf_rows(), weight_down(j))
        grad_hidden = (grad_active * m.slope[:, lanes]).astype(BF16)
        m.gh[:, lanes] = grad_hidden
        m.up_grad[:, lanes] = row_sum(grad_hidden.astype(F32))
    for j in range(4):
        lanes = slice(HALF * j, HALF * (j + 1))
        term = dot_nt(m.gh[:, lanes], weight_up(j))
        grad_first = term if grad_first is None else grad_first + term
    grad_first = m.gh2[...] + combine(grad_first, m.back2)
    normed_one = m.normed1[...]
    vec_grad[3:4, :] = row_sum(grad_first * normed_one)
    vec_grad[4:5, :] = row_sum(grad_first)
    grad_one = norm_back(grad_first, normed_one, m.inv1[...], vector(3))
    m.gh1[...] = grad_one
    grad_attn = grad_one.astype(BF16)
    vec_grad[2:3, :] = row_sum(grad_attn.astype(F32))
    share(m.ga_chip, grad_attn)

    def ga_rows():
        return m.ga_chip[...].reshape(4 * TOK, DM)

    turned = dot_nt(ga_rows(), weight_out()).astype(BF16).T
    for part in range(MB):
        m.g_send[6 * part : 6 * part + 6] = turned[:, 128 * part : 128 * (part + 1)].reshape(6, HD, 128)
    g_t = m.g_t
    g_sem = links.alloc(2)
    for slot in range(12):
        part, head = slot // 6, slot % 6
        pair, x_to = 3 * part + head % 3, head // 3
        mine = both(here.active, both(here.pair == pair, x == x_to))
        dev = seat_dev(*SEATS[pair], x_to)
        links.send(m.g_send.at[slot], g_t.at[:, chip_lanes], g_sem, g_sem + 1, dev, jnp.logical_not(mine))
    links.drain(m.g_send.at[pl.ds(0, 11)], g_sem, here.active)
    links.drain(m.g_send, g_sem, idle)

    def own_g():
        g_t[:, chip_lanes] = m.g_send[mix_slot]

    when(here.active, own_g)
    for j in range(4):
        lanes = slice(HALF * j, HALF * (j + 1))
        s_up.grad[:, :, :, :, lanes] = (
            dot_tn(fl_rows(), m.gh[:, lanes]).astype(BF16).reshape(4, 2, 4, 24, HALF)
        )
    s_out.grad[...] = dot(mixed_t[...], ga_rows()).astype(BF16).reshape(SHAPES[OUT])
    s_up.send_far(targets)
    s_out.send_far(targets)
    s_up.send_sides(targets)
    s_out.send_sides(targets)

    def planes(scatter, order=targets):
        for i, t in enumerate(order):
            scatter.plane(t)
            if i < 2:
                scatter.z_first(i)

    s_down.column_second()
    planes(s_down, targets[:3])
    links.recv(g_t.at[:, pl.ds(0, SEQ - 128)], g_sem + 1, here.active)

    d_send, d_in = m.d_send, m.d_in

    def own_kv():
        d_in[here.pair, HD : 3 * HD, :] = d_send[HD : 3 * HD, seat_lanes]

    def own_dq():
        d_in[here.pair, 0:HD, :] = d_send[0:HD, seat_lanes]

    grad_kv = ToSeats(
        lambda lanes: d_send.at[pl.ds(HD, 2 * HD), lanes], lambda slot: d_in.at[slot, pl.ds(HD, 2 * HD)],
        here.pair, PAIRS, 8, own_kv,
    )
    grad_q = ToSeats(
        lambda lanes: d_send.at[pl.ds(0, HD), lanes], lambda slot: d_in.at[slot, pl.ds(0, HD)],
        here.pair, PAIRS, 8, own_dq,
    )

    def turn_grads():
        grad = g_t[...].astype(F32)
        inverse = 1.0 / m.total[...]
        numer = grad * inverse
        m.gn_t[...] = numer.astype(BF16)
        m.g_rows[...] = numer.astype(BF16).T
        m.corr[...] = row_sum(grad * m.att_t[...]) * inverse
        m.dq_t[...] = jnp.zeros((HD, SEQ), F32)

    when(here.active, turn_grads)

    def back(k):
        keys = pl.ds(pl.multiple_of(k * CHUNK, CHUNK), CHUNK)
        value = m.v_rows[keys, :]
        for i in range(4):
            lanes = slice(512 * i, 512 * (i + 1))
            grad_weights = dot(value, m.gn_t[:, lanes])
            grown = weights[keys, lanes].astype(F32)
            m.ds[:, lanes] = (grown * (grad_weights - m.corr[:, lanes])).astype(BF16)
        ds = m.ds
        d_send[HD : 2 * HD, keys] = dot(ds[...], m.q_rows[...]).T.astype(BF16)
        d_send[2 * HD : 3 * HD, keys] = dot(weights[keys, :], m.g_rows[...]).T.astype(BF16)
        grad_kv.start(k)
        m.dq_t[...] += dot(qkv_t[HD : 2 * HD, keys], ds[...])

    some(back, 0, 4)
    s_down.column_last()
    for t in targets:
        s_up.relay(t)
    for t in targets:
        s_out.relay(t)
    some(back, 4, 8)

    def last_query():
        d_send[0:HD, :] = (m.dq_t[...] * (HD ** (-0.5))).astype(BF16)
        for other in range(8):
            grad_q.start(other)

    when(here.active, last_query)
    grad_kv.finish()
    grad_q.finish()
    s_down.relay_own()
    s_down.z_second()
    planes(s_up, targets[:2])
    grad_kv.wait()
    gp_kv, gp_q = m.gp_kv, m.gp_q
    for part in range(MB):
        heads = slice(3 * part, 3 * part + 3)
        rows = [d_in[heads, HD * j : HD * (j + 1), :].reshape(GROUP, 256) for j in (1, 2)]
        gp_kv[256 * part : 256 * (part + 1), :] = jnp.concatenate(rows, axis=0).T
    s_kv.grad[...] = dot_tn(x_rows(), gp_kv[...]).astype(BF16).reshape(SHAPES[KV])
    for t in targets:
        s_kv.send(t)
    for t in targets[2:]:
        s_up.plane(t)
    planes(s_out)
    s_down.plane(z)
    s_up.z_second()
    grad_q.wait()
    for part in range(MB):
        gp_q[256 * part : 256 * (part + 1), :] = d_in[3 * part : 3 * part + 3, 0:HD, :].reshape(GROUP, 256).T
    s_q.grad[...] = dot_tn(x_rows(), gp_q[...]).astype(BF16).reshape(SHAPES[Q])
    for t in targets:
        s_q.send(t)
    planes(s_kv)
    s_out.z_second()
    all_weights = weight_qkv()
    t_sem = links.alloc(4)
    for part in range(MB):
        rows = slice(256 * part, 256 * (part + 1))
        terms = dot_nt(gp_q[rows, :], all_weights[:, 0:GROUP]) + dot_nt(gp_kv[rows, :], all_weights[:, GROUP:])
        m.tok_part[part] = terms.reshape(2, 2, TOK, DM)
    links.send(m.tok_part.at[:, :, 1 - c], m.tok_back, t_sem, t_sem + 1, here.sib)
    links.drain(m.tok_back, t_sem)
    sum_q = row_sum(gp_q[...].astype(F32))
    sum_v = row_sum(gp_kv[:, GROUP:].astype(F32))
    for k in range(4):
        lanes = slice(GROUP * k, GROUP * (k + 1))
        vec_grad[0:1, lanes] = jnp.where(group == k, sum_q, 0.0)
        vec_grad[1:2, lanes] = jnp.where(group == k, sum_v, 0.0)
    links.recv(m.tok_back, t_sem + 1)
    for part in range(MB):
        m.tok_send[part] = (m.tok_part[part, 1 - x, c] + m.tok_back[part, 1 - x]).astype(BF16)
    links.send(m.tok_send, m.tok_last, t_sem + 2, t_sem + 3, here.dx)
    links.drain(m.tok_send, t_sem + 2)

    planes(s_q)
    s_kv.z_second()
    s_q.z_second()
    vec_send, vec_recv = m.vec_send, m.vec_recv
    spread = jnp.where(owner_24(32), vec_grad[...][None], 0.0).reshape(256, DM)
    vec_send[...] = exact_nt(spread, select_24()).reshape(32, 8, 128)
    spread = jnp.where(owner_96(), m.up_grad[...], 0.0)
    own_lines = pl.ds(16 * c, 16)
    vec_send[own_lines, 0, :] = vec_send[own_lines, 0, :] + exact_nt(spread, select_96())

    def grad_start(d, carry):
        other = lax.rem(line + d, 32)
        links.make(vec_send.at[other], vec_recv.at[line], vec_sem + 2, vec_sem + 3, peer(d)).start()
        return carry

    lax.fori_loop(1, 32, grad_start, 0)
    vec_recv[line] = vec_send[line]

    s_kv.z_last()
    s_down.z_last()
    s_out.z_last()
    s_up.z_last()
    s_q.z_last()
    links.recv(m.tok_last, t_sem + 3)
    for part in range(MB):
        rows = slice(TOK * part, TOK * (part + 1))
        own = m.tok_part[part, x, c] + m.tok_back[part, x]
        m.b_tok[part] = m.gh1[rows, :] + (own + m.tok_last[part].astype(F32))
    links.put(m.b_tok, o_tok)
    many_send, many_recv = vec_send.at[pl.ds(0, 31)], vec_recv.at[pl.ds(0, 31)]
    links.sent(many_send, vec_sem + 2)
    links.recv(many_recv, vec_sem + 3)
    m.b_vec[...] = jnp.sum(vec_recv[...], axis=0)
    links.put(m.b_vec, o_vec)
    s_down.finish(m.b_down)
    links.put(m.b_down, o_down)
    s_out.finish(m.b_wout)
    links.put(m.b_wout, o_wout)
    s_up.finish(m.b_up)
    links.put(m.b_up, o_up)
    s_kv.finish(m.b_qkv)
    s_q.finish(m.b_qkv)
    links.put(m.b_qkv, o_qkv)
    links.finish()


def place_kernel(*refs):
    ins, big_out, vec_out = refs[0:7], refs[7:13], refs[13:22]
    held, rows, sems = refs[22:29], refs[29:38], refs[38]
    loads = [pltpu.make_async_copy(src, dst, sems.at[i]) for i, (src, dst) in enumerate(zip(ins, held))]
    for load in reversed(loads):
        load.start()
    stores = [pltpu.make_async_copy(src, dst, sems.at[7 + i]) for i, (src, dst) in enumerate(zip(held, big_out))]
    stores += [pltpu.make_async_copy(src, dst, sems.at[13 + i]) for i, (src, dst) in enumerate(zip(rows, vec_out))]
    loads[6].wait()
    for j in range(8):
        rows[j][...] = held[6][j, 0:24]
    rows[8][...] = held[6][0, 32:128]
    for store in stores[6:]:
        store.start()
    for load, store in zip(loads, stores[:6]):
        load.wait()
        store.start()
    for store in stores:
        store.wait()


def fused(
    tokens, starts, w_qkv, bias_q, bias_v, w_out, bias_out, gain_one, shift_one,
    w_up, bias_up, w_down, bias_down, gain_two, shift_two, cotangent,
):
    anywhere = pl.BlockSpec(memory_space=pl.ANY)
    vectors = (bias_q, bias_v, bias_out, gain_one, shift_one, bias_down, gain_two, shift_two, bias_up)
    big = [tokens.shape, tokens.shape, w_qkv.shape, w_out.shape, w_up.shape, w_down.shape]
    big = [jax.ShapeDtypeStruct(shape, F32) for shape in big]
    small = [jax.ShapeDtypeStruct(vector.shape, F32) for vector in vectors]
    made = pl.pallas_call(
        layer_kernel,
        name="layer",
        out_shape=big + [jax.ShapeDtypeStruct((8, 128), F32)],
        in_specs=[anywhere, pl.BlockSpec(memory_space=pltpu.SMEM)] + [anywhere] * 14,
        out_specs=[anywhere] * 7,
        scratch_shapes=all_scratch(),
        compiler_params=pltpu.CompilerParams(
            collective_id=0, has_side_effects=True, vmem_limit_bytes=63 * 2**20
        ),
    )(tokens, starts, w_qkv, w_out, w_up, w_down, *vectors, cotangent)
    placed = pl.pallas_call(
        place_kernel,
        name="place",
        out_shape=big + small,
        in_specs=[anywhere] * 7,
        out_specs=[anywhere] * 15,
        scratch_shapes=[pltpu.VMEM(array.shape, F32) for array in (*made, *vectors)]
        + [pltpu.SemaphoreType.DMA((22,))],
    )(*made)
    out, tok, g_qkv, g_wout, g_up, g_down, bq, bv, bo, g1, s1, bd, g2, s2, bup = placed
    return (out, tok, g_qkv, bq, bv, g_wout, bo, g1, s1, g_up, bup, g_down, bd, g2, s2)


def solution(mesh):
    small = dict(mesh.shape) == {BLK: 8, HEAD: 4}
    return jax.shard_map(
        fused if small else per_device,
        mesh=mesh,
        in_specs=(
            P(None, BOTH, None),
            P(),
            P(BOTH, None),
            P(BOTH),
            P(BOTH),
            P(BOTH, None),
            P(BOTH),
            P(BOTH),
            P(BOTH),
            P(BOTH, None),
            P(BOTH),
            P(BOTH, None),
            P(BOTH),
            P(BOTH),
            P(BOTH),
            P(None, BOTH, None),
        ),
        out_specs=(
            P(None, BOTH, None),
            P(None, BOTH, None),
            P(BOTH, None),
            P(BOTH),
            P(BOTH),
            P(BOTH, None),
            P(BOTH),
            P(BOTH),
            P(BOTH),
            P(BOTH, None),
            P(BOTH),
            P(BOTH, None),
            P(BOTH),
            P(BOTH),
            P(BOTH),
        ),
        check_vma=False,
    )
```

```python
from functools import partial
from types import SimpleNamespace

import jax
import jax.numpy as jnp
from jax import lax
from jax.experimental import pallas as pl
from jax.experimental.pallas import tpu as pltpu
from jax.sharding import PartitionSpec as P

BLK = "blk"
HEAD = "head"
BOTH = (BLK, HEAD)
H = 12
HD = 64
MB = 2


EPS = 1e-05
NEG = -1e30


def norm_forward(values, gain_vec, shift_vec):
    center = values - jnp.mean(values, axis=-1, keepdims=True)
    inverse = lax.rsqrt(jnp.mean(center * center, axis=-1, keepdims=True) + EPS)
    normed = center * inverse
    return (normed * gain_vec + shift_vec, normed, inverse)


def norm_backward(upstream, normed, inverse, gain_vec):
    scaled = upstream * gain_vec
    inner = (
        scaled
        - jnp.mean(scaled, axis=-1, keepdims=True)
        - normed * jnp.mean(scaled * normed, axis=-1, keepdims=True)
    )
    return inner * inverse


def segment_of(starts_row, positions):
    return jnp.sum((starts_row[None, :] <= positions[:, None]).astype(jnp.int32), axis=1) - 1


def masked_scores(query_heads, key_heads, in_doc):
    scores = jnp.einsum(
        "qhd,khd->hqk", query_heads, key_heads, preferred_element_type=jnp.float32
    ) * HD ** (-0.5)
    return jnp.where(in_doc, scores, NEG)


def score_grads(query_heads, key_heads, value_heads, grad_numer, row_top, correction, in_doc):
    exp_score = jnp.where(
        in_doc, jnp.exp(masked_scores(query_heads, key_heads, in_doc) - row_top), 0.0
    )
    grad_weights = jnp.einsum(
        "qhd,khd->hqk", grad_numer, value_heads, preferred_element_type=jnp.float32
    )
    grad_scores = (exp_score * (grad_weights - correction)).astype(jnp.bfloat16)
    return (exp_score.astype(jnp.bfloat16), grad_scores)


def scatter_end(parts):
    (
        grad_proj_in,
        grad_query_bias,
        grad_value_bias,
        grad_proj_out,
        grad_out_bias,
        grad_norm_gain,
        grad_norm_shift,
        grad_up,
        grad_up_bias,
        grad_down,
        grad_down_bias,
        grad_final_gain,
        grad_final_shift,
    ) = parts
    return (
        lax.psum_scatter(grad_proj_in, BOTH, scatter_dimension=0, tiled=True),
        lax.psum_scatter(grad_query_bias, BOTH, scatter_dimension=0, tiled=True),
        lax.psum_scatter(grad_value_bias, BOTH, scatter_dimension=0, tiled=True),
        lax.psum_scatter(grad_proj_out, BOTH, scatter_dimension=0, tiled=True),
        lax.psum_scatter(grad_out_bias, BOTH, scatter_dimension=0, tiled=True),
        lax.psum_scatter(grad_norm_gain, BOTH, scatter_dimension=0, tiled=True),
        lax.psum_scatter(grad_norm_shift, BOTH, scatter_dimension=0, tiled=True),
        lax.psum_scatter(grad_up, BOTH, scatter_dimension=0, tiled=True),
        lax.psum_scatter(grad_up_bias, BOTH, scatter_dimension=0, tiled=True),
        lax.psum_scatter(grad_down, BOTH, scatter_dimension=0, tiled=True),
        lax.psum_scatter(grad_down_bias, BOTH, scatter_dimension=0, tiled=True),
        lax.psum_scatter(grad_final_gain, BOTH, scatter_dimension=0, tiled=True),
        lax.psum_scatter(grad_final_shift, BOTH, scatter_dimension=0, tiled=True),
    )


def per_device(
    tokens,
    starts,
    w_qkv,
    bias_q,
    bias_v,
    w_out,
    bias_out,
    gain_one,
    shift_one,
    w_up,
    bias_up,
    w_down,
    bias_down,
    gain_two,
    shift_two,
    cotangent,
):
    (
        proj_in,
        query_bias,
        value_bias,
        proj_out,
        out_bias,
        norm_gain,
        norm_shift,
        up_full,
        up_bias,
        down_full,
        down_bias,
        final_gain,
        final_shift,
    ) = (
        lax.all_gather(w_qkv, BOTH, axis=0, tiled=True),
        lax.all_gather(bias_q, BOTH, axis=0, tiled=True),
        lax.all_gather(bias_v, BOTH, axis=0, tiled=True),
        lax.all_gather(w_out, BOTH, axis=0, tiled=True),
        lax.all_gather(bias_out, BOTH, axis=0, tiled=True),
        lax.all_gather(gain_one, BOTH, axis=0, tiled=True),
        lax.all_gather(shift_one, BOTH, axis=0, tiled=True),
        lax.all_gather(w_up, BOTH, axis=0, tiled=True),
        lax.all_gather(bias_up, BOTH, axis=0, tiled=True),
        lax.all_gather(w_down, BOTH, axis=0, tiled=True),
        lax.all_gather(bias_down, BOTH, axis=0, tiled=True),
        lax.all_gather(gain_two, BOTH, axis=0, tiled=True),
        lax.all_gather(shift_two, BOTH, axis=0, tiled=True),
    )
    query_bias = query_bias.astype(jnp.float32)
    value_bias = value_bias.astype(jnp.float32)
    out_bias = out_bias.astype(jnp.float32)
    norm_gain = norm_gain.astype(jnp.float32)
    norm_shift = norm_shift.astype(jnp.float32)
    up_bias = up_bias.astype(jnp.float32)
    down_bias = down_bias.astype(jnp.float32)
    final_gain = final_gain.astype(jnp.float32)
    final_shift = final_shift.astype(jnp.float32)
    model_width = proj_out.shape[0]
    row_count = tokens.shape[1]
    head_count = lax.axis_size(HEAD)
    block_rows = row_count * head_count
    heads_dev = H // head_count
    local_width = heads_dev * HD
    scale = HD ** (-0.5)
    local_pos = lax.axis_index(BLK) * block_rows + jnp.arange(block_rows, dtype=jnp.int32)
    kept_list = []
    outputs = []
    for part_index in range(MB):
        inputs = tokens[part_index]
        starts_row = starts[part_index]
        projected = jnp.dot(inputs, proj_in, preferred_element_type=jnp.float32)
        query_rows = (projected[:, :model_width] + query_bias).astype(jnp.bfloat16)
        key_rows = projected[:, model_width : 2 * model_width].astype(jnp.bfloat16)
        value_rows = (projected[:, 2 * model_width :] + value_bias).astype(jnp.bfloat16)
        query_loc, key_loc, value_loc = (
            lax.all_to_all(query_rows, HEAD, split_axis=1, concat_axis=0, tiled=True),
            lax.all_to_all(key_rows, HEAD, split_axis=1, concat_axis=0, tiled=True),
            lax.all_to_all(value_rows, HEAD, split_axis=1, concat_axis=0, tiled=True),
        )
        doc_local = segment_of(starts_row, local_pos)
        query_heads = query_loc.reshape(block_rows, heads_dev, HD)

        def fold_keys(running, portion):
            row_top, row_total, weighted = running
            key_part, value_part = portion
            piece_len = key_part.shape[0]
            key_doc = segment_of(starts_row, jnp.arange(piece_len, dtype=jnp.int32))
            in_doc = (doc_local[:, None] == key_doc[None, :])[None]
            scores = masked_scores(query_heads, key_part.reshape(piece_len, heads_dev, HD), in_doc)
            new_top = jnp.maximum(row_top, jnp.max(scores, axis=-1, keepdims=True))
            exp_score = jnp.where(in_doc, jnp.exp(scores - new_top), 0.0)
            row_total = jnp.sum(exp_score, axis=-1, keepdims=True)
            weighted = jnp.einsum(
                "hqk,khd->hqd",
                exp_score.astype(jnp.bfloat16),
                value_part.reshape(piece_len, heads_dev, HD),
                preferred_element_type=jnp.float32,
            )
            return (new_top, row_total, weighted)

        start_state = (
            jnp.full((heads_dev, block_rows, 1), NEG, jnp.float32),
            jnp.zeros((heads_dev, block_rows, 1), jnp.float32),
            jnp.zeros((heads_dev, block_rows, HD), jnp.float32),
        )
        row_top, row_total, weighted = fold_keys(
            start_state,
            (
                lax.all_gather(key_loc, BLK, axis=0, tiled=True),
                lax.all_gather(value_loc, BLK, axis=0, tiled=True),
            ),
        )
        attended = jnp.transpose(weighted / row_total, (1, 0, 2))
        mixed_rows = lax.all_to_all(
            attended.reshape(block_rows, local_width).astype(jnp.bfloat16),
            HEAD,
            split_axis=0,
            concat_axis=1,
            tiled=True,
        )
        attn_out = jnp.dot(mixed_rows, proj_out, preferred_element_type=jnp.float32) + out_bias
        first_norm, normed_one, inverse_one = norm_forward(
            inputs.astype(jnp.float32) + attn_out, norm_gain, norm_shift
        )
        first_low = first_norm.astype(jnp.bfloat16)
        hidden = jnp.dot(first_low, up_full, preferred_element_type=jnp.float32) + up_bias
        active = jax.nn.gelu(hidden, approximate=False).astype(jnp.bfloat16)
        ffn_out = jnp.dot(active, down_full, preferred_element_type=jnp.float32) + down_bias
        result, normed_two, inverse_two = norm_forward(
            first_norm + ffn_out, final_gain, final_shift
        )
        outputs.append(result)
        kept_list.append(
            (
                inputs,
                starts_row,
                query_loc,
                key_loc,
                value_loc,
                doc_local,
                row_top,
                row_total,
                attended,
                mixed_rows,
                normed_one,
                inverse_one,
                first_low,
                hidden,
                active,
                normed_two,
                inverse_two,
            )
        )
    input_grads = []
    grad_sum = None
    for part_index in range(MB):
        (
            inputs,
            starts_row,
            query_loc,
            key_loc,
            value_loc,
            doc_local,
            row_top,
            row_total,
            attended,
            mixed_rows,
            normed_one,
            inverse_one,
            first_low,
            hidden,
            active,
            normed_two,
            inverse_two,
        ) = kept_list[part_index]
        grad_result = cotangent[part_index].astype(jnp.float32)
        grad_final_gain = jnp.sum(grad_result * normed_two, axis=0)
        grad_final_shift = jnp.sum(grad_result, axis=0)
        grad_two = norm_backward(grad_result, normed_two, inverse_two, final_gain)
        grad_ffn = grad_two.astype(jnp.bfloat16)
        grad_down_bias = jnp.sum(grad_ffn.astype(jnp.float32), axis=0)
        grad_down = jnp.einsum("rf,rd->fd", active, grad_ffn, preferred_element_type=jnp.float32)
        grad_active = jnp.einsum(
            "rd,fd->rf", grad_ffn, down_full, preferred_element_type=jnp.float32
        )
        gelu_pull = jax.vjp(partial(jax.nn.gelu, approximate=False), hidden)[1]
        grad_hidden = gelu_pull(grad_active)[0].astype(jnp.bfloat16)
        grad_up_bias = jnp.sum(grad_hidden.astype(jnp.float32), axis=0)
        grad_up = jnp.einsum(
            "rd,rf->df", first_low, grad_hidden, preferred_element_type=jnp.float32
        )
        grad_first = grad_two + jnp.einsum(
            "rf,df->rd", grad_hidden, up_full, preferred_element_type=jnp.float32
        )
        grad_norm_gain = jnp.sum(grad_first * normed_one, axis=0)
        grad_norm_shift = jnp.sum(grad_first, axis=0)
        grad_one = norm_backward(grad_first, normed_one, inverse_one, norm_gain)
        grad_attn = grad_one.astype(jnp.bfloat16)
        grad_out_bias = jnp.sum(grad_attn.astype(jnp.float32), axis=0)
        grad_proj_out = jnp.einsum(
            "rc,rd->cd", mixed_rows, grad_attn, preferred_element_type=jnp.float32
        )
        grad_mixed = jnp.einsum(
            "rd,cd->rc", grad_attn, proj_out, preferred_element_type=jnp.float32
        ).astype(jnp.bfloat16)
        grad_loc = lax.all_to_all(grad_mixed, HEAD, split_axis=1, concat_axis=0, tiled=True)
        grad_heads = grad_loc.astype(jnp.float32).reshape(block_rows, heads_dev, HD)
        total_rows = jnp.transpose(row_total, (1, 0, 2))
        correction = jnp.transpose(
            jnp.sum(grad_heads * attended, axis=-1, keepdims=True) / total_rows, (1, 0, 2)
        )
        grad_numer = (grad_heads / total_rows).astype(jnp.bfloat16)
        query_heads = query_loc.reshape(block_rows, heads_dev, HD)
        key_heads_loc = key_loc.reshape(block_rows, heads_dev, HD)
        value_heads_loc = value_loc.reshape(block_rows, heads_dev, HD)
        fold_key_part = lax.all_gather(key_loc, BLK, axis=0, tiled=True)
        fold_value_part = lax.all_gather(value_loc, BLK, axis=0, tiled=True)
        fold_piece_len = fold_key_part.shape[0]
        fold_key_doc = segment_of(starts_row, jnp.arange(fold_piece_len, dtype=jnp.int32))
        fold_in_doc = (doc_local[:, None] == fold_key_doc[None, :])[None]
        key_heads = fold_key_part.reshape(fold_piece_len, heads_dev, HD)
        exp_low, grad_scores = score_grads(
            query_heads,
            key_heads,
            fold_value_part.reshape(fold_piece_len, heads_dev, HD),
            grad_numer,
            row_top,
            correction,
            fold_in_doc,
        )
        grad_query = (
            jnp.einsum("hqk,khd->qhd", grad_scores, key_heads, preferred_element_type=jnp.float32)
            * scale
        )
        top_rows = jnp.transpose(row_top[:, :, 0])
        corr_rows = jnp.transpose(correction[:, :, 0])

        def fold_keygrad(portion):
            query_part, numer_part, top_part, corr_part = portion
            piece_len = query_part.shape[0]
            query_doc = segment_of(starts_row, jnp.arange(piece_len, dtype=jnp.int32))
            in_doc = (query_doc[:, None] == doc_local[None, :])[None]
            query_piece = query_part.reshape(piece_len, heads_dev, HD)
            numer_piece = numer_part.reshape(piece_len, heads_dev, HD)
            exp_low, grad_scores = score_grads(
                query_piece,
                key_heads_loc,
                value_heads_loc,
                numer_piece,
                jnp.transpose(top_part)[:, :, None],
                jnp.transpose(corr_part)[:, :, None],
                in_doc,
            )
            grad_key_run = (
                jnp.einsum(
                    "hqk,qhd->khd", grad_scores, query_piece, preferred_element_type=jnp.float32
                )
                * scale
            )
            grad_value_run = jnp.einsum(
                "hqk,qhd->khd", exp_low, numer_piece, preferred_element_type=jnp.float32
            )
            return (grad_key_run, grad_value_run)

        grad_key, grad_value = fold_keygrad(
            (
                lax.all_gather(query_loc, BLK, axis=0, tiled=True),
                lax.all_gather(
                    grad_numer.reshape(block_rows, local_width), BLK, axis=0, tiled=True
                ),
                lax.all_gather(top_rows.astype(jnp.bfloat16), BLK, axis=0, tiled=True).astype(
                    jnp.float32
                ),
                lax.all_gather(corr_rows.astype(jnp.bfloat16), BLK, axis=0, tiled=True).astype(
                    jnp.float32
                ),
            )
        )
        grad_q_rows, grad_k_rows, grad_v_rows = (
            lax.all_to_all(
                grad_query.reshape(block_rows, local_width).astype(jnp.bfloat16),
                HEAD,
                split_axis=0,
                concat_axis=1,
                tiled=True,
            ),
            lax.all_to_all(
                grad_key.reshape(block_rows, local_width).astype(jnp.bfloat16),
                HEAD,
                split_axis=0,
                concat_axis=1,
                tiled=True,
            ),
            lax.all_to_all(
                grad_value.reshape(block_rows, local_width).astype(jnp.bfloat16),
                HEAD,
                split_axis=0,
                concat_axis=1,
                tiled=True,
            ),
        )
        grad_proj = jnp.concatenate([grad_q_rows, grad_k_rows, grad_v_rows], axis=1)
        grad_query_bias = jnp.sum(grad_q_rows.astype(jnp.float32), axis=0)
        grad_value_bias = jnp.sum(grad_v_rows.astype(jnp.float32), axis=0)
        grad_proj_in = jnp.einsum(
            "rd,re->de", inputs, grad_proj, preferred_element_type=jnp.float32
        )
        input_grads.append(
            grad_one
            + jnp.einsum("re,de->rd", grad_proj, proj_in, preferred_element_type=jnp.float32)
        )
        part_grads = (
            grad_proj_in,
            grad_query_bias,
            grad_value_bias,
            grad_proj_out,
            grad_out_bias,
            grad_norm_gain,
            grad_norm_shift,
            grad_up,
            grad_up_bias,
            grad_down,
            grad_down_bias,
            grad_final_gain,
            grad_final_shift,
        )
        grad_sum = (
            part_grads
            if grad_sum is None
            else tuple((left + right for left, right in zip(grad_sum, part_grads)))
        )
    grad_sum = scatter_end(grad_sum)
    (
        grad_proj_in,
        grad_query_bias,
        grad_value_bias,
        grad_proj_out,
        grad_out_bias,
        grad_norm_gain,
        grad_norm_shift,
        grad_up,
        grad_up_bias,
        grad_down,
        grad_down_bias,
        grad_final_gain,
        grad_final_shift,
    ) = grad_sum
    return (
        jnp.stack(outputs),
        jnp.stack(input_grads),
        grad_proj_in,
        grad_query_bias,
        grad_value_bias,
        grad_proj_out,
        grad_out_bias,
        grad_norm_gain,
        grad_norm_shift,
        grad_up,
        grad_up_bias,
        grad_down,
        grad_down_bias,
        grad_final_gain,
        grad_final_shift,
    )


MESH = pl.DeviceIdType.MESH
F32 = jnp.float32
BF16 = jnp.bfloat16
DM = 768
FF = 3072
TOK = 64
SEQ = 2048
HALF = DM // 2
GROUP = 3 * HD
UP_N = FF // 2
CHUNK = 256
PAIRS = 6

QKV, OUT, UP, DOWN, KV, Q = range(6)
SHAPES = (
    (2, 2, 2, 4, 24, 3 * GROUP),
    (4, 4, 24, DM),
    (4, 2, 4, 24, UP_N),
    (4, 4, 96, DM),
    (2, 2, 2, 4, 24, 2 * GROUP),
    (2, 2, 2, 4, 24, GROUP),
)


def by_column(kind):
    return kind == UP


def piece_shape(kind):
    shape = SHAPES[kind]
    if kind in (QKV, KV, Q):
        return shape[1:3] + shape[4:]
    return (2,) + shape[3:] if by_column(kind) else shape[2:]


def when(cond, run):
    if cond is None:
        run()
    else:
        pl.when(cond)(run)


def both(left, right):
    return jnp.logical_and(left, right)


class Place:
    def __init__(self):
        b = lax.axis_index(BLK)
        z = lax.axis_index(HEAD)
        c = lax.rem(b, 2)
        x = lax.rem(lax.div(b, 2), 2)
        y = lax.div(b, 4)
        self.b, self.z, self.c, self.x, self.y = b, z, c, x, y
        self.line = 4 * b + z
        self.sib = (b + 1 - 2 * c, z)
        self.dx = (4 * y + 2 * (1 - x) + c, z)
        self.dy = (4 * (1 - y) + 2 * x + c, z)
        self.dx_other = (4 * y + 2 * (1 - x) + 1 - c, z)
        self.near = z + 1 - 2 * lax.rem(z, 2)
        self.far = lax.rem(z + 2, 4)
        self.cross = 3 - z
        self.swap = (4 * c + 2 * x + y, z)
        self.stays = y == c
        self.moves = y != c
        self.group = 2 * c + x
        self.seat = 4 * y + z
        self.chip = 2 * self.seat + x
        idle = jnp.logical_or(both(z == 0, y == 1), both(z == 3, y == 0))
        self.active = jnp.logical_not(idle)
        inner = jnp.where(z == 1, 4 * y, 1 + 4 * y)
        outer = jnp.where(z == 0, 2, 3)
        self.pair = jnp.where(jnp.logical_or(z == 1, z == 2), inner, outer)
        self.part = lax.div(self.pair, 3)

    def cols(self, kind):
        x, y = self.x, self.y
        if by_column(kind):
            return (2 * y + x, 2 * y + 1 - x, 2 * (1 - y) + x, 2 * (1 - y) + 1 - x)
        return (2 * x + y, 2 * (1 - x) + y, 2 * x + 1 - y, 2 * (1 - x) + 1 - y)


SEATS = ((0, 1), (0, 2), (0, 0), (1, 3), (1, 1), (1, 2))


def chunk(kind, ref, col, z):
    return ref.at[col, :, z] if by_column(kind) else ref.at[col, z]


class Links:
    def __init__(self, sems, here):
        self.sems, self.here, self.count = sems, here, 0
        self.waits = []

    def alloc(self, n=1):
        at = self.count
        self.count += n
        return at

    def make(self, src, dst, s, r, dev):
        return pltpu.make_async_remote_copy(
            src_ref=src, dst_ref=dst, send_sem=self.sems.at[s], recv_sem=self.sems.at[r],
            device_id=dev, device_id_type=MESH,
        )

    def send(self, src, dst, s, r, dev, cond=None):
        when(cond, lambda: self.make(src, dst, s, r, dev).start())

    def recv(self, dst, r, cond=None):
        when(cond, lambda: self.make(dst, dst, r, r, self.here.sib).wait_recv())

    def sent(self, src, s, cond=None):
        when(cond, lambda: self.make(src, src, s, s, self.here.sib).wait_send())

    def drain(self, like, s, cond=None):
        self.waits.append(lambda: self.sent(like, s, cond))

    def local(self, src, dst, cond=None):
        sem = self.sems.at[self.alloc()]
        when(cond, lambda: pltpu.make_async_copy(src, dst, sem).start())
        return lambda: when(cond, lambda: pltpu.make_async_copy(src, dst, sem).wait())

    def put(self, src, dst):
        self.waits.append(self.local(src, dst))

    def finish(self):
        for wait in self.waits:
            wait()


class Gather:
    def __init__(self, links, here, kind, ref):
        self.links, self.here, self.kind, self.ref = links, here, kind, ref
        self.s0, self.r0 = links.alloc(), links.alloc()
        self.sz, self.rz = links.alloc(), links.alloc(4)
        self.s_plane, self.s_relay = links.alloc(), links.alloc()
        self.r_relay, self.r_rest = links.alloc(4), links.alloc()
        self.col, self.col_x, self.col_y, self.col_d = here.cols(kind)
        links.drain(ref.at[0, :, pl.ds(0, 3)] if by_column(kind) else ref.at[0, pl.ds(0, 3)], self.sz)
        links.drain(ref.at[pl.ds(0, 2)], self.s_plane)
        links.drain(ref.at[0], self.s_relay)

    def first_wait(self):
        here = self.here
        if by_column(self.kind):
            self.links.recv(self.ref.at[self.col, 1 - here.c, here.z], self.r0)
        else:
            self.links.recv(self.ref.at[self.col, here.z], self.r0, here.moves)

    def piece(self, col, z):
        return chunk(self.kind, self.ref, col, z)

    def z_hop(self, z, to):
        piece = self.piece(self.col, z)
        self.links.send(piece, piece, self.sz, self.rz + z, (self.here.b, to))

    def spread(self, z):
        piece = self.piece(self.col, z)
        on_y = z < 1
        to_x = jnp.where(on_y, self.r_relay + z, self.r_rest)
        to_y = jnp.where(on_y, self.r_rest, self.r_relay + z)
        self.links.send(piece, piece, self.s_plane, to_x, self.here.dx)
        self.links.send(piece, piece, self.s_plane, to_y, self.here.dy)

    def own_z(self):
        here = self.here
        self.z_hop(here.z, here.far)
        self.z_hop(here.z, here.near)

    def own_plane(self):
        self.spread(self.here.z)

    def land(self, z):
        self.links.recv(self.piece(self.col, z), self.rz + z)

    def hop(self):
        self.z_hop(self.here.far, self.here.near)

    def relay(self, z):
        here = self.here
        on_y = z < 1
        piece = self.piece(jnp.where(on_y, self.col_x, self.col_y), z)
        self.links.recv(piece, self.r_relay + z)
        dev = (jnp.where(on_y, here.dy[0], here.dx[0]), here.z)
        self.links.send(piece, piece, self.s_relay, self.r_rest, dev)

    def done(self):
        self.links.recv(self.ref.at[pl.ds(0, 2)], self.r_rest)


class PairGather:
    def __init__(self, links, here, ref):
        self.links, self.here, self.ref = links, here, ref
        self.s0, self.r0 = links.alloc(), links.alloc()
        self.sz, self.rz = links.alloc(), links.alloc(4)
        self.sy, self.ry = links.alloc(), links.alloc()
        links.drain(ref.at[0, 0, 0, pl.ds(0, 3)], self.s0)
        links.drain(ref.at[0, :, :, pl.ds(0, 3)], self.sz)
        links.drain(ref.at[0], self.sy)

    def first_wait(self):
        self.links.recv(self.ref.at[0, 0, 0, pl.ds(0, 3)], self.r0)

    def piece(self, z):
        return self.ref.at[self.here.y, :, :, z]

    def z_hop(self, z, to):
        self.links.send(self.piece(z), self.piece(z), self.sz, self.rz + z, (self.here.b, to))

    def own_z(self):
        here = self.here
        self.z_hop(here.z, here.far)
        self.z_hop(here.z, here.near)

    def land(self, z):
        self.links.recv(self.piece(z), self.rz + z)

    def hop(self):
        self.z_hop(self.here.far, self.here.near)

    def spread(self, z):
        self.links.send(self.piece(z), self.piece(z), self.sy, self.ry, self.here.dy)

    def done(self):
        self.links.recv(self.ref.at[0], self.ry)


def add_blocks(dst, terms, blocks):
    for at in blocks:
        total = terms[0][at].astype(F32)
        for term in terms[1:]:
            total = total + term[at].astype(F32)
        dst[at] = total.astype(dst.dtype)


class Scatter:
    def __init__(self, links, here, kind, refs):
        self.links, self.here, self.kind = links, here, kind
        self.tilt = 2
        self.grad, self.far, self.cxy, self.zb, self.zr, self.fin, self.last = refs
        self.s_first, self.s_relay, self.sz = links.alloc(), links.alloc(), links.alloc()
        self.r_far, self.r_plane, self.rz = links.alloc(4), links.alloc(4), links.alloc(3)
        self.s_end, self.r_end = links.alloc(), links.alloc()
        self.col, self.col_x, self.col_y, self.col_d = here.cols(kind)
        links.drain(self.cxy, self.s_first)
        links.drain(self.far, self.s_relay)
        links.drain(self.zr.at[pl.ds(0, 3)], self.sz)
        if by_column(kind):
            links.drain(self.last, self.s_end)
        else:
            links.drain(self.last, self.s_end, here.moves)

    def piece(self, col, z):
        return chunk(self.kind, self.grad, col, z)

    def add(self, dst, terms):
        add_blocks(dst, terms, [(h,) for h in range(2)] if by_column(self.kind) else [(slice(0, None),)])

    def side(self, z, to_x, sem):
        here = self.here
        col = jnp.where(to_x, self.col_x, self.col_y)
        dev = (jnp.where(to_x, here.dx[0], here.dy[0]), here.z)
        slot = jnp.where(to_x, z, 4 + z)
        self.links.send(self.piece(col, z), self.cxy.at[slot], sem, self.r_plane + z, dev)

    def send_far(self, order):
        here = self.here
        for z in order:
            to_x = z >= self.tilt
            dev = (jnp.where(to_x, here.dx[0], here.dy[0]), here.z)
            self.links.send(self.piece(self.col_d, z), self.far.at[z], self.s_first, self.r_far + z, dev)

    def send_sides(self, order):
        for z in order:
            self.side(z, z >= self.tilt, self.s_first)

    def relay(self, z):
        to_y = z >= self.tilt
        self.links.recv(self.far.at[z], self.r_far + z)
        piece = self.piece(jnp.where(to_y, self.col_y, self.col_x), z)
        self.add(piece, (piece, self.far.at[z]))
        self.side(z, jnp.logical_not(to_y), self.s_relay)

    def plane(self, z):
        self.links.recv(self.cxy.at[pl.ds(0, 2)], self.r_plane + z)
        self.add(self.zb.at[z], (self.piece(self.col, z), self.cxy.at[z], self.cxy.at[4 + z]))

    def z_first(self, i):
        here = self.here
        z = here.cross if i else here.near
        self.links.send(self.zb.at[z], self.zr.at[i], self.sz, self.rz + i, (here.b, here.near))

    def z_second(self):
        here = self.here
        self.links.recv(self.zr.at[1], self.rz + 1)
        piece = self.zb.at[here.far]
        self.add(piece, (piece, self.zr.at[1]))
        self.links.send(piece, self.zr.at[2], self.sz, self.rz + 2, (here.b, here.far))

    def z_last(self):
        links, here = self.links, self.here
        links.recv(self.zr.at[0], self.rz)
        links.recv(self.zr.at[2], self.rz + 2)
        self.add(self.fin, [self.zb.at[here.z], self.zr.at[0], self.zr.at[2]])
        if by_column(self.kind):
            links.send(self.fin.at[1 - here.c], self.last, self.s_end, self.r_end, here.sib)
        else:
            links.send(self.fin, self.last, self.s_end, self.r_end, here.swap, here.moves)

    def finish(self, out):
        links, here, kind = self.links, self.here, self.kind
        c = here.c
        if by_column(kind):
            out[:, pl.ds(pl.multiple_of(UP_N * c, 128), UP_N)] = self.fin[c]
            links.recv(self.last, self.r_end)
            out[:, pl.ds(pl.multiple_of(UP_N * (1 - c), 128), UP_N)] = self.last[...]
        else:
            links.recv(self.last, self.r_end, here.moves)

            def keep():
                out[...] = self.fin[...]

            def take():
                out[...] = self.last[...]

            when(here.stays, keep)
            when(here.moves, take)


class ColumnScatter(Scatter):
    def __init__(self, links, here, kind, refs):
        self.links, self.here, self.kind = links, here, kind
        self.grad, self.far, self.cxy, self.zb, self.zr, self.fin, self.last = refs
        self.s_first, self.s_relay, self.sz = links.alloc(), links.alloc(), links.alloc()
        self.r_far, self.r_plane, self.rz = links.alloc(4), links.alloc(4), links.alloc(3)
        self.s_far, self.s_column = links.alloc(), links.alloc()
        self.s_end, self.r_end = links.alloc(), links.alloc()
        self.col, self.col_x, self.col_y, self.col_d = here.cols(kind)
        links.drain(self.cxy.at[pl.ds(0, 7)], self.s_first)
        links.drain(self.far.at[0], self.s_relay)
        links.drain(self.far.at[0], self.s_far)
        links.drain(self.far.at[pl.ds(0, 3)], self.s_column)
        links.drain(self.zr.at[pl.ds(0, 3)], self.sz)
        links.drain(self.last, self.s_end, None if by_column(kind) else here.moves)

    def to_side(self, z, to_x, sem):
        here = self.here
        col, slot, dev = (self.col_x, z, here.dx) if to_x else (self.col_y, 4 + z, here.dy)
        self.links.send(self.piece(col, z), self.cxy.at[slot], sem, self.r_plane + z, dev)

    def send_sides(self, order):
        for z in order:
            self.to_side(z, True, self.s_first)
            if z is not self.here.z:
                self.to_side(z, False, self.s_first)

    def column_first(self):
        here = self.here
        for i, z in enumerate((here.near, here.cross)):
            self.links.send(self.piece(self.col_d, z), self.far.at[i], self.s_column, self.r_far + i, (here.b, here.near))

    def column_second(self):
        here = self.here
        self.links.recv(self.far.at[1], self.r_far + 1)
        piece = self.piece(self.col_d, here.far)
        self.add(piece, (piece, self.far.at[1]))
        self.links.send(piece, self.far.at[2], self.s_column, self.r_far + 2, (here.b, here.far))

    def column_last(self):
        here = self.here
        self.links.recv(self.far.at[0], self.r_far)
        self.links.recv(self.far.at[2], self.r_far + 2)
        piece = self.piece(self.col_d, here.z)
        self.add(piece, (piece, self.far.at[0], self.far.at[2]))
        self.links.send(piece, self.far.at[3], self.s_far, self.r_far + 3, here.dx)

    def relay_own(self):
        here = self.here
        self.links.recv(self.far.at[3], self.r_far + 3)
        piece = self.piece(self.col_y, here.z)
        self.add(piece, (piece, self.far.at[3]))
        self.to_side(here.z, False, self.s_relay)


class PairScatter:
    def __init__(self, links, here, kind, refs):
        self.links, self.here, self.kind = links, here, kind
        self.grad, self.cy, self.zb, self.zr, self.fin, self.last = refs
        self.sy, self.ry = links.alloc(), links.alloc(4)
        self.sz, self.rz = links.alloc(), links.alloc(3)
        self.s_end, self.r_end = links.alloc(), links.alloc()
        links.drain(self.cy, self.sy)
        links.drain(self.zr.at[pl.ds(0, 3)], self.sz)
        links.drain(self.last.at[pl.ds(0, 3)], self.s_end)

    def add(self, dst, terms):
        add_blocks(dst, terms, [(i, j) for i in range(2) for j in range(2)])

    def send(self, z):
        here = self.here
        self.links.send(self.grad.at[1 - here.y, :, :, z], self.cy.at[z], self.sy, self.ry + z, here.dy)

    def plane(self, z):
        self.links.recv(self.cy.at[z], self.ry + z)
        self.add(self.zb.at[z], (self.grad.at[self.here.y, :, :, z], self.cy.at[z]))

    def z_first(self, i):
        here = self.here
        z = here.cross if i else here.near
        self.links.send(self.zb.at[z], self.zr.at[i], self.sz, self.rz + i, (here.b, here.near))

    def z_second(self):
        here = self.here
        self.links.recv(self.zr.at[1], self.rz + 1)
        piece = self.zb.at[here.far]
        self.add(piece, (piece, self.zr.at[1]))
        self.links.send(piece, self.zr.at[2], self.sz, self.rz + 2, (here.b, here.far))

    def z_last(self):
        links, here = self.links, self.here
        links.recv(self.zr.at[0], self.rz)
        links.recv(self.zr.at[2], self.rz + 2)
        self.add(self.fin, [self.zb.at[here.z], self.zr.at[0], self.zr.at[2]])
        x, c = here.x, here.c
        slot = self.last.at[here.group]
        links.send(self.fin.at[1 - x, c], slot, self.s_end, self.r_end, here.dx)
        links.send(self.fin.at[1 - x, 1 - c], slot, self.s_end, self.r_end, here.dx_other)
        links.send(self.fin.at[x, 1 - c], slot, self.s_end, self.r_end, here.sib)

    def finish(self, out):
        self.last[self.here.group] = self.fin[self.here.x, self.here.c]
        self.links.recv(self.last.at[pl.ds(0, 3)], self.r_end)
        for group in range(4):
            if self.kind == Q:
                out[:, GROUP * group : GROUP * (group + 1)] = self.last[group]
            else:
                for i in range(2):
                    at = DM * (i + 1) + GROUP * group
                    out[:, at : at + GROUP] = self.last[group, :, GROUP * i : GROUP * (i + 1)]


def dot(a, b):
    return jnp.dot(a, b, preferred_element_type=F32)


def dot_nt(a, b):
    return lax.dot_general(a, b, (((1,), (1,)), ((), ())), preferred_element_type=F32)


def dot_tn(a, b):
    return lax.dot_general(a, b, (((0,), (0,)), ((), ())), preferred_element_type=F32)


def row_sum(values):
    return jnp.sum(values, axis=0, keepdims=True)


def div24(n):
    return lax.shift_right_logical(n * 2731, 16)


def iota(shape, dim):
    return lax.broadcasted_iota(jnp.int32, shape, dim)


def select_24():
    n = iota((128, DM), 1)
    return (iota((128, DM), 0) == n - 24 * div24(n)).astype(BF16)


def select_96():
    n = iota((128, UP_N), 1)
    run = lax.shift_right_logical(div24(n), 2)
    return (iota((128, UP_N), 0) == 32 + n - 96 * run).astype(BF16)


def owner_24(lead):
    shape = (lead, 8, DM)
    return div24(iota(shape, 2)) == iota(shape, 0)


def owner_96():
    shape = (16, UP_N)
    return lax.shift_right_logical(div24(iota(shape, 1)), 2) == iota(shape, 0)


def exact_nt(values, select):
    high = values.astype(BF16)
    rest = values - high.astype(F32)
    mid = rest.astype(BF16)
    low = (rest - mid.astype(F32)).astype(BF16)
    return dot_nt(high, select) + dot_nt(mid, select) + dot_nt(low, select)


SCRATCH = dict(
    w_rows=((24, 3 * DM), BF16),
    w_parts=((4, 24, 3 * GROUP), BF16),
    vecs=((8, 128), F32),
    cot=((2, TOK, DM), BF16),
    b_out=((2, TOK, DM), F32),
    b_tok=((2, TOK, DM), F32),
    b_qkv=((24, 3 * DM), F32),
    b_wout=((24, DM), F32),
    b_up=((24, FF), F32),
    b_down=((96, DM), F32),
    b_vec=((8, 128), F32),
    vec_all=((32, 8, 128), F32),
    vec_rows=((8, DM), F32),
    up_row=((1, UP_N), F32),
    x_pair=((2, 2, 2, TOK, DM), BF16),
    fl_chip=((2, 2, TOK, DM), BF16),
    gf_chip=((2, 2, TOK, DM), BF16),
    ga_chip=((2, 2, TOK, DM), BF16),
    partial=((2, 2, TOK, DM), F32),
    partial_low=((2, TOK, DM), BF16),
    back0=((2, TOK, DM), BF16),
    back1=((2, TOK, DM), BF16),
    back2=((2, TOK, DM), BF16),
    tok_part=((2, 2, 2, TOK, DM), F32),
    tok_back=((2, 2, TOK, DM), F32),
    tok_send=((2, TOK, DM), BF16),
    tok_last=((2, TOK, DM), BF16),
    send_q=((PAIRS, GROUP, 256), BF16),
    qkv_t=((GROUP, SEQ), BF16),
    k_rows=((SEQ, HD), BF16),
    v_rows=((SEQ, HD), BF16),
    q_rows=((SEQ, HD), BF16),
    g_rows=((SEQ, HD), BF16),
    key_doc=((SEQ, 128), jnp.int32),
    query_doc=((1, SEQ), jnp.int32),
    scores=((SEQ, CHUNK), F32),
    weights=((SEQ, SEQ), BF16),
    total=((1, SEQ), F32),
    att_t=((HD, SEQ), F32),
    att_send=((HD, SEQ), BF16),
    mix_in=((12, HD, 128), BF16),
    g_send=((12, HD, 128), BF16),
    g_t=((HD, SEQ), BF16),
    gn_t=((HD, SEQ), BF16),
    corr=((1, SEQ), F32),
    ds=((CHUNK, SEQ), BF16),
    dq_t=((HD, SEQ), F32),
    d_send=((GROUP, SEQ), BF16),
    d_in=((PAIRS, GROUP, 256), BF16),
    mixed_t=((HALF, 2 * 128), BF16),
    first=((2 * TOK, DM), F32),
    normed1=((2 * TOK, DM), F32),
    inv1=((2 * TOK, 1), F32),
    active=((4 * TOK, UP_N), BF16),
    slope=((4 * TOK, UP_N), F32),
    gh=((4 * TOK, UP_N), BF16),
    gh2=((2 * TOK, DM), F32),
    gh1=((2 * TOK, DM), F32),
    gp_kv=((8 * TOK, 2 * GROUP), BF16),
    gp_q=((8 * TOK, GROUP), BF16),
    vec_grad=((8, DM), F32),
    up_grad=((1, UP_N), F32),
    vec_send=((32, 8, 128), F32),
    vec_recv=((32, 8, 128), F32),
)


def sum_scratch(kind):
    piece = piece_shape(kind)
    if kind in (KV, Q):
        low = [SHAPES[kind]] + [(4,) + piece] * 3
        last = (4,) + piece[2:]
    else:
        low = [SHAPES[kind], (4,) + piece, (8,) + piece, (4,) + piece, (4,) + piece]
        last = piece[1:] if by_column(kind) else piece
    return [(shape, BF16) for shape in low] + [(piece, F32), (last, F32)]


GATHERED = (QKV, OUT, UP, DOWN)
SUMMED = (OUT, UP, DOWN, KV, Q)
N_SEM = 181


def all_scratch():
    shapes = list(SCRATCH.values())
    shapes += [(SHAPES[kind], BF16) for kind in GATHERED]
    for kind in SUMMED:
        shapes += sum_scratch(kind)
    shapes += [((24,), BF16)] * 8 + [((96,), BF16)]
    return [pltpu.VMEM(shape, dtype) for shape, dtype in shapes] + [pltpu.SemaphoreType.DMA((N_SEM,))]


def layer_kernel(
    tokens, starts, w_qkv, w_out, w_up, w_down,
    v0, v1, v2, v3, v4, v5, v6, v7, v8, cotangent,
    o_out, o_tok, o_qkv, o_wout, o_up, o_down, o_vec,
    *scratch,
):
    vec_in = (v0, v1, v2, v3, v4, v5, v6, v7, v8)
    m = SimpleNamespace(**dict(zip(SCRATCH, scratch)))
    at = len(SCRATCH)
    gathered = scratch[at : at + 4]
    at += 4
    summed = []
    for kind in SUMMED:
        n = len(sum_scratch(kind))
        summed.append(scratch[at : at + n])
        at += n
    vec_rows_in = scratch[at : at + 9]
    sems = scratch[-1]
    here = Place()
    links = Links(sems, here)
    b, z, c, x = here.b, here.z, here.c, here.x
    line, chip, group = here.line, here.chip, here.group
    g_qkv = PairGather(links, here, gathered[0])
    g_out, g_up, g_down = [Gather(links, here, kind, ref) for kind, ref in zip(GATHERED[1:], gathered[1:])]
    s_out, s_up, s_down = [
        make(links, here, kind, refs)
        for make, kind, refs in zip((Scatter, Scatter, ColumnScatter), SUMMED[:3], summed[:3])
    ]
    s_kv, s_q = [PairScatter(links, here, kind, refs) for kind, refs in zip(SUMMED[3:], summed[3:])]
    ahead = (g_out, g_up)

    def peer(d):
        other = lax.rem(line + d, 32)
        return (lax.div(other, 4), lax.rem(other, 4))

    x_pair = m.x_pair

    def up_part(which):
        return w_up.at[:, pl.ds(pl.multiple_of(UP_N * which, 128), UP_N)]

    qkv_wait = links.local(w_qkv, m.w_rows)
    vec_waits = [links.local(src, dst) for src, dst in zip(vec_in, vec_rows_in)]
    x_wait = links.local(tokens, x_pair.at[:, x, c])
    up_wait = links.local(up_part(c), g_up.ref.at[g_up.col, c, z])
    row_waits = [
        links.local(shard, gather.ref.at[gather.col, z], here.stays)
        for gather, shard in ((g_out, w_out), (g_down, w_down))
    ]
    cot_wait = links.local(cotangent, m.cot)
    m.vec_grad[...] = jnp.zeros((8, DM), F32)
    m.vecs[...] = jnp.zeros((8, 128), F32)
    for wait in vec_waits:
        wait()
    for j in range(8):
        m.vecs[j : j + 1, 0:24] = vec_rows_in[j][...].astype(F32).reshape(1, 24)
    m.vecs[0:1, 32:128] = vec_rows_in[8][...].astype(F32).reshape(1, 96)
    qkv_wait()
    for k in range(4):
        for j in range(3):
            block = m.w_rows[:, DM * j + GROUP * k : DM * j + GROUP * (k + 1)]
            m.w_parts[k, :, GROUP * j : GROUP * (j + 1)] = block

    barrier = pltpu.get_barrier_semaphore()

    def greet(d, carry):
        pl.semaphore_signal(barrier, inc=1, device_id=peer(d), device_id_type=MESH)
        return carry

    lax.fori_loop(1, 32, greet, 0)
    pl.semaphore_wait(barrier, 31)

    slot = g_qkv.ref.at[here.y, x, c, z]
    links.send(m.w_parts.at[2 * c + 1 - x], slot, g_qkv.s0, g_qkv.r0, here.dx)
    links.send(m.w_parts.at[2 * (1 - c) + 1 - x], slot, g_qkv.s0, g_qkv.r0, here.dx_other)
    links.send(m.w_parts.at[2 * (1 - c) + x], slot, g_qkv.s0, g_qkv.r0, here.sib)
    x_sem = links.alloc(6)
    own_x = x_pair.at[:, x, c]
    links.send(tokens, own_x, x_sem, x_sem + 1, here.dx)
    links.send(tokens, own_x, x_sem + 2, x_sem + 3, here.sib)
    links.drain(own_x, x_sem)
    links.drain(own_x, x_sem + 2)
    up_slot = g_up.ref.at[g_up.col, c, z]
    links.send(up_part(1 - c), up_slot, g_up.s0, g_up.r0, here.sib)
    links.drain(up_slot, g_up.s0)
    for gather, shard in ((g_out, w_out), (g_down, w_down)):
        slot = gather.ref.at[2 * x + c, z]
        links.send(shard, slot, gather.s0, gather.r0, here.swap, here.moves)
        links.drain(slot, gather.s0, here.moves)
    vec_sem = links.alloc(4)
    vec_all = m.vec_all

    def vec_copy(d):
        return links.make(m.vecs, vec_all.at[line], vec_sem, vec_sem + 1, peer(d))

    def vec_start(d, carry):
        vec_copy(d).start()
        return carry

    lax.fori_loop(1, 32, vec_start, 0)
    vec_all[line] = m.vecs[...]
    g_qkv.ref[here.y, x, c, z] = m.w_parts[group]
    for wait in (x_wait, up_wait, *row_waits, cot_wait):
        wait()

    g_qkv.first_wait()
    g_qkv.own_z()
    g_qkv.spread(z)
    for gather in ahead:
        gather.first_wait()
        gather.own_plane()

    def documents():
        def position(n):
            z_part = lax.shift_left(jnp.bitwise_and(lax.shift_right_logical(n, 8), 3), 6)
            xc_part = lax.shift_left(jnp.bitwise_and(lax.shift_right_logical(n, 6), 3), 8)
            y_part = lax.shift_left(lax.shift_right_logical(n, 10), 10)
            return y_part + xc_part + z_part + jnp.bitwise_and(n, 63)

        def doc_of(n):
            place = position(n)
            doc = jnp.zeros(place.shape, jnp.int32)
            for j in range(starts.shape[1]):
                doc = doc + (starts[here.part, j] <= place).astype(jnp.int32)
            return doc

        m.query_doc[...] = doc_of(iota((1, SEQ), 1))

        def rows(i, carry):
            start = pl.multiple_of(i * 256, 256)
            m.key_doc[pl.ds(start, 256), :] = doc_of(iota((256, 128), 0) + i * 256)
            return carry

        lax.fori_loop(0, SEQ // 256, rows, 0)

    when(here.active, documents)

    other_x = x_pair.at[:, 1 - x, c]
    links.recv(other_x, x_sem + 1)
    links.send(other_x, other_x, x_sem + 4, x_sem + 5, here.sib)
    links.drain(other_x, x_sem + 4)
    g_qkv.land(here.far)
    g_qkv.hop()
    g_qkv.spread(here.far)
    for gather in ahead:
        gather.own_z()
    many = vec_all.at[pl.ds(0, 31)]
    links.sent(many, vec_sem)
    links.recv(many, vec_sem + 1)
    spread = dot(vec_all[...].reshape(256, 128).astype(BF16), select_24()).reshape(32, 8, DM)
    m.vec_rows[...] = jnp.sum(jnp.where(owner_24(32), spread, 0.0), axis=0)
    spread = dot(vec_all[pl.ds(16 * c, 16), 0, :].astype(BF16), select_96())
    m.up_row[...] = row_sum(jnp.where(owner_96(), spread, 0.0))

    def vector(j):
        return m.vec_rows[j : j + 1, :]

    def vector_group(j):
        total = jnp.zeros((1, GROUP), F32)
        for k in range(4):
            total = total + jnp.where(group == k, m.vec_rows[j : j + 1, GROUP * k : GROUP * (k + 1)], 0.0)
        return total

    g_qkv.land(here.near)
    g_qkv.spread(here.near)
    for gather in ahead:
        gather.relay(z)
    g_qkv.land(here.cross)
    g_qkv.spread(here.cross)
    for gather in ahead:
        gather.land(here.far)
        gather.hop()
        gather.spread(here.far)
    links.recv(x_pair.at[:, x, 1 - c], x_sem + 3)
    links.recv(x_pair.at[:, 1 - x, 1 - c], x_sem + 5)
    g_qkv.done()

    def weight_qkv():
        return g_qkv.ref[...].reshape(DM, 3 * GROUP)

    def x_rows():
        return x_pair[...].reshape(8 * TOK, DM)

    chip_lanes = pl.ds(pl.multiple_of(chip * 128, 128), 128)
    seat_lanes = pl.ds(pl.multiple_of(here.seat * 256, 256), 256)
    idle = jnp.logical_not(here.active)

    def seat_dev(y_to, z_to, x_to):
        return (4 * y_to + 2 * x_to + c, z_to)

    send_q, qkv_t = m.send_q, m.qkv_t
    q_sem = links.alloc(2)
    bias = jnp.concatenate([vector_group(0), jnp.zeros((1, GROUP), F32), vector_group(1)], axis=1)
    for part in range(MB):
        rows = (dot(x_pair[part].reshape(4 * TOK, DM), weight_qkv()) + bias).astype(BF16)
        turned = rows.T
        for i in range(3):
            for j in range(3):
                block = turned[GROUP * j + HD * i : GROUP * j + HD * (i + 1), :]
                if j == 0:
                    block = block * jnp.asarray(HD ** (-0.5), BF16)
                send_q[3 * part + i, HD * j : HD * (j + 1), :] = block
            pair = 3 * part + i
            other = jnp.logical_not(both(here.active, here.pair == pair))
            dev = seat_dev(*SEATS[pair], x)
            links.send(send_q.at[pair], qkv_t.at[:, seat_lanes], q_sem, q_sem + 1, dev, other)

    links.drain(send_q.at[pl.ds(0, PAIRS - 1)], q_sem, here.active)
    links.drain(send_q, q_sem, idle)

    def own_q():
        qkv_t[:, seat_lanes] = send_q[here.pair]

    when(here.active, own_q)

    class ToSeats:
        def __init__(self, src_of, dst_of, slot, slots, seats, own):
            self.src_of, self.dst_of, self.slot, self.slots = src_of, dst_of, slot, slots
            self.seats, self.own = seats, own
            self.s, self.r = links.alloc(), links.alloc()
            self.width = SEQ // seats

        def start(self, other):
            start = pl.multiple_of(self.width * other, self.width)
            src, dst = self.src_of(pl.ds(start, self.width)), self.dst_of(self.slot)
            if self.seats == 16:
                place, x_to, mine = lax.div(other, 2), lax.rem(other, 2), chip
            else:
                place, x_to, mine = other, x, here.seat
            dev = seat_dev(lax.div(place, 4), lax.rem(place, 4), x_to)
            links.send(src, dst, self.s, self.r, dev, mine != other)

        def finish(self):
            links.drain(self.src_of(pl.ds(0, SEQ - self.width)), self.s, here.active)
            when(here.active, self.own)

        def wait(self):
            links.recv(self.dst_of(pl.ds(0, self.slots - 1)), self.r, here.active)
            links.recv(self.dst_of(pl.ds(0, self.slots)), self.r, idle)

    g_down.first_wait()
    g_down.own_plane()
    for gather in ahead:
        gather.land(here.near)
        gather.spread(here.near)
    for gather in ahead:
        gather.relay(here.far)
    for gather in ahead:
        gather.land(here.cross)
        gather.spread(here.cross)
    links.recv(qkv_t.at[:, pl.ds(0, SEQ - 256)], q_sem + 1, here.active)
    g_down.own_z()
    for gather in ahead:
        gather.relay(here.near)
    g_down.relay(z)

    weights = m.weights
    mix_slot = 6 * here.part + 3 * x + here.pair - 3 * here.part

    def own_mix():
        m.mix_in[mix_slot] = m.att_send[:, chip_lanes]

    mix = ToSeats(
        lambda lanes: m.att_send.at[:, lanes], lambda slot: m.mix_in.at[slot], mix_slot, 12, 16, own_mix
    )

    def turn_keys():
        m.k_rows[...] = qkv_t[HD : 2 * HD, :].T
        m.v_rows[...] = qkv_t[2 * HD : 3 * HD, :].T
        m.q_rows[...] = qkv_t[0:HD, :].T

    when(here.active, turn_keys)

    def attend(step):
        i = 4 * lax.rem(step, 2) + lax.div(step, 2)
        lanes = pl.ds(pl.multiple_of(i * CHUNK, CHUNK), CHUNK)
        query = qkv_t[0:HD, lanes]
        doc = m.query_doc[:, lanes]
        top = None
        for k in range(8):
            rows = slice(256 * k, 256 * (k + 1))
            key_doc = m.key_doc[rows, :]
            same = jnp.concatenate([key_doc, key_doc], axis=1) == doc
            scores = jnp.where(same, dot(m.k_rows[rows, :], query), NEG)
            m.scores[rows, :] = scores
            here_top = jnp.max(scores, axis=0, keepdims=True)
            top = here_top if top is None else jnp.maximum(top, here_top)
        total = None
        for k in range(8):
            rows = slice(256 * k, 256 * (k + 1))
            grown = jnp.exp(m.scores[rows, :] - top)
            weights[rows, lanes] = grown.astype(BF16)
            part_sum = row_sum(grown)
            total = part_sum if total is None else total + part_sum
        numer = dot(qkv_t[2 * HD : 3 * HD, :], weights[:, lanes])
        attended = numer / total
        m.total[:, lanes] = total
        m.att_t[:, lanes] = attended
        m.att_send[:, lanes] = attended.astype(BF16)
        mix.start(2 * i)
        mix.start(2 * i + 1)

    def some(body, first, last):
        def run():
            def one(i, carry):
                body(i)
                return carry

            lax.fori_loop(first, last, one, 0)

        when(here.active, run)

    some(attend, 0, 4)
    for gather in ahead:
        gather.relay(here.cross)
    g_down.land(here.far)
    g_down.hop()
    g_down.spread(here.far)
    g_down.land(here.near)
    g_down.spread(here.near)
    some(attend, 4, 7)
    g_down.land(here.cross)
    g_down.spread(here.cross)
    some(attend, 7, 8)
    g_down.relay(here.far)
    g_down.relay(here.near)
    mix.finish()
    mix.wait()
    g_out.done()
    g_down.relay(here.cross)

    def share(buf, values):
        sem = links.alloc(2)
        buf[:, c] = values.reshape(MB, TOK, DM)
        links.send(buf.at[:, c], buf.at[:, c], sem, sem + 1, here.sib)
        links.drain(buf.at[:, c], sem)
        links.recv(buf.at[:, 1 - c], sem + 1)

    def combine(values, back):
        sem = links.alloc(2)
        partial, other = m.partial, m.partial_low
        partial[...] = values.reshape(MB, 2, TOK, DM)
        other[...] = partial[:, 1 - c].astype(BF16)
        links.send(other, back, sem, sem + 1, here.sib)
        links.recv(back, sem + 1)
        total = partial[:, c].reshape(2 * TOK, DM) + back[...].reshape(2 * TOK, DM).astype(F32)
        links.sent(other, sem)
        return total

    def norm_rows(values, gain, shift):
        center = values - jnp.mean(values, axis=-1, keepdims=True)
        inverse = lax.rsqrt(jnp.mean(center * center, axis=-1, keepdims=True) + EPS)
        normed = center * inverse
        return normed * gain + shift, normed, inverse

    def norm_back(upstream, normed, inverse, gain):
        scaled = upstream * gain
        return inverse * (
            scaled
            - jnp.mean(scaled, axis=-1, keepdims=True)
            - normed * jnp.mean(scaled * normed, axis=-1, keepdims=True)
        )

    mixed_t = m.mixed_t
    mixed = []
    for part in range(MB):
        piece = m.mix_in[6 * part : 6 * part + 6].reshape(HALF, 128)
        mixed_t[:, 128 * part : 128 * (part + 1)] = piece
        mixed.append(piece.T)
    mixed = jnp.concatenate(mixed, axis=0)

    def weight_out():
        return g_out.ref[...].reshape(HALF, DM)

    attn = combine(dot(mixed, weight_out()), m.back0) + vector(2)
    own_tokens = x_pair[:, x, c].reshape(2 * TOK, DM).astype(F32)
    first, normed_one, inverse_one = norm_rows(own_tokens + attn, vector(3), vector(4))
    m.first[...] = first
    m.normed1[...] = normed_one
    m.inv1[...] = inverse_one
    share(m.fl_chip, first.astype(BF16))

    g_up.done()
    def fl_rows():
        return m.fl_chip[...].reshape(4 * TOK, DM)

    def weight_up(j):
        return g_up.ref[:, :, :, :, HALF * j : HALF * (j + 1)].reshape(DM, HALF)

    def weight_down(j):
        return g_down.ref[j].reshape(HALF, DM)

    for j in range(4):
        lanes = slice(HALF * j, HALF * (j + 1))
        hidden = dot(fl_rows(), weight_up(j)) + m.up_row[:, lanes]
        cdf = 0.5 * (1.0 + lax.erf(hidden * (0.5**0.5)))
        m.slope[:, lanes] = cdf + hidden * (jnp.exp(-0.5 * hidden * hidden) * 0.3989422804014327)
        m.active[:, lanes] = (hidden * cdf).astype(BF16)
    g_down.done()
    ffn = None
    for j in range(4):
        lanes = slice(HALF * j, HALF * (j + 1))
        term = dot(m.active[:, lanes], weight_down(j))
        ffn = term if ffn is None else ffn + term
    ffn = combine(ffn, m.back1) + vector(5)
    result, normed_two, inverse_two = norm_rows(m.first[...] + ffn, vector(6), vector(7))
    m.b_out[...] = result.reshape(MB, TOK, DM)
    links.put(m.b_out, o_out)

    targets = (here.near, here.cross, here.far, z)
    vec_grad = m.vec_grad
    grad_result = m.cot[...].reshape(2 * TOK, DM).astype(F32)
    vec_grad[6:7, :] = row_sum(grad_result * normed_two)
    vec_grad[7:8, :] = row_sum(grad_result)
    grad_two = norm_back(grad_result, normed_two, inverse_two, vector(6))
    m.gh2[...] = grad_two
    grad_ffn = grad_two.astype(BF16)
    vec_grad[5:6, :] = row_sum(grad_ffn.astype(F32))
    share(m.gf_chip, grad_ffn)

    def gf_rows():
        return m.gf_chip[...].reshape(4 * TOK, DM)

    for j in range(4):
        lanes = slice(HALF * j, HALF * (j + 1))
        s_down.grad[j] = dot_tn(m.active[:, lanes], gf_rows()).astype(BF16).reshape(4, 96, DM)
    s_down.send_sides(targets)
    s_down.column_first()
    grad_first = None
    for j in range(4):
        lanes = slice(HALF * j, HALF * (j + 1))
        grad_active = dot_nt(gf_rows(), weight_down(j))
        grad_hidden = (grad_active * m.slope[:, lanes]).astype(BF16)
        m.gh[:, lanes] = grad_hidden
        m.up_grad[:, lanes] = row_sum(grad_hidden.astype(F32))
    for j in range(4):
        lanes = slice(HALF * j, HALF * (j + 1))
        term = dot_nt(m.gh[:, lanes], weight_up(j))
        grad_first = term if grad_first is None else grad_first + term
    grad_first = m.gh2[...] + combine(grad_first, m.back2)
    normed_one = m.normed1[...]
    vec_grad[3:4, :] = row_sum(grad_first * normed_one)
    vec_grad[4:5, :] = row_sum(grad_first)
    grad_one = norm_back(grad_first, normed_one, m.inv1[...], vector(3))
    m.gh1[...] = grad_one
    grad_attn = grad_one.astype(BF16)
    vec_grad[2:3, :] = row_sum(grad_attn.astype(F32))
    share(m.ga_chip, grad_attn)

    def ga_rows():
        return m.ga_chip[...].reshape(4 * TOK, DM)

    turned = dot_nt(ga_rows(), weight_out()).astype(BF16).T
    for part in range(MB):
        m.g_send[6 * part : 6 * part + 6] = turned[:, 128 * part : 128 * (part + 1)].reshape(6, HD, 128)
    g_t = m.g_t
    g_sem = links.alloc(2)
    for slot in range(12):
        part, head = slot // 6, slot % 6
        pair, x_to = 3 * part + head % 3, head // 3
        mine = both(here.active, both(here.pair == pair, x == x_to))
        dev = seat_dev(*SEATS[pair], x_to)
        links.send(m.g_send.at[slot], g_t.at[:, chip_lanes], g_sem, g_sem + 1, dev, jnp.logical_not(mine))
    links.drain(m.g_send.at[pl.ds(0, 11)], g_sem, here.active)
    links.drain(m.g_send, g_sem, idle)

    def own_g():
        g_t[:, chip_lanes] = m.g_send[mix_slot]

    when(here.active, own_g)
    for j in range(4):
        lanes = slice(HALF * j, HALF * (j + 1))
        s_up.grad[:, :, :, :, lanes] = (
            dot_tn(fl_rows(), m.gh[:, lanes]).astype(BF16).reshape(4, 2, 4, 24, HALF)
        )
    s_out.grad[...] = dot(mixed_t[...], ga_rows()).astype(BF16).reshape(SHAPES[OUT])
    s_up.send_far(targets)
    s_out.send_far(targets)
    s_up.send_sides(targets)
    s_out.send_sides(targets)

    def planes(scatter, order=targets):
        for i, t in enumerate(order):
            scatter.plane(t)
            if i < 2:
                scatter.z_first(i)

    s_down.column_second()
    links.recv(g_t.at[:, pl.ds(0, SEQ - 128)], g_sem + 1, here.active)
    planes(s_down, targets[:3])

    d_send, d_in = m.d_send, m.d_in

    def own_kv():
        d_in[here.pair, HD : 3 * HD, :] = d_send[HD : 3 * HD, seat_lanes]

    def own_dq():
        d_in[here.pair, 0:HD, :] = d_send[0:HD, seat_lanes]

    grad_kv = ToSeats(
        lambda lanes: d_send.at[pl.ds(HD, 2 * HD), lanes], lambda slot: d_in.at[slot, pl.ds(HD, 2 * HD)],
        here.pair, PAIRS, 8, own_kv,
    )
    grad_q = ToSeats(
        lambda lanes: d_send.at[pl.ds(0, HD), lanes], lambda slot: d_in.at[slot, pl.ds(0, HD)],
        here.pair, PAIRS, 8, own_dq,
    )

    def turn_grads():
        grad = g_t[...].astype(F32)
        inverse = 1.0 / m.total[...]
        numer = grad * inverse
        m.gn_t[...] = numer.astype(BF16)
        m.g_rows[...] = numer.astype(BF16).T
        m.corr[...] = row_sum(grad * m.att_t[...]) * inverse
        m.dq_t[...] = jnp.zeros((HD, SEQ), F32)

    when(here.active, turn_grads)

    def back(k):
        keys = pl.ds(pl.multiple_of(k * CHUNK, CHUNK), CHUNK)
        value = m.v_rows[keys, :]
        for i in range(4):
            lanes = slice(512 * i, 512 * (i + 1))
            grad_weights = dot(value, m.gn_t[:, lanes])
            grown = weights[keys, lanes].astype(F32)
            m.ds[:, lanes] = (grown * (grad_weights - m.corr[:, lanes])).astype(BF16)
        ds = m.ds
        d_send[HD : 2 * HD, keys] = dot(ds[...], m.q_rows[...]).T.astype(BF16)
        d_send[2 * HD : 3 * HD, keys] = dot(weights[keys, :], m.g_rows[...]).T.astype(BF16)
        grad_kv.start(k)
        m.dq_t[...] += dot(qkv_t[HD : 2 * HD, keys], ds[...])

    some(back, 0, 4)
    s_down.column_last()
    for t in targets:
        s_up.relay(t)
    for t in targets:
        s_out.relay(t)
    some(back, 4, 8)

    def last_query():
        d_send[0:HD, :] = (m.dq_t[...] * (HD ** (-0.5))).astype(BF16)
        for other in range(8):
            grad_q.start(other)

    when(here.active, last_query)
    grad_kv.finish()
    grad_q.finish()
    s_down.relay_own()
    s_down.z_second()
    planes(s_up, targets[:2])
    grad_kv.wait()
    gp_kv, gp_q = m.gp_kv, m.gp_q
    for part in range(MB):
        heads = slice(3 * part, 3 * part + 3)
        rows = [d_in[heads, HD * j : HD * (j + 1), :].reshape(GROUP, 256) for j in (1, 2)]
        gp_kv[256 * part : 256 * (part + 1), :] = jnp.concatenate(rows, axis=0).T
    s_kv.grad[...] = dot_tn(x_rows(), gp_kv[...]).astype(BF16).reshape(SHAPES[KV])
    for t in targets:
        s_kv.send(t)
    for t in targets[2:]:
        s_up.plane(t)
    planes(s_out)
    s_down.plane(z)
    s_up.z_second()
    grad_q.wait()
    for part in range(MB):
        gp_q[256 * part : 256 * (part + 1), :] = d_in[3 * part : 3 * part + 3, 0:HD, :].reshape(GROUP, 256).T
    s_q.grad[...] = dot_tn(x_rows(), gp_q[...]).astype(BF16).reshape(SHAPES[Q])
    for t in targets:
        s_q.send(t)
    planes(s_kv)
    s_out.z_second()
    all_weights = weight_qkv()
    t_sem = links.alloc(4)
    for part in range(MB):
        rows = slice(256 * part, 256 * (part + 1))
        terms = dot_nt(gp_q[rows, :], all_weights[:, 0:GROUP]) + dot_nt(gp_kv[rows, :], all_weights[:, GROUP:])
        m.tok_part[part] = terms.reshape(2, 2, TOK, DM)
    links.send(m.tok_part.at[:, :, 1 - c], m.tok_back, t_sem, t_sem + 1, here.sib)
    links.drain(m.tok_back, t_sem)
    sum_q = row_sum(gp_q[...].astype(F32))
    sum_v = row_sum(gp_kv[:, GROUP:].astype(F32))
    for k in range(4):
        lanes = slice(GROUP * k, GROUP * (k + 1))
        vec_grad[0:1, lanes] = jnp.where(group == k, sum_q, 0.0)
        vec_grad[1:2, lanes] = jnp.where(group == k, sum_v, 0.0)
    links.recv(m.tok_back, t_sem + 1)
    for part in range(MB):
        m.tok_send[part] = (m.tok_part[part, 1 - x, c] + m.tok_back[part, 1 - x]).astype(BF16)
    links.send(m.tok_send, m.tok_last, t_sem + 2, t_sem + 3, here.dx)
    links.drain(m.tok_send, t_sem + 2)

    planes(s_q)
    s_kv.z_second()
    s_q.z_second()
    vec_send, vec_recv = m.vec_send, m.vec_recv
    spread = jnp.where(owner_24(32), vec_grad[...][None], 0.0).reshape(256, DM)
    vec_send[...] = exact_nt(spread, select_24()).reshape(32, 8, 128)
    spread = jnp.where(owner_96(), m.up_grad[...], 0.0)
    own_lines = pl.ds(16 * c, 16)
    vec_send[own_lines, 0, :] = vec_send[own_lines, 0, :] + exact_nt(spread, select_96())

    def grad_start(d, carry):
        other = lax.rem(line + d, 32)
        links.make(vec_send.at[other], vec_recv.at[line], vec_sem + 2, vec_sem + 3, peer(d)).start()
        return carry

    lax.fori_loop(1, 32, grad_start, 0)
    vec_recv[line] = vec_send[line]

    s_kv.z_last()
    s_down.z_last()
    s_out.z_last()
    s_up.z_last()
    s_q.z_last()
    links.recv(m.tok_last, t_sem + 3)
    for part in range(MB):
        rows = slice(TOK * part, TOK * (part + 1))
        own = m.tok_part[part, x, c] + m.tok_back[part, x]
        m.b_tok[part] = m.gh1[rows, :] + (own + m.tok_last[part].astype(F32))
    links.put(m.b_tok, o_tok)
    many_send, many_recv = vec_send.at[pl.ds(0, 31)], vec_recv.at[pl.ds(0, 31)]
    links.sent(many_send, vec_sem + 2)
    links.recv(many_recv, vec_sem + 3)
    m.b_vec[...] = jnp.sum(vec_recv[...], axis=0)
    links.put(m.b_vec, o_vec)
    s_down.finish(m.b_down)
    links.put(m.b_down, o_down)
    s_out.finish(m.b_wout)
    links.put(m.b_wout, o_wout)
    s_up.finish(m.b_up)
    links.put(m.b_up, o_up)
    s_kv.finish(m.b_qkv)
    s_q.finish(m.b_qkv)
    links.put(m.b_qkv, o_qkv)
    links.finish()


def place_kernel(*refs):
    ins, big_out, vec_out = refs[0:7], refs[7:13], refs[13:22]
    held, rows, sems = refs[22:29], refs[29:38], refs[38]
    loads = [pltpu.make_async_copy(src, dst, sems.at[i]) for i, (src, dst) in enumerate(zip(ins, held))]
    for load in reversed(loads):
        load.start()
    stores = [pltpu.make_async_copy(src, dst, sems.at[7 + i]) for i, (src, dst) in enumerate(zip(held, big_out))]
    stores += [pltpu.make_async_copy(src, dst, sems.at[13 + i]) for i, (src, dst) in enumerate(zip(rows, vec_out))]
    loads[6].wait()
    for j in range(8):
        rows[j][...] = held[6][j, 0:24]
    rows[8][...] = held[6][0, 32:128]
    for store in stores[6:]:
        store.start()
    for load, store in zip(loads, stores[:6]):
        load.wait()
        store.start()
    for store in stores:
        store.wait()


def fused(
    tokens, starts, w_qkv, bias_q, bias_v, w_out, bias_out, gain_one, shift_one,
    w_up, bias_up, w_down, bias_down, gain_two, shift_two, cotangent,
):
    anywhere = pl.BlockSpec(memory_space=pl.ANY)
    vectors = (bias_q, bias_v, bias_out, gain_one, shift_one, bias_down, gain_two, shift_two, bias_up)
    big = [tokens.shape, tokens.shape, w_qkv.shape, w_out.shape, w_up.shape, w_down.shape]
    big = [jax.ShapeDtypeStruct(shape, F32) for shape in big]
    small = [jax.ShapeDtypeStruct(vector.shape, F32) for vector in vectors]
    made = pl.pallas_call(
        layer_kernel,
        name="layer",
        out_shape=big + [jax.ShapeDtypeStruct((8, 128), F32)],
        in_specs=[anywhere, pl.BlockSpec(memory_space=pltpu.SMEM)] + [anywhere] * 14,
        out_specs=[anywhere] * 7,
        scratch_shapes=all_scratch(),
        compiler_params=pltpu.CompilerParams(
            collective_id=0, has_side_effects=True, vmem_limit_bytes=63 * 2**20
        ),
    )(tokens, starts, w_qkv, w_out, w_up, w_down, *vectors, cotangent)
    placed = pl.pallas_call(
        place_kernel,
        name="place",
        out_shape=big + small,
        in_specs=[anywhere] * 7,
        out_specs=[anywhere] * 15,
        scratch_shapes=[pltpu.VMEM(array.shape, F32) for array in (*made, *vectors)]
        + [pltpu.SemaphoreType.DMA((22,))],
    )(*made)
    out, tok, g_qkv, g_wout, g_up, g_down, bq, bv, bo, g1, s1, bd, g2, s2, bup = placed
    return (out, tok, g_qkv, bq, bv, g_wout, bo, g1, s1, g_up, bup, g_down, bd, g2, s2)


def solution(mesh):
    small = dict(mesh.shape) == {BLK: 8, HEAD: 4}
    return jax.shard_map(
        fused if small else per_device,
        mesh=mesh,
        in_specs=(
            P(None, BOTH, None),
            P(),
            P(BOTH, None),
            P(BOTH),
            P(BOTH),
            P(BOTH, None),
            P(BOTH),
            P(BOTH),
            P(BOTH),
            P(BOTH, None),
            P(BOTH),
            P(BOTH, None),
            P(BOTH),
            P(BOTH),
            P(BOTH),
            P(None, BOTH, None),
        ),
        out_specs=(
            P(None, BOTH, None),
            P(None, BOTH, None),
            P(BOTH, None),
            P(BOTH),
            P(BOTH),
            P(BOTH, None),
            P(BOTH),
            P(BOTH),
            P(BOTH),
            P(BOTH, None),
            P(BOTH),
            P(BOTH, None),
            P(BOTH),
            P(BOTH),
            P(BOTH),
        ),
        check_vma=False,
    )
```
